32 devices in a mesh: reg: 8 (over z, core), lon: 4 (over y, x).
Axes of the slice: x: 2, y: 2, z: 4, core: 2. Of those that a mesh axis runs over, the one named last changes fastest.
Arguments:
- nodes: bfloat16 [1, 4096, 512], P(None, ('reg', 'lon')), may hold values from -6 to 6
- norm_gain: float32 [512], replicated, may hold values from 0.25 to 1.75
- w_qkv: bfloat16 [512, 1536], replicated
- w_out: bfloat16 [512, 512], replicated, may hold values from -0.25 to 0.25
- w_latent: bfloat16 [512, 512], replicated, may hold values from -0.25 to 0.25
- neighbours: int32 [32, 5], P(('reg', 'lon')), may hold values from 0 to 31, as said below
- assignment: int32 [16, 1024], P('reg', 'lon'), may hold values from 0 to 4095, as said below
- psi: float32 [9, 16, 5, 5], P(None, 'reg'), may hold values from -1.2 to 1.2
- w_dec: bfloat16 [9, 512, 84], replicated, may hold values from -0.09375 to 0.09375
Outputs:
- mesh_state: bfloat16 [1, 4096, 512], P(None, ('reg', 'lon'))
- fields: bfloat16 [1, 84, 16, 1024], P(None, None, 'reg', 'lon')
The draws below stay inside these ranges and needn't reach their ends.
Inputs may be any that keep to these rules, and one draw needn't show every extreme that they name: neighbours[b, 0] = b; the other entries of a row are distinct blocks adjacent to b (diagonals included) on the grid of 8 x 4 blocks, where block b has row b // 4 and column b % 4; columns wrap around, rows do not. `assignment`: the node of cell (i, j) lies in block (i // 2) * 4 + j // 256.
All inputs are finite; a program needn't handle non-finite values.
Results may differ from the reference program's by a relative error of at most 0.011.
Values may be sent and summed in bfloat16 or wider, within the bound.
No kernel may reach another device: no remote copies, remote signals or barrier semaphores. Data moves between devices by JAX's collectives and lax.ppermute only.
A program may use at most 64 MiB of HBM per device.

```python
import jax
import jax.numpy as jnp
from jax import lax

D = 512
HEADS = 16
HEAD_DIM = 32
CH = 512
C_OUT = 84
NBAS = 9
BLK = 128
KNB = 5
MEMB = 1
LATD = 2
LOND = 256
REGIONS = 8
SECTORS = 4
NBLK = 32
NODES = 4096
LAT = 16
LON = 1024


def draw_w_qkv(key, part):
    key_base = jax.random.fold_in(key, 0)
    base = jax.random.normal(key_base, (D, 3 * D), jnp.float32) * D ** (-0.5)
    return base.astype(jnp.bfloat16)


def draw_neighbours(key, part):
    blocks = jnp.arange(NBLK, dtype=jnp.int32)
    rows = blocks // SECTORS
    cols = blocks % SECTORS
    step_rows = jnp.array([-1, -1, -1, 0, 0, 1, 1, 1], jnp.int32)
    step_cols = jnp.array([-1, 0, 1, -1, 1, -1, 0, 1], jnp.int32)
    near_rows = rows[:, None] + step_rows[None, :]
    near_cols = (cols[:, None] + step_cols[None, :]) % SECTORS
    valid = (near_rows >= 0) & (near_rows < REGIONS)
    slots = jnp.arange(8, dtype=jnp.int32)[None, :]
    scores = jax.random.randint(key, (NBLK, 8), 0, 1024, jnp.int32) * 8 + slots
    scores = jnp.where(valid, scores, 100000 + slots)
    order = jnp.argsort(scores, axis=1, stable=True)[:, :KNB - 1]
    candidates = near_rows * SECTORS + near_cols
    picked = jnp.take_along_axis(candidates, order, axis=1)
    return jnp.concatenate([blocks[:, None], picked], axis=1).astype(jnp.int32)


def draw_assignment(key, part):
    lat_index = jnp.arange(LAT, dtype=jnp.int32)[:, None]
    lon_index = jnp.arange(LON, dtype=jnp.int32)[None, :]
    owner = lat_index // LATD * SECTORS + lon_index // LOND
    offset = jax.random.randint(key, (LAT, LON), 0, BLK, jnp.int32)
    return (owner * BLK + offset).astype(jnp.int32)


def block_scale(stream_key, shape, cuts, least, top_value):
    level, own = 1.0, jax.random.fold_in(stream_key, 6)
    for dim, parts in cuts:
        heights = jnp.exp(jax.random.uniform(jax.random.fold_in(own, dim), (parts,), jnp.float32, least / len(cuts), top_value / len(cuts)))
        level = level * jnp.repeat(heights, shape[dim] // parts).reshape([-1 if axis == dim else 1 for axis in range(len(shape))])
    return level


def noise(stream_key, extent, width, reach, cuts=(), kind=jnp.bfloat16):
    level = block_scale(stream_key, extent, cuts, -0.22, 0.18) if cuts else 1.0
    values = jax.random.normal(stream_key, extent, jnp.float32) * width * level
    return jnp.minimum(jnp.maximum(values, -reach), reach).astype(kind)


def setup_inputs(seed: int = 0) -> dict:
    keys = jax.random.split(jax.random.key(seed), 10)
    return {
        "nodes": noise(keys[0], (MEMB, NODES, D), 1.0, 6.0, ((1, 32),)),
        "norm_gain": jnp.clip(1.0 + 0.15 * jax.random.normal(keys[1], (D,), jnp.float32), 0.25, 1.75),
        "w_qkv": draw_w_qkv(jax.random.fold_in(keys[9], 71), 0),
        "w_out": noise(keys[3], (D, D), D ** -0.5, 0.25),
        "w_latent": noise(keys[4], (D, CH), D ** -0.5, 0.25),
        "neighbours": draw_neighbours(jax.random.fold_in(keys[9], 71), 0),
        "assignment": draw_assignment(jax.random.fold_in(keys[9], 71), 0),
        "psi": noise(keys[7], (NBAS, LAT, 5, 5), 0.2, 1.2, ((1, 8),), jnp.float32),
        "w_dec": noise(keys[8], (NBAS, CH, C_OUT), (NBAS * CH) ** -0.5, 0.09375),
    }


def layer_norm(nodes, gain):
    values = nodes.astype(jnp.float32)
    center = values - lax.optimization_barrier(jnp.mean(values, axis=-1, keepdims=True))
    spread = lax.optimization_barrier(jnp.mean(center * center, axis=-1, keepdims=True))
    return (center * lax.rsqrt(spread + 1e-05) * gain).astype(jnp.bfloat16)

def reference(nodes, norm_gain, w_qkv, w_out, w_latent, neighbours, assignment, psi, w_dec):
    members = nodes.shape[0]
    normed = layer_norm(nodes, norm_gain)
    flat = normed.reshape(-1, D)
    projected = jnp.dot(flat, w_qkv, preferred_element_type=jnp.float32)
    queries = projected[:, :D].astype(jnp.bfloat16).reshape(members, NBLK, BLK, HEADS, HEAD_DIM)
    keyvals = projected[:, D:].astype(jnp.bfloat16).reshape(members, NBLK, BLK, 2 * D)
    scale = 1.0 / HEAD_DIM ** 0.5

    def attend(block):
        query = lax.dynamic_index_in_dim(queries, block, axis=1, keepdims=False)
        listed = lax.dynamic_index_in_dim(neighbours, block, axis=0, keepdims=False)
        chosen = jnp.take(keyvals, listed, axis=1).reshape(members, KNB * BLK, 2 * D)
        key_part = chosen[..., :D].reshape(members, KNB * BLK, HEADS, HEAD_DIM)
        value_part = chosen[..., D:].reshape(members, KNB * BLK, HEADS, HEAD_DIM)
        scores = jnp.einsum('mqhd,mkhd->mhqk', query.astype(jnp.float32), key_part.astype(jnp.float32)) * scale
        top = lax.optimization_barrier(jnp.max(scores, axis=-1, keepdims=True))
        expo = jnp.exp(scores - top)
        total = lax.optimization_barrier(jnp.sum(expo, axis=-1, keepdims=True))
        rounded = lax.optimization_barrier(expo.astype(jnp.bfloat16))
        summed = jnp.einsum('mhqk,mkhd->mhqd', rounded.astype(jnp.float32), value_part.astype(jnp.float32)) / total
        return summed.transpose(0, 2, 1, 3).reshape(members, BLK, D).astype(jnp.bfloat16)
    blocks_out = lax.map(attend, jnp.arange(NBLK, dtype=jnp.int32))
    attended = blocks_out.transpose(1, 0, 2, 3).reshape(members * NODES, D)
    state = (nodes.reshape(-1, D).astype(jnp.float32) + jnp.dot(attended, w_out, preferred_element_type=jnp.float32)).astype(jnp.bfloat16)
    latent = jax.nn.silu(jnp.dot(state, w_latent, preferred_element_type=jnp.float32)).astype(jnp.bfloat16)
    latent = latent.reshape(members, NODES, CH)
    grid = jnp.take(latent, assignment.reshape(-1).astype(jnp.int32), axis=1).reshape(members * LAT * LON, CH)

    def basis_step(total, inputs):
        taps, mixing = inputs
        mixed = jnp.dot(grid, mixing, preferred_element_type=jnp.float32).reshape(members, LAT, LON, C_OUT)
        padded = jnp.pad(mixed, ((0, 0), (2, 2), (0, 0), (0, 0)))
        padded = jnp.concatenate([padded[:, :, -2:], padded, padded[:, :, :2]], axis=2)
        for row_off in range(5):
            for col_off in range(5):
                total = total + taps[:, row_off, col_off][None, :, None, None] * padded[:, row_off:row_off + LAT, col_off:col_off + LON]
        return (total, None)
    start = jnp.zeros((members, LAT, LON, C_OUT), jnp.float32)
    total, unused = lax.scan(basis_step, start, (psi, w_dec))
    fields = total.transpose(0, 3, 1, 2).astype(jnp.bfloat16)
    return (state.reshape(members, NODES, D), fields)
```

```python
import functools
import math

import jax
import jax.numpy as jnp
from jax import lax
from jax.experimental import pallas as pl
from jax.experimental.pallas import tpu as pltpu
from jax.sharding import PartitionSpec as P

HEADS = 16
REACH = 2
SIDE = 8
LANES = 128
F32 = jnp.float32
BF16 = jnp.bfloat16
NT = (((1,), (1,)), ((), ()))

BANDS = (
    ((-2, (0,)), (-1, (0, 1))),
    ((0, (0, 1)), (1, (0, 1))),
    ((2, (0, 1)), (3, (1,))),
)
TAPS = 2 * REACH + 1


def band_blocks(band):
    return [
        (out_row, src - out_row + REACH, off)
        for src, out_rows in BANDS[band]
        for off in range(TAPS)
        for out_row in out_rows
    ]


def iota(shape, dim):
    return lax.broadcasted_iota(jnp.int32, shape, dim)


def normalise(rows, gain):
    values = rows.astype(F32)
    center = values - jnp.mean(values, axis=-1, keepdims=True)
    spread = jnp.mean(center * center, axis=-1, keepdims=True)
    return (center * lax.rsqrt(spread + 1e-05) * gain).astype(BF16)


def prepare_kernel(x_ref, gain_ref, wqkv_ref, psi_ref, dec_ref, query_ref, key_ref, value_ref, wvt_ref, *out):
    band_refs, taps_ref = out[:3], out[3]
    rows, width = x_ref.shape
    group, members = query_ref.shape[1], query_ref.shape[2] // rows
    head = group // members
    normed = normalise(x_ref[...], gain_ref[...])
    query = jnp.dot(normed, wqkv_ref[:, :width], preferred_element_type=F32)
    query_t = query.T.astype(BF16)
    mask = (iota((group, members * rows), 0) // head) == (iota((group, members * rows), 1) // rows)
    for part in range(width // group):
        piece = query_t[part * group : (part + 1) * group]
        wide = jnp.concatenate([piece] * members, axis=1)
        query_ref[part] = jnp.where(mask, wide, jnp.zeros_like(wide))
    key_ref[...] = jnp.dot(
        normed, wqkv_ref[:, width : 2 * width], preferred_element_type=F32
    ).astype(BF16)
    wvt = wqkv_ref[:, 2 * width :].astype(F32).T.astype(BF16)
    wvt_ref[...] = wvt
    value_ref[...] = lax.dot_general(wvt, normed, NT, preferred_element_type=F32).astype(BF16)

    groups, depth, channels = dec_ref.shape
    basis = psi_ref.shape[1]
    own = depth // basis
    padded = band_refs[0].shape[1] // groups
    spread = (iota((basis, depth), 1) // own == iota((basis, depth), 0)).astype(F32)
    expanded = jnp.dot(psi_ref[...], spread, preferred_element_type=F32)
    pick = iota((padded, depth), 1) % own == iota((padded, depth), 0)
    blocks = [(band, at) + item for band in range(3) for at, item in enumerate(band_blocks(band))]
    for at, (_, _, out_row, tap, off) in enumerate(blocks):
        source = (out_row * TAPS + tap) * TAPS + off
        line = jnp.broadcast_to(expanded[source : source + 1], (padded, depth))
        taps_ref[at * padded : (at + 1) * padded, :] = jnp.where(pick, line, 0.0).astype(BF16)
    for piece in range(groups):
        start = 0
        for band in range(3):
            count = band_refs[band].shape[0]
            mixed = jnp.dot(
                taps_ref[start * padded : (start + count) * padded, :],
                dec_ref[piece],
                preferred_element_type=F32,
            ).astype(BF16)
            band_refs[band][:, piece * padded : (piece + 1) * padded, :] = mixed.reshape(
                count, padded, channels
            )
            start += count


def attend_kernel(
    sectors,
    listed_ref, assign_ref, x_ref, left_ref, right_ref, up_ref, down_ref, upper_ref, lower_ref,
    gain_ref, wqkv_ref, query_ref, key_ref, value_ref, wvt_ref, wout_ref, wlat_ref,
    state_ref, latent_ref, west_ref, east_ref,
    near_ref, keys_ref, values_ref, attended_ref,
):
    rows, width = x_ref.shape
    count = listed_ref.shape[1]
    parts, group, lanes = query_ref.shape
    members = lanes // rows
    head = group // members
    reg_here, lon_here = lax.axis_index("reg"), lax.axis_index("lon")
    sources = (
        (upper_ref, 0), (up_ref, 0), (upper_ref, rows),
        (left_ref, 0), None, (right_ref, 0),
        (lower_ref, 0), (down_ref, 0), (lower_ref, rows),
    )
    slots = []
    for at in range(1, count):
        block = listed_ref[0, at]
        step_reg = block // sectors - reg_here
        step_lon = (block % sectors - lon_here + 1 + sectors) % sectors - 1
        slots.append((step_reg + 1) * 3 + step_lon + 1)
    for slot, source in enumerate(sources):
        if source is None:
            continue
        ref, start = source
        place = jnp.int32(-1)
        for at, value in enumerate(slots):
            place = jnp.where(value == slot, at, place)

        @pl.when(place >= 0)
        def _():
            near_ref[place] = ref[start : start + rows, :]

    normed = normalise(near_ref[...].reshape((count - 1) * rows, width), gain_ref[...])
    keys_ref[:rows] = key_ref[...]
    keys_ref[rows:] = jnp.dot(
        normed, wqkv_ref[:, width : 2 * width], preferred_element_type=F32
    ).astype(BF16)
    values_ref[:, :rows] = value_ref[...]
    values_ref[:, rows:] = lax.dot_general(
        wvt_ref[...], normed, NT, preferred_element_type=F32
    ).astype(BF16)
    scale = math.log2(math.e) / head**0.5
    owner = iota((group, rows), 0) // head
    for part in range(parts):
        span = slice(part * group, (part + 1) * group)
        scores = jnp.dot(keys_ref[:, span], query_ref[part], preferred_element_type=F32)
        top = jnp.max(scores, axis=0, keepdims=True)
        expo = jnp.exp2((scores - top) * scale)
        total = jnp.sum(expo, axis=0, keepdims=True)
        summed = jnp.dot(values_ref[span, :], expo.astype(BF16), preferred_element_type=F32)
        summed = summed * (1.0 / total)
        merged = None
        for member in range(members):
            piece = summed[:, member * rows : (member + 1) * rows]
            merged = piece if merged is None else jnp.where(owner == member, piece, merged)
        attended_ref[:, span] = merged.T.astype(BF16)
    state = (
        x_ref[...].astype(F32)
        + jnp.dot(attended_ref[...], wout_ref[...], preferred_element_type=F32)
    ).astype(BF16)
    state_ref[...] = state
    value = jnp.dot(state, wlat_ref[...], preferred_element_type=F32)
    latent = (value / (1.0 + jnp.exp(-value))).astype(BF16)
    latent_ref[...] = latent
    lat_rows, lon_cols = assign_ref.shape
    for ref, first in ((west_ref, 0), (east_ref, lon_cols - REACH)):
        cells = ref.shape[0]
        line, node = iota((cells, rows), 0), iota((cells, rows), 1)
        hit = jnp.zeros((cells, rows), F32)
        for row in range(lat_rows):
            for col in range(REACH):
                local = assign_ref[row, first + col] % rows
                hit = jnp.where((line == row * REACH + col) & (node == local), 1.0, hit)
        ref[...] = jnp.dot(hit.astype(BF16), latent, preferred_element_type=F32).astype(BF16)


def band_sum(band, latent, weights_ref, places, acc):
    blocks, outputs, channels = weights_ref.shape
    nodes = latent.shape[0]
    cols = places[0].shape[1]
    rows = nodes - 2 * SIDE
    shares = lax.dot_general(
        weights_ref[...].reshape(blocks * outputs, channels), latent, NT, preferred_element_type=F32
    ).astype(BF16)
    column = iota((8, cols), 1)
    node = iota((nodes, cols), 0).astype(F32)
    start = 0
    for line, (_, out_rows) in enumerate(BANDS[band]):
        for off in range(TAPS):
            step = off - REACH
            where = jnp.broadcast_to(places[line], (8, cols))
            if step:
                where = pltpu.roll(where, (-step) % cols, 1)
            reach = column + step
            where = jnp.where(reach < 0, (rows + REACH * line + reach + REACH).astype(F32), where)
            where = jnp.where(
                reach >= cols, (rows + SIDE + REACH * line + reach - cols).astype(F32), where
            )
            hot = jnp.where(node == where[:1], 1.0, 0.0).astype(BF16)
            size = len(out_rows) * outputs
            part = jnp.dot(shares[start : start + size], hot, preferred_element_type=F32)
            start += size
            for at, out_row in enumerate(out_rows):
                piece = part[at * outputs : (at + 1) * outputs]
                acc[out_row] = piece if acc[out_row] is None else acc[out_row] + piece
    return acc


def lines_of(line_ref, start, cols):
    values = line_ref[start : start + 16, :].astype(F32)
    return [values[:1, :cols], values[:1, cols:]]


def own_kernel(line_ref, latent_ref, weights_ref, out_ref):
    cols = out_ref.shape[2]
    acc = band_sum(1, latent_ref[...], weights_ref, lines_of(line_ref, 0, cols), [None, None])
    for row in range(2):
        out_ref[row] = acc[row]


def fields_kernel(
    begin, upper_ref, lower_ref, up_ref, down_ref, above_ref, below_ref, own_ref, out_ref
):
    cols = own_ref.shape[2]
    acc = [own_ref[0], own_ref[1]]
    acc = band_sum(0, up_ref[...], above_ref, lines_of(upper_ref, begin, cols), acc)
    acc = band_sum(2, down_ref[...], below_ref, lines_of(lower_ref, begin, cols), acc)
    out_ch = out_ref.shape[0]
    groups = 3
    padded, size = own_ref.shape[1] // groups, out_ch // groups
    for row in range(2):
        for piece in range(groups):
            out_ref[piece * size : (piece + 1) * size, row, :] = acc[row][
                piece * padded : piece * padded + size
            ].astype(BF16)


def whole(memory=pltpu.VMEM):
    return pl.BlockSpec(memory_space=memory)


def struct(*shape, dtype=BF16):
    return jax.ShapeDtypeStruct(shape, dtype)


def params(limit):
    return pltpu.CompilerParams(vmem_limit_bytes=limit << 20)


def cost(flops, moved):
    return pl.CostEstimate(flops=int(flops), bytes_accessed=int(moved), transcendentals=0)


def shards(nodes, norm_gain, w_qkv, w_out, w_latent, neighbours, assignment, psi, w_dec):
    _, rows, width = nodes.shape
    channels = w_latent.shape[1]
    lat_rows, lon_cols = assignment.shape
    basis, _, out_ch = w_dec.shape
    sectors = lax.axis_size("lon")
    count = neighbours.shape[1]
    x = nodes.reshape(rows, width)
    gain = norm_gain.reshape(1, width)

    def shifted(array, axis, step, wrap):
        size = lax.axis_size(axis)
        pairs = [(i, (i + step) % size) for i in range(size) if wrap or 0 <= i + step < size]
        return lax.ppermute(array, axis, pairs)

    left = shifted(x, "lon", 1, True)
    right = shifted(x, "lon", -1, True)
    up = shifted(x, "reg", 1, False)
    down = shifted(x, "reg", -1, False)

    line = (assignment % rows).astype(BF16).reshape(1, lat_rows * lon_cols)
    line = jnp.pad(line, ((0, 15), (0, 0)))
    both = jnp.concatenate([left, right, line], axis=0)
    upper = shifted(both, "reg", 1, False)
    lower = shifted(both, "reg", -1, False)

    groups, padded = 3, 32
    own = out_ch // groups
    depth = basis * own
    dec = w_dec.transpose(0, 2, 1).reshape(basis, groups, own, channels).transpose(1, 0, 2, 3)
    dec = dec.reshape(groups, depth, channels)
    taps = psi.transpose(1, 2, 3, 0).reshape(lat_rows * TAPS * TAPS, basis)
    head = width // HEADS
    members = LANES // head
    parts = HEADS // members
    sizes = [len(band_blocks(band)) for band in range(3)]
    query, key, value, wvt, above, middle, below = pl.pallas_call(
        prepare_kernel,
        in_specs=[whole()] * 5,
        out_specs=[whole()] * 7,
        out_shape=[
            struct(parts, LANES, members * rows),
            struct(rows, width),
            struct(width, rows),
            struct(width, width),
        ]
        + [struct(size, groups * padded, channels) for size in sizes],
        scratch_shapes=[pltpu.VMEM((sum(sizes) * padded, depth), BF16)],
        compiler_params=params(32),
        cost_estimate=cost(3e9, 1.2e7),
        name="prepare",
    )(x, gain, w_qkv, taps, dec)

    state, latent, west, east = pl.pallas_call(
        functools.partial(attend_kernel, sectors),
        in_specs=[whole(pltpu.SMEM)] * 2 + [whole()] * 15,
        out_specs=[whole()] * 4,
        out_shape=[struct(rows, width), struct(rows, channels), struct(16, channels), struct(16, channels)],
        scratch_shapes=[
            pltpu.VMEM((count - 1, rows, width), BF16),
            pltpu.VMEM((count * rows, width), BF16),
            pltpu.VMEM((width, count * rows), BF16),
            pltpu.VMEM((rows, width), BF16),
        ],
        compiler_params=params(32),
        cost_estimate=cost(4e9, 6e6),
        name="attend",
    )(
        neighbours, assignment, x, left, right, up, down, upper, lower,
        gain, w_qkv, query, key, value, wvt, w_out, w_latent,
    )

    from_left = shifted(east, "lon", 1, True)
    from_right = shifted(west, "lon", -1, True)
    extended = jnp.concatenate([latent, from_left[:SIDE], from_right[:SIDE]], axis=0)
    north = shifted(extended, "reg", 1, False)
    south = shifted(extended, "reg", -1, False)

    partial = pl.pallas_call(
        own_kernel,
        in_specs=[whole()] * 3,
        out_specs=whole(),
        out_shape=struct(lat_rows, groups * padded, lon_cols, dtype=F32),
        compiler_params=params(32),
        cost_estimate=cost(1e9, 2.5e6),
        name="own_band",
    )(line, extended, middle)
    fields = pl.pallas_call(
        functools.partial(fields_kernel, 2 * rows),
        in_specs=[whole()] * 7,
        out_specs=whole(),
        out_shape=struct(out_ch, lat_rows, lon_cols),
        compiler_params=params(32),
        cost_estimate=cost(2e9, 4e6),
        name="fields",
    )(upper, lower, north, south, above, below, partial)
    return (state.reshape(1, rows, width), fields.reshape(1, out_ch, lat_rows, lon_cols))


def solution(mesh):
    in_specs = (
        P(None, ("reg", "lon"), None),
        P(),
        P(),
        P(),
        P(),
        P(("reg", "lon"), None),
        P("reg", "lon"),
        P(None, "reg", None, None),
        P(),
    )
    out_specs = (P(None, ("reg", "lon"), None), P(None, None, "reg", "lon"))
    return jax.shard_map(shards, mesh=mesh, in_specs=in_specs, out_specs=out_specs, check_vma=False)
```

```python
import functools
import math

import jax
import jax.numpy as jnp
from jax import lax
from jax.experimental import pallas as pl
from jax.experimental.pallas import tpu as pltpu
from jax.sharding import PartitionSpec as P

HEADS = 16
REACH = 2
SIDE = 8
ROWS = 16
LANES = 128
F32 = jnp.float32
BF16 = jnp.bfloat16
NT = (((1,), (1,)), ((), ()))

BANDS = (
    ((-2, (0,)), (-1, (0, 1))),
    ((0, (0, 1)), (1, (0, 1))),
    ((2, (0, 1)), (3, (1,))),
)
TAPS = 2 * REACH + 1


def band_blocks(band):
    return [
        (out_row, src - out_row + REACH, off)
        for src, out_rows in BANDS[band]
        for off in range(TAPS)
        for out_row in out_rows
    ]


def iota(shape, dim):
    return lax.broadcasted_iota(jnp.int32, shape, dim)


def normalise(rows, gain):
    values = rows.astype(F32)
    center = values - jnp.mean(values, axis=-1, keepdims=True)
    spread = jnp.mean(center * center, axis=-1, keepdims=True)
    return (center * lax.rsqrt(spread + 1e-05) * gain).astype(BF16)


def prepare_kernel(x_ref, gain_ref, wqkv_ref, psi_ref, dec_ref, query_ref, key_ref, value_ref, wvt_ref, *out):
    band_refs, taps_ref = out[:3], out[3]
    rows, width = x_ref.shape
    group, members = query_ref.shape[1], query_ref.shape[2] // rows
    head = group // members
    normed = normalise(x_ref[...], gain_ref[...])
    query = jnp.dot(normed, wqkv_ref[:, :width], preferred_element_type=F32)
    query_t = query.T.astype(BF16)
    mask = (iota((group, members * rows), 0) // head) == (iota((group, members * rows), 1) // rows)
    for part in range(width // group):
        piece = query_t[part * group : (part + 1) * group]
        wide = jnp.concatenate([piece] * members, axis=1)
        query_ref[part] = jnp.where(mask, wide, jnp.zeros_like(wide))
    key_ref[...] = jnp.dot(
        normed, wqkv_ref[:, width : 2 * width], preferred_element_type=F32
    ).astype(BF16)
    wvt = wqkv_ref[:, 2 * width :].astype(F32).T.astype(BF16)
    wvt_ref[...] = wvt
    value_ref[...] = lax.dot_general(wvt, normed, NT, preferred_element_type=F32).astype(BF16)

    basis, out_ch, channels = dec_ref.shape
    depth = basis * ROWS
    spread = (iota((basis, depth), 1) // ROWS == iota((basis, depth), 0)).astype(F32)
    expanded = jnp.dot(psi_ref[...], spread, preferred_element_type=F32)
    pick = iota((ROWS, depth), 1) % ROWS == iota((ROWS, depth), 0)
    blocks = [item for band in range(3) for item in band_blocks(band)]
    for at, (out_row, tap, off) in enumerate(blocks):
        source = (out_row * TAPS + tap) * TAPS + off
        line = jnp.broadcast_to(expanded[source : source + 1], (ROWS, depth))
        taps_ref[at * ROWS : (at + 1) * ROWS, :] = jnp.where(pick, line, 0.0).astype(BF16)
    for first in range(0, out_ch, ROWS):
        size = min(ROWS, out_ch - first)
        pieces = []
        for base in range(basis):
            pieces.append(dec_ref[base, first : first + size, :])
            if size < ROWS:
                pieces.append(jnp.zeros((ROWS - size, channels), BF16))
        mixing = jnp.concatenate(pieces, axis=0)
        start = 0
        for band_ref in band_refs:
            count = band_ref.shape[0]
            mixed = jnp.dot(
                taps_ref[start * ROWS : (start + count) * ROWS, :], mixing, preferred_element_type=F32
            ).astype(BF16)
            band_ref[:, first : first + ROWS, :] = mixed.reshape(count, ROWS, channels)
            start += count


def attend_kernel(
    sectors,
    listed_ref, assign_ref, x_ref, left_ref, right_ref, inner_ref, outer_ref,
    gain_ref, wqkv_ref, query_ref, key_ref, value_ref, wvt_ref, wout_ref, wlat_ref,
    state_ref, latent_ref, west_ref, east_ref,
    near_ref, keys_ref, values_ref, attended_ref,
):
    rows, width = x_ref.shape
    count = listed_ref.shape[1]
    parts, group, lanes = query_ref.shape
    members = lanes // rows
    head = group // members
    reg_here, lon_here = lax.axis_index("reg"), lax.axis_index("lon")
    odd = reg_here % 2
    inner, outer = 6 * (1 - odd), 6 * odd
    sources = [(left_ref, 0, 3), (right_ref, 0, 5)]
    for ref, base in ((inner_ref, inner), (outer_ref, outer)):
        sources += [(ref, 0, base), (ref, rows, base + 1), (ref, 2 * rows, base + 2)]
    slots = []
    for at in range(1, count):
        block = listed_ref[0, at]
        step_reg = block // sectors - reg_here
        step_lon = (block % sectors - lon_here + 1 + sectors) % sectors - 1
        slots.append((step_reg + 1) * 3 + step_lon + 1)
    for ref, start, slot in sources:
        place = jnp.int32(-1)
        for at, value in enumerate(slots):
            place = jnp.where(value == slot, at, place)

        @pl.when(place >= 0)
        def _():
            near_ref[place] = ref[start : start + rows, :]

    normed = normalise(near_ref[...].reshape((count - 1) * rows, width), gain_ref[...])
    keys_ref[:rows] = key_ref[...]
    keys_ref[rows:] = jnp.dot(
        normed, wqkv_ref[:, width : 2 * width], preferred_element_type=F32
    ).astype(BF16)
    values_ref[:, :rows] = value_ref[...]
    values_ref[:, rows:] = lax.dot_general(
        wvt_ref[...], normed, NT, preferred_element_type=F32
    ).astype(BF16)
    scale = math.log2(math.e) / head**0.5
    owner = iota((group, rows), 0) // head
    for part in range(parts):
        span = slice(part * group, (part + 1) * group)
        scores = jnp.dot(keys_ref[:, span], query_ref[part], preferred_element_type=F32)
        top = jnp.max(scores, axis=0, keepdims=True)
        expo = jnp.exp2((scores - top) * scale)
        total = jnp.sum(expo, axis=0, keepdims=True)
        summed = jnp.dot(values_ref[span, :], expo.astype(BF16), preferred_element_type=F32)
        summed = summed * (1.0 / total)
        merged = None
        for member in range(members):
            piece = summed[:, member * rows : (member + 1) * rows]
            merged = piece if merged is None else jnp.where(owner == member, piece, merged)
        attended_ref[:, span] = merged.T.astype(BF16)
    state = (
        x_ref[...].astype(F32)
        + jnp.dot(attended_ref[...], wout_ref[...], preferred_element_type=F32)
    ).astype(BF16)
    state_ref[...] = state
    value = jnp.dot(state, wlat_ref[...], preferred_element_type=F32)
    latent = (value / (1.0 + jnp.exp(-value))).astype(BF16)
    latent_ref[...] = latent
    lat_rows, lon_cols = assign_ref.shape
    for ref, first in ((west_ref, 0), (east_ref, lon_cols - REACH)):
        cells = ref.shape[0]
        line, node = iota((cells, rows), 0), iota((cells, rows), 1)
        hit = jnp.zeros((cells, rows), F32)
        for row in range(lat_rows):
            for col in range(REACH):
                local = assign_ref[row, first + col] % rows
                hit = jnp.where((line == row * REACH + col) & (node == local), 1.0, hit)
        ref[...] = jnp.dot(hit.astype(BF16), latent, preferred_element_type=F32).astype(BF16)


def hot_rows(values, rows, cols, line):
    column = iota((8, cols), 1)
    node = iota((rows + 2 * SIDE, cols), 0).astype(F32)
    for off in range(TAPS):
        step = off - REACH
        where = jnp.broadcast_to(values, (8, cols))
        if step:
            where = pltpu.roll(where, (-step) % cols, 1)
        reach = column + step
        before = (rows + REACH * line + reach + REACH).astype(F32)
        after = (rows + SIDE + REACH * line + reach - cols).astype(F32)
        where = jnp.where(reach < 0, before, jnp.where(reach >= cols, after, where))
        yield jnp.where(node == where[:1], 1.0, 0.0).astype(BF16)


def band_sum(band, latent, weights_ref, hot, acc):
    blocks, outputs, channels = weights_ref.shape
    shares = lax.dot_general(
        weights_ref[...].reshape(blocks * outputs, channels), latent, NT, preferred_element_type=F32
    ).astype(BF16)
    start = 0
    for line, (_, out_rows) in enumerate(BANDS[band]):
        for off in range(TAPS):
            size = len(out_rows) * outputs
            part = jnp.dot(
                shares[start : start + size], hot(line, off), preferred_element_type=F32
            )
            start += size
            for at, out_row in enumerate(out_rows):
                piece = part[at * outputs : (at + 1) * outputs]
                acc[out_row] = piece if acc[out_row] is None else acc[out_row] + piece
    return acc


def lines_of(line_ref, start, cols):
    values = line_ref[start : start + ROWS, :].astype(F32)
    return values[:1, :cols], values[:1, cols:]


def own_kernel(begin, line_ref, inner_ref, outer_ref, latent_ref, weights_ref, out_ref, hot_ref):
    cols = out_ref.shape[2]
    rows = latent_ref.shape[0] - 2 * SIDE
    own = lines_of(line_ref, 0, cols)
    table = [list(hot_rows(own[line], rows, cols, line)) for line in range(2)]
    acc = band_sum(
        1, latent_ref[...], weights_ref, lambda line, off: table[line][off], [None, None]
    )
    for row in range(2):
        out_ref[row] = acc[row]
    odd = lax.axis_index("reg") % 2 == 1
    inner, outer = lines_of(inner_ref, begin, cols), lines_of(outer_ref, begin, cols)
    for band, (yes, no) in enumerate(((inner, outer), (outer, inner))):
        for line in range(2):
            values = jnp.where(odd, yes[line], no[line])
            for off, hot in enumerate(hot_rows(values, rows, cols, line)):
                hot_ref[(band * 2 + line) * TAPS + off] = hot


def fields_kernel(inner_ref, outer_ref, above_ref, below_ref, own_ref, hot_ref, out_ref, up_ref, down_ref):
    odd = lax.axis_index("reg") % 2

    @pl.when(odd == 1)
    def _():
        up_ref[...] = inner_ref[...]
        down_ref[...] = outer_ref[...]

    @pl.when(odd == 0)
    def _():
        up_ref[...] = outer_ref[...]
        down_ref[...] = inner_ref[...]

    acc = [own_ref[0], own_ref[1]]
    acc = band_sum(0, up_ref[...], above_ref, lambda line, off: hot_ref[line * TAPS + off], acc)
    acc = band_sum(
        2, down_ref[...], below_ref, lambda line, off: hot_ref[(2 + line) * TAPS + off], acc
    )
    out_ch = out_ref.shape[0]
    for row in range(2):
        out_ref[:, row, :] = acc[row][:out_ch].astype(BF16)


def whole(memory=pltpu.VMEM):
    return pl.BlockSpec(memory_space=memory)


def struct(*shape, dtype=BF16):
    return jax.ShapeDtypeStruct(shape, dtype)


def params(limit):
    return pltpu.CompilerParams(vmem_limit_bytes=limit << 20)


def cost(flops, moved):
    return pl.CostEstimate(flops=int(flops), bytes_accessed=int(moved), transcendentals=0)


def shards(nodes, norm_gain, w_qkv, w_out, w_latent, neighbours, assignment, psi, w_dec):
    _, rows, width = nodes.shape
    channels = w_latent.shape[1]
    lat_rows, lon_cols = assignment.shape
    basis, _, out_ch = w_dec.shape
    sectors = lax.axis_size("lon")
    count = neighbours.shape[1]
    x = nodes.reshape(rows, width)
    gain = norm_gain.reshape(1, width)

    def shifted(array, axis, step, wrap):
        size = lax.axis_size(axis)
        pairs = [(i, (i + step) % size) for i in range(size) if wrap or 0 <= i + step < size]
        return lax.ppermute(array, axis, pairs)

    def exchanged(array, first):
        size = lax.axis_size("reg")
        pairs = [(i, i + 1) for i in range(first, size - 1, 2)]
        return lax.ppermute(array, "reg", pairs + [(j, i) for i, j in pairs])

    left = shifted(x, "lon", 1, True)
    right = shifted(x, "lon", -1, True)
    line = lax.rem(assignment, rows).astype(BF16).reshape(1, lat_rows * lon_cols)
    line = jnp.pad(line, ((0, ROWS - 1), (0, 0)))
    column = jnp.concatenate([left, x, right, line], axis=0)
    outer = exchanged(column, 1)
    inner = exchanged(column, 0)

    outputs = -(-out_ch // ROWS) * ROWS
    taps = psi.transpose(1, 2, 3, 0).reshape(lat_rows * TAPS * TAPS, basis)
    head = width // HEADS
    members = LANES // head
    parts = HEADS // members
    sizes = [len(band_blocks(band)) for band in range(3)]
    query, key, value, wvt, above, middle, below = pl.pallas_call(
        prepare_kernel,
        in_specs=[whole()] * 5,
        out_specs=[whole()] * 7,
        out_shape=[
            struct(parts, LANES, members * rows),
            struct(rows, width),
            struct(width, rows),
            struct(width, width),
        ]
        + [struct(size, outputs, channels) for size in sizes],
        scratch_shapes=[pltpu.VMEM((sum(sizes) * ROWS, basis * ROWS), BF16)],
        compiler_params=params(32),
        cost_estimate=cost(3e9, 1.2e7),
        name="prepare",
    )(x, gain, w_qkv, taps, w_dec.transpose(0, 2, 1))

    state, latent, west, east = pl.pallas_call(
        functools.partial(attend_kernel, sectors),
        in_specs=[whole(pltpu.SMEM)] * 2 + [whole()] * 13,
        out_specs=[whole()] * 4,
        out_shape=[struct(rows, width), struct(rows, channels), struct(16, channels), struct(16, channels)],
        scratch_shapes=[
            pltpu.VMEM((count - 1, rows, width), BF16),
            pltpu.VMEM((count * rows, width), BF16),
            pltpu.VMEM((width, count * rows), BF16),
            pltpu.VMEM((rows, width), BF16),
        ],
        compiler_params=params(32),
        cost_estimate=cost(4e9, 6e6),
        name="attend",
    )(
        neighbours, assignment, x, left, right, inner, outer,
        gain, w_qkv, query, key, value, wvt, w_out, w_latent,
    )

    from_left = shifted(east, "lon", 1, True)
    from_right = shifted(west, "lon", -1, True)
    extended = jnp.concatenate([latent, from_left[:SIDE], from_right[:SIDE]], axis=0)
    far = exchanged(extended, 1)
    near = exchanged(extended, 0)

    nodes_ext = rows + 2 * SIDE
    partial, hots = pl.pallas_call(
        functools.partial(own_kernel, 3 * rows),
        in_specs=[whole()] * 5,
        out_specs=[whole()] * 2,
        out_shape=[
            struct(lat_rows, outputs, lon_cols, dtype=F32),
            struct(4 * TAPS, nodes_ext, lon_cols),
        ],
        compiler_params=params(32),
        cost_estimate=cost(1e9, 2.5e6),
        name="own_band",
    )(line, inner, outer, extended, middle)
    fields = pl.pallas_call(
        fields_kernel,
        in_specs=[whole()] * 6,
        out_specs=whole(),
        out_shape=struct(out_ch, lat_rows, lon_cols),
        scratch_shapes=[pltpu.VMEM((nodes_ext, channels), BF16)] * 2,
        compiler_params=params(32),
        cost_estimate=cost(2e9, 4e6),
        name="fields",
    )(near, far, above, below, partial, hots)
    return (state.reshape(1, rows, width), fields.reshape(1, out_ch, lat_rows, lon_cols))


def solution(mesh):
    in_specs = (
        P(None, ("reg", "lon"), None),
        P(),
        P(),
        P(),
        P(),
        P(("reg", "lon"), None),
        P("reg", "lon"),
        P(None, "reg", None, None),
        P(),
    )
    out_specs = (P(None, ("reg", "lon"), None), P(None, None, "reg", "lon"))
    return jax.shard_map(shards, mesh=mesh, in_specs=in_specs, out_specs=out_specs, check_vma=False)
```

```python
import functools
import math

import jax
import jax.numpy as jnp
from jax import lax
from jax.experimental import pallas as pl
from jax.experimental.pallas import tpu as pltpu
from jax.sharding import PartitionSpec as P

HEADS = 16
REACH = 2
SIDE = 8
ROWS = 16
LANES = 128
F32 = jnp.float32
BF16 = jnp.bfloat16
NT = (((1,), (1,)), ((), ()))

BANDS = (
    ((-2, (0,)), (-1, (0, 1))),
    ((0, (0, 1)), (1, (0, 1))),
    ((2, (0, 1)), (3, (1,))),
)
TAPS = 2 * REACH + 1


def band_blocks(band):
    return [
        (out_row, src - out_row + REACH, off)
        for src, out_rows in BANDS[band]
        for off in range(TAPS)
        for out_row in out_rows
    ]


def iota(shape, dim):
    return lax.broadcasted_iota(jnp.int32, shape, dim)


def normalise(rows, gain):
    values = rows.astype(F32)
    center = values - jnp.mean(values, axis=-1, keepdims=True)
    spread = jnp.mean(center * center, axis=-1, keepdims=True)
    return (center * lax.rsqrt(spread + 1e-05) * gain).astype(BF16)


def prepare_kernel(
    x_ref, gain_ref, wqkv_ref, assign_ref, psi_ref, dec_ref,
    own_ref, query_ref, key_ref, value_ref, wvt_ref, above_ref, middle_ref, below_ref, taps_ref,
):
    band_refs = (above_ref, middle_ref, below_ref)
    rows, width = x_ref.shape
    group, members = query_ref.shape[1], query_ref.shape[2] // rows
    head = group // members
    own_ref[:rows] = x_ref[...]
    local = lax.rem(assign_ref[...], rows).astype(F32)
    line = jnp.concatenate([local[:1], local[1:2]], axis=1)
    line = jnp.broadcast_to(line, (ROWS, line.shape[1]))
    own_ref[rows:] = jnp.where(iota(line.shape, 0) == 0, line, 0.0).astype(BF16)
    normed = normalise(x_ref[...], gain_ref[...])
    query = jnp.dot(normed, wqkv_ref[:, :width], preferred_element_type=F32)
    query_t = (query * (math.log2(math.e) / head**0.5)).T.astype(BF16)
    mask = (iota((group, members * rows), 0) // head) == (iota((group, members * rows), 1) // rows)
    for part in range(width // group):
        piece = query_t[part * group : (part + 1) * group]
        wide = jnp.concatenate([piece] * members, axis=1)
        query_ref[part] = jnp.where(mask, wide, jnp.zeros_like(wide))
    key_ref[...] = jnp.dot(
        normed, wqkv_ref[:, width : 2 * width], preferred_element_type=F32
    ).astype(BF16)
    wvt = wqkv_ref[:, 2 * width :].astype(F32).T.astype(BF16)
    wvt_ref[...] = wvt
    value_ref[...] = lax.dot_general(wvt, normed, NT, preferred_element_type=F32).astype(BF16)

    basis, out_ch, channels = dec_ref.shape
    depth = basis * ROWS
    spread = (iota((basis, depth), 1) // ROWS == iota((basis, depth), 0)).astype(F32)
    expanded = jnp.dot(psi_ref[...], spread, preferred_element_type=F32)
    pick = iota((ROWS, depth), 1) % ROWS == iota((ROWS, depth), 0)
    blocks = [item for band in range(3) for item in band_blocks(band)]
    for at, (out_row, tap, off) in enumerate(blocks):
        source = (out_row * TAPS + tap) * TAPS + off
        line = jnp.broadcast_to(expanded[source : source + 1], (ROWS, depth))
        taps_ref[at * ROWS : (at + 1) * ROWS, :] = jnp.where(pick, line, 0.0).astype(BF16)
    for first in range(0, out_ch, ROWS):
        size = min(ROWS, out_ch - first)
        pieces = []
        for base in range(basis):
            pieces.append(dec_ref[base, first : first + size, :])
            if size < ROWS:
                pieces.append(jnp.zeros((ROWS - size, channels), BF16))
        mixing = jnp.concatenate(pieces, axis=0)
        start = 0
        for band_ref in band_refs:
            count = band_ref.shape[0]
            mixed = jnp.dot(
                taps_ref[start * ROWS : (start + count) * ROWS, :], mixing, preferred_element_type=F32
            ).astype(BF16)
            band_ref[:, first : first + ROWS, :] = mixed.reshape(count, ROWS, channels)
            start += count


def attend_kernel(
    sectors,
    listed_ref, assign_ref, column_ref, inner_ref, outer_ref,
    gain_ref, wqkv_ref, query_ref, key_ref, value_ref, wvt_ref, wout_ref, wlat_ref,
    state_ref, latent_ref, west_ref, east_ref,
    keys_ref, values_ref, attended_ref,
):
    rows, width = key_ref.shape
    count = listed_ref.shape[1]
    parts, group, lanes = query_ref.shape
    members = lanes // rows
    head = group // members
    reg_here, lon_here = lax.axis_index("reg"), lax.axis_index("lon")
    toward = 1 - 2 * (reg_here % 2)
    near = []
    for at in range(1, count):
        block = listed_ref[0, at]
        step_reg = block // sectors - reg_here
        step_lon = (block % sectors - lon_here + 1 + sectors) % sectors - 1
        place = jnp.where(step_lon == 0, 2, jnp.where(step_lon < 0, 0, 1))
        span = pl.ds(pl.multiple_of(place * rows, rows), rows)
        other = jnp.where(step_reg == toward, inner_ref[span, :], outer_ref[span, :])
        near.append(jnp.where(step_reg == 0, column_ref[span, :], other))
    normed = normalise(jnp.concatenate(near, axis=0), gain_ref[...])
    keys_ref[:rows] = key_ref[...]
    keys_ref[rows:] = jnp.dot(
        normed, wqkv_ref[:, width : 2 * width], preferred_element_type=F32
    ).astype(BF16)
    values = lax.dot_general(wvt_ref[...], normed, NT, preferred_element_type=F32).astype(BF16)
    for part in range(parts):
        span = slice(part * group, (part + 1) * group)
        values_ref[part, :group, :rows] = value_ref[span]
        values_ref[part, :group, rows:] = values[span]
        values_ref[part, group:, :] = jnp.ones((ROWS, count * rows), BF16)

    def scored(part):
        keys = keys_ref[:, part * group : (part + 1) * group]
        return jnp.dot(keys, query_ref[part], preferred_element_type=F32)

    owner = iota((group, rows), 0) // head
    scores = scored(0)
    for part in range(parts):
        now = scores
        if part + 1 < parts:
            scores = scored(part + 1)
        expo = jnp.exp2(now - jnp.max(now, axis=0, keepdims=True)).astype(BF16)
        summed = jnp.dot(values_ref[part], expo, preferred_element_type=F32)
        summed = summed[:group] * (1.0 / summed[group : group + 1])
        merged = None
        for member in range(members):
            piece = summed[:, member * rows : (member + 1) * rows]
            merged = piece if merged is None else jnp.where(owner == member, piece, merged)
        attended_ref[:, part * group : (part + 1) * group] = merged.T.astype(BF16)
    state = (
        column_ref[2 * rows : 3 * rows, :].astype(F32)
        + jnp.dot(attended_ref[...], wout_ref[...], preferred_element_type=F32)
    ).astype(BF16)
    state_ref[...] = state
    value = jnp.dot(state, wlat_ref[...], preferred_element_type=F32)
    latent = (value / (1.0 + jnp.exp(-value))).astype(BF16)
    latent_ref[...] = latent
    lat_rows, lon_cols = assign_ref.shape
    for ref, first in ((west_ref, 0), (east_ref, lon_cols - REACH)):
        cells = ref.shape[0]
        line, node = iota((cells, rows), 0), iota((cells, rows), 1)
        hit = jnp.zeros((cells, rows), F32)
        for row in range(lat_rows):
            for col in range(REACH):
                local = assign_ref[row, first + col] % rows
                hit = jnp.where((line == row * REACH + col) & (node == local), 1.0, hit)
        ref[...] = jnp.dot(hit.astype(BF16), latent, preferred_element_type=F32).astype(BF16)


def hot_rows(values, rows, cols, line):
    column = iota((8, cols), 1)
    node = iota((rows + 2 * SIDE, cols), 0).astype(F32)
    for off in range(TAPS):
        step = off - REACH
        where = jnp.broadcast_to(values, (8, cols))
        if step:
            where = pltpu.roll(where, (-step) % cols, 1)
        reach = column + step
        before = (rows + REACH * line + reach + REACH).astype(F32)
        after = (rows + SIDE + REACH * line + reach - cols).astype(F32)
        where = jnp.where(reach < 0, before, jnp.where(reach >= cols, after, where))
        yield jnp.where(node == where[:1], 1.0, 0.0).astype(BF16)


def band_shares(latent, weights_ref):
    blocks, outputs, channels = weights_ref.shape
    shares = lax.dot_general(
        weights_ref[...].reshape(blocks * outputs, channels), latent, NT, preferred_element_type=F32
    ).astype(BF16)
    return [shares[at * outputs : (at + 1) * outputs] for at in range(blocks)]


def lines_of(line_ref, start, cols):
    values = line_ref[start : start + ROWS, :].astype(F32)
    return values[:1, :cols], values[:1, cols:]


def own_kernel(begin, line_ref, inner_ref, outer_ref, latent_ref, weights_ref, out_ref, hot_ref):
    cols = out_ref.shape[2]
    rows = latent_ref.shape[0] - 2 * SIDE
    own = lines_of(line_ref, begin, cols)
    table = [list(hot_rows(own[line], rows, cols, line)) for line in range(2)]
    acc = [None, None]
    for (out_row, tap, off), share in zip(
        band_blocks(1), band_shares(latent_ref[...], weights_ref)
    ):
        line = out_row + tap - REACH
        piece = jnp.dot(share, table[line][off], preferred_element_type=F32)
        acc[out_row] = piece if acc[out_row] is None else acc[out_row] + piece
    for row in range(2):
        out_ref[row] = acc[row]
    odd = lax.axis_index("reg") % 2 == 1
    inner, outer = lines_of(inner_ref, begin, cols), lines_of(outer_ref, begin, cols)
    nodes = rows + 2 * SIDE
    for band, (yes, no) in enumerate(((inner, outer), (outer, inner))):
        for line in range(2):
            values = jnp.where(odd, yes[line], no[line])
            for off, hot in enumerate(hot_rows(values, rows, cols, line)):
                at = (band * 2 + line) * TAPS + off
                hot_ref[at, :nodes] = hot
                hot_ref[at, nodes:] = jnp.zeros((hot_ref.shape[1] - nodes, cols), BF16)


def fields_kernel(inner_ref, outer_ref, above_ref, below_ref, own_ref, hot_ref, out_ref, first_ref, second_ref):
    odd = lax.axis_index("reg") % 2 == 1
    inner, outer = inner_ref[...], outer_ref[...]
    lanes = hot_ref.shape[1]
    blank = jnp.zeros((lanes - inner.shape[0], inner.shape[1]), BF16)
    shares_refs = (first_ref, second_ref)
    for band, latent, weights_ref in (
        (0, jnp.where(odd, inner, outer), above_ref),
        (2, jnp.where(odd, outer, inner), below_ref),
    ):
        shares = band_shares(jnp.concatenate([latent, blank], axis=0), weights_ref)
        for (out_row, tap, off), share in zip(band_blocks(band), shares):
            line = out_row + tap - REACH
            at = (line + REACH if band == 0 else line) * TAPS + off - out_row * TAPS
            shares_refs[out_row][:, at * lanes : (at + 1) * lanes] = share
    out_ch, _, cols = out_ref.shape
    for row in range(2):
        hot = hot_ref[row * TAPS : (row + 3) * TAPS].reshape(3 * TAPS * lanes, cols)
        total = own_ref[row] + jnp.dot(shares_refs[row][...], hot, preferred_element_type=F32)
        out_ref[:, row, :] = total[:out_ch].astype(BF16)


def whole(memory=pltpu.VMEM):
    return pl.BlockSpec(memory_space=memory)


def struct(*shape, dtype=BF16):
    return jax.ShapeDtypeStruct(shape, dtype)


def params(limit):
    return pltpu.CompilerParams(vmem_limit_bytes=limit << 20)


def cost(flops, moved):
    return pl.CostEstimate(flops=int(flops), bytes_accessed=int(moved), transcendentals=0)


def shards(nodes, norm_gain, w_qkv, w_out, w_latent, neighbours, assignment, psi, w_dec):
    _, rows, width = nodes.shape
    channels = w_latent.shape[1]
    lat_rows, lon_cols = assignment.shape
    basis, _, out_ch = w_dec.shape
    sectors = lax.axis_size("lon")
    count = neighbours.shape[1]
    x = nodes.reshape(rows, width)
    gain = norm_gain.reshape(1, width)

    def shifted(array, axis, step, wrap):
        size = lax.axis_size(axis)
        pairs = [(i, (i + step) % size) for i in range(size) if wrap or 0 <= i + step < size]
        return lax.ppermute(array, axis, pairs)

    def exchanged(array, first):
        size = lax.axis_size("reg")
        pairs = [(i, i + 1) for i in range(first, size - 1, 2)]
        return lax.ppermute(array, "reg", pairs + [(j, i) for i, j in pairs])

    left = shifted(x, "lon", 1, True)
    right = shifted(x, "lon", -1, True)
    outputs = -(-out_ch // ROWS) * ROWS
    taps = psi.transpose(1, 2, 3, 0).reshape(lat_rows * TAPS * TAPS, basis)
    head = width // HEADS
    members = LANES // head
    parts = HEADS // members
    sizes = [len(band_blocks(band)) for band in range(3)]
    own, query, key, value, wvt, above, middle, below = pl.pallas_call(
        prepare_kernel,
        in_specs=[whole()] * 6,
        out_specs=[whole()] * 8,
        out_shape=[
            struct(rows + ROWS, width),
            struct(parts, LANES, members * rows),
            struct(rows, width),
            struct(width, rows),
            struct(width, width),
        ]
        + [struct(size, outputs, channels) for size in sizes],
        scratch_shapes=[pltpu.VMEM((sum(sizes) * ROWS, basis * ROWS), BF16)],
        compiler_params=params(32),
        cost_estimate=cost(3e9, 1.2e7),
        name="prepare",
    )(x, gain, w_qkv, assignment, taps, w_dec.transpose(0, 2, 1))
    column = jnp.concatenate([left, right, own], axis=0)
    outer = exchanged(column, 1)
    inner = exchanged(column, 0)

    state, latent, west, east = pl.pallas_call(
        functools.partial(attend_kernel, sectors),
        in_specs=[whole(pltpu.SMEM)] * 2 + [whole()] * 11,
        out_specs=[whole()] * 4,
        out_shape=[struct(rows, width), struct(rows, channels)] + [struct(ROWS, channels)] * 2,
        scratch_shapes=[
            pltpu.VMEM((count * rows, width), BF16),
            pltpu.VMEM((parts, LANES + ROWS, count * rows), BF16),
            pltpu.VMEM((rows, width), BF16),
        ],
        compiler_params=params(32),
        cost_estimate=cost(4e9, 6e6),
        name="attend",
    )(
        neighbours, assignment, column, inner, outer,
        gain, w_qkv, query, key, value, wvt, w_out, w_latent,
    )

    from_left = shifted(east, "lon", 1, True)
    from_right = shifted(west, "lon", -1, True)
    extended = jnp.concatenate([latent, from_left[:SIDE], from_right[:SIDE]], axis=0)
    far = exchanged(extended, 1)
    near = exchanged(extended, 0)

    lanes = -(-(rows + 2 * SIDE) // 256) * 256
    partial, hots = pl.pallas_call(
        functools.partial(own_kernel, 3 * rows),
        in_specs=[whole()] * 5,
        out_specs=[whole()] * 2,
        out_shape=[
            struct(lat_rows, outputs, lon_cols, dtype=F32),
            struct(4 * TAPS, lanes, lon_cols),
        ],
        compiler_params=params(32),
        cost_estimate=cost(1e9, 2.5e6),
        name="own_band",
    )(column, inner, outer, extended, middle)
    fields = pl.pallas_call(
        fields_kernel,
        in_specs=[whole()] * 6,
        out_specs=whole(),
        out_shape=struct(out_ch, lat_rows, lon_cols),
        scratch_shapes=[pltpu.VMEM((outputs, 3 * TAPS * lanes), BF16)] * 2,
        compiler_params=params(32),
        cost_estimate=cost(2e9, 4e6),
        name="fields",
    )(near, far, above, below, partial, hots)
    return (state.reshape(1, rows, width), fields.reshape(1, out_ch, lat_rows, lon_cols))


def solution(mesh):
    in_specs = (
        P(None, ("reg", "lon"), None),
        P(),
        P(),
        P(),
        P(),
        P(("reg", "lon"), None),
        P("reg", "lon"),
        P(None, "reg", None, None),
        P(),
    )
    out_specs = (P(None, ("reg", "lon"), None), P(None, None, "reg", "lon"))
    return jax.shard_map(shards, mesh=mesh, in_specs=in_specs, out_specs=out_specs, check_vma=False)
```

```python
import functools
import math

import jax
import jax.numpy as jnp
from jax import lax
from jax.experimental import pallas as pl
from jax.experimental.pallas import tpu as pltpu
from jax.sharding import PartitionSpec as P

HEADS = 16
REACH = 2
TAPS = 2 * REACH + 1
SIDE = 8
ROWS = 16
LANES = 128
EARLY = 2
F32 = jnp.float32
BF16 = jnp.bfloat16
NT = (((1,), (1,)), ((), ()))

ABOVE = ((-2, (0,)), (-1, (0, 1)))
OWN = ((0, (0, 1)), (1, (0, 1)))
BELOW = ((3, (1,)), (2, (0, 1)))


def blocks_of(band):
    return [
        (out_row, src - out_row + REACH, off)
        for src, out_rows in band
        for off in range(TAPS)
        for out_row in out_rows
    ]


def iota(shape, dim):
    return lax.broadcasted_iota(jnp.int32, shape, dim)


def normalise(rows, gain):
    values = rows.astype(F32)
    center = values - jnp.mean(values, axis=-1, keepdims=True)
    spread = jnp.mean(center * center, axis=-1, keepdims=True)
    return (center * lax.rsqrt(spread + 1e-05) * gain).astype(BF16)


def prepare_kernel(
    x_hbm, gain_hbm, wqkv_hbm, assign_hbm, psi_hbm, dec_hbm,
    own_ref, query_ref, key_ref, value_ref, wk_ref, wvt_ref, middle_ref, edges_ref,
    x_ref, gain_ref, wqkv_ref, assign_ref, psi_ref, dec_ref, psi_rows_ref, taps_ref, sems,
):
    copies = [
        pltpu.make_async_copy(source, target, sems.at[at])
        for at, (source, target) in enumerate(
            (
                (assign_hbm, assign_ref),
                (x_hbm, x_ref),
                (gain_hbm, gain_ref),
                (psi_hbm, psi_ref),
                (dec_hbm, dec_ref),
                (wqkv_hbm, wqkv_ref),
            )
        )
    ]
    for copy in copies:
        copy.start()
    rows, width = x_ref.shape
    group, members = query_ref.shape[1], query_ref.shape[2] // rows
    head = group // members
    copies[0].wait()
    local = lax.rem(assign_ref[...], rows).astype(F32)
    line = jnp.concatenate([local[:1], local[1:2]], axis=1)
    line = jnp.broadcast_to(line, (ROWS, line.shape[1]))
    own_ref[rows:] = jnp.where(iota(line.shape, 0) == 0, line, 0.0).astype(BF16)
    copies[1].wait()
    own_ref[:rows] = x_ref[...]
    copies[2].wait()
    normed = normalise(x_ref[...], gain_ref[...])

    copies[3].wait()
    basis, out_ch, channels = dec_ref.shape
    depth = basis * ROWS
    for tap in range(TAPS):
        for off in range(TAPS):
            at = (tap * TAPS + off) * 2
            psi_rows_ref[at : at + 2, :] = psi_ref[tap, off]
    spread = (iota((basis, depth), 1) // ROWS == iota((basis, depth), 0)).astype(F32)
    expanded = jnp.dot(psi_rows_ref[...], spread, preferred_element_type=F32)
    pick = iota((ROWS, depth), 1) % ROWS == iota((ROWS, depth), 0)
    for at, (out_row, tap, off) in enumerate(blocks_of(OWN) + blocks_of(ABOVE) + blocks_of(BELOW)):
        source = (tap * TAPS + off) * 2 + out_row
        taps = jnp.broadcast_to(expanded[source : source + 1], (ROWS, depth))
        taps_ref[at * ROWS : (at + 1) * ROWS, :] = jnp.where(pick, taps, 0.0).astype(BF16)
    copies[4].wait()
    inside = middle_ref.shape[0]
    outside = edges_ref.shape[1]
    for first in range(0, out_ch, ROWS):
        size = min(ROWS, out_ch - first)
        pieces = []
        for base in range(basis):
            pieces.append(dec_ref[base, first : first + size, :])
            if size < ROWS:
                pieces.append(jnp.zeros((ROWS - size, channels), BF16))
        mixing = jnp.concatenate(pieces, axis=0)
        mixed = jnp.dot(taps_ref[...], mixing, preferred_element_type=F32).astype(BF16)
        mixed = mixed.reshape(taps_ref.shape[0] // ROWS, ROWS, channels)
        middle_ref[:, first : first + ROWS, :] = mixed[:inside]
        edges_ref[0, :, first : first + ROWS, :] = mixed[inside : inside + outside]
        edges_ref[1, :, first : first + ROWS, :] = mixed[inside + outside :]

    copies[5].wait()
    query = jnp.dot(normed, wqkv_ref[:, :width], preferred_element_type=F32)
    query_t = (query * (math.log2(math.e) / head**0.5)).T.astype(BF16)
    mask = (iota((group, members * rows), 0) // head) == (iota((group, members * rows), 1) // rows)
    for part in range(width // group):
        piece = query_t[part * group : (part + 1) * group]
        wide = jnp.concatenate([piece] * members, axis=1)
        query_ref[part] = jnp.where(mask, wide, jnp.zeros_like(wide))
    wk = wqkv_ref[:, width : 2 * width]
    wk_ref[...] = wk
    key_ref[...] = jnp.dot(normed, wk, preferred_element_type=F32).astype(BF16)
    wvt = wqkv_ref[:, 2 * width :].astype(F32).T.astype(BF16)
    wvt_ref[...] = wvt
    value_ref[...] = lax.dot_general(wvt, normed, NT, preferred_element_type=F32).astype(BF16)


def listed_blocks(sectors, listed_ref):
    reg_here, lon_here = lax.axis_index("reg"), lax.axis_index("lon")
    toward = 1 - 2 * (reg_here % 2)
    found = []
    for at in range(1, listed_ref.shape[1]):
        block = listed_ref[0, at]
        step_reg = (block // sectors - reg_here) * toward
        step_lon = (block % sectors - lon_here + 1 + sectors) % sectors - 1
        place = jnp.where(step_lon == 0, 2, jnp.where(step_lon < 0, 0, 1))
        late = ((step_reg < 0) & (step_lon != 0)).astype(jnp.int32)
        found.append(late * 16 + (step_reg + 1) * 4 + place)
    for low in range(len(found)):
        for high in range(low + 1, len(found)):
            less, more = jnp.minimum(found[low], found[high]), jnp.maximum(found[low], found[high])
            found[low], found[high] = less, more
    return [(code % 16 // 4 - 1, code % 4) for code in found]


def chosen(blocks, rows, both_ref, inner_ref, center_ref, corners_ref):
    near = []
    for step, place in blocks:
        side = pl.ds(pl.multiple_of(jnp.minimum(place, 1) * rows, rows), rows)
        span = pl.ds(pl.multiple_of(place * rows, rows), rows)
        outer = center_ref[...]
        if corners_ref is not None:
            outer = jnp.where(place == 2, outer, corners_ref[side, :])
        other = jnp.where(step > 0, inner_ref[span, :], outer)
        near.append(jnp.where(step == 0, both_ref[side, :], other))
    return jnp.concatenate(near, axis=0)


def project(nodes, gain, wk_ref, wvt_ref):
    normed = normalise(nodes, gain)
    keys = jnp.dot(normed, wk_ref[...], preferred_element_type=F32).astype(BF16)
    values = lax.dot_general(wvt_ref[...], normed, NT, preferred_element_type=F32).astype(BF16)
    return keys, values


def early_kernel(
    sectors,
    listed_ref, both_ref, inner_ref, center_ref,
    gain_ref, wk_ref, wvt_ref, query_ref, key_ref, value_ref,
    top_ref, sum_ref, keys_ref, values_ref,
):
    rows = key_ref.shape[0]
    parts, group, _ = query_ref.shape
    blocks = listed_blocks(sectors, listed_ref)[:EARLY]
    nodes = chosen(blocks, rows, both_ref, inner_ref, center_ref, None)
    keys, values = project(nodes, gain_ref[...], wk_ref, wvt_ref)
    keys_ref[:rows] = key_ref[...]
    keys_ref[rows:] = keys
    for part in range(parts):
        span = slice(part * group, (part + 1) * group)
        values_ref[part, :group, :rows] = value_ref[span]
        values_ref[part, :group, rows:] = values[span]
        values_ref[part, group:, :] = jnp.ones((ROWS, keys_ref.shape[0]), BF16)

    def scored(part):
        span = slice(part * group, (part + 1) * group)
        return jnp.dot(keys_ref[:, span], query_ref[part], preferred_element_type=F32)

    scores = scored(0)
    for part in range(parts):
        now = scores
        if part + 1 < parts:
            scores = scored(part + 1)
        top = jnp.max(now, axis=0, keepdims=True)
        expo = jnp.exp2(now - top).astype(BF16)
        top_ref[part] = jnp.broadcast_to(top, top_ref.shape[1:])
        sum_ref[part] = jnp.dot(values_ref[part], expo, preferred_element_type=F32)


def late_kernel(
    sectors,
    listed_ref, assign_ref, both_ref, inner_ref, center_ref, corners_ref,
    own_ref, gain_ref, wk_ref, wvt_ref, query_ref, top_ref, sum_ref, wout_ref, wlat_ref,
    state_ref, latent_ref, west_ref, east_ref,
    attended_ref,
):
    rows, width = state_ref.shape
    parts, group, lanes = query_ref.shape
    members = lanes // rows
    head = group // members
    blocks = listed_blocks(sectors, listed_ref)[EARLY:]
    nodes = chosen(blocks, rows, both_ref, inner_ref, center_ref, corners_ref)
    keys, values = project(nodes, gain_ref[...], wk_ref, wvt_ref)
    ones = jnp.ones((ROWS, len(blocks) * rows), BF16)
    owner = iota((group, rows), 0) // head

    def scored(part):
        span = slice(part * group, (part + 1) * group)
        return jnp.dot(keys[:, span], query_ref[part], preferred_element_type=F32)

    scores = scored(0)
    for part in range(parts):
        now = scores
        if part + 1 < parts:
            scores = scored(part + 1)
        before = top_ref[part, :1]
        top = jnp.maximum(before, jnp.max(now, axis=0, keepdims=True))
        expo = jnp.exp2(now - top).astype(BF16)
        weights = jnp.concatenate([values[part * group : (part + 1) * group], ones], axis=0)
        summed = jnp.dot(weights, expo, preferred_element_type=F32)
        summed = summed + sum_ref[part] * jnp.exp2(before - top)
        summed = summed[:group] * (1.0 / summed[group : group + 1])
        merged = None
        for member in range(members):
            piece = summed[:, member * rows : (member + 1) * rows]
            merged = piece if merged is None else jnp.where(owner == member, piece, merged)
        attended_ref[:, part * group : (part + 1) * group] = merged.T.astype(BF16)
    state = (
        own_ref[:rows].astype(F32)
        + jnp.dot(attended_ref[...], wout_ref[...], preferred_element_type=F32)
    ).astype(BF16)
    state_ref[...] = state
    value = jnp.dot(state, wlat_ref[...], preferred_element_type=F32)
    latent = (value / (1.0 + jnp.exp(-value))).astype(BF16)
    latent_ref[...] = latent
    lat_rows, lon_cols = assign_ref.shape
    for ref, first in ((west_ref, 0), (east_ref, lon_cols - REACH)):
        cells = ref.shape[0]
        line, node = iota((cells, rows), 0), iota((cells, rows), 1)
        hit = jnp.zeros((cells, rows), F32)
        for row in range(lat_rows):
            for col in range(REACH):
                local = assign_ref[row, first + col] % rows
                hit = jnp.where((line == row * REACH + col) & (node == local), 1.0, hit)
        ref[...] = jnp.dot(hit.astype(BF16), latent, preferred_element_type=F32).astype(BF16)


def hot_rows(values, rows, cols, line):
    column = iota((8, cols), 1)
    node = iota((rows + 2 * SIDE, cols), 0).astype(F32)
    for off in range(TAPS):
        step = off - REACH
        where = jnp.broadcast_to(values, (8, cols))
        if step:
            where = pltpu.roll(where, (-step) % cols, 1)
        reach = column + step
        before = (rows + REACH * line + reach + REACH).astype(F32)
        after = (rows + SIDE + REACH * line + reach - cols).astype(F32)
        where = jnp.where(reach < 0, before, jnp.where(reach >= cols, after, where))
        yield jnp.where(node == where[:1], 1.0, 0.0).astype(BF16)


def shares_of(latent, weights):
    blocks, outputs, channels = weights.shape
    shares = lax.dot_general(
        weights.reshape(blocks * outputs, channels), latent, NT, preferred_element_type=F32
    ).astype(BF16)
    return [shares[at * outputs : (at + 1) * outputs] for at in range(blocks)]


def lines_of(line_ref, start, cols):
    values = line_ref[start : start + ROWS, :].astype(F32)
    return values[:1, :cols], values[:1, cols:]


def own_kernel(
    begin, own_ref, inner_ref, corners_ref, latent_ref, weights_ref, out_ref, hot_ref
):
    cols = out_ref.shape[2]
    rows = latent_ref.shape[0] - 2 * SIDE
    own = lines_of(own_ref, begin[0], cols)
    table = [list(hot_rows(own[line], rows, cols, line)) for line in range(2)]
    acc = [None, None]
    for (out_row, tap, off), share in zip(
        blocks_of(OWN), shares_of(latent_ref[...], weights_ref[...])
    ):
        line = out_row + tap - REACH
        piece = jnp.dot(share, table[line][off], preferred_element_type=F32)
        acc[out_row] = piece if acc[out_row] is None else acc[out_row] + piece
    for row in range(2):
        out_ref[row] = acc[row]
    odd = lax.axis_index("reg") % 2 == 1
    inner, outer = lines_of(inner_ref, begin[1], cols), lines_of(corners_ref, begin[2], cols)
    nodes = rows + 2 * SIDE
    for band, (yes, no) in enumerate(((inner, outer), (outer, inner))):
        for at, line in enumerate((0, 1) if band == 0 else (1, 0)):
            values = jnp.where(odd, yes[line], no[line])
            for off, hot in enumerate(hot_rows(values, rows, cols, line)):
                hot_ref[band, at, off, :nodes] = hot
                hot_ref[band, at, off, nodes:] = jnp.zeros((hot_ref.shape[3] - nodes, cols), BF16)


def band_kernel(from_inner, latent_ref, weights_ref, hot_ref, partial_ref, out_ref, one_ref, two_ref):
    odd = lax.axis_index("reg") % 2
    band = 1 - odd if from_inner else odd
    latent = latent_ref[...]
    lanes, cols = hot_ref.shape[3:]
    outputs = weights_ref.shape[2]
    blank = jnp.zeros((lanes - latent.shape[0], latent.shape[1]), BF16)
    shares = shares_of(jnp.concatenate([latent, blank], axis=0), weights_ref[band])
    for off in range(TAPS):
        span = slice(off * lanes, (off + 1) * lanes)
        one_ref[:, span] = shares[off]
        for row in range(2):
            two_ref[row * outputs : (row + 1) * outputs, span] = shares[TAPS + 2 * off + row]
    depth = TAPS * lanes
    one = jnp.dot(one_ref[...], hot_ref[band, 0].reshape(depth, cols), preferred_element_type=F32)
    two = jnp.dot(two_ref[...], hot_ref[band, 1].reshape(depth, cols), preferred_element_type=F32)
    for row in range(2):
        total = partial_ref[row] + two[row * outputs : (row + 1) * outputs]
        total = total + jnp.where(band == row, one, 0.0)
        if from_inner:
            out_ref[row] = total
        else:
            out_ref[:, row, :] = total[: out_ref.shape[0]].astype(BF16)


def whole(memory=pltpu.VMEM):
    return pl.BlockSpec(memory_space=memory)


def struct(*shape, dtype=BF16):
    return jax.ShapeDtypeStruct(shape, dtype)


def params(limit):
    return pltpu.CompilerParams(vmem_limit_bytes=limit << 20)


def cost(flops, moved):
    return pl.CostEstimate(flops=int(flops), bytes_accessed=int(moved), transcendentals=0)


def shards(nodes, norm_gain, w_qkv, w_out, w_latent, neighbours, assignment, psi, w_dec):
    _, rows, width = nodes.shape
    channels = w_latent.shape[1]
    lat_rows, lon_cols = assignment.shape
    basis, _, out_ch = w_dec.shape
    sectors = lax.axis_size("lon")
    count = neighbours.shape[1]
    x = nodes.reshape(rows, width)
    gain = norm_gain.reshape(1, width)

    def shifted(array, step):
        return lax.ppermute(array, "lon", [(i, (i + step) % sectors) for i in range(sectors)])

    def exchanged(array, first):
        size = lax.axis_size("reg")
        pairs = [(i, i + 1) for i in range(first, size - 1, 2)]
        return lax.ppermute(array, "reg", pairs + [(j, i) for i, j in pairs])

    left = shifted(x, 1)
    right = shifted(x, -1)
    center = exchanged(x, 1)

    outputs = -(-out_ch // ROWS) * ROWS
    head = width // HEADS
    members = LANES // head
    parts = HEADS // members
    inside, outside = len(blocks_of(OWN)), len(blocks_of(ABOVE))
    taps = psi.transpose(2, 3, 1, 0)
    mixing = w_dec.transpose(0, 2, 1)
    own, query, key, value, wk, wvt, middle, edges = pl.pallas_call(
        prepare_kernel,
        in_specs=[whole(pltpu.HBM)] * 6,
        out_specs=[whole()] * 8,
        out_shape=[
            struct(rows + ROWS, width),
            struct(parts, LANES, members * rows),
            struct(rows, width),
            struct(width, rows),
            struct(width, width),
            struct(width, width),
            struct(inside, outputs, channels),
            struct(2, outside, outputs, channels),
        ],
        scratch_shapes=[
            pltpu.VMEM((rows, width), BF16),
            pltpu.VMEM((1, width), F32),
            pltpu.VMEM(w_qkv.shape, BF16),
            pltpu.VMEM(assignment.shape, jnp.int32),
            pltpu.VMEM(taps.shape, F32),
            pltpu.VMEM(mixing.shape, BF16),
            pltpu.VMEM((2 * TAPS * TAPS, basis), F32),
            pltpu.VMEM(((inside + 2 * outside) * ROWS, basis * ROWS), BF16),
            pltpu.SemaphoreType.DMA((6,)),
        ],
        compiler_params=params(32),
        cost_estimate=cost(3e9, 1.2e7),
        name="prepare",
    )(x, gain, w_qkv, assignment, taps, mixing)
    both = jnp.concatenate([left, right, own[rows:]], axis=0)
    corners = exchanged(both, 1)
    inner = exchanged(jnp.concatenate([left, right, own], axis=0), 0)

    top, summed = pl.pallas_call(
        functools.partial(early_kernel, sectors),
        in_specs=[whole(pltpu.SMEM)] + [whole()] * 9,
        out_specs=[whole()] * 2,
        out_shape=[
            struct(parts, 8, members * rows, dtype=F32),
            struct(parts, LANES + ROWS, members * rows, dtype=F32),
        ],
        scratch_shapes=[
            pltpu.VMEM(((1 + EARLY) * rows, width), BF16),
            pltpu.VMEM((parts, LANES + ROWS, (1 + EARLY) * rows), BF16),
        ],
        compiler_params=params(32),
        cost_estimate=cost(3e9, 6e6),
        name="early",
    )(neighbours, both, inner, center, gain, wk, wvt, query, key, value)
    state, latent, west, east = pl.pallas_call(
        functools.partial(late_kernel, sectors),
        in_specs=[whole(pltpu.SMEM)] * 2 + [whole()] * 13,
        out_specs=[whole()] * 4,
        out_shape=[struct(rows, width), struct(rows, channels)] + [struct(ROWS, channels)] * 2,
        scratch_shapes=[pltpu.VMEM((rows, width), BF16)],
        compiler_params=params(32),
        cost_estimate=cost(3e9, 6e6),
        name="late",
    )(
        neighbours, assignment, both, inner, center, corners,
        own, gain, wk, wvt, query, top, summed, w_out, w_latent,
    )

    from_left = shifted(east, 1)
    from_right = shifted(west, -1)
    extended = jnp.concatenate([latent, from_left[:SIDE], from_right[:SIDE]], axis=0)
    far = exchanged(extended, 1)
    near = exchanged(extended, 0)

    lanes = -(-(rows + 2 * SIDE) // 256) * 256
    partial, hots = pl.pallas_call(
        functools.partial(own_kernel, (rows, 3 * rows, 2 * rows)),
        in_specs=[whole()] * 5,
        out_specs=[whole()] * 2,
        out_shape=[
            struct(lat_rows, outputs, lon_cols, dtype=F32),
            struct(2, 2, TAPS, lanes, lon_cols),
        ],
        compiler_params=params(32),
        cost_estimate=cost(1e9, 2.5e6),
        name="own_band",
    )(own, inner, corners, extended, middle)
    band_scratch = [
        pltpu.VMEM((outputs, TAPS * lanes), BF16),
        pltpu.VMEM((2 * outputs, TAPS * lanes), BF16),
    ]
    partial = pl.pallas_call(
        functools.partial(band_kernel, True),
        in_specs=[whole()] * 4,
        out_specs=whole(),
        out_shape=struct(lat_rows, outputs, lon_cols, dtype=F32),
        scratch_shapes=band_scratch,
        compiler_params=params(32),
        cost_estimate=cost(1e9, 2.5e6),
        name="inner_band",
    )(near, edges, hots, partial)
    fields = pl.pallas_call(
        functools.partial(band_kernel, False),
        in_specs=[whole()] * 4,
        out_specs=whole(),
        out_shape=struct(out_ch, lat_rows, lon_cols),
        scratch_shapes=band_scratch,
        compiler_params=params(32),
        cost_estimate=cost(1e9, 2.5e6),
        name="outer_band",
    )(far, edges, hots, partial)
    return (state.reshape(1, rows, width), fields.reshape(1, out_ch, lat_rows, lon_cols))


def solution(mesh):
    in_specs = (
        P(None, ("reg", "lon"), None),
        P(),
        P(),
        P(),
        P(),
        P(("reg", "lon"), None),
        P("reg", "lon"),
        P(None, "reg", None, None),
        P(),
    )
    out_specs = (P(None, ("reg", "lon"), None), P(None, None, "reg", "lon"))
    return jax.shard_map(shards, mesh=mesh, in_specs=in_specs, out_specs=out_specs, check_vma=False)
```

```python
import functools
import math

import jax
import jax.numpy as jnp
from jax import lax
from jax.experimental import pallas as pl
from jax.experimental.pallas import tpu as pltpu
from jax.sharding import PartitionSpec as P

HEADS = 16
REACH = 2
TAPS = 2 * REACH + 1
SIDE = 8
ROWS = 16
LANES = 128
EARLY = 2
F32 = jnp.float32
BF16 = jnp.bfloat16
NT = (((1,), (1,)), ((), ()))

ABOVE = ((-2, (0,)), (-1, (0, 1)))
OWN = ((0, (0, 1)), (1, (0, 1)))
BELOW = ((3, (1,)), (2, (0, 1)))


def blocks_of(band):
    return [
        (out_row, src - out_row + REACH, off)
        for src, out_rows in band
        for off in range(TAPS)
        for out_row in out_rows
    ]


def iota(shape, dim):
    return lax.broadcasted_iota(jnp.int32, shape, dim)


def normalise(rows, gain):
    values = rows.astype(F32)
    center = values - jnp.mean(values, axis=-1, keepdims=True)
    spread = jnp.mean(center * center, axis=-1, keepdims=True)
    return (center * lax.rsqrt(spread + 1e-05) * gain).astype(BF16)


def prepare_kernel(
    x_hbm, gain_hbm, wqkv_hbm, assign_hbm, psi_hbm, dec_hbm,
    own_ref, query_ref, key_ref, value_ref, wk_ref, wvt_ref, middle_ref, edges_ref,
    x_ref, gain_ref, wqkv_ref, assign_ref, psi_ref, dec_ref, psi_rows_ref, taps_ref, sems,
):
    copies = [
        pltpu.make_async_copy(source, target, sems.at[at])
        for at, (source, target) in enumerate(
            (
                (assign_hbm, assign_ref),
                (x_hbm, x_ref),
                (gain_hbm, gain_ref),
                (psi_hbm, psi_ref),
                (dec_hbm, dec_ref),
                (wqkv_hbm, wqkv_ref),
            )
        )
    ]
    for copy in copies:
        copy.start()
    rows, width = x_ref.shape
    group, members = query_ref.shape[1], query_ref.shape[2] // rows
    head = group // members
    copies[0].wait()
    local = lax.rem(assign_ref[...], rows).astype(F32)
    line = jnp.concatenate([local[:1], local[1:2]], axis=1)
    line = jnp.broadcast_to(line, (ROWS, line.shape[1]))
    own_ref[rows:] = jnp.where(iota(line.shape, 0) == 0, line, 0.0).astype(BF16)
    copies[1].wait()
    own_ref[:rows] = x_ref[...]
    copies[2].wait()
    normed = normalise(x_ref[...], gain_ref[...])

    copies[3].wait()
    basis, out_ch, channels = dec_ref.shape
    depth = basis * ROWS
    for tap in range(TAPS):
        for off in range(TAPS):
            at = (tap * TAPS + off) * 2
            psi_rows_ref[at : at + 2, :] = psi_ref[tap, off]
    spread = (iota((basis, depth), 1) // ROWS == iota((basis, depth), 0)).astype(F32)
    expanded = jnp.dot(psi_rows_ref[...], spread, preferred_element_type=F32)
    pick = iota((ROWS, depth), 1) % ROWS == iota((ROWS, depth), 0)
    for at, (out_row, tap, off) in enumerate(blocks_of(OWN) + blocks_of(ABOVE) + blocks_of(BELOW)):
        source = (tap * TAPS + off) * 2 + out_row
        taps = jnp.broadcast_to(expanded[source : source + 1], (ROWS, depth))
        taps_ref[at * ROWS : (at + 1) * ROWS, :] = jnp.where(pick, taps, 0.0).astype(BF16)
    copies[4].wait()
    inside = middle_ref.shape[0]
    outside = edges_ref.shape[1]
    for first in range(0, out_ch, ROWS):
        size = min(ROWS, out_ch - first)
        pieces = []
        for base in range(basis):
            pieces.append(dec_ref[base, first : first + size, :])
            if size < ROWS:
                pieces.append(jnp.zeros((ROWS - size, channels), BF16))
        mixing = jnp.concatenate(pieces, axis=0)
        mixed = jnp.dot(taps_ref[...], mixing, preferred_element_type=F32).astype(BF16)
        mixed = mixed.reshape(taps_ref.shape[0] // ROWS, ROWS, channels)
        middle_ref[:, first : first + ROWS, :] = mixed[:inside]
        edges_ref[0, :, first : first + ROWS, :] = mixed[inside : inside + outside]
        edges_ref[1, :, first : first + ROWS, :] = mixed[inside + outside :]

    copies[5].wait()
    query = jnp.dot(normed, wqkv_ref[:, :width], preferred_element_type=F32)
    query_t = (query * (math.log2(math.e) / head**0.5)).T.astype(BF16)
    mask = (iota((group, members * rows), 0) // head) == (iota((group, members * rows), 1) // rows)
    for part in range(width // group):
        piece = query_t[part * group : (part + 1) * group]
        wide = jnp.concatenate([piece] * members, axis=1)
        query_ref[part] = jnp.where(mask, wide, jnp.zeros_like(wide))
    wk = wqkv_ref[:, width : 2 * width]
    wk_ref[...] = wk
    key_ref[...] = jnp.dot(normed, wk, preferred_element_type=F32).astype(BF16)
    wvt = wqkv_ref[:, 2 * width :].astype(F32).T.astype(BF16)
    wvt_ref[...] = wvt
    value_ref[...] = lax.dot_general(wvt, normed, NT, preferred_element_type=F32).astype(BF16)


def listed_blocks(sectors, listed_ref):
    reg_here, lon_here = lax.axis_index("reg"), lax.axis_index("lon")
    toward = 1 - 2 * (reg_here % 2)
    found = []
    for at in range(1, listed_ref.shape[1]):
        block = listed_ref[0, at]
        step_reg = (block // sectors - reg_here) * toward
        step_lon = (block % sectors - lon_here + 1 + sectors) % sectors - 1
        place = jnp.where(step_lon == 0, 2, jnp.where(step_lon < 0, 0, 1))
        late = ((step_reg < 0) & (step_lon != 0)).astype(jnp.int32)
        found.append(late * 16 + (step_reg + 1) * 4 + place)
    for low in range(len(found)):
        for high in range(low + 1, len(found)):
            less, more = jnp.minimum(found[low], found[high]), jnp.maximum(found[low], found[high])
            found[low], found[high] = less, more
    return [(code % 16 // 4 - 1, code % 4) for code in found]


def chosen(blocks, rows, both_ref, inner_ref, center_ref, corners_ref):
    near = []
    for step, place in blocks:
        side = pl.ds(pl.multiple_of(jnp.minimum(place, 1) * rows, rows), rows)
        span = pl.ds(pl.multiple_of(place * rows, rows), rows)
        outer = center_ref[...]
        if corners_ref is not None:
            outer = jnp.where(place == 2, outer, corners_ref[side, :])
        other = jnp.where(step > 0, inner_ref[span, :], outer)
        near.append(jnp.where(step == 0, both_ref[side, :], other))
    return jnp.concatenate(near, axis=0)


def project(nodes, gain, wk_ref, wvt_ref):
    normed = normalise(nodes, gain)
    keys = jnp.dot(normed, wk_ref[...], preferred_element_type=F32).astype(BF16)
    values = lax.dot_general(wvt_ref[...], normed, NT, preferred_element_type=F32).astype(BF16)
    return keys, values


def early_kernel(
    sectors,
    listed_ref, both_ref, inner_ref, center_ref,
    gain_ref, wk_ref, wvt_ref, query_ref, key_ref, value_ref,
    top_ref, sum_ref, keys_ref, values_ref,
):
    rows = key_ref.shape[0]
    parts, group, _ = query_ref.shape
    blocks = listed_blocks(sectors, listed_ref)[:EARLY]
    nodes = chosen(blocks, rows, both_ref, inner_ref, center_ref, None)
    keys, values = project(nodes, gain_ref[...], wk_ref, wvt_ref)
    keys_ref[:rows] = key_ref[...]
    keys_ref[rows:] = keys
    for part in range(parts):
        span = slice(part * group, (part + 1) * group)
        values_ref[part, :group, :rows] = value_ref[span]
        values_ref[part, :group, rows:] = values[span]
        values_ref[part, group:, :] = jnp.ones((ROWS, keys_ref.shape[0]), BF16)

    def scored(part):
        span = slice(part * group, (part + 1) * group)
        return jnp.dot(keys_ref[:, span], query_ref[part], preferred_element_type=F32)

    scores = scored(0)
    for part in range(parts):
        now = scores
        if part + 1 < parts:
            scores = scored(part + 1)
        top = jnp.max(now, axis=0, keepdims=True)
        expo = jnp.exp2(now - top).astype(BF16)
        top_ref[part] = jnp.broadcast_to(top, top_ref.shape[1:])
        sum_ref[part] = jnp.dot(values_ref[part], expo, preferred_element_type=F32)


def late_kernel(
    sectors,
    listed_ref, assign_ref, both_ref, inner_ref, center_ref, corners_ref,
    own_ref, gain_ref, wk_ref, wvt_ref, query_ref, top_ref, sum_ref, wout_ref, wlat_ref,
    state_ref, latent_ref, west_ref, east_ref,
    attended_ref,
):
    rows, width = state_ref.shape
    parts, group, lanes = query_ref.shape
    members = lanes // rows
    head = group // members
    blocks = listed_blocks(sectors, listed_ref)[EARLY:]
    nodes = chosen(blocks, rows, both_ref, inner_ref, center_ref, corners_ref)
    keys, values = project(nodes, gain_ref[...], wk_ref, wvt_ref)
    ones = jnp.ones((ROWS, len(blocks) * rows), BF16)
    owner = iota((group, rows), 0) // head

    def scored(part):
        span = slice(part * group, (part + 1) * group)
        return jnp.dot(keys[:, span], query_ref[part], preferred_element_type=F32)

    scores = scored(0)
    for part in range(parts):
        now = scores
        if part + 1 < parts:
            scores = scored(part + 1)
        before = top_ref[part, :1]
        top = jnp.maximum(before, jnp.max(now, axis=0, keepdims=True))
        expo = jnp.exp2(now - top).astype(BF16)
        weights = jnp.concatenate([values[part * group : (part + 1) * group], ones], axis=0)
        summed = jnp.dot(weights, expo, preferred_element_type=F32)
        summed = summed + sum_ref[part] * jnp.exp2(before - top)
        summed = summed[:group] * (1.0 / summed[group : group + 1])
        merged = None
        for member in range(members):
            piece = summed[:, member * rows : (member + 1) * rows]
            merged = piece if merged is None else jnp.where(owner == member, piece, merged)
        attended_ref[:, part * group : (part + 1) * group] = merged.T.astype(BF16)
    state = (
        own_ref[:rows].astype(F32)
        + jnp.dot(attended_ref[...], wout_ref[...], preferred_element_type=F32)
    ).astype(BF16)
    state_ref[...] = state
    value = jnp.dot(state, wlat_ref[...], preferred_element_type=F32)
    latent = (value / (1.0 + jnp.exp(-value))).astype(BF16)
    latent_ref[...] = latent
    lat_rows, lon_cols = assign_ref.shape
    for ref, first in ((west_ref, 0), (east_ref, lon_cols - REACH)):
        cells = ref.shape[0]
        line, node = iota((cells, rows), 0), iota((cells, rows), 1)
        hit = jnp.zeros((cells, rows), F32)
        for row in range(lat_rows):
            for col in range(REACH):
                local = assign_ref[row, first + col] % rows
                hit = jnp.where((line == row * REACH + col) & (node == local), 1.0, hit)
        ref[...] = jnp.dot(hit.astype(BF16), latent, preferred_element_type=F32).astype(BF16)


def hot_rows(values, rows, cols, line):
    column = iota((8, cols), 1)
    node = iota((rows + 2 * SIDE, cols), 0).astype(F32)
    for off in range(TAPS):
        step = off - REACH
        where = jnp.broadcast_to(values, (8, cols))
        if step:
            where = pltpu.roll(where, (-step) % cols, 1)
        reach = column + step
        before = (rows + REACH * line + reach + REACH).astype(F32)
        after = (rows + SIDE + REACH * line + reach - cols).astype(F32)
        where = jnp.where(reach < 0, before, jnp.where(reach >= cols, after, where))
        yield jnp.where(node == where[:1], 1.0, 0.0).astype(BF16)


def shares_of(latent, weights):
    blocks, outputs, channels = weights.shape
    shares = lax.dot_general(
        weights.reshape(blocks * outputs, channels), latent, NT, preferred_element_type=F32
    ).astype(BF16)
    return [shares[at * outputs : (at + 1) * outputs] for at in range(blocks)]


def lines_of(line_ref, start, cols):
    values = line_ref[start : start + ROWS, :].astype(F32)
    return values[:1, :cols], values[:1, cols:]


def own_kernel(
    begin, own_ref, inner_ref, corners_ref, latent_ref, weights_ref, out_ref, hot_ref
):
    cols = out_ref.shape[2]
    rows = latent_ref.shape[0] - 2 * SIDE
    own = lines_of(own_ref, begin[0], cols)
    table = [list(hot_rows(own[line], rows, cols, line)) for line in range(2)]
    acc = [None, None]
    for (out_row, tap, off), share in zip(
        blocks_of(OWN), shares_of(latent_ref[...], weights_ref[...])
    ):
        line = out_row + tap - REACH
        piece = jnp.dot(share, table[line][off], preferred_element_type=F32)
        acc[out_row] = piece if acc[out_row] is None else acc[out_row] + piece
    for row in range(2):
        out_ref[row] = acc[row]
    odd = lax.axis_index("reg") % 2 == 1
    inner, outer = lines_of(inner_ref, begin[1], cols), lines_of(corners_ref, begin[2], cols)
    nodes = rows + 2 * SIDE
    for band, (yes, no) in enumerate(((inner, outer), (outer, inner))):
        for at, line in enumerate((0, 1) if band == 0 else (1, 0)):
            values = jnp.where(odd, yes[line], no[line])
            for off, hot in enumerate(hot_rows(values, rows, cols, line)):
                hot_ref[band, at, off, :nodes] = hot
                hot_ref[band, at, off, nodes:] = jnp.zeros((hot_ref.shape[3] - nodes, cols), BF16)


def band_kernel(from_inner, latent_ref, weights_ref, hot_ref, partial_ref, out_ref, one_ref, two_ref):
    odd = lax.axis_index("reg") % 2
    band = 1 - odd if from_inner else odd
    latent = latent_ref[...]
    lanes, cols = hot_ref.shape[3:]
    outputs = weights_ref.shape[2]
    blank = jnp.zeros((lanes - latent.shape[0], latent.shape[1]), BF16)
    shares = shares_of(jnp.concatenate([latent, blank], axis=0), weights_ref[band])
    for off in range(TAPS):
        span = slice(off * lanes, (off + 1) * lanes)
        one_ref[:, span] = shares[off]
        for row in range(2):
            two_ref[row * outputs : (row + 1) * outputs, span] = shares[TAPS + 2 * off + row]
    depth = TAPS * lanes
    one = jnp.dot(one_ref[...], hot_ref[band, 0].reshape(depth, cols), preferred_element_type=F32)
    two = jnp.dot(two_ref[...], hot_ref[band, 1].reshape(depth, cols), preferred_element_type=F32)
    for row in range(2):
        total = partial_ref[row] + two[row * outputs : (row + 1) * outputs]
        total = total + jnp.where(band == row, one, 0.0)
        if from_inner:
            out_ref[row] = total
        else:
            out_ref[:, row, :] = total[: out_ref.shape[0]].astype(BF16)


def whole(memory=pltpu.VMEM):
    return pl.BlockSpec(memory_space=memory)


def struct(*shape, dtype=BF16):
    return jax.ShapeDtypeStruct(shape, dtype)


def params(limit):
    return pltpu.CompilerParams(vmem_limit_bytes=limit << 20)


def cost(flops, moved):
    return pl.CostEstimate(flops=int(flops), bytes_accessed=int(moved), transcendentals=0)


def shards(nodes, norm_gain, w_qkv, w_out, w_latent, neighbours, assignment, psi, w_dec):
    _, rows, width = nodes.shape
    channels = w_latent.shape[1]
    lat_rows, lon_cols = assignment.shape
    basis, _, out_ch = w_dec.shape
    sectors = lax.axis_size("lon")
    count = neighbours.shape[1]
    x = nodes.reshape(rows, width)
    gain = norm_gain.reshape(1, width)

    def shifted(array, step):
        return lax.ppermute(array, "lon", [(i, (i + step) % sectors) for i in range(sectors)])

    def exchanged(array, first):
        size = lax.axis_size("reg")
        pairs = [(i, i + 1) for i in range(first, size - 1, 2)]
        return lax.ppermute(array, "reg", pairs + [(j, i) for i, j in pairs])

    left = shifted(x, 1)
    right = shifted(x, -1)
    center = exchanged(x, 1)

    outputs = -(-out_ch // ROWS) * ROWS
    head = width // HEADS
    members = LANES // head
    parts = HEADS // members
    inside, outside = len(blocks_of(OWN)), len(blocks_of(ABOVE))
    taps = psi.transpose(2, 3, 1, 0)
    mixing = w_dec.transpose(0, 2, 1)
    own, query, key, value, wk, wvt, middle, edges = pl.pallas_call(
        prepare_kernel,
        in_specs=[whole(pltpu.HBM)] * 6,
        out_specs=[whole()] * 8,
        out_shape=[
            struct(rows + ROWS, width),
            struct(parts, LANES, members * rows),
            struct(rows, width),
            struct(width, rows),
            struct(width, width),
            struct(width, width),
            struct(inside, outputs, channels),
            struct(2, outside, outputs, channels),
        ],
        scratch_shapes=[
            pltpu.VMEM((rows, width), BF16),
            pltpu.VMEM((1, width), F32),
            pltpu.VMEM(w_qkv.shape, BF16),
            pltpu.VMEM(assignment.shape, jnp.int32),
            pltpu.VMEM(taps.shape, F32),
            pltpu.VMEM(mixing.shape, BF16),
            pltpu.VMEM((2 * TAPS * TAPS, basis), F32),
            pltpu.VMEM(((inside + 2 * outside) * ROWS, basis * ROWS), BF16),
            pltpu.SemaphoreType.DMA((6,)),
        ],
        compiler_params=params(32),
        cost_estimate=cost(3e9, 1.2e7),
        name="prepare",
    )(*[pltpu.with_memory_space_constraint(a, pltpu.HBM) for a in (x, gain, w_qkv, assignment, taps, mixing)])
    left, right, center = lax.optimization_barrier((left, right, center))
    both = jnp.concatenate([left, right, own[rows:]], axis=0)
    corners = exchanged(both, 1)
    inner = exchanged(jnp.concatenate([left, right, own], axis=0), 0)

    listed = pltpu.with_memory_space_constraint(neighbours, pltpu.SMEM)
    cells = pltpu.with_memory_space_constraint(assignment, pltpu.SMEM)
    top, summed = pl.pallas_call(
        functools.partial(early_kernel, sectors),
        in_specs=[whole(pltpu.SMEM)] + [whole()] * 9,
        out_specs=[whole()] * 2,
        out_shape=[
            struct(parts, 8, members * rows, dtype=F32),
            struct(parts, LANES + ROWS, members * rows, dtype=F32),
        ],
        scratch_shapes=[
            pltpu.VMEM(((1 + EARLY) * rows, width), BF16),
            pltpu.VMEM((parts, LANES + ROWS, (1 + EARLY) * rows), BF16),
        ],
        compiler_params=params(32),
        cost_estimate=cost(3e9, 6e6),
        name="early",
    )(listed, both, inner, center, gain, wk, wvt, query, key, value)
    state, latent, west, east = pl.pallas_call(
        functools.partial(late_kernel, sectors),
        in_specs=[whole(pltpu.SMEM)] * 2 + [whole()] * 13,
        out_specs=[whole()] * 4,
        out_shape=[struct(rows, width), struct(rows, channels)] + [struct(ROWS, channels)] * 2,
        scratch_shapes=[pltpu.VMEM((rows, width), BF16)],
        compiler_params=params(32),
        cost_estimate=cost(3e9, 6e6),
        name="late",
    )(
        listed, cells, both, inner, center, corners,
        own, gain, wk, wvt, query, top, summed, w_out, w_latent,
    )

    from_left = shifted(east, 1)
    from_right = shifted(west, -1)
    extended = jnp.concatenate([latent, from_left[:SIDE], from_right[:SIDE]], axis=0)
    far = exchanged(extended, 1)
    near = exchanged(extended, 0)

    lanes = -(-(rows + 2 * SIDE) // 256) * 256
    partial, hots = pl.pallas_call(
        functools.partial(own_kernel, (rows, 3 * rows, 2 * rows)),
        in_specs=[whole()] * 5,
        out_specs=[whole()] * 2,
        out_shape=[
            struct(lat_rows, outputs, lon_cols, dtype=F32),
            struct(2, 2, TAPS, lanes, lon_cols),
        ],
        compiler_params=params(32),
        cost_estimate=cost(1e9, 2.5e6),
        name="own_band",
    )(own, inner, corners, extended, middle)
    band_scratch = [
        pltpu.VMEM((outputs, TAPS * lanes), BF16),
        pltpu.VMEM((2 * outputs, TAPS * lanes), BF16),
    ]
    partial = pl.pallas_call(
        functools.partial(band_kernel, True),
        in_specs=[whole()] * 4,
        out_specs=whole(),
        out_shape=struct(lat_rows, outputs, lon_cols, dtype=F32),
        scratch_shapes=band_scratch,
        compiler_params=params(32),
        cost_estimate=cost(1e9, 2.5e6),
        name="inner_band",
    )(near, edges, hots, partial)
    fields = pl.pallas_call(
        functools.partial(band_kernel, False),
        in_specs=[whole()] * 4,
        out_specs=whole(),
        out_shape=struct(out_ch, lat_rows, lon_cols),
        scratch_shapes=band_scratch,
        compiler_params=params(32),
        cost_estimate=cost(1e9, 2.5e6),
        name="outer_band",
    )(far, edges, hots, partial)
    return (state.reshape(1, rows, width), fields.reshape(1, out_ch, lat_rows, lon_cols))


def solution(mesh):
    in_specs = (
        P(None, ("reg", "lon"), None),
        P(),
        P(),
        P(),
        P(),
        P(("reg", "lon"), None),
        P("reg", "lon"),
        P(None, "reg", None, None),
        P(),
    )
    out_specs = (P(None, ("reg", "lon"), None), P(None, None, "reg", "lon"))
    return jax.shard_map(shards, mesh=mesh, in_specs=in_specs, out_specs=out_specs, check_vma=False)
```

```python
import functools
import math

import jax
import jax.numpy as jnp
from jax import lax
from jax.experimental import pallas as pl
from jax.experimental.pallas import tpu as pltpu
from jax.sharding import PartitionSpec as P

HEADS = 16
REACH = 2
TAPS = 2 * REACH + 1
SIDE = 8
ROWS = 16
LANES = 128
EARLY = 2
CANDIDATES = 8
F32 = jnp.float32
BF16 = jnp.bfloat16
NT = (((1,), (1,)), ((), ()))

ABOVE = ((-2, (0,)), (-1, (0, 1)))
OWN = ((0, (0, 1)), (1, (0, 1)))
BELOW = ((3, (1,)), (2, (0, 1)))


def blocks_of(band):
    return [
        (out_row, src - out_row + REACH, off)
        for src, out_rows in band
        for off in range(TAPS)
        for out_row in out_rows
    ]


def iota(shape, dim):
    return lax.broadcasted_iota(jnp.int32, shape, dim)


def normalise(rows, gain):
    values = rows.astype(F32)
    center = values - jnp.mean(values, axis=-1, keepdims=True)
    spread = jnp.mean(center * center, axis=-1, keepdims=True)
    return (center * lax.rsqrt(spread + 1e-05) * gain).astype(BF16)


def mix_kernel(psi_hbm, dec_hbm, middle_ref, edges_ref, psi_ref, dec_ref, psi_rows_ref, taps_ref, sems):
    copies = [
        pltpu.make_async_copy(psi_hbm, psi_ref, sems.at[0]),
        pltpu.make_async_copy(dec_hbm, dec_ref, sems.at[1]),
    ]
    for copy in copies:
        copy.start()
    copies[0].wait()
    basis, out_ch, channels = dec_ref.shape
    depth = basis * ROWS
    for tap in range(TAPS):
        for off in range(TAPS):
            at = (tap * TAPS + off) * 2
            psi_rows_ref[at : at + 2, :] = psi_ref[tap, off]
    spread = (iota((basis, depth), 1) // ROWS == iota((basis, depth), 0)).astype(F32)
    expanded = jnp.dot(psi_rows_ref[...], spread, preferred_element_type=F32)
    pick = iota((ROWS, depth), 1) % ROWS == iota((ROWS, depth), 0)
    for at, (out_row, tap, off) in enumerate(blocks_of(OWN) + blocks_of(ABOVE) + blocks_of(BELOW)):
        source = (tap * TAPS + off) * 2 + out_row
        taps = jnp.broadcast_to(expanded[source : source + 1], (ROWS, depth))
        taps_ref[at * ROWS : (at + 1) * ROWS, :] = jnp.where(pick, taps, 0.0).astype(BF16)
    copies[1].wait()
    inside = middle_ref.shape[0]
    outside = edges_ref.shape[1]
    for first in range(0, out_ch, ROWS):
        size = min(ROWS, out_ch - first)
        pieces = []
        for base in range(basis):
            pieces.append(dec_ref[base, first : first + size, :])
            if size < ROWS:
                pieces.append(jnp.zeros((ROWS - size, channels), BF16))
        mixing = jnp.concatenate(pieces, axis=0)
        mixed = jnp.dot(taps_ref[...], mixing, preferred_element_type=F32).astype(BF16)
        mixed = mixed.reshape(taps_ref.shape[0] // ROWS, ROWS, channels)
        middle_ref[:, first : first + ROWS, :] = mixed[:inside]
        edges_ref[0, :, first : first + ROWS, :] = mixed[inside : inside + outside]
        edges_ref[1, :, first : first + ROWS, :] = mixed[inside + outside :]


def listed_blocks(sectors, listed_ref):
    reg_here, lon_here = lax.axis_index("reg"), lax.axis_index("lon")
    toward = 1 - 2 * (reg_here % 2)
    found = []
    for at in range(1, listed_ref.shape[1]):
        block = listed_ref[0, at]
        step_reg = (block // sectors - reg_here) * toward
        step_lon = (block % sectors - lon_here + 1 + sectors) % sectors - 1
        place = jnp.where(step_lon == 0, 2, jnp.where(step_lon < 0, 0, 1))
        outer = jnp.where(step_lon == 0, 5, 6 + place)
        found.append(jnp.where(step_reg == 0, place, jnp.where(step_reg > 0, 2 + place, outer)))
    for low in range(len(found)):
        for high in range(low + 1, len(found)):
            less, more = jnp.minimum(found[low], found[high]), jnp.maximum(found[low], found[high])
            found[low], found[high] = less, more
    return found


def prepare_kernel(
    sectors,
    x_hbm, gain_hbm, wqkv_hbm, assign_hbm, listed_hbm,
    own_ref, query_ref, key_ref, value_ref, wk_ref, wvt_ref, choice_ref, cells_ref,
    x_ref, gain_ref, wqkv_ref, assign_ref, cell_ref, listed_ref, sems,
):
    copies = [
        pltpu.make_async_copy(source, target, sems.at[at])
        for at, (source, target) in enumerate(
            (
                (x_hbm, x_ref),
                (gain_hbm, gain_ref),
                (wqkv_hbm, wqkv_ref),
                (assign_hbm, assign_ref),
                (assign_hbm, cell_ref),
                (listed_hbm, listed_ref),
            )
        )
    ]
    for copy in copies:
        copy.start()
    rows, width = x_ref.shape
    group, members = query_ref.shape[1], query_ref.shape[2] // rows
    head = group // members
    for copy in copies[3:]:
        copy.wait()
    local = lax.rem(assign_ref[...], rows).astype(F32)
    line = jnp.concatenate([local[:1], local[1:2]], axis=1)
    line = jnp.broadcast_to(line, (ROWS, line.shape[1]))
    own_ref[rows:] = jnp.where(iota(line.shape, 0) == 0, line, 0.0).astype(BF16)
    for at, number in enumerate(listed_blocks(sectors, listed_ref)):
        for candidate in range(CANDIDATES):
            same = jnp.full((ROWS, LANES), jnp.where(number == candidate, 1.0, 0.0), F32)
            choice_ref[at, candidate] = same.astype(BF16)
    lat_rows, lon_cols = cell_ref.shape
    place, node = iota((ROWS, rows), 0), iota((ROWS, rows), 1)
    for side, first in enumerate((0, lon_cols - REACH)):
        hit = jnp.zeros((ROWS, rows), F32)
        for row in range(lat_rows):
            for col in range(REACH):
                cell = cell_ref[row, first + col] % rows
                hit = jnp.where((place == row * REACH + col) & (node == cell), 1.0, hit)
        cells_ref[side * ROWS : (side + 1) * ROWS] = hit.astype(BF16)
    copies[0].wait()
    own_ref[:rows] = x_ref[...]
    copies[1].wait()
    normed = normalise(x_ref[...], gain_ref[...])
    copies[2].wait()
    query = jnp.dot(normed, wqkv_ref[:, :width], preferred_element_type=F32)
    query_t = (query * (math.log2(math.e) / head**0.5)).T.astype(BF16)
    mask = (iota((group, members * rows), 0) // head) == (iota((group, members * rows), 1) // rows)
    for part in range(width // group):
        piece = query_t[part * group : (part + 1) * group]
        wide = jnp.concatenate([piece] * members, axis=1)
        query_ref[part] = jnp.where(mask, wide, jnp.zeros_like(wide))
    wk = wqkv_ref[:, width : 2 * width]
    wk_ref[...] = wk
    key_ref[...] = jnp.dot(normed, wk, preferred_element_type=F32).astype(BF16)
    wvt = wqkv_ref[:, 2 * width :].astype(F32).T.astype(BF16)
    wvt_ref[...] = wvt
    value_ref[...] = lax.dot_general(wvt, normed, NT, preferred_element_type=F32).astype(BF16)


def chosen(entries, rows, choice_ref, both_ref, inner_ref, center_ref, corners_ref):
    candidates = [both_ref[:rows], both_ref[rows : 2 * rows]]
    candidates += [inner_ref[at * rows : (at + 1) * rows] for at in range(3)]
    candidates.append(center_ref[...])
    if corners_ref is not None:
        candidates += [corners_ref[:rows], corners_ref[rows : 2 * rows]]
    tall, wide = rows // ROWS, center_ref.shape[1] // LANES
    near = []
    for entry in entries:
        total = None
        for at, candidate in enumerate(candidates):
            weight = jnp.concatenate([choice_ref[entry, at]] * wide, axis=1)
            part = candidate * jnp.concatenate([weight] * tall, axis=0)
            total = part if total is None else total + part
        near.append(total)
    return jnp.concatenate(near, axis=0)


def project(nodes, gain, wk_ref, wvt_ref):
    normed = normalise(nodes, gain)
    keys = jnp.dot(normed, wk_ref[...], preferred_element_type=F32).astype(BF16)
    values = lax.dot_general(wvt_ref[...], normed, NT, preferred_element_type=F32).astype(BF16)
    return keys, values


def early_kernel(
    choice_ref, both_ref, inner_ref, center_ref,
    gain_ref, wk_ref, wvt_ref, query_ref, key_ref, value_ref,
    top_ref, sum_ref, keys_ref, values_ref,
):
    rows = key_ref.shape[0]
    parts, group, _ = query_ref.shape
    nodes = chosen(range(EARLY), rows, choice_ref, both_ref, inner_ref, center_ref, None)
    keys, values = project(nodes, gain_ref[...], wk_ref, wvt_ref)
    keys_ref[:rows] = key_ref[...]
    keys_ref[rows:] = keys
    for part in range(parts):
        span = slice(part * group, (part + 1) * group)
        values_ref[part, :group, :rows] = value_ref[span]
        values_ref[part, :group, rows:] = values[span]
        values_ref[part, group:, :] = jnp.ones((ROWS, keys_ref.shape[0]), BF16)

    def scored(part):
        span = slice(part * group, (part + 1) * group)
        return jnp.dot(keys_ref[:, span], query_ref[part], preferred_element_type=F32)

    scores = scored(0)
    for part in range(parts):
        now = scores
        if part + 1 < parts:
            scores = scored(part + 1)
        top = jnp.max(now, axis=0, keepdims=True)
        expo = jnp.exp2(now - top).astype(BF16)
        top_ref[part] = jnp.broadcast_to(top, top_ref.shape[1:])
        sum_ref[part] = jnp.dot(values_ref[part], expo, preferred_element_type=F32)


def late_kernel(
    choice_ref, cells_ref, both_ref, inner_ref, center_ref, corners_ref,
    own_ref, gain_ref, wk_ref, wvt_ref, query_ref, top_ref, sum_ref, wout_ref, wlat_ref,
    state_ref, latent_ref, west_ref, east_ref,
    attended_ref,
):
    rows, width = state_ref.shape
    parts, group, lanes = query_ref.shape
    members = lanes // rows
    head = group // members
    entries = range(EARLY, choice_ref.shape[0])
    nodes = chosen(entries, rows, choice_ref, both_ref, inner_ref, center_ref, corners_ref)
    keys, values = project(nodes, gain_ref[...], wk_ref, wvt_ref)
    ones = jnp.ones((ROWS, nodes.shape[0]), BF16)
    owner = iota((group, rows), 0) // head

    def scored(part):
        span = slice(part * group, (part + 1) * group)
        return jnp.dot(keys[:, span], query_ref[part], preferred_element_type=F32)

    scores = scored(0)
    for part in range(parts):
        now = scores
        if part + 1 < parts:
            scores = scored(part + 1)
        before = top_ref[part, :1]
        top = jnp.maximum(before, jnp.max(now, axis=0, keepdims=True))
        expo = jnp.exp2(now - top).astype(BF16)
        weights = jnp.concatenate([values[part * group : (part + 1) * group], ones], axis=0)
        summed = jnp.dot(weights, expo, preferred_element_type=F32)
        summed = summed + sum_ref[part] * jnp.exp2(before - top)
        summed = summed[:group] * (1.0 / summed[group : group + 1])
        merged = None
        for member in range(members):
            piece = summed[:, member * rows : (member + 1) * rows]
            merged = piece if merged is None else jnp.where(owner == member, piece, merged)
        attended_ref[:, part * group : (part + 1) * group] = merged.T.astype(BF16)
    state = (
        own_ref[:rows].astype(F32)
        + jnp.dot(attended_ref[...], wout_ref[...], preferred_element_type=F32)
    ).astype(BF16)
    state_ref[...] = state
    value = jnp.dot(state, wlat_ref[...], preferred_element_type=F32)
    latent = (value / (1.0 + jnp.exp(-value))).astype(BF16)
    latent_ref[...] = latent
    cells = jnp.dot(cells_ref[...], latent, preferred_element_type=F32).astype(BF16)
    west_ref[...] = cells[:ROWS]
    east_ref[...] = cells[ROWS:]


def hot_rows(values, rows, cols, line):
    column = iota((8, cols), 1)
    node = iota((rows + 2 * SIDE, cols), 0).astype(F32)
    for off in range(TAPS):
        step = off - REACH
        where = jnp.broadcast_to(values, (8, cols))
        if step:
            where = pltpu.roll(where, (-step) % cols, 1)
        reach = column + step
        before = (rows + REACH * line + reach + REACH).astype(F32)
        after = (rows + SIDE + REACH * line + reach - cols).astype(F32)
        where = jnp.where(reach < 0, before, jnp.where(reach >= cols, after, where))
        yield jnp.where(node == where[:1], 1.0, 0.0).astype(BF16)


def shares_of(latent, weights):
    blocks, outputs, channels = weights.shape
    shares = lax.dot_general(
        weights.reshape(blocks * outputs, channels), latent, NT, preferred_element_type=F32
    ).astype(BF16)
    return [shares[at * outputs : (at + 1) * outputs] for at in range(blocks)]


def lines_of(line_ref, start, cols):
    values = line_ref[start : start + ROWS, :].astype(F32)
    return values[:1, :cols], values[:1, cols:]


def own_kernel(
    begin, state_ref, own_ref, inner_ref, corners_ref, latent_ref, weights_ref,
    out_ref, hot_ref, kept_ref,
):
    kept_ref[...] = state_ref[...]
    cols = out_ref.shape[2]
    rows = latent_ref.shape[0] - 2 * SIDE
    own = lines_of(own_ref, begin[0], cols)
    table = [list(hot_rows(own[line], rows, cols, line)) for line in range(2)]
    acc = [None, None]
    for (out_row, tap, off), share in zip(
        blocks_of(OWN), shares_of(latent_ref[...], weights_ref[...])
    ):
        line = out_row + tap - REACH
        piece = jnp.dot(share, table[line][off], preferred_element_type=F32)
        acc[out_row] = piece if acc[out_row] is None else acc[out_row] + piece
    for row in range(2):
        out_ref[row] = acc[row]
    odd = lax.axis_index("reg") % 2 == 1
    inner, outer = lines_of(inner_ref, begin[1], cols), lines_of(corners_ref, begin[2], cols)
    nodes = rows + 2 * SIDE
    for band, (yes, no) in enumerate(((inner, outer), (outer, inner))):
        for at, line in enumerate((0, 1) if band == 0 else (1, 0)):
            values = jnp.where(odd, yes[line], no[line])
            for off, hot in enumerate(hot_rows(values, rows, cols, line)):
                hot_ref[band, at, off, :nodes] = hot
                hot_ref[band, at, off, nodes:] = jnp.zeros((hot_ref.shape[3] - nodes, cols), BF16)


def band_kernel(from_inner, latent_ref, weights_ref, hot_ref, partial_ref, out_ref, one_ref, two_ref):
    odd = lax.axis_index("reg") % 2
    band = 1 - odd if from_inner else odd
    latent = latent_ref[...]
    lanes, cols = hot_ref.shape[3:]
    outputs = weights_ref.shape[2]
    blank = jnp.zeros((lanes - latent.shape[0], latent.shape[1]), BF16)
    shares = shares_of(jnp.concatenate([latent, blank], axis=0), weights_ref[band])
    for off in range(TAPS):
        span = slice(off * lanes, (off + 1) * lanes)
        one_ref[:, span] = shares[off]
        for row in range(2):
            two_ref[row * outputs : (row + 1) * outputs, span] = shares[TAPS + 2 * off + row]
    depth = TAPS * lanes
    one = jnp.dot(one_ref[...], hot_ref[band, 0].reshape(depth, cols), preferred_element_type=F32)
    two = jnp.dot(two_ref[...], hot_ref[band, 1].reshape(depth, cols), preferred_element_type=F32)
    for row in range(2):
        total = partial_ref[row] + two[row * outputs : (row + 1) * outputs]
        total = total + jnp.where(band == row, one, 0.0)
        if from_inner:
            out_ref[row] = total
        else:
            out_ref[:, row, :] = total[: out_ref.shape[0]].astype(BF16)


def whole(memory=pltpu.VMEM):
    return pl.BlockSpec(memory_space=memory)


def struct(*shape, dtype=BF16):
    return jax.ShapeDtypeStruct(shape, dtype)


def params(limit):
    return pltpu.CompilerParams(vmem_limit_bytes=limit << 20)


def cost(flops, moved):
    return pl.CostEstimate(flops=int(flops), bytes_accessed=int(moved), transcendentals=0)


def shards(nodes, norm_gain, w_qkv, w_out, w_latent, neighbours, assignment, psi, w_dec):
    _, rows, width = nodes.shape
    channels = w_latent.shape[1]
    lat_rows, lon_cols = assignment.shape
    basis, _, out_ch = w_dec.shape
    sectors = lax.axis_size("lon")
    count = neighbours.shape[1]
    x = nodes.reshape(rows, width)
    gain = norm_gain.reshape(1, width)

    def shifted(array, step):
        return lax.ppermute(array, "lon", [(i, (i + step) % sectors) for i in range(sectors)])

    def exchanged(array, first):
        size = lax.axis_size("reg")
        pairs = [(i, i + 1) for i in range(first, size - 1, 2)]
        return lax.ppermute(array, "reg", pairs + [(j, i) for i, j in pairs])

    def in_hbm(*arrays):
        return [pltpu.with_memory_space_constraint(array, pltpu.HBM) for array in arrays]

    center = exchanged(x, 1)
    left = shifted(x, 1)
    right = shifted(x, -1)

    outputs = -(-out_ch // ROWS) * ROWS
    head = width // HEADS
    members = LANES // head
    parts = HEADS // members
    inside, outside = len(blocks_of(OWN)), len(blocks_of(ABOVE))
    taps = psi.transpose(2, 3, 1, 0)
    mixing = w_dec.transpose(0, 2, 1)
    own, query, key, value, wk, wvt, choice, cells = pl.pallas_call(
        functools.partial(prepare_kernel, sectors),
        in_specs=[whole(pltpu.HBM)] * 5,
        out_specs=[whole()] * 8,
        out_shape=[
            struct(rows + ROWS, width),
            struct(parts, LANES, members * rows),
            struct(rows, width),
            struct(width, rows),
            struct(width, width),
            struct(width, width),
            struct(count - 1, CANDIDATES, ROWS, LANES),
            struct(2 * ROWS, rows),
        ],
        scratch_shapes=[
            pltpu.VMEM((rows, width), BF16),
            pltpu.VMEM((1, width), F32),
            pltpu.VMEM(w_qkv.shape, BF16),
            pltpu.VMEM(assignment.shape, jnp.int32),
            pltpu.SMEM(assignment.shape, jnp.int32),
            pltpu.SMEM(neighbours.shape, jnp.int32),
            pltpu.SemaphoreType.DMA((6,)),
        ],
        compiler_params=params(32),
        cost_estimate=cost(2e9, 5e6),
        name="prepare",
    )(*in_hbm(x, gain, w_qkv, assignment, neighbours))
    center, left = lax.optimization_barrier((center, left))
    center, right = lax.optimization_barrier((center, right))
    both = jnp.concatenate([left, right, own[rows:]], axis=0)
    corners = exchanged(both, 1)
    inner = exchanged(jnp.concatenate([left, right, own], axis=0), 0)

    top, summed = pl.pallas_call(
        early_kernel,
        in_specs=[whole()] * 10,
        out_specs=[whole()] * 2,
        out_shape=[
            struct(parts, 8, members * rows, dtype=F32),
            struct(parts, LANES + ROWS, members * rows, dtype=F32),
        ],
        scratch_shapes=[
            pltpu.VMEM(((1 + EARLY) * rows, width), BF16),
            pltpu.VMEM((parts, LANES + ROWS, (1 + EARLY) * rows), BF16),
        ],
        compiler_params=params(32),
        cost_estimate=cost(3e9, 6e6),
        name="early",
    )(choice, both, inner, center, gain, wk, wvt, query, key, value)
    taps, mixing, top = lax.optimization_barrier((taps, mixing, top))
    middle, edges = pl.pallas_call(
        mix_kernel,
        in_specs=[whole(pltpu.HBM)] * 2,
        out_specs=[whole()] * 2,
        out_shape=[struct(inside, outputs, channels), struct(2, outside, outputs, channels)],
        scratch_shapes=[
            pltpu.VMEM(taps.shape, F32),
            pltpu.VMEM(mixing.shape, BF16),
            pltpu.VMEM((2 * TAPS * TAPS, basis), F32),
            pltpu.VMEM(((inside + 2 * outside) * ROWS, basis * ROWS), BF16),
            pltpu.SemaphoreType.DMA((2,)),
        ],
        compiler_params=params(32),
        cost_estimate=cost(2e9, 5e6),
        name="mix",
    )(*in_hbm(taps, mixing))
    top, middle = lax.optimization_barrier((top, middle))
    state, latent, west, east = pl.pallas_call(
        late_kernel,
        in_specs=[whole()] * 15,
        out_specs=[whole()] * 4,
        out_shape=[pltpu.VMEM((rows, width), BF16), struct(rows, channels)]
        + [struct(ROWS, channels)] * 2,
        scratch_shapes=[pltpu.VMEM((rows, width), BF16)],
        compiler_params=params(32),
        cost_estimate=cost(3e9, 6e6),
        name="late",
    )(
        choice, cells, both, inner, center, corners,
        own, gain, wk, wvt, query, top, summed, w_out, w_latent,
    )

    from_left = shifted(east, 1)
    from_right = shifted(west, -1)
    extended = jnp.concatenate([latent, from_left[:SIDE], from_right[:SIDE]], axis=0)
    far = exchanged(extended, 1)
    near = exchanged(extended, 0)

    lanes = -(-(rows + 2 * SIDE) // 256) * 256
    partial, hots, state = pl.pallas_call(
        functools.partial(own_kernel, (rows, 3 * rows, 2 * rows)),
        in_specs=[whole()] * 6,
        out_specs=[whole()] * 3,
        out_shape=[
            struct(lat_rows, outputs, lon_cols, dtype=F32),
            struct(2, 2, TAPS, lanes, lon_cols),
            struct(rows, width),
        ],
        compiler_params=params(32),
        cost_estimate=cost(1e9, 2.5e6),
        name="own_band",
    )(state, own, inner, corners, extended, middle)
    band_scratch = [
        pltpu.VMEM((outputs, TAPS * lanes), BF16),
        pltpu.VMEM((2 * outputs, TAPS * lanes), BF16),
    ]
    partial = pl.pallas_call(
        functools.partial(band_kernel, True),
        in_specs=[whole()] * 4,
        out_specs=whole(),
        out_shape=struct(lat_rows, outputs, lon_cols, dtype=F32),
        scratch_shapes=band_scratch,
        compiler_params=params(32),
        cost_estimate=cost(1e9, 2.5e6),
        name="inner_band",
    )(near, edges, hots, partial)
    fields = pl.pallas_call(
        functools.partial(band_kernel, False),
        in_specs=[whole()] * 4,
        out_specs=whole(),
        out_shape=struct(out_ch, lat_rows, lon_cols),
        scratch_shapes=band_scratch,
        compiler_params=params(32),
        cost_estimate=cost(1e9, 2.5e6),
        name="outer_band",
    )(far, edges, hots, partial)
    return (state.reshape(1, rows, width), fields.reshape(1, out_ch, lat_rows, lon_cols))


def solution(mesh):
    in_specs = (
        P(None, ("reg", "lon"), None),
        P(),
        P(),
        P(),
        P(),
        P(("reg", "lon"), None),
        P("reg", "lon"),
        P(None, "reg", None, None),
        P(),
    )
    out_specs = (P(None, ("reg", "lon"), None), P(None, None, "reg", "lon"))
    return jax.shard_map(shards, mesh=mesh, in_specs=in_specs, out_specs=out_specs, check_vma=False)
```

```python
import functools
import math

import jax
import jax.numpy as jnp
from jax import lax
from jax.experimental import pallas as pl
from jax.experimental.pallas import tpu as pltpu
from jax.sharding import PartitionSpec as P

HEADS = 16
REACH = 2
TAPS = 2 * REACH + 1
SIDE = 8
ROWS = 16
LANES = 128
EARLY = 2
CANDIDATES = 8
F32 = jnp.float32
BF16 = jnp.bfloat16
NT = (((1,), (1,)), ((), ()))

ABOVE = ((-2, (0,)), (-1, (0, 1)))
OWN = ((0, (0, 1)), (1, (0, 1)))
BELOW = ((3, (1,)), (2, (0, 1)))


def blocks_of(band):
    return [
        (out_row, src - out_row + REACH, off)
        for src, out_rows in band
        for off in range(TAPS)
        for out_row in out_rows
    ]


def iota(shape, dim):
    return lax.broadcasted_iota(jnp.int32, shape, dim)


def normalise(rows, gain):
    values = rows.astype(F32)
    center = values - jnp.mean(values, axis=-1, keepdims=True)
    spread = jnp.mean(center * center, axis=-1, keepdims=True)
    return (center * lax.rsqrt(spread + 1e-05) * gain).astype(BF16)


def mix_kernel(blocks, psi_ref, dec_ref, mixed_ref, psi_rows_ref, taps_ref):
    basis, out_ch, channels = dec_ref.shape
    depth = basis * ROWS
    for tap in range(TAPS):
        for off in range(TAPS):
            at = (tap * TAPS + off) * 2
            psi_rows_ref[at : at + 2, :] = psi_ref[tap, off]
    spread = (iota((basis, depth), 1) // ROWS == iota((basis, depth), 0)).astype(F32)
    expanded = jnp.dot(psi_rows_ref[...], spread, preferred_element_type=F32)
    pick = iota((ROWS, depth), 1) % ROWS == iota((ROWS, depth), 0)
    for at, (out_row, tap, off) in enumerate(blocks):
        source = (tap * TAPS + off) * 2 + out_row
        taps = jnp.broadcast_to(expanded[source : source + 1], (ROWS, depth))
        taps_ref[at * ROWS : (at + 1) * ROWS, :] = jnp.where(pick, taps, 0.0).astype(BF16)
    for first in range(0, out_ch, ROWS):
        size = min(ROWS, out_ch - first)
        pieces = []
        for base in range(basis):
            pieces.append(dec_ref[base, first : first + size, :])
            if size < ROWS:
                pieces.append(jnp.zeros((ROWS - size, channels), BF16))
        mixing = jnp.concatenate(pieces, axis=0)
        mixed = jnp.dot(taps_ref[...], mixing, preferred_element_type=F32).astype(BF16)
        mixed_ref[:, first : first + ROWS, :] = mixed.reshape(len(blocks), ROWS, channels)


def listed_blocks(sectors, listed_ref):
    reg_here, lon_here = lax.axis_index("reg"), lax.axis_index("lon")
    toward = 1 - 2 * (reg_here % 2)
    found = []
    for at in range(1, listed_ref.shape[1]):
        block = listed_ref[0, at]
        step_reg = (block // sectors - reg_here) * toward
        step_lon = (block % sectors - lon_here + 1 + sectors) % sectors - 1
        place = jnp.where(step_lon == 0, 2, jnp.where(step_lon < 0, 0, 1))
        outer = jnp.where(step_lon == 0, 5, 7 - place)
        found.append(jnp.where(step_reg == 0, place, jnp.where(step_reg > 0, 2 + place, outer)))
    for low in range(len(found)):
        for high in range(low + 1, len(found)):
            less, more = jnp.minimum(found[low], found[high]), jnp.maximum(found[low], found[high])
            found[low], found[high] = less, more
    return found


def gather_kernel(x_hbm, assign_hbm, own_ref, assign_ref, sems):
    rows = own_ref.shape[0] - ROWS
    copies = [
        pltpu.make_async_copy(assign_hbm, assign_ref, sems.at[0]),
        pltpu.make_async_copy(x_hbm, own_ref.at[pl.ds(0, rows)], sems.at[1]),
    ]
    for copy in copies:
        copy.start()
    copies[0].wait()
    local = lax.rem(assign_ref[...], rows).astype(F32)
    line = jnp.concatenate([local[:1], local[1:2]], axis=1)
    line = jnp.broadcast_to(line, (ROWS, line.shape[1]))
    own_ref[rows:] = jnp.where(iota(line.shape, 0) == 0, line, 0.0).astype(BF16)
    copies[1].wait()


def prepare_kernel(
    sectors,
    own_ref, gain_hbm, wqkv_hbm, assign_hbm, listed_hbm,
    query_ref, key_ref, value_ref, wk_ref, wvt_ref, choice_ref, cells_ref,
    gain_ref, wqkv_ref, cell_ref, listed_ref, sems,
):
    copies = [
        pltpu.make_async_copy(source, target, sems.at[at])
        for at, (source, target) in enumerate(
            (
                (gain_hbm, gain_ref),
                (wqkv_hbm, wqkv_ref),
                (assign_hbm, cell_ref),
                (listed_hbm, listed_ref),
            )
        )
    ]
    for copy in copies:
        copy.start()
    rows, width = key_ref.shape
    group, members = query_ref.shape[1], query_ref.shape[2] // rows
    head = group // members
    for copy in copies[2:]:
        copy.wait()
    for at, number in enumerate(listed_blocks(sectors, listed_ref)):
        for candidate in range(CANDIDATES):
            same = jnp.full((ROWS, LANES), jnp.where(number == candidate, 1.0, 0.0), F32)
            choice_ref[at, candidate] = same.astype(BF16)
    lat_rows, lon_cols = cell_ref.shape
    place, node = iota((ROWS, rows), 0), iota((ROWS, rows), 1)
    for side, first in enumerate((0, lon_cols - REACH)):
        hit = jnp.zeros((ROWS, rows), F32)
        for row in range(lat_rows):
            for col in range(REACH):
                cell = cell_ref[row, first + col] % rows
                hit = jnp.where((place == row * REACH + col) & (node == cell), 1.0, hit)
        cells_ref[side * ROWS : (side + 1) * ROWS] = hit.astype(BF16)
    copies[0].wait()
    normed = normalise(own_ref[:rows], gain_ref[...])
    copies[1].wait()
    query = jnp.dot(normed, wqkv_ref[:, :width], preferred_element_type=F32)
    query_t = (query * (math.log2(math.e) / head**0.5)).T.astype(BF16)
    mask = (iota((group, members * rows), 0) // head) == (iota((group, members * rows), 1) // rows)
    for part in range(width // group):
        piece = query_t[part * group : (part + 1) * group]
        wide = jnp.concatenate([piece] * members, axis=1)
        query_ref[part] = jnp.where(mask, wide, jnp.zeros_like(wide))
    wk = wqkv_ref[:, width : 2 * width]
    wk_ref[...] = wk
    key_ref[...] = jnp.dot(normed, wk, preferred_element_type=F32).astype(BF16)
    wvt = wqkv_ref[:, 2 * width :].astype(F32).T.astype(BF16)
    wvt_ref[...] = wvt
    value_ref[...] = lax.dot_general(wvt, normed, NT, preferred_element_type=F32).astype(BF16)


def chosen(entries, rows, choice_ref, west_ref, east_ref, beside_ref, inner_ref, outer_ref, corner_ref):
    candidates = [west_ref[...], east_ref[...]]
    candidates += [beside_ref[...], inner_ref[:rows], inner_ref[rows : 2 * rows]]
    candidates.append(outer_ref[rows : 2 * rows])
    if corner_ref is not None:
        candidates += [outer_ref[:rows], corner_ref[...]]
    tall, wide = rows // ROWS, west_ref.shape[1] // LANES
    near = []
    for entry in entries:
        total = None
        for at, candidate in enumerate(candidates):
            weight = jnp.concatenate([choice_ref[entry, at]] * wide, axis=1)
            part = candidate * jnp.concatenate([weight] * tall, axis=0)
            total = part if total is None else total + part
        near.append(total)
    return jnp.concatenate(near, axis=0)


def project(nodes, gain, wk_ref, wvt_ref):
    normed = normalise(nodes, gain)
    keys = jnp.dot(normed, wk_ref[...], preferred_element_type=F32).astype(BF16)
    values = lax.dot_general(wvt_ref[...], normed, NT, preferred_element_type=F32).astype(BF16)
    return keys, values


def early_kernel(
    choice_ref, west_ref, east_ref, beside_ref, inner_ref, outer_ref,
    gain_ref, wk_ref, wvt_ref, query_ref, key_ref, value_ref,
    top_ref, sum_ref, keys_ref, values_ref,
):
    rows = key_ref.shape[0]
    parts, group, _ = query_ref.shape
    nodes = chosen(range(EARLY), rows, choice_ref, west_ref, east_ref, beside_ref, inner_ref, outer_ref, None)
    keys, values = project(nodes, gain_ref[...], wk_ref, wvt_ref)
    keys_ref[:rows] = key_ref[...]
    keys_ref[rows:] = keys
    for part in range(parts):
        span = slice(part * group, (part + 1) * group)
        values_ref[part, :group, :rows] = value_ref[span]
        values_ref[part, :group, rows:] = values[span]
        values_ref[part, group:, :] = jnp.ones((ROWS, keys_ref.shape[0]), BF16)

    def scored(part):
        span = slice(part * group, (part + 1) * group)
        return jnp.dot(keys_ref[:, span], query_ref[part], preferred_element_type=F32)

    scores = scored(0)
    for part in range(parts):
        now = scores
        if part + 1 < parts:
            scores = scored(part + 1)
        top = jnp.max(now, axis=0, keepdims=True)
        expo = jnp.exp2(now - top).astype(BF16)
        top_ref[part] = jnp.broadcast_to(top, top_ref.shape[1:])
        sum_ref[part] = jnp.dot(values_ref[part], expo, preferred_element_type=F32)


def late_kernel(
    choice_ref, cells_ref, west_ref, east_ref, beside_ref, inner_ref, outer_ref, corner_ref,
    own_ref, gain_ref, wk_ref, wvt_ref, query_ref, top_ref, sum_ref, wout_ref, wlat_ref,
    state_ref, latent_ref, first_ref, last_ref,
    attended_ref,
):
    rows, width = state_ref.shape
    parts, group, lanes = query_ref.shape
    members = lanes // rows
    head = group // members
    entries = range(EARLY, choice_ref.shape[0])
    nodes = chosen(
        entries, rows, choice_ref, west_ref, east_ref, beside_ref, inner_ref, outer_ref, corner_ref
    )
    keys, values = project(nodes, gain_ref[...], wk_ref, wvt_ref)
    ones = jnp.ones((ROWS, nodes.shape[0]), BF16)
    owner = iota((group, rows), 0) // head

    def scored(part):
        span = slice(part * group, (part + 1) * group)
        return jnp.dot(keys[:, span], query_ref[part], preferred_element_type=F32)

    scores = scored(0)
    for part in range(parts):
        now = scores
        if part + 1 < parts:
            scores = scored(part + 1)
        before = top_ref[part, :1]
        top = jnp.maximum(before, jnp.max(now, axis=0, keepdims=True))
        expo = jnp.exp2(now - top).astype(BF16)
        weights = jnp.concatenate([values[part * group : (part + 1) * group], ones], axis=0)
        summed = jnp.dot(weights, expo, preferred_element_type=F32)
        summed = summed + sum_ref[part] * jnp.exp2(before - top)
        summed = summed[:group] * (1.0 / summed[group : group + 1])
        merged = None
        for member in range(members):
            piece = summed[:, member * rows : (member + 1) * rows]
            merged = piece if merged is None else jnp.where(owner == member, piece, merged)
        attended_ref[:, part * group : (part + 1) * group] = merged.T.astype(BF16)
    state = (
        own_ref[:rows].astype(F32)
        + jnp.dot(attended_ref[...], wout_ref[...], preferred_element_type=F32)
    ).astype(BF16)
    state_ref[...] = state
    value = jnp.dot(state, wlat_ref[...], preferred_element_type=F32)
    latent = (value / (1.0 + jnp.exp(-value))).astype(BF16)
    latent_ref[...] = latent
    cells = jnp.dot(cells_ref[...], latent, preferred_element_type=F32).astype(BF16)
    first_ref[...] = cells[:ROWS]
    last_ref[...] = cells[ROWS:]


def hot_rows(values, rows, cols, line):
    column = iota((8, cols), 1)
    node = iota((rows + 2 * SIDE, cols), 0).astype(F32)
    for off in range(TAPS):
        step = off - REACH
        where = jnp.broadcast_to(values, (8, cols))
        if step:
            where = pltpu.roll(where, (-step) % cols, 1)
        reach = column + step
        before = (rows + REACH * line + reach + REACH).astype(F32)
        after = (rows + SIDE + REACH * line + reach - cols).astype(F32)
        where = jnp.where(reach < 0, before, jnp.where(reach >= cols, after, where))
        yield jnp.where(node == where[:1], 1.0, 0.0).astype(BF16)


def shares_of(latent, weights):
    blocks, outputs, channels = weights.shape
    shares = lax.dot_general(
        weights.reshape(blocks * outputs, channels), latent, NT, preferred_element_type=F32
    ).astype(BF16)
    return [shares[at * outputs : (at + 1) * outputs] for at in range(blocks)]


def lines_of(line_ref, start, cols):
    values = line_ref[start : start + ROWS, :].astype(F32)
    return values[:1, :cols], values[:1, cols:]


def own_kernel(
    begin, state_ref, own_ref, inner_ref, outer_ref, latent_ref, weights_ref,
    out_ref, hot_ref, kept_ref,
):
    kept_ref[...] = state_ref[...]
    cols = out_ref.shape[2]
    rows = latent_ref.shape[0] - 2 * SIDE
    own = lines_of(own_ref, begin[0], cols)
    table = [list(hot_rows(own[line], rows, cols, line)) for line in range(2)]
    acc = [None, None]
    for (out_row, tap, off), share in zip(
        blocks_of(OWN), shares_of(latent_ref[...], weights_ref[...])
    ):
        line = out_row + tap - REACH
        piece = jnp.dot(share, table[line][off], preferred_element_type=F32)
        acc[out_row] = piece if acc[out_row] is None else acc[out_row] + piece
    for row in range(2):
        out_ref[row] = acc[row]
    odd = lax.axis_index("reg") % 2 == 1
    inner, outer = lines_of(inner_ref, begin[1], cols), lines_of(outer_ref, begin[2], cols)
    nodes = rows + 2 * SIDE
    for band, (yes, no) in enumerate(((inner, outer), (outer, inner))):
        for at, line in enumerate((0, 1) if band == 0 else (1, 0)):
            values = jnp.where(odd, yes[line], no[line])
            for off, hot in enumerate(hot_rows(values, rows, cols, line)):
                hot_ref[band, at, off, :nodes] = hot
                hot_ref[band, at, off, nodes:] = jnp.zeros((hot_ref.shape[3] - nodes, cols), BF16)


def band_kernel(from_inner, latent_ref, weights_ref, hot_ref, partial_ref, out_ref, one_ref, two_ref):
    odd = lax.axis_index("reg") % 2
    band = 1 - odd if from_inner else odd
    latent = latent_ref[...]
    lanes, cols = hot_ref.shape[3:]
    outputs = weights_ref.shape[1]
    blank = jnp.zeros((lanes - latent.shape[0], latent.shape[1]), BF16)
    blocks = len(blocks_of(ABOVE))
    weights = weights_ref[pl.ds(band * blocks, blocks)]
    shares = shares_of(jnp.concatenate([latent, blank], axis=0), weights)
    for off in range(TAPS):
        span = slice(off * lanes, (off + 1) * lanes)
        one_ref[:, span] = shares[off]
        for row in range(2):
            two_ref[row * outputs : (row + 1) * outputs, span] = shares[TAPS + 2 * off + row]
    depth = TAPS * lanes
    one = jnp.dot(one_ref[...], hot_ref[band, 0].reshape(depth, cols), preferred_element_type=F32)
    two = jnp.dot(two_ref[...], hot_ref[band, 1].reshape(depth, cols), preferred_element_type=F32)
    for row in range(2):
        total = partial_ref[row] + two[row * outputs : (row + 1) * outputs]
        total = total + jnp.where(band == row, one, 0.0)
        if from_inner:
            out_ref[row] = total
        else:
            out_ref[:, row, :] = total[: out_ref.shape[0]].astype(BF16)


def whole(memory=pltpu.VMEM):
    return pl.BlockSpec(memory_space=memory)


def struct(*shape, dtype=BF16):
    return jax.ShapeDtypeStruct(shape, dtype)


def params(limit):
    return pltpu.CompilerParams(vmem_limit_bytes=limit << 20)


def cost(flops, moved):
    return pl.CostEstimate(flops=int(flops), bytes_accessed=int(moved), transcendentals=0)


def shards(nodes, norm_gain, w_qkv, w_out, w_latent, neighbours, assignment, psi, w_dec):
    _, rows, width = nodes.shape
    channels = w_latent.shape[1]
    lat_rows, lon_cols = assignment.shape
    basis, _, out_ch = w_dec.shape
    sectors = lax.axis_size("lon")
    count = neighbours.shape[1]
    x = nodes.reshape(rows, width)
    gain = norm_gain.reshape(1, width)

    def shifted(array, step):
        return lax.ppermute(array, "lon", [(i, (i + step) % sectors) for i in range(sectors)])

    def exchanged(array, first):
        size = lax.axis_size("reg")
        pairs = [(i, i + 1) for i in range(first, size - 1, 2)]
        return lax.ppermute(array, "reg", pairs + [(j, i) for i, j in pairs])

    def in_hbm(*arrays):
        return [pltpu.with_memory_space_constraint(array, pltpu.HBM) for array in arrays]

    west = shifted(x, 1)
    east = shifted(x, -1)

    outputs = -(-out_ch // ROWS) * ROWS
    head = width // HEADS
    members = LANES // head
    parts = HEADS // members
    def mixed(blocks, name, after):
        taps = psi.transpose(2, 3, 1, 0)
        mixing = w_dec.transpose(0, 2, 1)
        taps, mixing, after = lax.optimization_barrier((taps, mixing, after))
        weights = pl.pallas_call(
            functools.partial(mix_kernel, blocks),
            in_specs=[whole()] * 2,
            out_specs=whole(),
            out_shape=struct(len(blocks), outputs, channels),
            scratch_shapes=[
                pltpu.VMEM((2 * TAPS * TAPS, basis), F32),
                pltpu.VMEM((len(blocks) * ROWS, basis * ROWS), BF16),
            ],
            compiler_params=params(32),
            cost_estimate=cost(1e9, 3e6),
            name=name,
        )(taps, mixing)
        return weights, after

    own = pl.pallas_call(
        gather_kernel,
        in_specs=[whole(pltpu.HBM)] * 2,
        out_specs=whole(),
        out_shape=struct(rows + ROWS, width),
        scratch_shapes=[
            pltpu.VMEM(assignment.shape, jnp.int32),
            pltpu.SemaphoreType.DMA((2,)),
        ],
        compiler_params=params(32),
        cost_estimate=cost(1e8, 1e6),
        name="gather",
    )(*in_hbm(x, assignment))
    query, key, value, wk, wvt, choice, cells = pl.pallas_call(
        functools.partial(prepare_kernel, sectors),
        in_specs=[whole()] + [whole(pltpu.HBM)] * 4,
        out_specs=[whole()] * 7,
        out_shape=[
            struct(parts, LANES, members * rows),
            struct(rows, width),
            struct(width, rows),
            struct(width, width),
            struct(width, width),
            struct(count - 1, CANDIDATES, ROWS, LANES),
            struct(2 * ROWS, rows),
        ],
        scratch_shapes=[
            pltpu.VMEM((1, width), F32),
            pltpu.VMEM(w_qkv.shape, BF16),
            pltpu.SMEM(assignment.shape, jnp.int32),
            pltpu.SMEM(neighbours.shape, jnp.int32),
            pltpu.SemaphoreType.DMA((4,)),
        ],
        compiler_params=params(32),
        cost_estimate=cost(2e9, 5e6),
        name="prepare",
    )(own, *in_hbm(gain, w_qkv, assignment, neighbours))
    east, query = lax.optimization_barrier((east, query))
    message = jnp.concatenate([east, own], axis=0)
    outer = exchanged(message, 1)
    inner = exchanged(message, 0)
    corner = exchanged(west, 1)
    beside = exchanged(west, 0)
    edges, beside = mixed(blocks_of(ABOVE) + blocks_of(BELOW), "mix_edges", beside)
    beside, edges = lax.optimization_barrier((beside, edges))


    top, summed = pl.pallas_call(
        early_kernel,
        in_specs=[whole()] * 12,
        out_specs=[whole()] * 2,
        out_shape=[
            struct(parts, 8, members * rows, dtype=F32),
            struct(parts, LANES + ROWS, members * rows, dtype=F32),
        ],
        scratch_shapes=[
            pltpu.VMEM(((1 + EARLY) * rows, width), BF16),
            pltpu.VMEM((parts, LANES + ROWS, (1 + EARLY) * rows), BF16),
        ],
        compiler_params=params(32),
        cost_estimate=cost(3e9, 6e6),
        name="early",
    )(choice, west, east, beside, inner, outer, gain, wk, wvt, query, key, value)
    state, latent, first, last = pl.pallas_call(
        late_kernel,
        in_specs=[whole()] * 17,
        out_specs=[whole()] * 4,
        out_shape=[pltpu.VMEM((rows, width), BF16), struct(rows, channels)]
        + [struct(ROWS, channels)] * 2,
        scratch_shapes=[pltpu.VMEM((rows, width), BF16)],
        compiler_params=params(32),
        cost_estimate=cost(3e9, 6e6),
        name="late",
    )(
        choice, cells, west, east, beside, inner, outer, corner,
        own, gain, wk, wvt, query, top, summed, w_out, w_latent,
    )

    from_left = shifted(last, 1)
    from_right = shifted(first, -1)
    middle, latent = mixed(blocks_of(OWN), "mix_own", latent)
    from_left, middle = lax.optimization_barrier((from_left, middle))
    extended = jnp.concatenate([latent, from_left[:SIDE], from_right[:SIDE]], axis=0)
    far = exchanged(extended, 1)
    near = exchanged(extended, 0)

    lanes = -(-(rows + 2 * SIDE) // 256) * 256
    partial, hots, state = pl.pallas_call(
        functools.partial(own_kernel, (rows, 2 * rows, 2 * rows)),
        in_specs=[whole()] * 6,
        out_specs=[whole()] * 3,
        out_shape=[
            struct(lat_rows, outputs, lon_cols, dtype=F32),
            struct(2, 2, TAPS, lanes, lon_cols),
            struct(rows, width),
        ],
        compiler_params=params(32),
        cost_estimate=cost(1e9, 2.5e6),
        name="own_band",
    )(state, own, inner, outer, extended, middle)
    band_scratch = [
        pltpu.VMEM((outputs, TAPS * lanes), BF16),
        pltpu.VMEM((2 * outputs, TAPS * lanes), BF16),
    ]
    partial = pl.pallas_call(
        functools.partial(band_kernel, True),
        in_specs=[whole()] * 4,
        out_specs=whole(),
        out_shape=struct(lat_rows, outputs, lon_cols, dtype=F32),
        scratch_shapes=band_scratch,
        compiler_params=params(32),
        cost_estimate=cost(1e9, 2.5e6),
        name="inner_band",
    )(near, edges, hots, partial)
    fields = pl.pallas_call(
        functools.partial(band_kernel, False),
        in_specs=[whole()] * 4,
        out_specs=whole(),
        out_shape=struct(out_ch, lat_rows, lon_cols),
        scratch_shapes=band_scratch,
        compiler_params=params(32),
        cost_estimate=cost(1e9, 2.5e6),
        name="outer_band",
    )(far, edges, hots, partial)
    return (state.reshape(1, rows, width), fields.reshape(1, out_ch, lat_rows, lon_cols))


def solution(mesh):
    in_specs = (
        P(None, ("reg", "lon"), None),
        P(),
        P(),
        P(),
        P(),
        P(("reg", "lon"), None),
        P("reg", "lon"),
        P(None, "reg", None, None),
        P(),
    )
    out_specs = (P(None, ("reg", "lon"), None), P(None, None, "reg", "lon"))
    return jax.shard_map(shards, mesh=mesh, in_specs=in_specs, out_specs=out_specs, check_vma=False)
```

```python
import functools
import math

import jax
import jax.numpy as jnp
from jax import lax
from jax.experimental import pallas as pl
from jax.experimental.pallas import tpu as pltpu
from jax.sharding import PartitionSpec as P

HEADS = 16
REACH = 2
TAPS = 2 * REACH + 1
SIDE = 8
ROWS = 16
LANES = 128
EARLY = 2
CANDIDATES = 5
F32 = jnp.float32
BF16 = jnp.bfloat16
NT = (((1,), (1,)), ((), ()))

ABOVE = ((-2, (0,)), (-1, (0, 1)))
OWN = ((0, (0, 1)), (1, (0, 1)))
BELOW = ((3, (1,)), (2, (0, 1)))


def blocks_of(band):
    return [
        (out_row, src - out_row + REACH, off)
        for src, out_rows in band
        for off in range(TAPS)
        for out_row in out_rows
    ]


def iota(shape, dim):
    return lax.broadcasted_iota(jnp.int32, shape, dim)


def normalise(rows, gain):
    values = rows.astype(F32)
    center = values - jnp.mean(values, axis=-1, keepdims=True)
    spread = jnp.mean(center * center, axis=-1, keepdims=True)
    return (center * lax.rsqrt(spread + 1e-05) * gain).astype(BF16)


def mix_kernel(blocks, psi_ref, dec_ref, mixed_ref, psi_rows_ref, taps_ref):
    basis, out_ch, channels = dec_ref.shape
    depth = basis * ROWS
    for tap in range(TAPS):
        for off in range(TAPS):
            at = (tap * TAPS + off) * 2
            psi_rows_ref[at : at + 2, :] = psi_ref[tap, off]
    spread = (iota((basis, depth), 1) // ROWS == iota((basis, depth), 0)).astype(F32)
    expanded = jnp.dot(psi_rows_ref[...], spread, preferred_element_type=F32)
    pick = iota((ROWS, depth), 1) % ROWS == iota((ROWS, depth), 0)
    for at, (out_row, tap, off) in enumerate(blocks):
        source = (tap * TAPS + off) * 2 + out_row
        taps = jnp.broadcast_to(expanded[source : source + 1], (ROWS, depth))
        taps_ref[at * ROWS : (at + 1) * ROWS, :] = jnp.where(pick, taps, 0.0).astype(BF16)
    for first in range(0, out_ch, ROWS):
        size = min(ROWS, out_ch - first)
        pieces = []
        for base in range(basis):
            pieces.append(dec_ref[base, first : first + size, :])
            if size < ROWS:
                pieces.append(jnp.zeros((ROWS - size, channels), BF16))
        mixing = jnp.concatenate(pieces, axis=0)
        mixed = jnp.dot(taps_ref[...], mixing, preferred_element_type=F32).astype(BF16)
        mixed_ref[:, first : first + ROWS, :] = mixed.reshape(len(blocks), ROWS, channels)


def listed_blocks(sectors, listed_ref):
    reg_here, lon_here = lax.axis_index("reg"), lax.axis_index("lon")
    toward = 1 - 2 * (reg_here % 2)
    found = []
    for at in range(1, listed_ref.shape[1]):
        block = listed_ref[0, at]
        step_reg = (block // sectors - reg_here) * toward
        step_lon = (block % sectors - lon_here + 1 + sectors) % sectors - 1
        place = jnp.where(step_lon == 0, 2, jnp.where(step_lon < 0, 0, 1))
        outer = jnp.where(step_lon == 0, 5, 6 + place)
        found.append(jnp.where(step_reg == 0, place, jnp.where(step_reg > 0, 2 + place, outer)))
    for low in range(len(found)):
        for high in range(low + 1, len(found)):
            less, more = jnp.minimum(found[low], found[high]), jnp.maximum(found[low], found[high])
            found[low], found[high] = less, more
    return found


def prepare_kernel(
    sectors,
    x_hbm, gain_hbm, wqkv_hbm, assign_hbm, listed_hbm,
    own_ref, query_ref, key_ref, value_ref, wk_ref, wvt_ref, choice_ref, cells_ref,
    gain_ref, wqkv_ref, assign_ref, cell_ref, listed_ref, sems,
):
    rows, width = key_ref.shape
    copies = [
        pltpu.make_async_copy(source, target, sems.at[at])
        for at, (source, target) in enumerate(
            (
                (x_hbm, own_ref.at[pl.ds(0, rows)]),
                (gain_hbm, gain_ref),
                (wqkv_hbm, wqkv_ref),
                (assign_hbm, assign_ref),
                (assign_hbm, cell_ref),
                (listed_hbm, listed_ref),
            )
        )
    ]
    for copy in copies:
        copy.start()
    group, members = query_ref.shape[1], query_ref.shape[2] // rows
    head = group // members
    for copy in copies[3:]:
        copy.wait()
    local = lax.rem(assign_ref[...], rows).astype(F32)
    line = jnp.concatenate([local[:1], local[1:2]], axis=1)
    line = jnp.broadcast_to(line, (ROWS, line.shape[1]))
    own_ref[rows:] = jnp.where(iota(line.shape, 0) == 0, line, 0.0).astype(BF16)
    for at, number in enumerate(listed_blocks(sectors, listed_ref)):
        for candidate in range(CANDIDATES):
            same = jnp.full((ROWS, LANES), jnp.where(number == at + candidate, 1.0, 0.0), F32)
            choice_ref[at, candidate] = same.astype(BF16)
    lat_rows, lon_cols = cell_ref.shape
    place, node = iota((ROWS, rows), 0), iota((ROWS, rows), 1)
    for side, first in enumerate((0, lon_cols - REACH)):
        hit = jnp.zeros((ROWS, rows), F32)
        for row in range(lat_rows):
            for col in range(REACH):
                cell = cell_ref[row, first + col] % rows
                hit = jnp.where((place == row * REACH + col) & (node == cell), 1.0, hit)
        cells_ref[side * ROWS : (side + 1) * ROWS] = hit.astype(BF16)
    copies[0].wait()
    copies[1].wait()
    normed = normalise(own_ref[:rows], gain_ref[...])
    copies[2].wait()
    query = jnp.dot(normed, wqkv_ref[:, :width], preferred_element_type=F32)
    query_t = (query * (math.log2(math.e) / head**0.5)).T.astype(BF16)
    mask = (iota((group, members * rows), 0) // head) == (iota((group, members * rows), 1) // rows)
    for part in range(width // group):
        piece = query_t[part * group : (part + 1) * group]
        wide = jnp.concatenate([piece] * members, axis=1)
        query_ref[part] = jnp.where(mask, wide, jnp.zeros_like(wide))
    wk = wqkv_ref[:, width : 2 * width]
    wk_ref[...] = wk
    key_ref[...] = jnp.dot(normed, wk, preferred_element_type=F32).astype(BF16)
    wvt = wqkv_ref[:, 2 * width :].astype(F32).T.astype(BF16)
    wvt_ref[...] = wvt
    value_ref[...] = lax.dot_general(wvt, normed, NT, preferred_element_type=F32).astype(BF16)


def chosen(entries, rows, choice_ref, candidates):
    tall, wide = rows // ROWS, candidates[-1].shape[1] // LANES
    near = []
    for entry in entries:
        total = None
        for at in range(CANDIDATES):
            weight = jnp.concatenate([choice_ref[entry, at]] * wide, axis=1)
            part = candidates[entry + at] * jnp.concatenate([weight] * tall, axis=0)
            total = part if total is None else total + part
        near.append(total)
    return jnp.concatenate(near, axis=0)


def project(nodes, gain, wk_ref, wvt_ref):
    normed = normalise(nodes, gain)
    keys = jnp.dot(normed, wk_ref[...], preferred_element_type=F32).astype(BF16)
    values = lax.dot_general(wvt_ref[...], normed, NT, preferred_element_type=F32).astype(BF16)
    return keys, values


def early_kernel(
    choice_ref, west_ref, east_ref, inner_ref, center_ref,
    gain_ref, wk_ref, wvt_ref, query_ref, key_ref, value_ref,
    top_ref, sum_ref, keys_ref, values_ref,
):
    rows = key_ref.shape[0]
    parts, group, _ = query_ref.shape
    candidates = [west_ref[...], east_ref[...]]
    candidates += [inner_ref[at * rows : (at + 1) * rows] for at in range(3)]
    candidates.append(center_ref[...])
    nodes = chosen(range(EARLY), rows, choice_ref, candidates)
    keys, values = project(nodes, gain_ref[...], wk_ref, wvt_ref)
    keys_ref[:rows] = key_ref[...]
    keys_ref[rows:] = keys
    for part in range(parts):
        span = slice(part * group, (part + 1) * group)
        values_ref[part, :group, :rows] = value_ref[span]
        values_ref[part, :group, rows:] = values[span]
        values_ref[part, group:, :] = jnp.ones((ROWS, keys_ref.shape[0]), BF16)

    def scored(part):
        span = slice(part * group, (part + 1) * group)
        return jnp.dot(keys_ref[:, span], query_ref[part], preferred_element_type=F32)

    scores = scored(0)
    for part in range(parts):
        now = scores
        if part + 1 < parts:
            scores = scored(part + 1)
        top = jnp.max(now, axis=0, keepdims=True)
        expo = jnp.exp2(now - top).astype(BF16)
        top_ref[part] = jnp.broadcast_to(top, top_ref.shape[1:])
        sum_ref[part] = jnp.dot(values_ref[part], expo, preferred_element_type=F32)


def late_kernel(
    choice_ref, cells_ref, inner_ref, center_ref, outer_ref,
    own_ref, gain_ref, wk_ref, wvt_ref, query_ref, top_ref, sum_ref, wout_ref, wlat_ref,
    state_ref, latent_ref, first_ref, last_ref,
    attended_ref,
):
    rows, width = state_ref.shape
    parts, group, lanes = query_ref.shape
    members = lanes // rows
    head = group // members
    candidates = [None, None] + [inner_ref[at * rows : (at + 1) * rows] for at in range(3)]
    candidates += [center_ref[...], outer_ref[:rows], outer_ref[rows : 2 * rows]]
    nodes = chosen(range(EARLY, choice_ref.shape[0]), rows, choice_ref, candidates)
    keys, values = project(nodes, gain_ref[...], wk_ref, wvt_ref)
    ones = jnp.ones((ROWS, nodes.shape[0]), BF16)
    owner = iota((group, rows), 0) // head

    def scored(part):
        span = slice(part * group, (part + 1) * group)
        return jnp.dot(keys[:, span], query_ref[part], preferred_element_type=F32)

    scores = scored(0)
    for part in range(parts):
        now = scores
        if part + 1 < parts:
            scores = scored(part + 1)
        before = top_ref[part, :1]
        top = jnp.maximum(before, jnp.max(now, axis=0, keepdims=True))
        expo = jnp.exp2(now - top).astype(BF16)
        weights = jnp.concatenate([values[part * group : (part + 1) * group], ones], axis=0)
        summed = jnp.dot(weights, expo, preferred_element_type=F32)
        summed = summed + sum_ref[part] * jnp.exp2(before - top)
        summed = summed[:group] * (1.0 / summed[group : group + 1])
        merged = None
        for member in range(members):
            piece = summed[:, member * rows : (member + 1) * rows]
            merged = piece if merged is None else jnp.where(owner == member, piece, merged)
        attended_ref[:, part * group : (part + 1) * group] = merged.T.astype(BF16)
    state = (
        own_ref[:rows].astype(F32)
        + jnp.dot(attended_ref[...], wout_ref[...], preferred_element_type=F32)
    ).astype(BF16)
    state_ref[...] = state
    value = jnp.dot(state, wlat_ref[...], preferred_element_type=F32)
    latent = (value / (1.0 + jnp.exp(-value))).astype(BF16)
    latent_ref[...] = latent
    cells = jnp.dot(cells_ref[...], latent, preferred_element_type=F32).astype(BF16)
    first_ref[...] = cells[:ROWS]
    last_ref[...] = cells[ROWS:]


def hot_rows(values, rows, cols, line):
    column = iota((8, cols), 1)
    node = iota((rows + 2 * SIDE, cols), 0).astype(F32)
    for off in range(TAPS):
        step = off - REACH
        where = jnp.broadcast_to(values, (8, cols))
        if step:
            where = pltpu.roll(where, (-step) % cols, 1)
        reach = column + step
        before = (rows + REACH * line + reach + REACH).astype(F32)
        after = (rows + SIDE + REACH * line + reach - cols).astype(F32)
        where = jnp.where(reach < 0, before, jnp.where(reach >= cols, after, where))
        yield jnp.where(node == where[:1], 1.0, 0.0).astype(BF16)


def shares_of(latent, weights):
    blocks, outputs, channels = weights.shape
    shares = lax.dot_general(
        weights.reshape(blocks * outputs, channels), latent, NT, preferred_element_type=F32
    ).astype(BF16)
    return [shares[at * outputs : (at + 1) * outputs] for at in range(blocks)]


def lines_of(line_ref, start, cols):
    values = line_ref[start : start + ROWS, :].astype(F32)
    return values[:1, :cols], values[:1, cols:]


def own_kernel(
    begin, state_ref, own_ref, inner_ref, outer_ref, latent_ref, weights_ref,
    out_ref, hot_ref, kept_ref,
):
    kept_ref[...] = state_ref[...]
    cols = out_ref.shape[2]
    rows = latent_ref.shape[0] - 2 * SIDE
    own = lines_of(own_ref, begin[0], cols)
    table = [list(hot_rows(own[line], rows, cols, line)) for line in range(2)]
    acc = [None, None]
    for (out_row, tap, off), share in zip(
        blocks_of(OWN), shares_of(latent_ref[...], weights_ref[...])
    ):
        line = out_row + tap - REACH
        piece = jnp.dot(share, table[line][off], preferred_element_type=F32)
        acc[out_row] = piece if acc[out_row] is None else acc[out_row] + piece
    for row in range(2):
        out_ref[row] = acc[row]
    odd = lax.axis_index("reg") % 2 == 1
    inner, outer = lines_of(inner_ref, begin[1], cols), lines_of(outer_ref, begin[2], cols)
    nodes = rows + 2 * SIDE
    for band, (yes, no) in enumerate(((inner, outer), (outer, inner))):
        for at, line in enumerate((0, 1) if band == 0 else (1, 0)):
            values = jnp.where(odd, yes[line], no[line])
            for off, hot in enumerate(hot_rows(values, rows, cols, line)):
                hot_ref[band, at, off, :nodes] = hot
                hot_ref[band, at, off, nodes:] = jnp.zeros((hot_ref.shape[3] - nodes, cols), BF16)


def band_kernel(from_inner, latent_ref, weights_ref, hot_ref, partial_ref, out_ref, one_ref, two_ref):
    odd = lax.axis_index("reg") % 2
    band = 1 - odd if from_inner else odd
    latent = latent_ref[...]
    lanes, cols = hot_ref.shape[3:]
    outputs = weights_ref.shape[1]
    blank = jnp.zeros((lanes - latent.shape[0], latent.shape[1]), BF16)
    blocks = len(blocks_of(ABOVE))
    weights = weights_ref[pl.ds(band * blocks, blocks)]
    shares = shares_of(jnp.concatenate([latent, blank], axis=0), weights)
    for off in range(TAPS):
        span = slice(off * lanes, (off + 1) * lanes)
        one_ref[:, span] = shares[off]
        for row in range(2):
            two_ref[row * outputs : (row + 1) * outputs, span] = shares[TAPS + 2 * off + row]
    depth = TAPS * lanes
    one = jnp.dot(one_ref[...], hot_ref[band, 0].reshape(depth, cols), preferred_element_type=F32)
    two = jnp.dot(two_ref[...], hot_ref[band, 1].reshape(depth, cols), preferred_element_type=F32)
    for row in range(2):
        total = partial_ref[row] + two[row * outputs : (row + 1) * outputs]
        total = total + jnp.where(band == row, one, 0.0)
        if from_inner:
            out_ref[row] = total
        else:
            out_ref[:, row, :] = total[: out_ref.shape[0]].astype(BF16)


def whole(memory=pltpu.VMEM):
    return pl.BlockSpec(memory_space=memory)


def struct(*shape, dtype=BF16):
    return jax.ShapeDtypeStruct(shape, dtype)


def params(limit):
    return pltpu.CompilerParams(vmem_limit_bytes=limit << 20)


def cost(flops, moved):
    return pl.CostEstimate(flops=int(flops), bytes_accessed=int(moved), transcendentals=0)


def shards(nodes, norm_gain, w_qkv, w_out, w_latent, neighbours, assignment, psi, w_dec):
    _, rows, width = nodes.shape
    channels = w_latent.shape[1]
    lat_rows, lon_cols = assignment.shape
    basis, _, out_ch = w_dec.shape
    sectors = lax.axis_size("lon")
    count = neighbours.shape[1]
    x = nodes.reshape(rows, width)
    gain = norm_gain.reshape(1, width)

    def shifted(array, step):
        return lax.ppermute(array, "lon", [(i, (i + step) % sectors) for i in range(sectors)])

    def exchanged(array, first):
        size = lax.axis_size("reg")
        pairs = [(i, i + 1) for i in range(first, size - 1, 2)]
        return lax.ppermute(array, "reg", pairs + [(j, i) for i, j in pairs])

    def in_hbm(*arrays):
        return [pltpu.with_memory_space_constraint(array, pltpu.HBM) for array in arrays]

    center = exchanged(x, 1)
    west = shifted(x, 1)
    east = shifted(x, -1)

    outputs = -(-out_ch // ROWS) * ROWS
    head = width // HEADS
    members = LANES // head
    parts = HEADS // members
    def mixed(blocks, name, after):
        taps = psi.transpose(2, 3, 1, 0)
        mixing = w_dec.transpose(0, 2, 1)
        taps, mixing, after = lax.optimization_barrier((taps, mixing, after))
        weights = pl.pallas_call(
            functools.partial(mix_kernel, blocks),
            in_specs=[whole()] * 2,
            out_specs=whole(),
            out_shape=struct(len(blocks), outputs, channels),
            scratch_shapes=[
                pltpu.VMEM((2 * TAPS * TAPS, basis), F32),
                pltpu.VMEM((len(blocks) * ROWS, basis * ROWS), BF16),
            ],
            compiler_params=params(32),
            cost_estimate=cost(1e9, 3e6),
            name=name,
        )(taps, mixing)
        return weights, after

    own, query, key, value, wk, wvt, choice, cells = pl.pallas_call(
        functools.partial(prepare_kernel, sectors),
        in_specs=[whole(pltpu.HBM)] * 5,
        out_specs=[whole()] * 8,
        out_shape=[
            struct(rows + ROWS, width),
            struct(parts, LANES, members * rows),
            struct(rows, width),
            struct(width, rows),
            struct(width, width),
            struct(width, width),
            struct(count - 1, CANDIDATES, ROWS, LANES),
            struct(2 * ROWS, rows),
        ],
        scratch_shapes=[
            pltpu.VMEM((1, width), F32),
            pltpu.VMEM(w_qkv.shape, BF16),
            pltpu.VMEM(assignment.shape, jnp.int32),
            pltpu.SMEM(assignment.shape, jnp.int32),
            pltpu.SMEM(neighbours.shape, jnp.int32),
            pltpu.SemaphoreType.DMA((6,)),
        ],
        compiler_params=params(32),
        cost_estimate=cost(2e9, 5e6),
        name="prepare",
    )(*in_hbm(x, gain, w_qkv, assignment, neighbours))
    center, west = lax.optimization_barrier((center, west))
    center, east = lax.optimization_barrier((center, east))
    outer = exchanged(jnp.concatenate([west, east, own[rows:]], axis=0), 1)
    inner = exchanged(jnp.concatenate([west, east, own], axis=0), 0)
    top, summed = pl.pallas_call(
        early_kernel,
        in_specs=[whole()] * 11,
        out_specs=[whole()] * 2,
        out_shape=[
            struct(parts, 8, members * rows, dtype=F32),
            struct(parts, LANES + ROWS, members * rows, dtype=F32),
        ],
        scratch_shapes=[
            pltpu.VMEM(((1 + EARLY) * rows, width), BF16),
            pltpu.VMEM((parts, LANES + ROWS, (1 + EARLY) * rows), BF16),
        ],
        compiler_params=params(32),
        cost_estimate=cost(3e9, 6e6),
        name="early",
    )(choice, west, east, inner, center, gain, wk, wvt, query, key, value)
    edges, top = mixed(blocks_of(ABOVE) + blocks_of(BELOW), "mix_edges", top)
    top, edges = lax.optimization_barrier((top, edges))
    state, latent, first, last = pl.pallas_call(
        late_kernel,
        in_specs=[whole()] * 14,
        out_specs=[whole()] * 4,
        out_shape=[pltpu.VMEM((rows, width), BF16), struct(rows, channels)]
        + [struct(ROWS, channels)] * 2,
        scratch_shapes=[pltpu.VMEM((rows, width), BF16)],
        compiler_params=params(32),
        cost_estimate=cost(3e9, 6e6),
        name="late",
    )(
        choice, cells, inner, center, outer,
        own, gain, wk, wvt, query, top, summed, w_out, w_latent,
    )

    from_left = shifted(last, 1)
    from_right = shifted(first, -1)
    middle, latent = mixed(blocks_of(OWN), "mix_own", latent)
    from_left, middle = lax.optimization_barrier((from_left, middle))
    extended = jnp.concatenate([latent, from_left[:SIDE], from_right[:SIDE]], axis=0)
    far = exchanged(extended, 1)
    near = exchanged(extended, 0)

    lanes = -(-(rows + 2 * SIDE) // 256) * 256
    partial, hots, state = pl.pallas_call(
        functools.partial(own_kernel, (rows, 3 * rows, 2 * rows)),
        in_specs=[whole()] * 6,
        out_specs=[whole()] * 3,
        out_shape=[
            struct(lat_rows, outputs, lon_cols, dtype=F32),
            struct(2, 2, TAPS, lanes, lon_cols),
            struct(rows, width),
        ],
        compiler_params=params(32),
        cost_estimate=cost(1e9, 2.5e6),
        name="own_band",
    )(state, own, inner, outer, extended, middle)
    band_scratch = [
        pltpu.VMEM((outputs, TAPS * lanes), BF16),
        pltpu.VMEM((2 * outputs, TAPS * lanes), BF16),
    ]
    partial = pl.pallas_call(
        functools.partial(band_kernel, True),
        in_specs=[whole()] * 4,
        out_specs=whole(),
        out_shape=struct(lat_rows, outputs, lon_cols, dtype=F32),
        scratch_shapes=band_scratch,
        compiler_params=params(32),
        cost_estimate=cost(1e9, 2.5e6),
        name="inner_band",
    )(near, edges, hots, partial)
    fields = pl.pallas_call(
        functools.partial(band_kernel, False),
        in_specs=[whole()] * 4,
        out_specs=whole(),
        out_shape=struct(out_ch, lat_rows, lon_cols),
        scratch_shapes=band_scratch,
        compiler_params=params(32),
        cost_estimate=cost(1e9, 2.5e6),
        name="outer_band",
    )(far, edges, hots, partial)
    return (state.reshape(1, rows, width), fields.reshape(1, out_ch, lat_rows, lon_cols))


def solution(mesh):
    in_specs = (
        P(None, ("reg", "lon"), None),
        P(),
        P(),
        P(),
        P(),
        P(("reg", "lon"), None),
        P("reg", "lon"),
        P(None, "reg", None, None),
        P(),
    )
    out_specs = (P(None, ("reg", "lon"), None), P(None, None, "reg", "lon"))
    return jax.shard_map(shards, mesh=mesh, in_specs=in_specs, out_specs=out_specs, check_vma=False)
```

```python
import functools
import math

import jax
import jax.numpy as jnp
from jax import lax
from jax.experimental import pallas as pl
from jax.experimental.pallas import tpu as pltpu
from jax.sharding import PartitionSpec as P

HEADS = 16
REACH = 2
TAPS = 2 * REACH + 1
SIDE = 8
ROWS = 16
LANES = 128
EARLY = 2
CANDIDATES = 5
F32 = jnp.float32
BF16 = jnp.bfloat16
NT = (((1,), (1,)), ((), ()))

ABOVE = ((-2, (0,)), (-1, (0, 1)))
OWN = ((0, (0, 1)), (1, (0, 1)))
BELOW = ((3, (1,)), (2, (0, 1)))


def blocks_of(band):
    return [
        (out_row, src - out_row + REACH, off)
        for src, out_rows in band
        for off in range(TAPS)
        for out_row in out_rows
    ]


def iota(shape, dim):
    return lax.broadcasted_iota(jnp.int32, shape, dim)


def normalise(rows, gain):
    values = rows.astype(F32)
    center = values - jnp.mean(values, axis=-1, keepdims=True)
    spread = jnp.mean(center * center, axis=-1, keepdims=True)
    return (center * lax.rsqrt(spread + 1e-05) * gain).astype(BF16)


def mix_kernel(blocks, psi_ref, dec_ref, mixed_ref, psi_rows_ref, taps_ref):
    basis, out_ch, channels = dec_ref.shape
    depth = basis * ROWS
    for tap in range(TAPS):
        for off in range(TAPS):
            at = (tap * TAPS + off) * 2
            psi_rows_ref[at : at + 2, :] = psi_ref[tap, off]
    spread = (iota((basis, depth), 1) // ROWS == iota((basis, depth), 0)).astype(F32)
    expanded = jnp.dot(psi_rows_ref[...], spread, preferred_element_type=F32)
    pick = iota((ROWS, depth), 1) % ROWS == iota((ROWS, depth), 0)
    for at, (out_row, tap, off) in enumerate(blocks):
        source = (tap * TAPS + off) * 2 + out_row
        taps = jnp.broadcast_to(expanded[source : source + 1], (ROWS, depth))
        taps_ref[at * ROWS : (at + 1) * ROWS, :] = jnp.where(pick, taps, 0.0).astype(BF16)
    for first in range(0, out_ch, ROWS):
        size = min(ROWS, out_ch - first)
        pieces = []
        for base in range(basis):
            pieces.append(dec_ref[base, first : first + size, :])
            if size < ROWS:
                pieces.append(jnp.zeros((ROWS - size, channels), BF16))
        mixing = jnp.concatenate(pieces, axis=0)
        mixed = jnp.dot(taps_ref[...], mixing, preferred_element_type=F32).astype(BF16)
        mixed_ref[:, first : first + ROWS, :] = mixed.reshape(len(blocks), ROWS, channels)


def listed_blocks(sectors, listed_ref):
    reg_here, lon_here = lax.axis_index("reg"), lax.axis_index("lon")
    toward = 1 - 2 * (reg_here % 2)
    found = []
    for at in range(1, listed_ref.shape[1]):
        block = listed_ref[0, at]
        step_reg = (block // sectors - reg_here) * toward
        step_lon = (block % sectors - lon_here + 1 + sectors) % sectors - 1
        place = jnp.where(step_lon == 0, 2, jnp.where(step_lon < 0, 0, 1))
        outer = jnp.where(step_lon == 0, 5, 6 + place)
        found.append(jnp.where(step_reg == 0, place, jnp.where(step_reg > 0, 2 + place, outer)))
    for low in range(len(found)):
        for high in range(low + 1, len(found)):
            less, more = jnp.minimum(found[low], found[high]), jnp.maximum(found[low], found[high])
            found[low], found[high] = less, more
    return found


def prepare_kernel(
    sectors,
    x_hbm, gain_hbm, wqkv_hbm, assign_hbm, listed_hbm,
    own_ref, query_ref, key_ref, value_ref, wk_ref, wvt_ref, choice_ref, cells_ref,
    gain_ref, wqkv_ref, assign_ref, cell_ref, listed_ref, sems,
):
    rows, width = key_ref.shape
    copies = [
        pltpu.make_async_copy(source, target, sems.at[at])
        for at, (source, target) in enumerate(
            (
                (x_hbm, own_ref.at[pl.ds(0, rows)]),
                (gain_hbm, gain_ref),
                (wqkv_hbm, wqkv_ref),
                (assign_hbm, assign_ref),
                (assign_hbm, cell_ref),
                (listed_hbm, listed_ref),
            )
        )
    ]
    for copy in copies:
        copy.start()
    group, members = query_ref.shape[1], query_ref.shape[2] // rows
    head = group // members
    for copy in copies[3:]:
        copy.wait()
    local = lax.rem(assign_ref[...], rows).astype(F32)
    line = jnp.concatenate([local[:1], local[1:2]], axis=1)
    line = jnp.broadcast_to(line, (ROWS, line.shape[1]))
    own_ref[rows:] = jnp.where(iota(line.shape, 0) == 0, line, 0.0).astype(BF16)
    for at, number in enumerate(listed_blocks(sectors, listed_ref)):
        for candidate in range(CANDIDATES):
            same = jnp.full((ROWS, LANES), jnp.where(number == at + candidate, 1.0, 0.0), F32)
            choice_ref[at, candidate] = same.astype(BF16)
    lat_rows, lon_cols = cell_ref.shape
    place, node = iota((ROWS, rows), 0), iota((ROWS, rows), 1)
    for side, first in enumerate((0, lon_cols - REACH)):
        hit = jnp.zeros((ROWS, rows), F32)
        for row in range(lat_rows):
            for col in range(REACH):
                cell = cell_ref[row, first + col] % rows
                hit = jnp.where((place == row * REACH + col) & (node == cell), 1.0, hit)
        cells_ref[side * ROWS : (side + 1) * ROWS] = hit.astype(BF16)
    copies[0].wait()
    copies[1].wait()
    normed = normalise(own_ref[:rows], gain_ref[...])
    copies[2].wait()
    query = jnp.dot(normed, wqkv_ref[:, :width], preferred_element_type=F32)
    query_t = (query * (math.log2(math.e) / head**0.5)).T.astype(BF16)
    mask = (iota((group, members * rows), 0) // head) == (iota((group, members * rows), 1) // rows)
    for part in range(width // group):
        piece = query_t[part * group : (part + 1) * group]
        wide = jnp.concatenate([piece] * members, axis=1)
        query_ref[part] = jnp.where(mask, wide, jnp.zeros_like(wide))
    wk = wqkv_ref[:, width : 2 * width]
    wk_ref[...] = wk
    key_ref[...] = jnp.dot(normed, wk, preferred_element_type=F32).astype(BF16)
    wvt = wqkv_ref[:, 2 * width :].astype(F32).T.astype(BF16)
    wvt_ref[...] = wvt
    value_ref[...] = lax.dot_general(wvt, normed, NT, preferred_element_type=F32).astype(BF16)


def chosen(entries, rows, choice_ref, candidates):
    tall, wide = rows // ROWS, candidates[-1].shape[1] // LANES
    near = []
    for entry in entries:
        total = None
        for at in range(CANDIDATES):
            weight = jnp.concatenate([choice_ref[entry, at]] * wide, axis=1)
            part = candidates[entry + at] * jnp.concatenate([weight] * tall, axis=0)
            total = part if total is None else total + part
        near.append(total)
    return jnp.concatenate(near, axis=0)


def project(nodes, gain, wk_ref, wvt_ref):
    normed = normalise(nodes, gain)
    keys = jnp.dot(normed, wk_ref[...], preferred_element_type=F32).astype(BF16)
    values = lax.dot_general(wvt_ref[...], normed, NT, preferred_element_type=F32).astype(BF16)
    return keys, values


def early_kernel(
    choice_ref, west_ref, east_ref, inner_ref, center_ref,
    gain_ref, wk_ref, wvt_ref, query_ref, key_ref, value_ref,
    top_ref, sum_ref, keys_ref, values_ref,
):
    rows = key_ref.shape[0]
    parts, group, _ = query_ref.shape
    candidates = [west_ref[...], east_ref[...]]
    candidates += [inner_ref[at * rows : (at + 1) * rows] for at in range(3)]
    candidates.append(center_ref[...])
    nodes = chosen(range(EARLY), rows, choice_ref, candidates)
    keys, values = project(nodes, gain_ref[...], wk_ref, wvt_ref)
    keys_ref[:rows] = key_ref[...]
    keys_ref[rows:] = keys
    for part in range(parts):
        span = slice(part * group, (part + 1) * group)
        values_ref[part, :group, :rows] = value_ref[span]
        values_ref[part, :group, rows:] = values[span]
        values_ref[part, group:, :] = jnp.ones((ROWS, keys_ref.shape[0]), BF16)

    def scored(part):
        span = slice(part * group, (part + 1) * group)
        return jnp.dot(keys_ref[:, span], query_ref[part], preferred_element_type=F32)

    scores = scored(0)
    for part in range(parts):
        now = scores
        if part + 1 < parts:
            scores = scored(part + 1)
        top = jnp.max(now, axis=0, keepdims=True)
        expo = jnp.exp2(now - top).astype(BF16)
        top_ref[part] = jnp.broadcast_to(top, top_ref.shape[1:])
        sum_ref[part] = jnp.dot(values_ref[part], expo, preferred_element_type=F32)


def late_kernel(
    choice_ref, cells_ref, inner_ref, center_ref, outer_ref,
    own_ref, gain_ref, wk_ref, wvt_ref, query_ref, top_ref, sum_ref, wout_ref, wlat_ref,
    state_ref, latent_ref, first_ref, last_ref,
    attended_ref,
):
    rows, width = state_ref.shape
    parts, group, lanes = query_ref.shape
    members = lanes // rows
    head = group // members
    candidates = [None, None] + [inner_ref[at * rows : (at + 1) * rows] for at in range(3)]
    candidates += [center_ref[...], outer_ref[:rows], outer_ref[rows : 2 * rows]]
    nodes = chosen(range(EARLY, choice_ref.shape[0]), rows, choice_ref, candidates)
    keys, values = project(nodes, gain_ref[...], wk_ref, wvt_ref)
    ones = jnp.ones((ROWS, nodes.shape[0]), BF16)
    owner = iota((group, rows), 0) // head
    state = own_ref[:rows].astype(F32)

    def scored(part):
        span = slice(part * group, (part + 1) * group)
        return jnp.dot(keys[:, span], query_ref[part], preferred_element_type=F32)

    scores = scored(0)
    for part in range(parts):
        now = scores
        if part + 1 < parts:
            scores = scored(part + 1)
        before = top_ref[part, :1]
        top = jnp.maximum(before, jnp.max(now, axis=0, keepdims=True))
        expo = jnp.exp2(now - top).astype(BF16)
        weights = jnp.concatenate([values[part * group : (part + 1) * group], ones], axis=0)
        summed = jnp.dot(weights, expo, preferred_element_type=F32)
        summed = summed + sum_ref[part] * jnp.exp2(before - top)
        summed = summed[:group] * (1.0 / summed[group : group + 1])
        merged = None
        for member in range(members):
            piece = summed[:, member * rows : (member + 1) * rows]
            merged = piece if merged is None else jnp.where(owner == member, piece, merged)
        attended_ref[:, part * group : (part + 1) * group] = merged.T.astype(BF16)
        if part % 2:
            span = slice((part - 1) * group, (part + 1) * group)
            state = state + jnp.dot(
                attended_ref[:, span], wout_ref[span, :], preferred_element_type=F32
            )
    state = state.astype(BF16)
    state_ref[...] = state
    value = jnp.dot(state, wlat_ref[...], preferred_element_type=F32)
    latent = (value / (1.0 + jnp.exp(-value))).astype(BF16)
    latent_ref[...] = latent
    cells = jnp.dot(cells_ref[...], latent, preferred_element_type=F32).astype(BF16)
    first_ref[...] = cells[:ROWS]
    last_ref[...] = cells[ROWS:]


def hot_rows(values, rows, cols, line):
    column = iota((8, cols), 1)
    node = iota((rows + 2 * SIDE, cols), 0).astype(F32)
    for off in range(TAPS):
        step = off - REACH
        where = jnp.broadcast_to(values, (8, cols))
        if step:
            where = pltpu.roll(where, (-step) % cols, 1)
        reach = column + step
        before = (rows + REACH * line + reach + REACH).astype(F32)
        after = (rows + SIDE + REACH * line + reach - cols).astype(F32)
        where = jnp.where(reach < 0, before, jnp.where(reach >= cols, after, where))
        yield jnp.where(node == where[:1], 1.0, 0.0).astype(BF16)


def shares_of(latent, weights):
    blocks, outputs, channels = weights.shape
    shares = lax.dot_general(
        weights.reshape(blocks * outputs, channels), latent, NT, preferred_element_type=F32
    ).astype(BF16)
    return [shares[at * outputs : (at + 1) * outputs] for at in range(blocks)]


def lines_of(line_ref, start, cols):
    values = line_ref[start : start + ROWS, :].astype(F32)
    return values[:1, :cols], values[:1, cols:]


def own_kernel(
    begin, state_ref, own_ref, inner_ref, outer_ref, latent_ref, weights_ref,
    out_ref, hot_ref, kept_ref,
):
    kept_ref[...] = state_ref[...]
    cols = out_ref.shape[2]
    rows = latent_ref.shape[0] - 2 * SIDE
    own = lines_of(own_ref, begin[0], cols)
    table = [list(hot_rows(own[line], rows, cols, line)) for line in range(2)]
    acc = [None, None]
    for (out_row, tap, off), share in zip(
        blocks_of(OWN), shares_of(latent_ref[...], weights_ref[...])
    ):
        line = out_row + tap - REACH
        piece = jnp.dot(share, table[line][off], preferred_element_type=F32)
        acc[out_row] = piece if acc[out_row] is None else acc[out_row] + piece
    for row in range(2):
        out_ref[row] = acc[row]
    odd = lax.axis_index("reg") % 2 == 1
    inner, outer = lines_of(inner_ref, begin[1], cols), lines_of(outer_ref, begin[2], cols)
    nodes = rows + 2 * SIDE
    for band, (yes, no) in enumerate(((inner, outer), (outer, inner))):
        for at, line in enumerate((0, 1) if band == 0 else (1, 0)):
            values = jnp.where(odd, yes[line], no[line])
            for off, hot in enumerate(hot_rows(values, rows, cols, line)):
                hot_ref[band, at, off, :nodes] = hot
                hot_ref[band, at, off, nodes:] = jnp.zeros((hot_ref.shape[3] - nodes, cols), BF16)


def band_kernel(from_inner, latent_ref, weights_ref, hot_ref, partial_ref, out_ref, one_ref, two_ref):
    odd = lax.axis_index("reg") % 2
    band = 1 - odd if from_inner else odd
    latent = latent_ref[...]
    lanes, cols = hot_ref.shape[3:]
    outputs = weights_ref.shape[1]
    blank = jnp.zeros((lanes - latent.shape[0], latent.shape[1]), BF16)
    blocks = len(blocks_of(ABOVE))
    weights = weights_ref[pl.ds(band * blocks, blocks)]
    shares = shares_of(jnp.concatenate([latent, blank], axis=0), weights)
    for off in range(TAPS):
        span = slice(off * lanes, (off + 1) * lanes)
        one_ref[:, span] = shares[off]
        for row in range(2):
            two_ref[row * outputs : (row + 1) * outputs, span] = shares[TAPS + 2 * off + row]
    depth = TAPS * lanes
    one = jnp.dot(one_ref[...], hot_ref[band, 0].reshape(depth, cols), preferred_element_type=F32)
    two = jnp.dot(two_ref[...], hot_ref[band, 1].reshape(depth, cols), preferred_element_type=F32)
    totals = []
    for row in range(2):
        total = partial_ref[row] + two[row * outputs : (row + 1) * outputs]
        totals.append(total + jnp.where(band == row, one, 0.0))
    if from_inner:
        out_ref[0], out_ref[1] = totals
    else:
        out_ch = out_ref.shape[0]
        rounded = jnp.concatenate(totals, axis=0).astype(BF16)
        place, source = iota((2 * out_ch, 2 * outputs), 0), iota((2 * out_ch, 2 * outputs), 1)
        order = (source == place % 2 * outputs + place // 2).astype(F32).astype(BF16)
        paired = jnp.dot(order, rounded, preferred_element_type=F32).astype(BF16)
        out_ref[...] = paired.reshape(out_ref.shape)


def whole(memory=pltpu.VMEM):
    return pl.BlockSpec(memory_space=memory)


def struct(*shape, dtype=BF16):
    return jax.ShapeDtypeStruct(shape, dtype)


def params(limit):
    return pltpu.CompilerParams(vmem_limit_bytes=limit << 20)


def cost(flops, moved):
    return pl.CostEstimate(flops=int(flops), bytes_accessed=int(moved), transcendentals=0)


def shards(nodes, norm_gain, w_qkv, w_out, w_latent, neighbours, assignment, psi, w_dec):
    _, rows, width = nodes.shape
    channels = w_latent.shape[1]
    lat_rows, lon_cols = assignment.shape
    basis, _, out_ch = w_dec.shape
    sectors = lax.axis_size("lon")
    count = neighbours.shape[1]
    x = nodes.reshape(rows, width)
    gain = norm_gain.reshape(1, width)

    def shifted(array, step):
        return lax.ppermute(array, "lon", [(i, (i + step) % sectors) for i in range(sectors)])

    def exchanged(array, first):
        size = lax.axis_size("reg")
        pairs = [(i, i + 1) for i in range(first, size - 1, 2)]
        return lax.ppermute(array, "reg", pairs + [(j, i) for i, j in pairs])

    def in_hbm(*arrays):
        return [pltpu.with_memory_space_constraint(array, pltpu.HBM) for array in arrays]

    center = exchanged(x, 1)
    west = shifted(x, 1)
    east = shifted(x, -1)

    outputs = -(-out_ch // ROWS) * ROWS
    head = width // HEADS
    members = LANES // head
    parts = HEADS // members
    def mixed(blocks, name, after):
        taps = psi.transpose(2, 3, 1, 0)
        mixing = w_dec.transpose(0, 2, 1)
        taps, mixing, after = lax.optimization_barrier((taps, mixing, after))
        weights = pl.pallas_call(
            functools.partial(mix_kernel, blocks),
            in_specs=[whole()] * 2,
            out_specs=whole(),
            out_shape=struct(len(blocks), outputs, channels),
            scratch_shapes=[
                pltpu.VMEM((2 * TAPS * TAPS, basis), F32),
                pltpu.VMEM((len(blocks) * ROWS, basis * ROWS), BF16),
            ],
            compiler_params=params(32),
            cost_estimate=cost(1e9, 3e6),
            name=name,
        )(taps, mixing)
        return weights, after

    own, query, key, value, wk, wvt, choice, cells = pl.pallas_call(
        functools.partial(prepare_kernel, sectors),
        in_specs=[whole(pltpu.HBM)] * 5,
        out_specs=[whole()] * 8,
        out_shape=[
            struct(rows + ROWS, width),
            struct(parts, LANES, members * rows),
            struct(rows, width),
            struct(width, rows),
            struct(width, width),
            struct(width, width),
            struct(count - 1, CANDIDATES, ROWS, LANES),
            struct(2 * ROWS, rows),
        ],
        scratch_shapes=[
            pltpu.VMEM((1, width), F32),
            pltpu.VMEM(w_qkv.shape, BF16),
            pltpu.VMEM(assignment.shape, jnp.int32),
            pltpu.SMEM(assignment.shape, jnp.int32),
            pltpu.SMEM(neighbours.shape, jnp.int32),
            pltpu.SemaphoreType.DMA((6,)),
        ],
        compiler_params=params(32),
        cost_estimate=cost(2e9, 5e6),
        name="prepare",
    )(*in_hbm(x, gain, w_qkv, assignment, neighbours))
    center, west = lax.optimization_barrier((center, west))
    center, east = lax.optimization_barrier((center, east))
    outer = exchanged(jnp.concatenate([west, east, own[rows:]], axis=0), 1)
    inner = exchanged(jnp.concatenate([west, east, own], axis=0), 0)
    top, summed = pl.pallas_call(
        early_kernel,
        in_specs=[whole()] * 11,
        out_specs=[whole()] * 2,
        out_shape=[
            struct(parts, 8, members * rows, dtype=F32),
            struct(parts, LANES + ROWS, members * rows, dtype=F32),
        ],
        scratch_shapes=[
            pltpu.VMEM(((1 + EARLY) * rows, width), BF16),
            pltpu.VMEM((parts, LANES + ROWS, (1 + EARLY) * rows), BF16),
        ],
        compiler_params=params(32),
        cost_estimate=cost(3e9, 6e6),
        name="early",
    )(choice, west, east, inner, center, gain, wk, wvt, query, key, value)
    edges, top = mixed(blocks_of(ABOVE) + blocks_of(BELOW), "mix_edges", top)
    top, edges = lax.optimization_barrier((top, edges))
    state, latent, first, last = pl.pallas_call(
        late_kernel,
        in_specs=[whole()] * 14,
        out_specs=[whole()] * 4,
        out_shape=[pltpu.VMEM((rows, width), BF16), struct(rows, channels)]
        + [struct(ROWS, channels)] * 2,
        scratch_shapes=[pltpu.VMEM((rows, width), BF16)],
        compiler_params=params(32),
        cost_estimate=cost(3e9, 6e6),
        name="late",
    )(
        choice, cells, inner, center, outer,
        own, gain, wk, wvt, query, top, summed, w_out, w_latent,
    )

    from_left = shifted(last, 1)
    from_right = shifted(first, -1)
    middle, latent = mixed(blocks_of(OWN), "mix_own", latent)
    from_left, middle = lax.optimization_barrier((from_left, middle))
    extended = jnp.concatenate([latent, from_left[:SIDE], from_right[:SIDE]], axis=0)
    far = exchanged(extended, 1)
    near = exchanged(extended, 0)

    lanes = -(-(rows + 2 * SIDE) // 256) * 256
    partial, hots, state = pl.pallas_call(
        functools.partial(own_kernel, (rows, 3 * rows, 2 * rows)),
        in_specs=[whole()] * 6,
        out_specs=[whole()] * 3,
        out_shape=[
            struct(lat_rows, outputs, lon_cols, dtype=F32),
            struct(2, 2, TAPS, lanes, lon_cols),
            struct(rows, width),
        ],
        compiler_params=params(32),
        cost_estimate=cost(1e9, 2.5e6),
        name="own_band",
    )(state, own, inner, outer, extended, middle)
    band_scratch = [
        pltpu.VMEM((outputs, TAPS * lanes), BF16),
        pltpu.VMEM((2 * outputs, TAPS * lanes), BF16),
    ]
    partial = pl.pallas_call(
        functools.partial(band_kernel, True),
        in_specs=[whole()] * 4,
        out_specs=whole(),
        out_shape=struct(lat_rows, outputs, lon_cols, dtype=F32),
        scratch_shapes=band_scratch,
        compiler_params=params(32),
        cost_estimate=cost(1e9, 2.5e6),
        name="inner_band",
    )(near, edges, hots, partial)
    fields = pl.pallas_call(
        functools.partial(band_kernel, False),
        in_specs=[whole()] * 4,
        out_specs=whole(),
        out_shape=struct(out_ch, lat_rows, lon_cols),
        scratch_shapes=band_scratch,
        compiler_params=params(32),
        cost_estimate=cost(1e9, 2.5e6),
        name="outer_band",
    )(far, edges, hots, partial)
    return (state.reshape(1, rows, width), fields.reshape(1, out_ch, lat_rows, lon_cols))


def solution(mesh):
    in_specs = (
        P(None, ("reg", "lon"), None),
        P(),
        P(),
        P(),
        P(),
        P(("reg", "lon"), None),
        P("reg", "lon"),
        P(None, "reg", None, None),
        P(),
    )
    out_specs = (P(None, ("reg", "lon"), None), P(None, None, "reg", "lon"))
    return jax.shard_map(shards, mesh=mesh, in_specs=in_specs, out_specs=out_specs, check_vma=False)
```

```python
import functools
import math

import jax
import jax.numpy as jnp
from jax import lax
from jax.experimental import pallas as pl
from jax.experimental.pallas import tpu as pltpu
from jax.sharding import PartitionSpec as P

HEADS = 16
REACH = 2
TAPS = 2 * REACH + 1
SIDE = 8
ROWS = 16
LANES = 128
EARLY = 2
CANDIDATES = 5
F32 = jnp.float32
BF16 = jnp.bfloat16
NT = (((1,), (1,)), ((), ()))

ABOVE = ((-2, (0,)), (-1, (0, 1)))
OWN = ((0, (0, 1)), (1, (0, 1)))
BELOW = ((3, (1,)), (2, (0, 1)))


def blocks_of(band):
    return [
        (out_row, src - out_row + REACH, off)
        for src, out_rows in band
        for off in range(TAPS)
        for out_row in out_rows
    ]


def iota(shape, dim):
    return lax.broadcasted_iota(jnp.int32, shape, dim)


def normalise(rows, gain):
    values = rows.astype(F32)
    center = values - jnp.mean(values, axis=-1, keepdims=True)
    spread = jnp.mean(center * center, axis=-1, keepdims=True)
    return (center * lax.rsqrt(spread + 1e-05) * gain).astype(BF16)


def mix_kernel(blocks, psi_ref, dec_ref, mixed_ref, psi_rows_ref, taps_ref):
    basis, out_ch, channels = dec_ref.shape
    depth = basis * ROWS
    for tap in range(TAPS):
        for off in range(TAPS):
            at = (tap * TAPS + off) * 2
            psi_rows_ref[at : at + 2, :] = psi_ref[tap, off]
    spread = (iota((basis, depth), 1) // ROWS == iota((basis, depth), 0)).astype(F32)
    expanded = jnp.dot(psi_rows_ref[...], spread, preferred_element_type=F32)
    pick = iota((ROWS, depth), 1) % ROWS == iota((ROWS, depth), 0)
    for at, (out_row, tap, off) in enumerate(blocks):
        source = (tap * TAPS + off) * 2 + out_row
        taps = jnp.broadcast_to(expanded[source : source + 1], (ROWS, depth))
        taps_ref[at * ROWS : (at + 1) * ROWS, :] = jnp.where(pick, taps, 0.0).astype(BF16)
    for first in range(0, out_ch, ROWS):
        size = min(ROWS, out_ch - first)
        pieces = []
        for base in range(basis):
            pieces.append(dec_ref[base, first : first + size, :])
            if size < ROWS:
                pieces.append(jnp.zeros((ROWS - size, channels), BF16))
        mixing = jnp.concatenate(pieces, axis=0)
        mixed = jnp.dot(taps_ref[...], mixing, preferred_element_type=F32).astype(BF16)
        mixed_ref[:, first : first + ROWS, :] = mixed.reshape(len(blocks), ROWS, channels)


def listed_blocks(sectors, listed_ref):
    reg_here, lon_here = lax.axis_index("reg"), lax.axis_index("lon")
    toward = 1 - 2 * (reg_here % 2)
    found = []
    for at in range(1, listed_ref.shape[1]):
        block = listed_ref[0, at]
        step_reg = (block // sectors - reg_here) * toward
        step_lon = (block % sectors - lon_here + 1 + sectors) % sectors - 1
        side = jnp.where(step_lon == 0, 0, jnp.where(step_lon > 0, 1, 4))
        ahead = jnp.where(step_lon < 0, 0, 1)
        behind = jnp.where(step_lon < 0, 7, 4 + side)
        found.append(jnp.where(step_reg == 0, ahead, jnp.where(step_reg > 0, 2 + side, behind)))
    for low in range(len(found)):
        for high in range(low + 1, len(found)):
            less, more = jnp.minimum(found[low], found[high]), jnp.maximum(found[low], found[high])
            found[low], found[high] = less, more
    return found


def gather_kernel(x_hbm, assign_hbm, own_ref, assign_ref, sems):
    rows = own_ref.shape[0] - ROWS
    copies = [
        pltpu.make_async_copy(assign_hbm, assign_ref, sems.at[0]),
        pltpu.make_async_copy(x_hbm, own_ref.at[pl.ds(0, rows)], sems.at[1]),
    ]
    for copy in copies:
        copy.start()
    copies[0].wait()
    local = lax.rem(assign_ref[...], rows).astype(F32)
    line = jnp.concatenate([local[:1], local[1:2]], axis=1)
    line = jnp.broadcast_to(line, (ROWS, line.shape[1]))
    own_ref[rows:] = jnp.where(iota(line.shape, 0) == 0, line, 0.0).astype(BF16)
    copies[1].wait()


def prepare_kernel(
    sectors,
    own_ref, gain_hbm, wqkv_hbm, assign_hbm, listed_hbm,
    query_ref, key_ref, value_ref, wk_ref, wvt_ref, choice_ref, cells_ref,
    gain_ref, wqkv_ref, cell_ref, listed_ref, sems,
):
    copies = [
        pltpu.make_async_copy(source, target, sems.at[at])
        for at, (source, target) in enumerate(
            (
                (gain_hbm, gain_ref),
                (wqkv_hbm, wqkv_ref),
                (assign_hbm, cell_ref),
                (listed_hbm, listed_ref),
            )
        )
    ]
    for copy in copies:
        copy.start()
    rows, width = key_ref.shape
    group, members = query_ref.shape[1], query_ref.shape[2] // rows
    head = group // members
    for copy in copies[2:]:
        copy.wait()
    for at, number in enumerate(listed_blocks(sectors, listed_ref)):
        for candidate in range(CANDIDATES):
            same = jnp.full((ROWS, LANES), jnp.where(number == at + candidate, 1.0, 0.0), F32)
            choice_ref[at, candidate] = same.astype(BF16)
    lat_rows, lon_cols = cell_ref.shape
    place, node = iota((ROWS, rows), 0), iota((ROWS, rows), 1)
    for side, first in enumerate((0, lon_cols - REACH)):
        hit = jnp.zeros((ROWS, rows), F32)
        for row in range(lat_rows):
            for col in range(REACH):
                cell = cell_ref[row, first + col] % rows
                hit = jnp.where((place == row * REACH + col) & (node == cell), 1.0, hit)
        cells_ref[side * ROWS : (side + 1) * ROWS] = hit.astype(BF16)
    copies[0].wait()
    normed = normalise(own_ref[:rows], gain_ref[...])
    copies[1].wait()
    query = jnp.dot(normed, wqkv_ref[:, :width], preferred_element_type=F32)
    query_t = (query * (math.log2(math.e) / head**0.5)).T.astype(BF16)
    mask = (iota((group, members * rows), 0) // head) == (iota((group, members * rows), 1) // rows)
    for part in range(width // group):
        piece = query_t[part * group : (part + 1) * group]
        wide = jnp.concatenate([piece] * members, axis=1)
        query_ref[part] = jnp.where(mask, wide, jnp.zeros_like(wide))
    wk = wqkv_ref[:, width : 2 * width]
    wk_ref[...] = wk
    key_ref[...] = jnp.dot(normed, wk, preferred_element_type=F32).astype(BF16)
    wvt = wqkv_ref[:, 2 * width :].astype(F32).T.astype(BF16)
    wvt_ref[...] = wvt
    value_ref[...] = lax.dot_general(wvt, normed, NT, preferred_element_type=F32).astype(BF16)


def chosen(entries, rows, choice_ref, candidates):
    tall, wide = rows // ROWS, candidates[-1].shape[1] // LANES
    near = []
    for entry in entries:
        total = None
        for at in range(CANDIDATES):
            weight = jnp.concatenate([choice_ref[entry, at]] * wide, axis=1)
            part = candidates[entry + at] * jnp.concatenate([weight] * tall, axis=0)
            total = part if total is None else total + part
        near.append(total)
    return jnp.concatenate(near, axis=0)


def project(nodes, gain, wk_ref, wvt_ref):
    normed = normalise(nodes, gain)
    keys = jnp.dot(normed, wk_ref[...], preferred_element_type=F32).astype(BF16)
    values = lax.dot_general(wvt_ref[...], normed, NT, preferred_element_type=F32).astype(BF16)
    return keys, values


def early_kernel(
    choice_ref, west_ref, east_ref, inner_ref, outer_ref,
    gain_ref, wk_ref, wvt_ref, query_ref, key_ref, value_ref,
    top_ref, sum_ref, keys_ref, values_ref,
):
    rows = key_ref.shape[0]
    parts, group, _ = query_ref.shape
    candidates = [west_ref[...], east_ref[...]]
    candidates += [ref[rows : 2 * rows] if center else ref[:rows] for ref in (inner_ref, outer_ref) for center in (1, 0)]
    nodes = chosen(range(EARLY), rows, choice_ref, candidates)
    keys, values = project(nodes, gain_ref[...], wk_ref, wvt_ref)
    keys_ref[:rows] = key_ref[...]
    keys_ref[rows:] = keys
    for part in range(parts):
        span = slice(part * group, (part + 1) * group)
        values_ref[part, :group, :rows] = value_ref[span]
        values_ref[part, :group, rows:] = values[span]
        values_ref[part, group:, :] = jnp.ones((ROWS, keys_ref.shape[0]), BF16)

    def scored(part):
        span = slice(part * group, (part + 1) * group)
        return jnp.dot(keys_ref[:, span], query_ref[part], preferred_element_type=F32)

    scores = scored(0)
    for part in range(parts):
        now = scores
        if part + 1 < parts:
            scores = scored(part + 1)
        top = jnp.max(now, axis=0, keepdims=True)
        expo = jnp.exp2(now - top).astype(BF16)
        top_ref[part] = jnp.broadcast_to(top, top_ref.shape[1:])
        sum_ref[part] = jnp.dot(values_ref[part], expo, preferred_element_type=F32)


def late_kernel(
    choice_ref, cells_ref, inner_ref, outer_ref, beside_ref, corner_ref,
    own_ref, gain_ref, wk_ref, wvt_ref, query_ref, top_ref, sum_ref, wout_ref, wlat_ref,
    state_ref, latent_ref, first_ref, last_ref,
    attended_ref,
):
    rows, width = state_ref.shape
    parts, group, lanes = query_ref.shape
    members = lanes // rows
    head = group // members
    candidates = [None, None]
    candidates += [ref[rows : 2 * rows] if center else ref[:rows] for ref in (inner_ref, outer_ref) for center in (1, 0)]
    candidates += [beside_ref[...], corner_ref[...]]
    nodes = chosen(range(EARLY, choice_ref.shape[0]), rows, choice_ref, candidates)
    keys, values = project(nodes, gain_ref[...], wk_ref, wvt_ref)
    ones = jnp.ones((ROWS, nodes.shape[0]), BF16)
    owner = iota((group, rows), 0) // head

    def scored(part):
        span = slice(part * group, (part + 1) * group)
        return jnp.dot(keys[:, span], query_ref[part], preferred_element_type=F32)

    scores = scored(0)
    for part in range(parts):
        now = scores
        if part + 1 < parts:
            scores = scored(part + 1)
        before = top_ref[part, :1]
        top = jnp.maximum(before, jnp.max(now, axis=0, keepdims=True))
        expo = jnp.exp2(now - top).astype(BF16)
        weights = jnp.concatenate([values[part * group : (part + 1) * group], ones], axis=0)
        summed = jnp.dot(weights, expo, preferred_element_type=F32)
        summed = summed + sum_ref[part] * jnp.exp2(before - top)
        summed = summed[:group] * (1.0 / summed[group : group + 1])
        merged = None
        for member in range(members):
            piece = summed[:, member * rows : (member + 1) * rows]
            merged = piece if merged is None else jnp.where(owner == member, piece, merged)
        attended_ref[:, part * group : (part + 1) * group] = merged.T.astype(BF16)
    state = (
        own_ref[:rows].astype(F32)
        + jnp.dot(attended_ref[...], wout_ref[...], preferred_element_type=F32)
    ).astype(BF16)
    state_ref[...] = state
    value = jnp.dot(state, wlat_ref[...], preferred_element_type=F32)
    latent = (value / (1.0 + jnp.exp(-value))).astype(BF16)
    latent_ref[...] = latent
    cells = jnp.dot(cells_ref[...], latent, preferred_element_type=F32).astype(BF16)
    first_ref[...] = cells[:ROWS]
    last_ref[...] = cells[ROWS:]


def hot_rows(values, rows, cols, line):
    column = iota((8, cols), 1)
    node = iota((rows + 2 * SIDE, cols), 0).astype(F32)
    for off in range(TAPS):
        step = off - REACH
        where = jnp.broadcast_to(values, (8, cols))
        if step:
            where = pltpu.roll(where, (-step) % cols, 1)
        reach = column + step
        before = (rows + REACH * line + reach + REACH).astype(F32)
        after = (rows + SIDE + REACH * line + reach - cols).astype(F32)
        where = jnp.where(reach < 0, before, jnp.where(reach >= cols, after, where))
        yield jnp.where(node == where[:1], 1.0, 0.0).astype(BF16)


def shares_of(latent, weights):
    blocks, outputs, channels = weights.shape
    shares = lax.dot_general(
        weights.reshape(blocks * outputs, channels), latent, NT, preferred_element_type=F32
    ).astype(BF16)
    return [shares[at * outputs : (at + 1) * outputs] for at in range(blocks)]


def lines_of(line_ref, start, cols):
    values = line_ref[start : start + ROWS, :].astype(F32)
    return values[:1, :cols], values[:1, cols:]


def own_kernel(
    begin, state_ref, own_ref, inner_ref, outer_ref, latent_ref, weights_ref,
    out_ref, hot_ref, kept_ref,
):
    kept_ref[...] = state_ref[...]
    cols = out_ref.shape[2]
    rows = latent_ref.shape[0] - 2 * SIDE
    own = lines_of(own_ref, begin[0], cols)
    table = [list(hot_rows(own[line], rows, cols, line)) for line in range(2)]
    acc = [None, None]
    for (out_row, tap, off), share in zip(
        blocks_of(OWN), shares_of(latent_ref[...], weights_ref[...])
    ):
        line = out_row + tap - REACH
        piece = jnp.dot(share, table[line][off], preferred_element_type=F32)
        acc[out_row] = piece if acc[out_row] is None else acc[out_row] + piece
    for row in range(2):
        out_ref[row] = acc[row]
    odd = lax.axis_index("reg") % 2 == 1
    inner, outer = lines_of(inner_ref, begin[1], cols), lines_of(outer_ref, begin[2], cols)
    nodes = rows + 2 * SIDE
    for band, (yes, no) in enumerate(((inner, outer), (outer, inner))):
        for at, line in enumerate((0, 1) if band == 0 else (1, 0)):
            values = jnp.where(odd, yes[line], no[line])
            for off, hot in enumerate(hot_rows(values, rows, cols, line)):
                hot_ref[band, at, off, :nodes] = hot
                hot_ref[band, at, off, nodes:] = jnp.zeros((hot_ref.shape[3] - nodes, cols), BF16)


def band_kernel(from_inner, latent_ref, weights_ref, hot_ref, partial_ref, out_ref, one_ref, two_ref):
    odd = lax.axis_index("reg") % 2
    band = 1 - odd if from_inner else odd
    latent = latent_ref[...]
    lanes, cols = hot_ref.shape[3:]
    outputs = weights_ref.shape[1]
    blank = jnp.zeros((lanes - latent.shape[0], latent.shape[1]), BF16)
    blocks = len(blocks_of(ABOVE))
    weights = weights_ref[pl.ds(band * blocks, blocks)]
    shares = shares_of(jnp.concatenate([latent, blank], axis=0), weights)
    for off in range(TAPS):
        span = slice(off * lanes, (off + 1) * lanes)
        one_ref[:, span] = shares[off]
        for row in range(2):
            two_ref[row * outputs : (row + 1) * outputs, span] = shares[TAPS + 2 * off + row]
    depth = TAPS * lanes
    one = jnp.dot(one_ref[...], hot_ref[band, 0].reshape(depth, cols), preferred_element_type=F32)
    two = jnp.dot(two_ref[...], hot_ref[band, 1].reshape(depth, cols), preferred_element_type=F32)
    for row in range(2):
        total = partial_ref[row] + two[row * outputs : (row + 1) * outputs]
        total = total + jnp.where(band == row, one, 0.0)
        if from_inner:
            out_ref[row] = total
        else:
            out_ref[:, row, :] = total[: out_ref.shape[0]].astype(BF16)


def whole(memory=pltpu.VMEM):
    return pl.BlockSpec(memory_space=memory)


def struct(*shape, dtype=BF16):
    return jax.ShapeDtypeStruct(shape, dtype)


def params(limit):
    return pltpu.CompilerParams(vmem_limit_bytes=limit << 20)


def cost(flops, moved):
    return pl.CostEstimate(flops=int(flops), bytes_accessed=int(moved), transcendentals=0)


def shards(nodes, norm_gain, w_qkv, w_out, w_latent, neighbours, assignment, psi, w_dec):
    _, rows, width = nodes.shape
    channels = w_latent.shape[1]
    lat_rows, lon_cols = assignment.shape
    basis, _, out_ch = w_dec.shape
    sectors = lax.axis_size("lon")
    count = neighbours.shape[1]
    x = nodes.reshape(rows, width)
    gain = norm_gain.reshape(1, width)

    def shifted(array, step):
        return lax.ppermute(array, "lon", [(i, (i + step) % sectors) for i in range(sectors)])

    def exchanged(array, first):
        size = lax.axis_size("reg")
        pairs = [(i, i + 1) for i in range(first, size - 1, 2)]
        return lax.ppermute(array, "reg", pairs + [(j, i) for i, j in pairs])

    def in_hbm(*arrays):
        return [pltpu.with_memory_space_constraint(array, pltpu.HBM) for array in arrays]

    west = shifted(x, 1)
    east = shifted(x, -1)

    outputs = -(-out_ch // ROWS) * ROWS
    head = width // HEADS
    members = LANES // head
    parts = HEADS // members
    def mixed(blocks, name, after):
        taps = psi.transpose(2, 3, 1, 0)
        mixing = w_dec.transpose(0, 2, 1)
        taps, mixing, after = lax.optimization_barrier((taps, mixing, after))
        weights = pl.pallas_call(
            functools.partial(mix_kernel, blocks),
            in_specs=[whole()] * 2,
            out_specs=whole(),
            out_shape=struct(len(blocks), outputs, channels),
            scratch_shapes=[
                pltpu.VMEM((2 * TAPS * TAPS, basis), F32),
                pltpu.VMEM((len(blocks) * ROWS, basis * ROWS), BF16),
            ],
            compiler_params=params(32),
            cost_estimate=cost(1e3, 1e3),
            name=name,
        )(taps, mixing)
        return weights, after

    own = pl.pallas_call(
        gather_kernel,
        in_specs=[whole(pltpu.HBM)] * 2,
        out_specs=whole(),
        out_shape=struct(rows + ROWS, width),
        scratch_shapes=[
            pltpu.VMEM(assignment.shape, jnp.int32),
            pltpu.SemaphoreType.DMA((2,)),
        ],
        compiler_params=params(32),
        cost_estimate=cost(1e3, 1e3),
        name="gather",
    )(*in_hbm(x, assignment))
    query, key, value, wk, wvt, choice, cells = pl.pallas_call(
        functools.partial(prepare_kernel, sectors),
        in_specs=[whole()] + [whole(pltpu.HBM)] * 4,
        out_specs=[whole()] * 7,
        out_shape=[
            struct(parts, LANES, members * rows),
            struct(rows, width),
            struct(width, rows),
            struct(width, width),
            struct(width, width),
            struct(count - 1, CANDIDATES, ROWS, LANES),
            struct(2 * ROWS, rows),
        ],
        scratch_shapes=[
            pltpu.VMEM((1, width), F32),
            pltpu.VMEM(w_qkv.shape, BF16),
            pltpu.SMEM(assignment.shape, jnp.int32),
            pltpu.SMEM(neighbours.shape, jnp.int32),
            pltpu.SemaphoreType.DMA((4,)),
        ],
        compiler_params=params(32),
        cost_estimate=cost(2e9, 5e6),
        name="prepare",
    )(own, *in_hbm(gain, w_qkv, assignment, neighbours))
    message = jnp.concatenate([east, own], axis=0)
    message_a = message
    west_a = west
    inner = exchanged(message_a, 0)
    outer = exchanged(message, 1)
    west, message = lax.optimization_barrier((west, message))
    corner = exchanged(west, 1)
    beside = exchanged(west_a, 0)
    edges, inner = mixed(blocks_of(ABOVE) + blocks_of(BELOW), "mix_edges", inner)
    inner, edges = lax.optimization_barrier((inner, edges))

    top, summed = pl.pallas_call(
        early_kernel,
        in_specs=[whole()] * 11,
        out_specs=[whole()] * 2,
        out_shape=[
            struct(parts, 8, members * rows, dtype=F32),
            struct(parts, LANES + ROWS, members * rows, dtype=F32),
        ],
        scratch_shapes=[
            pltpu.VMEM(((1 + EARLY) * rows, width), BF16),
            pltpu.VMEM((parts, LANES + ROWS, (1 + EARLY) * rows), BF16),
        ],
        compiler_params=params(32),
        cost_estimate=cost(1e3, 1e3),
        name="early",
    )(choice, west, east, inner, outer, gain, wk, wvt, query, key, value)
    state, latent, first, last = pl.pallas_call(
        late_kernel,
        in_specs=[whole()] * 15,
        out_specs=[whole()] * 4,
        out_shape=[pltpu.VMEM((rows, width), BF16), struct(rows, channels)]
        + [struct(ROWS, channels)] * 2,
        scratch_shapes=[pltpu.VMEM((rows, width), BF16)],
        compiler_params=params(32),
        cost_estimate=cost(3e9, 6e6),
        name="late",
    )(
        choice, cells, inner, outer, beside, corner,
        own, gain, wk, wvt, query, top, summed, w_out, w_latent,
    )

    from_left = shifted(last, 1)
    from_right = shifted(first, -1)
    middle, latent = mixed(blocks_of(OWN), "mix_own", latent)
    from_left, middle = lax.optimization_barrier((from_left, middle))
    extended = jnp.concatenate([latent, from_left[:SIDE], from_right[:SIDE]], axis=0)
    far = exchanged(extended, 1)
    near = exchanged(extended, 0)

    lanes = -(-(rows + 2 * SIDE) // 256) * 256
    partial, hots, state = pl.pallas_call(
        functools.partial(own_kernel, (rows, 2 * rows, 2 * rows)),
        in_specs=[whole()] * 6,
        out_specs=[whole()] * 3,
        out_shape=[
            struct(lat_rows, outputs, lon_cols, dtype=F32),
            struct(2, 2, TAPS, lanes, lon_cols),
            struct(rows, width),
        ],
        compiler_params=params(32),
        cost_estimate=cost(1e9, 2.5e6),
        name="own_band",
    )(state, own, inner, outer, extended, middle)
    band_scratch = [
        pltpu.VMEM((outputs, TAPS * lanes), BF16),
        pltpu.VMEM((2 * outputs, TAPS * lanes), BF16),
    ]
    partial = pl.pallas_call(
        functools.partial(band_kernel, True),
        in_specs=[whole()] * 4,
        out_specs=whole(),
        out_shape=struct(lat_rows, outputs, lon_cols, dtype=F32),
        scratch_shapes=band_scratch,
        compiler_params=params(32),
        cost_estimate=cost(1e9, 2.5e6),
        name="inner_band",
    )(near, edges, hots, partial)
    fields = pl.pallas_call(
        functools.partial(band_kernel, False),
        in_specs=[whole()] * 4,
        out_specs=whole(),
        out_shape=struct(out_ch, lat_rows, lon_cols),
        scratch_shapes=band_scratch,
        compiler_params=params(32),
        cost_estimate=cost(1e9, 2.5e6),
        name="outer_band",
    )(far, edges, hots, partial)
    return (state.reshape(1, rows, width), fields.reshape(1, out_ch, lat_rows, lon_cols))


def solution(mesh):
    in_specs = (
        P(None, ("reg", "lon"), None),
        P(),
        P(),
        P(),
        P(),
        P(("reg", "lon"), None),
        P("reg", "lon"),
        P(None, "reg", None, None),
        P(),
    )
    out_specs = (P(None, ("reg", "lon"), None), P(None, None, "reg", "lon"))
    return jax.shard_map(shards, mesh=mesh, in_specs=in_specs, out_specs=out_specs, check_vma=False)
```

```python
import functools
import math

import jax
import jax.numpy as jnp
from jax import lax
from jax.experimental import pallas as pl
from jax.experimental.pallas import tpu as pltpu
from jax.sharding import PartitionSpec as P

HEADS = 16
REACH = 2
TAPS = 2 * REACH + 1
SIDE = 8
ROWS = 16
LANES = 128
EARLY = 2
CANDIDATES = 5
F32 = jnp.float32
BF16 = jnp.bfloat16
NT = (((1,), (1,)), ((), ()))

ABOVE = ((-2, (0,)), (-1, (0, 1)))
OWN = ((0, (0, 1)), (1, (0, 1)))
BELOW = ((3, (1,)), (2, (0, 1)))


def blocks_of(band):
    return [
        (out_row, src - out_row + REACH, off)
        for src, out_rows in band
        for off in range(TAPS)
        for out_row in out_rows
    ]


def iota(shape, dim):
    return lax.broadcasted_iota(jnp.int32, shape, dim)


def normalise(rows, gain):
    values = rows.astype(F32)
    center = values - jnp.mean(values, axis=-1, keepdims=True)
    spread = jnp.mean(center * center, axis=-1, keepdims=True)
    return (center * lax.rsqrt(spread + 1e-05) * gain).astype(BF16)


def mix_kernel(blocks, psi_ref, dec_ref, mixed_ref, psi_rows_ref, taps_ref):
    basis, out_ch, channels = dec_ref.shape
    depth = basis * ROWS
    for tap in range(TAPS):
        for off in range(TAPS):
            at = (tap * TAPS + off) * 2
            psi_rows_ref[at : at + 2, :] = psi_ref[tap, off]
    spread = (iota((basis, depth), 1) // ROWS == iota((basis, depth), 0)).astype(F32)
    expanded = jnp.dot(psi_rows_ref[...], spread, preferred_element_type=F32)
    pick = iota((ROWS, depth), 1) % ROWS == iota((ROWS, depth), 0)
    for at, (out_row, tap, off) in enumerate(blocks):
        source = (tap * TAPS + off) * 2 + out_row
        taps = jnp.broadcast_to(expanded[source : source + 1], (ROWS, depth))
        taps_ref[at * ROWS : (at + 1) * ROWS, :] = jnp.where(pick, taps, 0.0).astype(BF16)
    for first in range(0, out_ch, ROWS):
        size = min(ROWS, out_ch - first)
        pieces = []
        for base in range(basis):
            pieces.append(dec_ref[base, first : first + size, :])
            if size < ROWS:
                pieces.append(jnp.zeros((ROWS - size, channels), BF16))
        mixing = jnp.concatenate(pieces, axis=0)
        mixed = jnp.dot(taps_ref[...], mixing, preferred_element_type=F32).astype(BF16)
        mixed_ref[:, first : first + ROWS, :] = mixed.reshape(len(blocks), ROWS, channels)


def listed_blocks(sectors, listed_ref):
    reg_here, lon_here = lax.axis_index("reg"), lax.axis_index("lon")
    toward = 1 - 2 * (reg_here % 2)
    found = []
    for at in range(1, listed_ref.shape[1]):
        block = listed_ref[0, at]
        step_reg = (block // sectors - reg_here) * toward
        step_lon = (block % sectors - lon_here + 1 + sectors) % sectors - 1
        side = jnp.where(step_lon == 0, 0, jnp.where(step_lon > 0, 1, 4))
        ahead = jnp.where(step_lon < 0, 0, 1)
        behind = jnp.where(step_lon < 0, 7, 4 + side)
        found.append(jnp.where(step_reg == 0, ahead, jnp.where(step_reg > 0, 2 + side, behind)))
    for low in range(len(found)):
        for high in range(low + 1, len(found)):
            less, more = jnp.minimum(found[low], found[high]), jnp.maximum(found[low], found[high])
            found[low], found[high] = less, more
    return found


def gather_kernel(x_hbm, assign_hbm, own_ref, assign_ref, sems):
    rows = own_ref.shape[0] - ROWS
    copies = [
        pltpu.make_async_copy(assign_hbm, assign_ref, sems.at[0]),
        pltpu.make_async_copy(x_hbm, own_ref.at[pl.ds(0, rows)], sems.at[1]),
    ]
    for copy in copies:
        copy.start()
    copies[0].wait()
    local = lax.rem(assign_ref[...], rows).astype(F32)
    line = jnp.concatenate([local[:1], local[1:2]], axis=1)
    line = jnp.broadcast_to(line, (ROWS, line.shape[1]))
    own_ref[rows:] = jnp.where(iota(line.shape, 0) == 0, line, 0.0).astype(BF16)
    copies[1].wait()


def prepare_kernel(
    sectors,
    own_ref, gain_hbm, wqkv_hbm, assign_hbm, listed_hbm,
    query_ref, key_ref, value_ref, wk_ref, wvt_ref, choice_ref, cells_ref,
    gain_ref, wqkv_ref, cell_ref, listed_ref, sems,
):
    copies = [
        pltpu.make_async_copy(source, target, sems.at[at])
        for at, (source, target) in enumerate(
            (
                (gain_hbm, gain_ref),
                (wqkv_hbm, wqkv_ref),
                (assign_hbm, cell_ref),
                (listed_hbm, listed_ref),
            )
        )
    ]
    for copy in copies:
        copy.start()
    rows, width = key_ref.shape
    group, members = query_ref.shape[1], query_ref.shape[2] // rows
    head = group // members
    for copy in copies[2:]:
        copy.wait()
    for at, number in enumerate(listed_blocks(sectors, listed_ref)):
        for candidate in range(CANDIDATES):
            same = jnp.full((ROWS, LANES), jnp.where(number == at + candidate, 1.0, 0.0), F32)
            choice_ref[at, candidate] = same.astype(BF16)
    lat_rows, lon_cols = cell_ref.shape
    place, node = iota((ROWS, rows), 0), iota((ROWS, rows), 1)
    for side, first in enumerate((0, lon_cols - REACH)):
        hit = jnp.zeros((ROWS, rows), F32)
        for row in range(lat_rows):
            for col in range(REACH):
                cell = cell_ref[row, first + col] % rows
                hit = jnp.where((place == row * REACH + col) & (node == cell), 1.0, hit)
        cells_ref[side * ROWS : (side + 1) * ROWS] = hit.astype(BF16)
    copies[0].wait()
    normed = normalise(own_ref[:rows], gain_ref[...])
    copies[1].wait()
    query = jnp.dot(normed, wqkv_ref[:, :width], preferred_element_type=F32)
    query_t = (query * (math.log2(math.e) / head**0.5)).T.astype(BF16)
    mask = (iota((group, members * rows), 0) // head) == (iota((group, members * rows), 1) // rows)
    for part in range(width // group):
        piece = query_t[part * group : (part + 1) * group]
        wide = jnp.concatenate([piece] * members, axis=1)
        query_ref[part] = jnp.where(mask, wide, jnp.zeros_like(wide))
    wk = wqkv_ref[:, width : 2 * width]
    wk_ref[...] = wk
    key_ref[...] = jnp.dot(normed, wk, preferred_element_type=F32).astype(BF16)
    wvt = wqkv_ref[:, 2 * width :].astype(F32).T.astype(BF16)
    wvt_ref[...] = wvt
    value_ref[...] = lax.dot_general(wvt, normed, NT, preferred_element_type=F32).astype(BF16)


def chosen(entries, rows, choice_ref, candidates):
    tall, wide = rows // ROWS, candidates[-1].shape[1] // LANES
    near = []
    for entry in entries:
        total = None
        for at in range(CANDIDATES):
            weight = jnp.concatenate([choice_ref[entry, at]] * wide, axis=1)
            part = candidates[entry + at] * jnp.concatenate([weight] * tall, axis=0)
            total = part if total is None else total + part
        near.append(total)
    return jnp.concatenate(near, axis=0)


def project(nodes, gain, wk_ref, wvt_ref):
    normed = normalise(nodes, gain)
    keys = jnp.dot(normed, wk_ref[...], preferred_element_type=F32).astype(BF16)
    values = lax.dot_general(wvt_ref[...], normed, NT, preferred_element_type=F32).astype(BF16)
    return keys, values


def early_kernel(
    choice_ref, west_ref, east_ref, inner_ref, outer_ref,
    gain_ref, wk_ref, wvt_ref, query_ref, key_ref, value_ref,
    top_ref, sum_ref, keys_ref, values_ref,
):
    rows = key_ref.shape[0]
    parts, group, _ = query_ref.shape
    candidates = [west_ref[...], east_ref[...]]
    candidates += [ref[rows : 2 * rows] if center else ref[:rows] for ref in (inner_ref, outer_ref) for center in (1, 0)]
    nodes = chosen(range(EARLY), rows, choice_ref, candidates)
    keys, values = project(nodes, gain_ref[...], wk_ref, wvt_ref)
    keys_ref[:rows] = key_ref[...]
    keys_ref[rows:] = keys
    for part in range(parts):
        span = slice(part * group, (part + 1) * group)
        values_ref[part, :group, :rows] = value_ref[span]
        values_ref[part, :group, rows:] = values[span]
        values_ref[part, group:, :] = jnp.ones((ROWS, keys_ref.shape[0]), BF16)

    def scored(part):
        span = slice(part * group, (part + 1) * group)
        return jnp.dot(keys_ref[:, span], query_ref[part], preferred_element_type=F32)

    scores = scored(0)
    for part in range(parts):
        now = scores
        if part + 1 < parts:
            scores = scored(part + 1)
        top = jnp.max(now, axis=0, keepdims=True)
        expo = jnp.exp2(now - top).astype(BF16)
        top_ref[part] = jnp.broadcast_to(top, top_ref.shape[1:])
        sum_ref[part] = jnp.dot(values_ref[part], expo, preferred_element_type=F32)


def late_kernel(
    choice_ref, cells_ref, inner_ref, outer_ref, beside_ref, corner_ref,
    own_ref, gain_ref, wk_ref, wvt_ref, query_ref, top_ref, sum_ref, wout_ref, wlat_ref,
    state_ref, latent_ref, first_ref, last_ref,
    attended_ref,
):
    rows, width = state_ref.shape
    parts, group, lanes = query_ref.shape
    members = lanes // rows
    head = group // members
    candidates = [None, None]
    candidates += [ref[rows : 2 * rows] if center else ref[:rows] for ref in (inner_ref, outer_ref) for center in (1, 0)]
    candidates += [beside_ref[...], corner_ref[...]]
    nodes = chosen(range(EARLY, choice_ref.shape[0]), rows, choice_ref, candidates)
    keys, values = project(nodes, gain_ref[...], wk_ref, wvt_ref)
    ones = jnp.ones((ROWS, nodes.shape[0]), BF16)
    owner = iota((group, rows), 0) // head

    def scored(part):
        span = slice(part * group, (part + 1) * group)
        return jnp.dot(keys[:, span], query_ref[part], preferred_element_type=F32)

    scores = scored(0)
    for part in range(parts):
        now = scores
        if part + 1 < parts:
            scores = scored(part + 1)
        before = top_ref[part, :1]
        top = jnp.maximum(before, jnp.max(now, axis=0, keepdims=True))
        expo = jnp.exp2(now - top).astype(BF16)
        weights = jnp.concatenate([values[part * group : (part + 1) * group], ones], axis=0)
        summed = jnp.dot(weights, expo, preferred_element_type=F32)
        summed = summed + sum_ref[part] * jnp.exp2(before - top)
        summed = summed[:group] * (1.0 / summed[group : group + 1])
        merged = None
        for member in range(members):
            piece = summed[:, member * rows : (member + 1) * rows]
            merged = piece if merged is None else jnp.where(owner == member, piece, merged)
        attended_ref[:, part * group : (part + 1) * group] = merged.T.astype(BF16)
    state = (
        own_ref[:rows].astype(F32)
        + jnp.dot(attended_ref[...], wout_ref[...], preferred_element_type=F32)
    ).astype(BF16)
    state_ref[...] = state
    value = jnp.dot(state, wlat_ref[...], preferred_element_type=F32)
    latent = (value / (1.0 + jnp.exp(-value))).astype(BF16)
    latent_ref[...] = latent
    cells = jnp.dot(cells_ref[...], latent, preferred_element_type=F32).astype(BF16)
    first_ref[...] = cells[:ROWS]
    last_ref[...] = cells[ROWS:]


def hot_rows(values, rows, cols, line):
    column = iota((8, cols), 1)
    node = iota((rows + 2 * SIDE, cols), 0).astype(F32)
    for off in range(TAPS):
        step = off - REACH
        where = jnp.broadcast_to(values, (8, cols))
        if step:
            where = pltpu.roll(where, (-step) % cols, 1)
        reach = column + step
        before = (rows + REACH * line + reach + REACH).astype(F32)
        after = (rows + SIDE + REACH * line + reach - cols).astype(F32)
        where = jnp.where(reach < 0, before, jnp.where(reach >= cols, after, where))
        yield jnp.where(node == where[:1], 1.0, 0.0).astype(BF16)


def shares_of(latent, weights):
    blocks, outputs, channels = weights.shape
    shares = lax.dot_general(
        weights.reshape(blocks * outputs, channels), latent, NT, preferred_element_type=F32
    ).astype(BF16)
    return [shares[at * outputs : (at + 1) * outputs] for at in range(blocks)]


def lines_of(line_ref, start, cols):
    values = line_ref[start : start + ROWS, :].astype(F32)
    return values[:1, :cols], values[:1, cols:]


def own_kernel(
    begin, state_ref, own_ref, inner_ref, outer_ref, latent_ref, weights_ref,
    out_ref, hot_ref, kept_ref,
):
    kept_ref[...] = state_ref[...]
    cols = out_ref.shape[2]
    rows = latent_ref.shape[0] - 2 * SIDE
    own = lines_of(own_ref, begin[0], cols)
    table = [list(hot_rows(own[line], rows, cols, line)) for line in range(2)]
    acc = [None, None]
    for (out_row, tap, off), share in zip(
        blocks_of(OWN), shares_of(latent_ref[...], weights_ref[...])
    ):
        line = out_row + tap - REACH
        piece = jnp.dot(share, table[line][off], preferred_element_type=F32)
        acc[out_row] = piece if acc[out_row] is None else acc[out_row] + piece
    for row in range(2):
        out_ref[row] = acc[row]
    odd = lax.axis_index("reg") % 2 == 1
    inner, outer = lines_of(inner_ref, begin[1], cols), lines_of(outer_ref, begin[2], cols)
    nodes = rows + 2 * SIDE
    for band, (yes, no) in enumerate(((inner, outer), (outer, inner))):
        for at, line in enumerate((0, 1) if band == 0 else (1, 0)):
            values = jnp.where(odd, yes[line], no[line])
            for off, hot in enumerate(hot_rows(values, rows, cols, line)):
                hot_ref[band, at, off, :nodes] = hot
                hot_ref[band, at, off, nodes:] = jnp.zeros((hot_ref.shape[3] - nodes, cols), BF16)


def band_kernel(from_inner, latent_ref, weights_ref, hot_ref, partial_ref, out_ref, one_ref, two_ref):
    odd = lax.axis_index("reg") % 2
    band = 1 - odd if from_inner else odd
    latent = latent_ref[...]
    lanes, cols = hot_ref.shape[3:]
    outputs = weights_ref.shape[1]
    blank = jnp.zeros((lanes - latent.shape[0], latent.shape[1]), BF16)
    blocks = len(blocks_of(ABOVE))
    weights = weights_ref[pl.ds(band * blocks, blocks)]
    shares = shares_of(jnp.concatenate([latent, blank], axis=0), weights)
    for off in range(TAPS):
        span = slice(off * lanes, (off + 1) * lanes)
        one_ref[:, span] = shares[off]
        for row in range(2):
            two_ref[row * outputs : (row + 1) * outputs, span] = shares[TAPS + 2 * off + row]
    depth = TAPS * lanes
    one = jnp.dot(one_ref[...], hot_ref[band, 0].reshape(depth, cols), preferred_element_type=F32)
    two = jnp.dot(two_ref[...], hot_ref[band, 1].reshape(depth, cols), preferred_element_type=F32)
    for row in range(2):
        total = partial_ref[row] + two[row * outputs : (row + 1) * outputs]
        total = total + jnp.where(band == row, one, 0.0)
        if from_inner:
            out_ref[row] = total
        else:
            out_ref[:, row, :] = total[: out_ref.shape[0]].astype(BF16)


def whole(memory=pltpu.VMEM):
    return pl.BlockSpec(memory_space=memory)


def struct(*shape, dtype=BF16):
    return jax.ShapeDtypeStruct(shape, dtype)


def params(limit):
    return pltpu.CompilerParams(vmem_limit_bytes=limit << 20)


def cost(flops, moved):
    return pl.CostEstimate(flops=int(flops), bytes_accessed=int(moved), transcendentals=0)


def shards(nodes, norm_gain, w_qkv, w_out, w_latent, neighbours, assignment, psi, w_dec):
    _, rows, width = nodes.shape
    channels = w_latent.shape[1]
    lat_rows, lon_cols = assignment.shape
    basis, _, out_ch = w_dec.shape
    sectors = lax.axis_size("lon")
    count = neighbours.shape[1]
    x = nodes.reshape(rows, width)
    gain = norm_gain.reshape(1, width)

    def shifted(array, step):
        return lax.ppermute(array, "lon", [(i, (i + step) % sectors) for i in range(sectors)])

    def exchanged(array, first):
        size = lax.axis_size("reg")
        pairs = [(i, i + 1) for i in range(first, size - 1, 2)]
        return lax.ppermute(array, "reg", pairs + [(j, i) for i, j in pairs])

    def in_hbm(*arrays):
        return [pltpu.with_memory_space_constraint(array, pltpu.HBM) for array in arrays]

    west = shifted(x, 1)
    east = shifted(x, -1)

    outputs = -(-out_ch // ROWS) * ROWS
    head = width // HEADS
    members = LANES // head
    parts = HEADS // members
    def mixed(blocks, name, after):
        taps = psi.transpose(2, 3, 1, 0)
        mixing = w_dec.transpose(0, 2, 1)
        taps, mixing, after = lax.optimization_barrier((taps, mixing, after))
        weights = pl.pallas_call(
            functools.partial(mix_kernel, blocks),
            in_specs=[whole()] * 2,
            out_specs=whole(),
            out_shape=struct(len(blocks), outputs, channels),
            scratch_shapes=[
                pltpu.VMEM((2 * TAPS * TAPS, basis), F32),
                pltpu.VMEM((len(blocks) * ROWS, basis * ROWS), BF16),
            ],
            compiler_params=params(32),
            cost_estimate=cost(2e9, 6e6),
            name=name,
        )(taps, mixing)
        return weights, after

    own = pl.pallas_call(
        gather_kernel,
        in_specs=[whole(pltpu.HBM)] * 2,
        out_specs=whole(),
        out_shape=struct(rows + ROWS, width),
        scratch_shapes=[
            pltpu.VMEM(assignment.shape, jnp.int32),
            pltpu.SemaphoreType.DMA((2,)),
        ],
        compiler_params=params(32),
        cost_estimate=cost(1e3, 1e3),
        name="gather",
    )(*in_hbm(x, assignment))
    query, key, value, wk, wvt, choice, cells = pl.pallas_call(
        functools.partial(prepare_kernel, sectors),
        in_specs=[whole()] + [whole(pltpu.HBM)] * 4,
        out_specs=[whole()] * 7,
        out_shape=[
            struct(parts, LANES, members * rows),
            struct(rows, width),
            struct(width, rows),
            struct(width, width),
            struct(width, width),
            struct(count - 1, CANDIDATES, ROWS, LANES),
            struct(2 * ROWS, rows),
        ],
        scratch_shapes=[
            pltpu.VMEM((1, width), F32),
            pltpu.VMEM(w_qkv.shape, BF16),
            pltpu.SMEM(assignment.shape, jnp.int32),
            pltpu.SMEM(neighbours.shape, jnp.int32),
            pltpu.SemaphoreType.DMA((4,)),
        ],
        compiler_params=params(32),
        cost_estimate=cost(5e8, 1e6),
        name="prepare",
    )(own, *in_hbm(gain, w_qkv, assignment, neighbours))
    own, query = lax.optimization_barrier((own, query))
    message = jnp.concatenate([east, own], axis=0)
    message_a = message
    west_a = west
    inner = exchanged(message_a, 0)
    outer = exchanged(message, 1)
    corner = exchanged(west, 1)
    beside = exchanged(west_a, 0)

    edges, west_m = mixed(blocks_of(ABOVE) + blocks_of(BELOW), "mix_edges", west)
    inner, edges = lax.optimization_barrier((inner, edges))
    top, summed = pl.pallas_call(
        early_kernel,
        in_specs=[whole()] * 11,
        out_specs=[whole()] * 2,
        out_shape=[
            struct(parts, 8, members * rows, dtype=F32),
            struct(parts, LANES + ROWS, members * rows, dtype=F32),
        ],
        scratch_shapes=[
            pltpu.VMEM(((1 + EARLY) * rows, width), BF16),
            pltpu.VMEM((parts, LANES + ROWS, (1 + EARLY) * rows), BF16),
        ],
        compiler_params=params(32),
        cost_estimate=cost(3e9, 6e6),
        name="early",
    )(choice, west, east, inner, outer, gain, wk, wvt, query, key, value)
    state, latent, first, last = pl.pallas_call(
        late_kernel,
        in_specs=[whole()] * 15,
        out_specs=[whole()] * 4,
        out_shape=[pltpu.VMEM((rows, width), BF16), struct(rows, channels)]
        + [struct(ROWS, channels)] * 2,
        scratch_shapes=[pltpu.VMEM((rows, width), BF16)],
        compiler_params=params(32),
        cost_estimate=cost(3e9, 6e6),
        name="late",
    )(
        choice, cells, inner, outer, beside, corner,
        own, gain, wk, wvt, query, top, summed, w_out, w_latent,
    )

    from_left = shifted(last, 1)
    from_right = shifted(first, -1)
    middle, latent = mixed(blocks_of(OWN), "mix_own", latent)
    from_left, middle = lax.optimization_barrier((from_left, middle))
    extended = jnp.concatenate([latent, from_left[:SIDE], from_right[:SIDE]], axis=0)
    far = exchanged(extended, 1)
    near = exchanged(extended, 0)

    lanes = -(-(rows + 2 * SIDE) // 256) * 256
    partial, hots, state = pl.pallas_call(
        functools.partial(own_kernel, (rows, 2 * rows, 2 * rows)),
        in_specs=[whole()] * 6,
        out_specs=[whole()] * 3,
        out_shape=[
            struct(lat_rows, outputs, lon_cols, dtype=F32),
            struct(2, 2, TAPS, lanes, lon_cols),
            struct(rows, width),
        ],
        compiler_params=params(32),
        cost_estimate=cost(1e9, 2.5e6),
        name="own_band",
    )(state, own, inner, outer, extended, middle)
    band_scratch = [
        pltpu.VMEM((outputs, TAPS * lanes), BF16),
        pltpu.VMEM((2 * outputs, TAPS * lanes), BF16),
    ]
    partial = pl.pallas_call(
        functools.partial(band_kernel, True),
        in_specs=[whole()] * 4,
        out_specs=whole(),
        out_shape=struct(lat_rows, outputs, lon_cols, dtype=F32),
        scratch_shapes=band_scratch,
        compiler_params=params(32),
        cost_estimate=cost(1e9, 2.5e6),
        name="inner_band",
    )(near, edges, hots, partial)
    fields = pl.pallas_call(
        functools.partial(band_kernel, False),
        in_specs=[whole()] * 4,
        out_specs=whole(),
        out_shape=struct(out_ch, lat_rows, lon_cols),
        scratch_shapes=band_scratch,
        compiler_params=params(32),
        cost_estimate=cost(1e9, 2.5e6),
        name="outer_band",
    )(far, edges, hots, partial)
    return (state.reshape(1, rows, width), fields.reshape(1, out_ch, lat_rows, lon_cols))


def solution(mesh):
    in_specs = (
        P(None, ("reg", "lon"), None),
        P(),
        P(),
        P(),
        P(),
        P(("reg", "lon"), None),
        P("reg", "lon"),
        P(None, "reg", None, None),
        P(),
    )
    out_specs = (P(None, ("reg", "lon"), None), P(None, None, "reg", "lon"))
    return jax.shard_map(shards, mesh=mesh, in_specs=in_specs, out_specs=out_specs, check_vma=False)
```

```python
import functools
import math

import jax
import jax.numpy as jnp
from jax import lax
from jax.experimental import pallas as pl
from jax.experimental.pallas import tpu as pltpu
from jax.sharding import PartitionSpec as P

HEADS = 16
REACH = 2
TAPS = 2 * REACH + 1
SIDE = 8
ROWS = 16
LANES = 128
EARLY = 2
CANDIDATES = 5
F32 = jnp.float32
BF16 = jnp.bfloat16
NT = (((1,), (1,)), ((), ()))

ABOVE = ((-2, (0,)), (-1, (0, 1)))
OWN = ((0, (0, 1)), (1, (0, 1)))
BELOW = ((3, (1,)), (2, (0, 1)))


def blocks_of(band):
    return [
        (out_row, src - out_row + REACH, off)
        for src, out_rows in band
        for off in range(TAPS)
        for out_row in out_rows
    ]


def iota(shape, dim):
    return lax.broadcasted_iota(jnp.int32, shape, dim)


def normalise(rows, gain):
    values = rows.astype(F32)
    center = values - jnp.mean(values, axis=-1, keepdims=True)
    spread = jnp.mean(center * center, axis=-1, keepdims=True)
    return (center * lax.rsqrt(spread + 1e-05) * gain).astype(BF16)


def mix_kernel(blocks, psi_ref, dec_ref, mixed_ref, psi_rows_ref, taps_ref):
    basis, out_ch, channels = dec_ref.shape
    depth = basis * ROWS
    for tap in range(TAPS):
        for off in range(TAPS):
            at = (tap * TAPS + off) * 2
            psi_rows_ref[at : at + 2, :] = psi_ref[tap, off]
    spread = (iota((basis, depth), 1) // ROWS == iota((basis, depth), 0)).astype(F32)
    expanded = jnp.dot(psi_rows_ref[...], spread, preferred_element_type=F32)
    pick = iota((ROWS, depth), 1) % ROWS == iota((ROWS, depth), 0)
    for at, (out_row, tap, off) in enumerate(blocks):
        source = (tap * TAPS + off) * 2 + out_row
        taps = jnp.broadcast_to(expanded[source : source + 1], (ROWS, depth))
        taps_ref[at * ROWS : (at + 1) * ROWS, :] = jnp.where(pick, taps, 0.0).astype(BF16)
    for first in range(0, out_ch, ROWS):
        size = min(ROWS, out_ch - first)
        pieces = []
        for base in range(basis):
            pieces.append(dec_ref[base, first : first + size, :])
            if size < ROWS:
                pieces.append(jnp.zeros((ROWS - size, channels), BF16))
        mixing = jnp.concatenate(pieces, axis=0)
        mixed = jnp.dot(taps_ref[...], mixing, preferred_element_type=F32).astype(BF16)
        mixed_ref[:, first : first + ROWS, :] = mixed.reshape(len(blocks), ROWS, channels)


def listed_blocks(sectors, listed_ref):
    reg_here, lon_here = lax.axis_index("reg"), lax.axis_index("lon")
    toward = 1 - 2 * (reg_here % 2)
    found = []
    for at in range(1, listed_ref.shape[1]):
        block = listed_ref[0, at]
        step_reg = (block // sectors - reg_here) * toward
        step_lon = (block % sectors - lon_here + 1 + sectors) % sectors - 1
        lean = step_lon * (1 - 2 * (lon_here % 2))
        side = jnp.where(lean == 0, 0, jnp.where(lean > 0, 1, 4))
        ahead = jnp.where(lean < 0, 0, 1)
        behind = jnp.where(lean < 0, 7, 4 + side)
        found.append(jnp.where(step_reg == 0, ahead, jnp.where(step_reg > 0, 2 + side, behind)))
    for low in range(len(found)):
        for high in range(low + 1, len(found)):
            less, more = jnp.minimum(found[low], found[high]), jnp.maximum(found[low], found[high])
            found[low], found[high] = less, more
    return found


def gather_kernel(x_hbm, assign_hbm, own_ref, assign_ref, sems):
    rows = own_ref.shape[0] - ROWS
    copies = [
        pltpu.make_async_copy(assign_hbm, assign_ref, sems.at[0]),
        pltpu.make_async_copy(x_hbm, own_ref.at[pl.ds(0, rows)], sems.at[1]),
    ]
    for copy in copies:
        copy.start()
    copies[0].wait()
    local = lax.rem(assign_ref[...], rows).astype(F32)
    line = jnp.concatenate([local[:1], local[1:2]], axis=1)
    line = jnp.broadcast_to(line, (ROWS, line.shape[1]))
    own_ref[rows:] = jnp.where(iota(line.shape, 0) == 0, line, 0.0).astype(BF16)
    copies[1].wait()


def prepare_kernel(
    sectors,
    own_ref, gain_hbm, wqkv_hbm, assign_hbm, listed_hbm,
    query_ref, key_ref, value_ref, wk_ref, wvt_ref, choice_ref, cells_ref,
    gain_ref, wqkv_ref, cell_ref, listed_ref, sems,
):
    copies = [
        pltpu.make_async_copy(source, target, sems.at[at])
        for at, (source, target) in enumerate(
            (
                (gain_hbm, gain_ref),
                (wqkv_hbm, wqkv_ref),
                (assign_hbm, cell_ref),
                (listed_hbm, listed_ref),
            )
        )
    ]
    for copy in copies:
        copy.start()
    rows, width = key_ref.shape
    group, members = query_ref.shape[1], query_ref.shape[2] // rows
    head = group // members
    for copy in copies[2:]:
        copy.wait()
    for at, number in enumerate(listed_blocks(sectors, listed_ref)):
        for candidate in range(CANDIDATES):
            same = jnp.full((ROWS, LANES), jnp.where(number == at + candidate, 1.0, 0.0), F32)
            choice_ref[at, candidate] = same.astype(BF16)
    lat_rows, lon_cols = cell_ref.shape
    place, node = iota((ROWS, rows), 0), iota((ROWS, rows), 1)
    odd = lax.axis_index("lon") % 2
    for side, first in enumerate(((1 - odd) * (lon_cols - REACH), odd * (lon_cols - REACH))):
        hit = jnp.zeros((ROWS, rows), F32)
        for row in range(lat_rows):
            for col in range(REACH):
                cell = cell_ref[row, first + col] % rows
                hit = jnp.where((place == row * REACH + col) & (node == cell), 1.0, hit)
        cells_ref[side * ROWS : (side + 1) * ROWS] = hit.astype(BF16)
    copies[0].wait()
    normed = normalise(own_ref[:rows], gain_ref[...])
    copies[1].wait()
    query = jnp.dot(normed, wqkv_ref[:, :width], preferred_element_type=F32)
    query_t = (query * (math.log2(math.e) / head**0.5)).T.astype(BF16)
    mask = (iota((group, members * rows), 0) // head) == (iota((group, members * rows), 1) // rows)
    for part in range(width // group):
        piece = query_t[part * group : (part + 1) * group]
        wide = jnp.concatenate([piece] * members, axis=1)
        query_ref[part] = jnp.where(mask, wide, jnp.zeros_like(wide))
    wk = wqkv_ref[:, width : 2 * width]
    wk_ref[...] = wk
    key_ref[...] = jnp.dot(normed, wk, preferred_element_type=F32).astype(BF16)
    wvt = wqkv_ref[:, 2 * width :].astype(F32).T.astype(BF16)
    wvt_ref[...] = wvt
    value_ref[...] = lax.dot_general(wvt, normed, NT, preferred_element_type=F32).astype(BF16)


def chosen(entries, rows, choice_ref, candidates):
    tall, wide = rows // ROWS, candidates[-1].shape[1] // LANES
    near = []
    for entry in entries:
        total = None
        for at in range(CANDIDATES):
            weight = jnp.concatenate([choice_ref[entry, at]] * wide, axis=1)
            part = candidates[entry + at] * jnp.concatenate([weight] * tall, axis=0)
            total = part if total is None else total + part
        near.append(total)
    return jnp.concatenate(near, axis=0)


def project(nodes, gain, wk_ref, wvt_ref):
    normed = normalise(nodes, gain)
    keys = jnp.dot(normed, wk_ref[...], preferred_element_type=F32).astype(BF16)
    values = lax.dot_general(wvt_ref[...], normed, NT, preferred_element_type=F32).astype(BF16)
    return keys, values


def early_kernel(
    choice_ref, other_ref, pair_ref, inner_ref, outer_ref,
    gain_ref, wk_ref, wvt_ref, query_ref, key_ref, value_ref,
    top_ref, sum_ref, keys_ref, values_ref,
):
    rows = key_ref.shape[0]
    parts, group, _ = query_ref.shape
    candidates = [other_ref[...], pair_ref[...]]
    candidates += [ref[rows : 2 * rows] if center else ref[:rows] for ref in (inner_ref, outer_ref) for center in (1, 0)]
    nodes = chosen(range(EARLY), rows, choice_ref, candidates)
    keys, values = project(nodes, gain_ref[...], wk_ref, wvt_ref)
    keys_ref[:rows] = key_ref[...]
    keys_ref[rows:] = keys
    for part in range(parts):
        span = slice(part * group, (part + 1) * group)
        values_ref[part, :group, :rows] = value_ref[span]
        values_ref[part, :group, rows:] = values[span]
        values_ref[part, group:, :] = jnp.ones((ROWS, keys_ref.shape[0]), BF16)

    def scored(part):
        span = slice(part * group, (part + 1) * group)
        return jnp.dot(keys_ref[:, span], query_ref[part], preferred_element_type=F32)

    scores = scored(0)
    for part in range(parts):
        now = scores
        if part + 1 < parts:
            scores = scored(part + 1)
        top = jnp.max(now, axis=0, keepdims=True)
        expo = jnp.exp2(now - top).astype(BF16)
        top_ref[part] = jnp.broadcast_to(top, top_ref.shape[1:])
        sum_ref[part] = jnp.dot(values_ref[part], expo, preferred_element_type=F32)


def late_kernel(
    choice_ref, cells_ref, inner_ref, outer_ref, beside_ref, corner_ref,
    own_ref, gain_ref, wk_ref, wvt_ref, query_ref, top_ref, sum_ref, wout_ref, wlat_ref,
    state_ref, latent_ref, to_pair_ref, to_other_ref,
    attended_ref,
):
    rows, width = state_ref.shape
    parts, group, lanes = query_ref.shape
    members = lanes // rows
    head = group // members
    candidates = [None, None]
    candidates += [ref[rows : 2 * rows] if center else ref[:rows] for ref in (inner_ref, outer_ref) for center in (1, 0)]
    candidates += [beside_ref[...], corner_ref[...]]
    nodes = chosen(range(EARLY, choice_ref.shape[0]), rows, choice_ref, candidates)
    keys, values = project(nodes, gain_ref[...], wk_ref, wvt_ref)
    ones = jnp.ones((ROWS, nodes.shape[0]), BF16)
    owner = iota((group, rows), 0) // head

    def scored(part):
        span = slice(part * group, (part + 1) * group)
        return jnp.dot(keys[:, span], query_ref[part], preferred_element_type=F32)

    scores = scored(0)
    for part in range(parts):
        now = scores
        if part + 1 < parts:
            scores = scored(part + 1)
        before = top_ref[part, :1]
        top = jnp.maximum(before, jnp.max(now, axis=0, keepdims=True))
        expo = jnp.exp2(now - top).astype(BF16)
        weights = jnp.concatenate([values[part * group : (part + 1) * group], ones], axis=0)
        summed = jnp.dot(weights, expo, preferred_element_type=F32)
        summed = summed + sum_ref[part] * jnp.exp2(before - top)
        summed = summed[:group] * (1.0 / summed[group : group + 1])
        merged = None
        for member in range(members):
            piece = summed[:, member * rows : (member + 1) * rows]
            merged = piece if merged is None else jnp.where(owner == member, piece, merged)
        attended_ref[:, part * group : (part + 1) * group] = merged.T.astype(BF16)
    state = (
        own_ref[:rows].astype(F32)
        + jnp.dot(attended_ref[...], wout_ref[...], preferred_element_type=F32)
    ).astype(BF16)
    state_ref[...] = state
    value = jnp.dot(state, wlat_ref[...], preferred_element_type=F32)
    latent = (value / (1.0 + jnp.exp(-value))).astype(BF16)
    latent_ref[...] = latent
    cells = jnp.dot(cells_ref[...], latent, preferred_element_type=F32).astype(BF16)
    to_pair_ref[...] = cells[:ROWS]
    to_other_ref[...] = cells[ROWS:]


def hot_rows(values, rows, cols, line):
    odd = lax.axis_index("lon") % 2
    column = iota((8, cols), 1)
    node = iota((rows + 2 * SIDE, cols), 0).astype(F32)
    for off in range(TAPS):
        step = off - REACH
        where = jnp.broadcast_to(values, (8, cols))
        if step:
            where = pltpu.roll(where, (-step) % cols, 1)
        reach = column + step
        before = (rows + (1 - odd) * SIDE + REACH * line + reach + REACH).astype(F32)
        after = (rows + odd * SIDE + REACH * line + reach - cols).astype(F32)
        where = jnp.where(reach < 0, before, jnp.where(reach >= cols, after, where))
        yield jnp.where(node == where[:1], 1.0, 0.0).astype(BF16)


def shares_of(latent, weights):
    blocks, outputs, channels = weights.shape
    shares = lax.dot_general(
        weights.reshape(blocks * outputs, channels), latent, NT, preferred_element_type=F32
    ).astype(BF16)
    return [shares[at * outputs : (at + 1) * outputs] for at in range(blocks)]


def lines_of(line_ref, start, cols):
    values = line_ref[start : start + ROWS, :].astype(F32)
    return values[:1, :cols], values[:1, cols:]


def own_kernel(
    begin, state_ref, own_ref, inner_ref, outer_ref, latent_ref, weights_ref,
    out_ref, hot_ref, kept_ref,
):
    kept_ref[...] = state_ref[...]
    cols = out_ref.shape[2]
    rows = latent_ref.shape[0] - 2 * SIDE
    own = lines_of(own_ref, begin[0], cols)
    table = [list(hot_rows(own[line], rows, cols, line)) for line in range(2)]
    acc = [None, None]
    for (out_row, tap, off), share in zip(
        blocks_of(OWN), shares_of(latent_ref[...], weights_ref[...])
    ):
        line = out_row + tap - REACH
        piece = jnp.dot(share, table[line][off], preferred_element_type=F32)
        acc[out_row] = piece if acc[out_row] is None else acc[out_row] + piece
    for row in range(2):
        out_ref[row] = acc[row]
    odd = lax.axis_index("reg") % 2 == 1
    inner, outer = lines_of(inner_ref, begin[1], cols), lines_of(outer_ref, begin[2], cols)
    nodes = rows + 2 * SIDE
    for band, (yes, no) in enumerate(((inner, outer), (outer, inner))):
        for at, line in enumerate((0, 1) if band == 0 else (1, 0)):
            values = jnp.where(odd, yes[line], no[line])
            for off, hot in enumerate(hot_rows(values, rows, cols, line)):
                hot_ref[band, at, off, :nodes] = hot
                hot_ref[band, at, off, nodes:] = jnp.zeros((hot_ref.shape[3] - nodes, cols), BF16)


def band_kernel(from_inner, latent_ref, weights_ref, hot_ref, partial_ref, out_ref, one_ref, two_ref):
    odd = lax.axis_index("reg") % 2
    band = 1 - odd if from_inner else odd
    latent = latent_ref[...]
    lanes, cols = hot_ref.shape[3:]
    outputs = weights_ref.shape[1]
    blank = jnp.zeros((lanes - latent.shape[0], latent.shape[1]), BF16)
    blocks = len(blocks_of(ABOVE))
    weights = weights_ref[pl.ds(band * blocks, blocks)]
    shares = shares_of(jnp.concatenate([latent, blank], axis=0), weights)
    for off in range(TAPS):
        span = slice(off * lanes, (off + 1) * lanes)
        one_ref[:, span] = shares[off]
        for row in range(2):
            two_ref[row * outputs : (row + 1) * outputs, span] = shares[TAPS + 2 * off + row]
    depth = TAPS * lanes
    one = jnp.dot(one_ref[...], hot_ref[band, 0].reshape(depth, cols), preferred_element_type=F32)
    two = jnp.dot(two_ref[...], hot_ref[band, 1].reshape(depth, cols), preferred_element_type=F32)
    for row in range(2):
        total = partial_ref[row] + two[row * outputs : (row + 1) * outputs]
        total = total + jnp.where(band == row, one, 0.0)
        if from_inner:
            out_ref[row] = total
        else:
            out_ref[:, row, :] = total[: out_ref.shape[0]].astype(BF16)


def whole(memory=pltpu.VMEM):
    return pl.BlockSpec(memory_space=memory)


def struct(*shape, dtype=BF16):
    return jax.ShapeDtypeStruct(shape, dtype)


def params(limit):
    return pltpu.CompilerParams(vmem_limit_bytes=limit << 20)


def cost(flops, moved):
    return pl.CostEstimate(flops=int(flops), bytes_accessed=int(moved), transcendentals=0)


def shards(nodes, norm_gain, w_qkv, w_out, w_latent, neighbours, assignment, psi, w_dec):
    _, rows, width = nodes.shape
    channels = w_latent.shape[1]
    lat_rows, lon_cols = assignment.shape
    basis, _, out_ch = w_dec.shape
    sectors = lax.axis_size("lon")
    count = neighbours.shape[1]
    x = nodes.reshape(rows, width)
    gain = norm_gain.reshape(1, width)

    def paired(array, first):
        pairs = [(i, (i + 1) % sectors) for i in range(first, sectors, 2)]
        return lax.ppermute(array, "lon", pairs + [(j, i) for i, j in pairs])

    def exchanged(array, first):
        size = lax.axis_size("reg")
        pairs = [(i, i + 1) for i in range(first, size - 1, 2)]
        return lax.ppermute(array, "reg", pairs + [(j, i) for i, j in pairs])

    def in_hbm(*arrays):
        return [pltpu.with_memory_space_constraint(array, pltpu.HBM) for array in arrays]

    other = paired(x, 1)
    pair = paired(x, 0)

    outputs = -(-out_ch // ROWS) * ROWS
    head = width // HEADS
    members = LANES // head
    parts = HEADS // members
    def mixed(blocks, name, after):
        taps = psi.transpose(2, 3, 1, 0)
        mixing = w_dec.transpose(0, 2, 1)
        taps, mixing, after = lax.optimization_barrier((taps, mixing, after))
        weights = pl.pallas_call(
            functools.partial(mix_kernel, blocks),
            in_specs=[whole()] * 2,
            out_specs=whole(),
            out_shape=struct(len(blocks), outputs, channels),
            scratch_shapes=[
                pltpu.VMEM((2 * TAPS * TAPS, basis), F32),
                pltpu.VMEM((len(blocks) * ROWS, basis * ROWS), BF16),
            ],
            compiler_params=params(32),
            cost_estimate=cost(2e9, 6e6),
            name=name,
        )(taps, mixing)
        return weights, after

    own = pl.pallas_call(
        gather_kernel,
        in_specs=[whole(pltpu.HBM)] * 2,
        out_specs=whole(),
        out_shape=struct(rows + ROWS, width),
        scratch_shapes=[
            pltpu.VMEM(assignment.shape, jnp.int32),
            pltpu.SemaphoreType.DMA((2,)),
        ],
        compiler_params=params(32),
        cost_estimate=cost(1e3, 1e3),
        name="gather",
    )(*in_hbm(x, assignment))
    query, key, value, wk, wvt, choice, cells = pl.pallas_call(
        functools.partial(prepare_kernel, sectors),
        in_specs=[whole()] + [whole(pltpu.HBM)] * 4,
        out_specs=[whole()] * 7,
        out_shape=[
            struct(parts, LANES, members * rows),
            struct(rows, width),
            struct(width, rows),
            struct(width, width),
            struct(width, width),
            struct(count - 1, CANDIDATES, ROWS, LANES),
            struct(2 * ROWS, rows),
        ],
        scratch_shapes=[
            pltpu.VMEM((1, width), F32),
            pltpu.VMEM(w_qkv.shape, BF16),
            pltpu.SMEM(assignment.shape, jnp.int32),
            pltpu.SMEM(neighbours.shape, jnp.int32),
            pltpu.SemaphoreType.DMA((4,)),
        ],
        compiler_params=params(32),
        cost_estimate=cost(5e8, 1e6),
        name="prepare",
    )(own, *in_hbm(gain, w_qkv, assignment, neighbours))
    own, query = lax.optimization_barrier((own, query))
    message = jnp.concatenate([pair, own], axis=0)
    message_a = message
    other_a = other
    inner = exchanged(message_a, 0)
    outer = exchanged(message, 1)
    corner = exchanged(other, 1)
    beside = exchanged(other_a, 0)

    edges, other_m = mixed(blocks_of(ABOVE) + blocks_of(BELOW), "mix_edges", other)
    inner, edges = lax.optimization_barrier((inner, edges))
    top, summed = pl.pallas_call(
        early_kernel,
        in_specs=[whole()] * 11,
        out_specs=[whole()] * 2,
        out_shape=[
            struct(parts, 8, members * rows, dtype=F32),
            struct(parts, LANES + ROWS, members * rows, dtype=F32),
        ],
        scratch_shapes=[
            pltpu.VMEM(((1 + EARLY) * rows, width), BF16),
            pltpu.VMEM((parts, LANES + ROWS, (1 + EARLY) * rows), BF16),
        ],
        compiler_params=params(32),
        cost_estimate=cost(3e9, 6e6),
        name="early",
    )(choice, other, pair, inner, outer, gain, wk, wvt, query, key, value)
    state, latent, to_pair, to_other = pl.pallas_call(
        late_kernel,
        in_specs=[whole()] * 15,
        out_specs=[whole()] * 4,
        out_shape=[pltpu.VMEM((rows, width), BF16), struct(rows, channels)]
        + [struct(ROWS, channels)] * 2,
        scratch_shapes=[pltpu.VMEM((rows, width), BF16)],
        compiler_params=params(32),
        cost_estimate=cost(3e9, 6e6),
        name="late",
    )(
        choice, cells, inner, outer, beside, corner,
        own, gain, wk, wvt, query, top, summed, w_out, w_latent,
    )

    from_pair = paired(to_pair, 0)
    from_other = paired(to_other, 1)
    middle, latent = mixed(blocks_of(OWN), "mix_own", latent)
    from_pair, middle = lax.optimization_barrier((from_pair, middle))
    extended = jnp.concatenate([latent, from_pair[:SIDE], from_other[:SIDE]], axis=0)
    far = exchanged(extended, 1)
    near = exchanged(extended, 0)

    lanes = -(-(rows + 2 * SIDE) // 256) * 256
    partial, hots, state = pl.pallas_call(
        functools.partial(own_kernel, (rows, 2 * rows, 2 * rows)),
        in_specs=[whole()] * 6,
        out_specs=[whole()] * 3,
        out_shape=[
            struct(lat_rows, outputs, lon_cols, dtype=F32),
            struct(2, 2, TAPS, lanes, lon_cols),
            struct(rows, width),
        ],
        compiler_params=params(32),
        cost_estimate=cost(1e9, 2.5e6),
        name="own_band",
    )(state, own, inner, outer, extended, middle)
    band_scratch = [
        pltpu.VMEM((outputs, TAPS * lanes), BF16),
        pltpu.VMEM((2 * outputs, TAPS * lanes), BF16),
    ]
    partial = pl.pallas_call(
        functools.partial(band_kernel, True),
        in_specs=[whole()] * 4,
        out_specs=whole(),
        out_shape=struct(lat_rows, outputs, lon_cols, dtype=F32),
        scratch_shapes=band_scratch,
        compiler_params=params(32),
        cost_estimate=cost(1e9, 2.5e6),
        name="inner_band",
    )(near, edges, hots, partial)
    fields = pl.pallas_call(
        functools.partial(band_kernel, False),
        in_specs=[whole()] * 4,
        out_specs=whole(),
        out_shape=struct(out_ch, lat_rows, lon_cols),
        scratch_shapes=band_scratch,
        compiler_params=params(32),
        cost_estimate=cost(1e9, 2.5e6),
        name="outer_band",
    )(far, edges, hots, partial)
    return (state.reshape(1, rows, width), fields.reshape(1, out_ch, lat_rows, lon_cols))


def solution(mesh):
    in_specs = (
        P(None, ("reg", "lon"), None),
        P(),
        P(),
        P(),
        P(),
        P(("reg", "lon"), None),
        P("reg", "lon"),
        P(None, "reg", None, None),
        P(),
    )
    out_specs = (P(None, ("reg", "lon"), None), P(None, None, "reg", "lon"))
    return jax.shard_map(shards, mesh=mesh, in_specs=in_specs, out_specs=out_specs, check_vma=False)
```

```python
import functools
import math

import jax
import jax.numpy as jnp
from jax import lax
from jax.experimental import pallas as pl
from jax.experimental.pallas import tpu as pltpu
from jax.sharding import PartitionSpec as P

HEADS = 16
REACH = 2
TAPS = 2 * REACH + 1
SIDE = 8
ROWS = 16
LANES = 128
EARLY = 1
CANDIDATES = 5
F32 = jnp.float32
BF16 = jnp.bfloat16
NT = (((1,), (1,)), ((), ()))

ABOVE = ((-2, (0,)), (-1, (0, 1)))
OWN = ((0, (0, 1)), (1, (0, 1)))
BELOW = ((3, (1,)), (2, (0, 1)))


def blocks_of(band):
    return [
        (out_row, src - out_row + REACH, off)
        for src, out_rows in band
        for off in range(TAPS)
        for out_row in out_rows
    ]


def iota(shape, dim):
    return lax.broadcasted_iota(jnp.int32, shape, dim)


def normalise(rows, gain):
    values = rows.astype(F32)
    center = values - jnp.mean(values, axis=-1, keepdims=True)
    spread = jnp.mean(center * center, axis=-1, keepdims=True)
    return (center * lax.rsqrt(spread + 1e-05) * gain).astype(BF16)


def mix_kernel(blocks, psi_ref, dec_ref, mixed_ref, psi_rows_ref, taps_ref):
    basis, out_ch, channels = dec_ref.shape
    depth = basis * ROWS
    for tap in range(TAPS):
        for off in range(TAPS):
            at = (tap * TAPS + off) * 2
            psi_rows_ref[at : at + 2, :] = psi_ref[tap, off]
    spread = (iota((basis, depth), 1) // ROWS == iota((basis, depth), 0)).astype(F32)
    expanded = jnp.dot(psi_rows_ref[...], spread, preferred_element_type=F32)
    pick = iota((ROWS, depth), 1) % ROWS == iota((ROWS, depth), 0)
    for at, (out_row, tap, off) in enumerate(blocks):
        source = (tap * TAPS + off) * 2 + out_row
        taps = jnp.broadcast_to(expanded[source : source + 1], (ROWS, depth))
        taps_ref[at * ROWS : (at + 1) * ROWS, :] = jnp.where(pick, taps, 0.0).astype(BF16)
    for first in range(0, out_ch, ROWS):
        size = min(ROWS, out_ch - first)
        pieces = []
        for base in range(basis):
            pieces.append(dec_ref[base, first : first + size, :])
            if size < ROWS:
                pieces.append(jnp.zeros((ROWS - size, channels), BF16))
        mixing = jnp.concatenate(pieces, axis=0)
        mixed = jnp.dot(taps_ref[...], mixing, preferred_element_type=F32).astype(BF16)
        mixed_ref[:, first : first + ROWS, :] = mixed.reshape(len(blocks), ROWS, channels)


def listed_blocks(sectors, listed_ref):
    reg_here, lon_here = lax.axis_index("reg"), lax.axis_index("lon")
    toward = 1 - 2 * (reg_here % 2)
    found = []
    for at in range(1, listed_ref.shape[1]):
        block = listed_ref[0, at]
        step_reg = (block // sectors - reg_here) * toward
        step_lon = (block % sectors - lon_here + 1 + sectors) % sectors - 1
        lean = step_lon * (1 - 2 * (lon_here % 2))
        place = jnp.where(lean == 0, 0, jnp.where(lean > 0, 1, 2))
        ahead = jnp.where(lean < 0, 0, 1)
        found.append(jnp.where(step_reg == 0, ahead, jnp.where(step_reg > 0, 2, 5) + jnp.where(step_reg == 0, 0, place)))
    for low in range(len(found)):
        for high in range(low + 1, len(found)):
            less, more = jnp.minimum(found[low], found[high]), jnp.maximum(found[low], found[high])
            found[low], found[high] = less, more
    return found


def gather_kernel(x_hbm, assign_hbm, own_ref, assign_ref, sems):
    rows = own_ref.shape[0] - ROWS
    copies = [
        pltpu.make_async_copy(assign_hbm, assign_ref, sems.at[0]),
        pltpu.make_async_copy(x_hbm, own_ref.at[pl.ds(0, rows)], sems.at[1]),
    ]
    for copy in copies:
        copy.start()
    copies[0].wait()
    local = lax.rem(assign_ref[...], rows).astype(F32)
    line = jnp.concatenate([local[:1], local[1:2]], axis=1)
    line = jnp.broadcast_to(line, (ROWS, line.shape[1]))
    own_ref[rows:] = jnp.where(iota(line.shape, 0) == 0, line, 0.0).astype(BF16)
    copies[1].wait()


def prepare_kernel(
    sectors,
    own_ref, gain_hbm, wqkv_hbm, assign_hbm, listed_hbm,
    query_ref, key_ref, value_ref, wk_ref, wvt_ref, choice_ref, cells_ref,
    gain_ref, wqkv_ref, cell_ref, listed_ref, sems,
):
    copies = [
        pltpu.make_async_copy(source, target, sems.at[at])
        for at, (source, target) in enumerate(
            (
                (gain_hbm, gain_ref),
                (wqkv_hbm, wqkv_ref),
                (assign_hbm, cell_ref),
                (listed_hbm, listed_ref),
            )
        )
    ]
    for copy in copies:
        copy.start()
    rows, width = key_ref.shape
    group, members = query_ref.shape[1], query_ref.shape[2] // rows
    head = group // members
    for copy in copies[2:]:
        copy.wait()
    for at, number in enumerate(listed_blocks(sectors, listed_ref)):
        for candidate in range(CANDIDATES):
            same = jnp.full((ROWS, LANES), jnp.where(number == at + candidate, 1.0, 0.0), F32)
            choice_ref[at, candidate] = same.astype(BF16)
    lat_rows, lon_cols = cell_ref.shape
    place, node = iota((ROWS, rows), 0), iota((ROWS, rows), 1)
    odd = lax.axis_index("lon") % 2
    for side, first in enumerate(((1 - odd) * (lon_cols - REACH), odd * (lon_cols - REACH))):
        hit = jnp.zeros((ROWS, rows), F32)
        for row in range(lat_rows):
            for col in range(REACH):
                cell = cell_ref[row, first + col] % rows
                hit = jnp.where((place == row * REACH + col) & (node == cell), 1.0, hit)
        cells_ref[side * ROWS : (side + 1) * ROWS] = hit.astype(BF16)
    copies[0].wait()
    normed = normalise(own_ref[:rows], gain_ref[...])
    copies[1].wait()
    query = jnp.dot(normed, wqkv_ref[:, :width], preferred_element_type=F32)
    query_t = (query * (math.log2(math.e) / head**0.5)).T.astype(BF16)
    mask = (iota((group, members * rows), 0) // head) == (iota((group, members * rows), 1) // rows)
    for part in range(width // group):
        piece = query_t[part * group : (part + 1) * group]
        wide = jnp.concatenate([piece] * members, axis=1)
        query_ref[part] = jnp.where(mask, wide, jnp.zeros_like(wide))
    wk = wqkv_ref[:, width : 2 * width]
    wk_ref[...] = wk
    key_ref[...] = jnp.dot(normed, wk, preferred_element_type=F32).astype(BF16)
    wvt = wqkv_ref[:, 2 * width :].astype(F32).T.astype(BF16)
    wvt_ref[...] = wvt
    value_ref[...] = lax.dot_general(wvt, normed, NT, preferred_element_type=F32).astype(BF16)


def chosen(entries, rows, choice_ref, candidates):
    tall, wide = rows // ROWS, candidates[-1].shape[1] // LANES
    near = []
    for entry in entries:
        total = None
        for at in range(CANDIDATES):
            weight = jnp.concatenate([choice_ref[entry, at]] * wide, axis=1)
            part = candidates[entry + at] * jnp.concatenate([weight] * tall, axis=0)
            total = part if total is None else total + part
        near.append(total)
    return jnp.concatenate(near, axis=0)


def project(nodes, gain, wk_ref, wvt_ref):
    normed = normalise(nodes, gain)
    keys = jnp.dot(normed, wk_ref[...], preferred_element_type=F32).astype(BF16)
    values = lax.dot_general(wvt_ref[...], normed, NT, preferred_element_type=F32).astype(BF16)
    return keys, values


def own_heads(summed, rows):
    members = summed.shape[1] // rows
    head = summed.shape[0] // members
    return [
        summed[at * head : (at + 1) * head, at * rows : (at + 1) * rows] for at in range(members)
    ]


def early_kernel(
    choice_ref, other_ref, pair_ref, inner_ref, beside_ref,
    gain_ref, wk_ref, wvt_ref, query_ref, key_ref, value_ref,
    top_ref, sum_ref, keys_ref, values_ref,
):
    rows = key_ref.shape[0]
    parts, group, _ = query_ref.shape
    candidates = [other_ref[...], pair_ref[...]]
    candidates += [inner_ref[rows : 2 * rows], inner_ref[:rows], beside_ref[...]]
    nodes = chosen(range(EARLY), rows, choice_ref, candidates)
    keys, values = project(nodes, gain_ref[...], wk_ref, wvt_ref)
    keys_ref[:rows] = key_ref[...]
    keys_ref[rows:] = keys
    for part in range(parts):
        span = slice(part * group, (part + 1) * group)
        values_ref[part, :group, :rows] = value_ref[span]
        values_ref[part, :group, rows:] = values[span]
        values_ref[part, group:, :] = jnp.ones((ROWS, keys_ref.shape[0]), BF16)

    def scored(part):
        span = slice(part * group, (part + 1) * group)
        return jnp.dot(keys_ref[:, span], query_ref[part], preferred_element_type=F32)

    scores = scored(0)
    for part in range(parts):
        now = scores
        if part + 1 < parts:
            scores = scored(part + 1)
        top = jnp.max(now, axis=0, keepdims=True)
        expo = jnp.exp2(now - top).astype(BF16)
        summed = jnp.dot(values_ref[part], expo, preferred_element_type=F32)
        top_ref[part, 0] = jnp.broadcast_to(top, top_ref.shape[2:])
        top_ref[part, 1] = jnp.broadcast_to(summed[group : group + 1], top_ref.shape[2:])
        sum_ref[part] = jnp.concatenate(own_heads(summed[:group], rows), axis=0)


def late_kernel(
    choice_ref, cells_ref, pair_ref, inner_ref, beside_ref, outer_ref, corner_ref,
    own_ref, gain_ref, wk_ref, wvt_ref, query_ref, top_ref, sum_ref, wout_ref, wlat_ref,
    state_ref, latent_ref, to_pair_ref, to_other_ref,
    attended_ref,
):
    rows, width = state_ref.shape
    parts, group, lanes = query_ref.shape
    members = lanes // rows
    head = group // members
    candidates = [None, pair_ref[...], inner_ref[rows : 2 * rows], inner_ref[:rows], beside_ref[...]]
    candidates += [outer_ref[rows : 2 * rows], outer_ref[:rows], corner_ref[...]]
    nodes = chosen(range(EARLY, choice_ref.shape[0]), rows, choice_ref, candidates)
    keys, values = project(nodes, gain_ref[...], wk_ref, wvt_ref)
    ones = jnp.ones((ROWS, nodes.shape[0]), BF16)

    def scored(part):
        span = slice(part * group, (part + 1) * group)
        return jnp.dot(keys[:, span], query_ref[part], preferred_element_type=F32)

    scores = scored(0)
    for part in range(parts):
        now = scores
        if part + 1 < parts:
            scores = scored(part + 1)
        before = top_ref[part, 0, :1]
        top = jnp.maximum(before, jnp.max(now, axis=0, keepdims=True))
        expo = jnp.exp2(now - top).astype(BF16)
        weights = jnp.concatenate([values[part * group : (part + 1) * group], ones], axis=0)
        summed = jnp.dot(weights, expo, preferred_element_type=F32)
        shrink = jnp.exp2(before - top)
        share = 1.0 / (summed[group : group + 1] + top_ref[part, 1, :1] * shrink)
        merged = []
        for member, piece in enumerate(own_heads(summed[:group], rows)):
            span = slice(member * rows, (member + 1) * rows)
            earlier = sum_ref[part, member * head : (member + 1) * head]
            merged.append((piece + earlier * shrink[:, span]) * share[:, span])
        merged = jnp.concatenate(merged, axis=0)
        attended_ref[:, part * group : (part + 1) * group] = merged.T.astype(BF16)
    state = (
        own_ref[:rows].astype(F32)
        + jnp.dot(attended_ref[...], wout_ref[...], preferred_element_type=F32)
    ).astype(BF16)
    state_ref[...] = state
    value = jnp.dot(state, wlat_ref[...], preferred_element_type=F32)
    latent = (value / (1.0 + jnp.exp(-value))).astype(BF16)
    latent_ref[...] = latent
    cells = jnp.dot(cells_ref[...], latent, preferred_element_type=F32).astype(BF16)
    to_pair_ref[...] = cells[:ROWS]
    to_other_ref[...] = cells[ROWS:]


def hot_rows(values, rows, cols, line):
    odd = lax.axis_index("lon") % 2
    column = iota((8, cols), 1)
    node = iota((rows + 2 * SIDE, cols), 0).astype(F32)
    for off in range(TAPS):
        step = off - REACH
        where = jnp.broadcast_to(values, (8, cols))
        if step:
            where = pltpu.roll(where, (-step) % cols, 1)
        reach = column + step
        before = (rows + (1 - odd) * SIDE + REACH * line + reach + REACH).astype(F32)
        after = (rows + odd * SIDE + REACH * line + reach - cols).astype(F32)
        where = jnp.where(reach < 0, before, jnp.where(reach >= cols, after, where))
        yield jnp.where(node == where[:1], 1.0, 0.0).astype(BF16)


def shares_of(latent, weights):
    blocks, outputs, channels = weights.shape
    shares = lax.dot_general(
        weights.reshape(blocks * outputs, channels), latent, NT, preferred_element_type=F32
    ).astype(BF16)
    return [shares[at * outputs : (at + 1) * outputs] for at in range(blocks)]


def lines_of(line_ref, start, cols):
    values = line_ref[start : start + ROWS, :].astype(F32)
    return values[:1, :cols], values[:1, cols:]


def own_kernel(
    begin, state_ref, own_ref, inner_ref, outer_ref, latent_ref, weights_ref,
    out_ref, hot_ref, kept_ref,
):
    kept_ref[...] = state_ref[...]
    cols = out_ref.shape[2]
    rows = latent_ref.shape[0] - 2 * SIDE
    own = lines_of(own_ref, begin[0], cols)
    table = [list(hot_rows(own[line], rows, cols, line)) for line in range(2)]
    acc = [None, None]
    for (out_row, tap, off), share in zip(
        blocks_of(OWN), shares_of(latent_ref[...], weights_ref[...])
    ):
        line = out_row + tap - REACH
        piece = jnp.dot(share, table[line][off], preferred_element_type=F32)
        acc[out_row] = piece if acc[out_row] is None else acc[out_row] + piece
    for row in range(2):
        out_ref[row] = acc[row]
    odd = lax.axis_index("reg") % 2 == 1
    inner, outer = lines_of(inner_ref, begin[1], cols), lines_of(outer_ref, begin[2], cols)
    nodes = rows + 2 * SIDE
    for band, (yes, no) in enumerate(((inner, outer), (outer, inner))):
        for at, line in enumerate((0, 1) if band == 0 else (1, 0)):
            values = jnp.where(odd, yes[line], no[line])
            for off, hot in enumerate(hot_rows(values, rows, cols, line)):
                hot_ref[band, at, off, :nodes] = hot
                hot_ref[band, at, off, nodes:] = jnp.zeros((hot_ref.shape[3] - nodes, cols), BF16)


def band_kernel(from_inner, latent_ref, weights_ref, hot_ref, partial_ref, out_ref, one_ref, two_ref):
    odd = lax.axis_index("reg") % 2
    band = 1 - odd if from_inner else odd
    latent = latent_ref[...]
    lanes, cols = hot_ref.shape[3:]
    outputs = weights_ref.shape[1]
    blank = jnp.zeros((lanes - latent.shape[0], latent.shape[1]), BF16)
    blocks = len(blocks_of(ABOVE))
    weights = weights_ref[pl.ds(band * blocks, blocks)]
    shares = shares_of(jnp.concatenate([latent, blank], axis=0), weights)
    for off in range(TAPS):
        span = slice(off * lanes, (off + 1) * lanes)
        one_ref[:, span] = shares[off]
        for row in range(2):
            two_ref[row * outputs : (row + 1) * outputs, span] = shares[TAPS + 2 * off + row]
    depth = TAPS * lanes
    one = jnp.dot(one_ref[...], hot_ref[band, 0].reshape(depth, cols), preferred_element_type=F32)
    two = jnp.dot(two_ref[...], hot_ref[band, 1].reshape(depth, cols), preferred_element_type=F32)
    for row in range(2):
        total = partial_ref[row] + two[row * outputs : (row + 1) * outputs]
        total = total + jnp.where(band == row, one, 0.0)
        if from_inner:
            out_ref[row] = total
        else:
            out_ref[:, row, :] = total[: out_ref.shape[0]].astype(BF16)


def whole(memory=pltpu.VMEM):
    return pl.BlockSpec(memory_space=memory)


def struct(*shape, dtype=BF16):
    return jax.ShapeDtypeStruct(shape, dtype)


def params(limit):
    return pltpu.CompilerParams(vmem_limit_bytes=limit << 20)


def cost(flops, moved):
    return pl.CostEstimate(flops=int(flops), bytes_accessed=int(moved), transcendentals=0)


def shards(nodes, norm_gain, w_qkv, w_out, w_latent, neighbours, assignment, psi, w_dec):
    _, rows, width = nodes.shape
    channels = w_latent.shape[1]
    lat_rows, lon_cols = assignment.shape
    basis, _, out_ch = w_dec.shape
    sectors = lax.axis_size("lon")
    count = neighbours.shape[1]
    x = nodes.reshape(rows, width)
    gain = norm_gain.reshape(1, width)

    def paired(array, first):
        pairs = [(i, (i + 1) % sectors) for i in range(first, sectors, 2)]
        return lax.ppermute(array, "lon", pairs + [(j, i) for i, j in pairs])

    def exchanged(array, first):
        size = lax.axis_size("reg")
        pairs = [(i, i + 1) for i in range(first, size - 1, 2)]
        return lax.ppermute(array, "reg", pairs + [(j, i) for i, j in pairs])

    def in_hbm(*arrays):
        return [pltpu.with_memory_space_constraint(array, pltpu.HBM) for array in arrays]

    other = paired(x, 1)
    pair = paired(x, 0)

    outputs = -(-out_ch // ROWS) * ROWS
    head = width // HEADS
    members = LANES // head
    parts = HEADS // members
    def mixed(blocks, name, after):
        taps = psi.transpose(2, 3, 1, 0)
        mixing = w_dec.transpose(0, 2, 1)
        taps, mixing, after = lax.optimization_barrier((taps, mixing, after))
        weights = pl.pallas_call(
            functools.partial(mix_kernel, blocks),
            in_specs=[whole()] * 2,
            out_specs=whole(),
            out_shape=struct(len(blocks), outputs, channels),
            scratch_shapes=[
                pltpu.VMEM((2 * TAPS * TAPS, basis), F32),
                pltpu.VMEM((len(blocks) * ROWS, basis * ROWS), BF16),
            ],
            compiler_params=params(32),
            cost_estimate=cost(2e9, 6e6),
            name=name,
        )(taps, mixing)
        return weights, after

    own = pl.pallas_call(
        gather_kernel,
        in_specs=[whole(pltpu.HBM)] * 2,
        out_specs=whole(),
        out_shape=struct(rows + ROWS, width),
        scratch_shapes=[
            pltpu.VMEM(assignment.shape, jnp.int32),
            pltpu.SemaphoreType.DMA((2,)),
        ],
        compiler_params=params(32),
        cost_estimate=cost(1e3, 1e3),
        name="gather",
    )(*in_hbm(x, assignment))
    query, key, value, wk, wvt, choice, cells = pl.pallas_call(
        functools.partial(prepare_kernel, sectors),
        in_specs=[whole()] + [whole(pltpu.HBM)] * 4,
        out_specs=[whole()] * 7,
        out_shape=[
            struct(parts, LANES, members * rows),
            struct(rows, width),
            struct(width, rows),
            struct(width, width),
            struct(width, width),
            struct(count - 1, CANDIDATES, ROWS, LANES),
            struct(2 * ROWS, rows),
        ],
        scratch_shapes=[
            pltpu.VMEM((1, width), F32),
            pltpu.VMEM(w_qkv.shape, BF16),
            pltpu.SMEM(assignment.shape, jnp.int32),
            pltpu.SMEM(neighbours.shape, jnp.int32),
            pltpu.SemaphoreType.DMA((4,)),
        ],
        compiler_params=params(32),
        cost_estimate=cost(5e8, 1e6),
        name="prepare",
    )(own, *in_hbm(gain, w_qkv, assignment, neighbours))
    own, query = lax.optimization_barrier((own, query))
    message = jnp.concatenate([pair, own], axis=0)
    message_a = message
    other_a = other
    inner = exchanged(message_a, 0)
    outer = exchanged(message, 1)
    corner = exchanged(other, 1)
    beside = exchanged(other_a, 0)

    edges, other_m = mixed(blocks_of(ABOVE) + blocks_of(BELOW), "mix_edges", other)
    inner, edges = lax.optimization_barrier((inner, edges))
    top, summed = pl.pallas_call(
        early_kernel,
        in_specs=[whole()] * 11,
        out_specs=[whole()] * 2,
        out_shape=[
            struct(parts, 2, 8, members * rows, dtype=F32),
            struct(parts, LANES, rows, dtype=F32),
        ],
        scratch_shapes=[
            pltpu.VMEM(((1 + EARLY) * rows, width), BF16),
            pltpu.VMEM((parts, LANES + ROWS, (1 + EARLY) * rows), BF16),
        ],
        compiler_params=params(32),
        cost_estimate=cost(3e9, 6e6),
        name="early",
    )(choice, other, pair, inner, beside, gain, wk, wvt, query, key, value)
    state, latent, to_pair, to_other = pl.pallas_call(
        late_kernel,
        in_specs=[whole()] * 16,
        out_specs=[whole()] * 4,
        out_shape=[pltpu.VMEM((rows, width), BF16), struct(rows, channels)]
        + [struct(ROWS, channels)] * 2,
        scratch_shapes=[pltpu.VMEM((rows, width), BF16)],
        compiler_params=params(32),
        cost_estimate=cost(3e9, 6e6),
        name="late",
    )(
        choice, cells, pair, inner, beside, outer, corner,
        own, gain, wk, wvt, query, top, summed, w_out, w_latent,
    )

    from_pair = paired(to_pair, 0)
    from_other = paired(to_other, 1)
    middle, latent = mixed(blocks_of(OWN), "mix_own", latent)
    from_pair, middle = lax.optimization_barrier((from_pair, middle))
    extended = jnp.concatenate([latent, from_pair[:SIDE], from_other[:SIDE]], axis=0)
    far = exchanged(extended, 1)
    near = exchanged(extended, 0)

    lanes = -(-(rows + 2 * SIDE) // 256) * 256
    partial, hots, state = pl.pallas_call(
        functools.partial(own_kernel, (rows, 2 * rows, 2 * rows)),
        in_specs=[whole()] * 6,
        out_specs=[whole()] * 3,
        out_shape=[
            struct(lat_rows, outputs, lon_cols, dtype=F32),
            struct(2, 2, TAPS, lanes, lon_cols),
            struct(rows, width),
        ],
        compiler_params=params(32),
        cost_estimate=cost(1e9, 2.5e6),
        name="own_band",
    )(state, own, inner, outer, extended, middle)
    band_scratch = [
        pltpu.VMEM((outputs, TAPS * lanes), BF16),
        pltpu.VMEM((2 * outputs, TAPS * lanes), BF16),
    ]
    partial = pl.pallas_call(
        functools.partial(band_kernel, True),
        in_specs=[whole()] * 4,
        out_specs=whole(),
        out_shape=struct(lat_rows, outputs, lon_cols, dtype=F32),
        scratch_shapes=band_scratch,
        compiler_params=params(32),
        cost_estimate=cost(1e9, 2.5e6),
        name="inner_band",
    )(near, edges, hots, partial)
    fields = pl.pallas_call(
        functools.partial(band_kernel, False),
        in_specs=[whole()] * 4,
        out_specs=whole(),
        out_shape=struct(out_ch, lat_rows, lon_cols),
        scratch_shapes=band_scratch,
        compiler_params=params(32),
        cost_estimate=cost(1e9, 2.5e6),
        name="outer_band",
    )(far, edges, hots, partial)
    return (state.reshape(1, rows, width), fields.reshape(1, out_ch, lat_rows, lon_cols))


def solution(mesh):
    in_specs = (
        P(None, ("reg", "lon"), None),
        P(),
        P(),
        P(),
        P(),
        P(("reg", "lon"), None),
        P("reg", "lon"),
        P(None, "reg", None, None),
        P(),
    )
    out_specs = (P(None, ("reg", "lon"), None), P(None, None, "reg", "lon"))
    return jax.shard_map(shards, mesh=mesh, in_specs=in_specs, out_specs=out_specs, check_vma=False)
```

```python
import functools
import math

import jax
import jax.numpy as jnp
from jax import lax
from jax.experimental import pallas as pl
from jax.experimental.pallas import tpu as pltpu
from jax.sharding import PartitionSpec as P

HEADS = 16
REACH = 2
TAPS = 2 * REACH + 1
SIDE = 8
ROWS = 16
LANES = 128
EARLY = 1
MIDDLE = 2
CANDIDATES = 5
F32 = jnp.float32
BF16 = jnp.bfloat16
NT = (((1,), (1,)), ((), ()))

ABOVE = ((-2, (0,)), (-1, (0, 1)))
OWN = ((0, (0, 1)), (1, (0, 1)))
BELOW = ((3, (1,)), (2, (0, 1)))


def blocks_of(band):
    return [
        (out_row, src - out_row + REACH, off)
        for src, out_rows in band
        for off in range(TAPS)
        for out_row in out_rows
    ]


def iota(shape, dim):
    return lax.broadcasted_iota(jnp.int32, shape, dim)


def normalise(rows, gain):
    values = rows.astype(F32)
    center = values - jnp.mean(values, axis=-1, keepdims=True)
    spread = jnp.mean(center * center, axis=-1, keepdims=True)
    return (center * lax.rsqrt(spread + 1e-05) * gain).astype(BF16)


def mix_kernel(blocks, psi_ref, dec_ref, mixed_ref, psi_rows_ref, taps_ref):
    basis, out_ch, channels = dec_ref.shape
    depth = basis * ROWS
    for tap in range(TAPS):
        for off in range(TAPS):
            at = (tap * TAPS + off) * 2
            psi_rows_ref[at : at + 2, :] = psi_ref[tap, off]
    spread = (iota((basis, depth), 1) // ROWS == iota((basis, depth), 0)).astype(F32)
    expanded = jnp.dot(psi_rows_ref[...], spread, preferred_element_type=F32)
    pick = iota((ROWS, depth), 1) % ROWS == iota((ROWS, depth), 0)
    for at, (out_row, tap, off) in enumerate(blocks):
        source = (tap * TAPS + off) * 2 + out_row
        taps = jnp.broadcast_to(expanded[source : source + 1], (ROWS, depth))
        taps_ref[at * ROWS : (at + 1) * ROWS, :] = jnp.where(pick, taps, 0.0).astype(BF16)
    for first in range(0, out_ch, ROWS):
        size = min(ROWS, out_ch - first)
        pieces = []
        for base in range(basis):
            pieces.append(dec_ref[base, first : first + size, :])
            if size < ROWS:
                pieces.append(jnp.zeros((ROWS - size, channels), BF16))
        mixing = jnp.concatenate(pieces, axis=0)
        mixed = jnp.dot(taps_ref[...], mixing, preferred_element_type=F32).astype(BF16)
        mixed_ref[:, first : first + ROWS, :] = mixed.reshape(len(blocks), ROWS, channels)


def listed_blocks(sectors, listed_ref):
    reg_here, lon_here = lax.axis_index("reg"), lax.axis_index("lon")
    toward = 1 - 2 * (reg_here % 2)
    found = []
    for at in range(1, listed_ref.shape[1]):
        block = listed_ref[0, at]
        step_reg = (block // sectors - reg_here) * toward
        step_lon = (block % sectors - lon_here + 1 + sectors) % sectors - 1
        lean = step_lon * (1 - 2 * (lon_here % 2))
        place = jnp.where(lean == 0, 0, jnp.where(lean > 0, 1, 2))
        ahead = jnp.where(lean < 0, 0, 1)
        found.append(jnp.where(step_reg == 0, ahead, jnp.where(step_reg > 0, 2, 5) + jnp.where(step_reg == 0, 0, place)))
    for low in range(len(found)):
        for high in range(low + 1, len(found)):
            less, more = jnp.minimum(found[low], found[high]), jnp.maximum(found[low], found[high])
            found[low], found[high] = less, more
    return found


def gather_kernel(x_hbm, assign_hbm, own_ref, assign_ref, sems):
    rows = own_ref.shape[0] - ROWS
    copies = [
        pltpu.make_async_copy(assign_hbm, assign_ref, sems.at[0]),
        pltpu.make_async_copy(x_hbm, own_ref.at[pl.ds(0, rows)], sems.at[1]),
    ]
    for copy in copies:
        copy.start()
    copies[0].wait()
    local = lax.rem(assign_ref[...], rows).astype(F32)
    line = jnp.concatenate([local[:1], local[1:2]], axis=1)
    line = jnp.broadcast_to(line, (ROWS, line.shape[1]))
    own_ref[rows:] = jnp.where(iota(line.shape, 0) == 0, line, 0.0).astype(BF16)
    copies[1].wait()


def prepare_kernel(
    sectors,
    own_ref, gain_hbm, wqkv_hbm, assign_hbm, listed_hbm,
    query_ref, key_ref, value_ref, wk_ref, wvt_ref, choice_ref, cells_ref,
    gain_ref, wqkv_ref, cell_ref, listed_ref, sems,
):
    copies = [
        pltpu.make_async_copy(source, target, sems.at[at])
        for at, (source, target) in enumerate(
            (
                (gain_hbm, gain_ref),
                (wqkv_hbm, wqkv_ref),
                (assign_hbm, cell_ref),
                (listed_hbm, listed_ref),
            )
        )
    ]
    for copy in copies:
        copy.start()
    rows, width = key_ref.shape
    group, members = query_ref.shape[1], query_ref.shape[2] // rows
    head = group // members
    for copy in copies[2:]:
        copy.wait()
    for at, number in enumerate(listed_blocks(sectors, listed_ref)):
        for candidate in range(CANDIDATES):
            same = jnp.full((ROWS, LANES), jnp.where(number == at + candidate, 1.0, 0.0), F32)
            choice_ref[at, candidate] = same.astype(BF16)
    lat_rows, lon_cols = cell_ref.shape
    place, node = iota((ROWS, rows), 0), iota((ROWS, rows), 1)
    odd = lax.axis_index("lon") % 2
    for side, first in enumerate(((1 - odd) * (lon_cols - REACH), odd * (lon_cols - REACH))):
        hit = jnp.zeros((ROWS, rows), F32)
        for row in range(lat_rows):
            for col in range(REACH):
                cell = cell_ref[row, first + col] % rows
                hit = jnp.where((place == row * REACH + col) & (node == cell), 1.0, hit)
        cells_ref[side * ROWS : (side + 1) * ROWS] = hit.astype(BF16)
    copies[0].wait()
    normed = normalise(own_ref[:rows], gain_ref[...])
    copies[1].wait()
    query = jnp.dot(normed, wqkv_ref[:, :width], preferred_element_type=F32)
    query_t = (query * (math.log2(math.e) / head**0.5)).T.astype(BF16)
    mask = (iota((group, members * rows), 0) // head) == (iota((group, members * rows), 1) // rows)
    for part in range(width // group):
        piece = query_t[part * group : (part + 1) * group]
        wide = jnp.concatenate([piece] * members, axis=1)
        query_ref[part] = jnp.where(mask, wide, jnp.zeros_like(wide))
    wk = wqkv_ref[:, width : 2 * width]
    wk_ref[...] = wk
    key_ref[...] = jnp.dot(normed, wk, preferred_element_type=F32).astype(BF16)
    wvt = wqkv_ref[:, 2 * width :].astype(F32).T.astype(BF16)
    wvt_ref[...] = wvt
    value_ref[...] = lax.dot_general(wvt, normed, NT, preferred_element_type=F32).astype(BF16)


def chosen(entries, rows, choice_ref, candidates):
    tall, wide = rows // ROWS, candidates[-1].shape[1] // LANES
    near = []
    for entry in entries:
        total = None
        for at in range(CANDIDATES):
            weight = jnp.concatenate([choice_ref[entry, at]] * wide, axis=1)
            part = candidates[entry + at] * jnp.concatenate([weight] * tall, axis=0)
            total = part if total is None else total + part
        near.append(total)
    return jnp.concatenate(near, axis=0)


def project(nodes, gain, wk_ref, wvt_ref):
    normed = normalise(nodes, gain)
    keys = jnp.dot(normed, wk_ref[...], preferred_element_type=F32).astype(BF16)
    values = lax.dot_general(wvt_ref[...], normed, NT, preferred_element_type=F32).astype(BF16)
    return keys, values


def own_heads(summed, rows):
    members = summed.shape[1] // rows
    head = summed.shape[0] // members
    return [
        summed[at * head : (at + 1) * head, at * rows : (at + 1) * rows] for at in range(members)
    ]


def early_kernel(
    choice_ref, other_ref, pair_ref, inner_ref, beside_ref,
    gain_ref, wk_ref, wvt_ref, query_ref, key_ref, value_ref,
    top_ref, sum_ref, keys_ref, values_ref,
):
    rows = key_ref.shape[0]
    parts, group, _ = query_ref.shape
    candidates = [other_ref[...], pair_ref[...]]
    candidates += [inner_ref[rows : 2 * rows], inner_ref[:rows], beside_ref[...]]
    nodes = chosen(range(EARLY), rows, choice_ref, candidates)
    keys, values = project(nodes, gain_ref[...], wk_ref, wvt_ref)
    keys_ref[:rows] = key_ref[...]
    keys_ref[rows:] = keys
    for part in range(parts):
        span = slice(part * group, (part + 1) * group)
        values_ref[part, :group, :rows] = value_ref[span]
        values_ref[part, :group, rows:] = values[span]
        values_ref[part, group:, :] = jnp.ones((ROWS, keys_ref.shape[0]), BF16)

    def scored(part):
        span = slice(part * group, (part + 1) * group)
        return jnp.dot(keys_ref[:, span], query_ref[part], preferred_element_type=F32)

    scores = scored(0)
    for part in range(parts):
        now = scores
        if part + 1 < parts:
            scores = scored(part + 1)
        top = jnp.max(now, axis=0, keepdims=True)
        expo = jnp.exp2(now - top).astype(BF16)
        summed = jnp.dot(values_ref[part], expo, preferred_element_type=F32)
        top_ref[part, 0] = jnp.broadcast_to(top, top_ref.shape[2:])
        top_ref[part, 1] = jnp.broadcast_to(summed[group : group + 1], top_ref.shape[2:])
        sum_ref[part] = jnp.concatenate(own_heads(summed[:group], rows), axis=0)


def updated(keys, values, query_ref, top_ref, sum_ref, part):
    group, rows = query_ref.shape[1], sum_ref.shape[2]
    span = slice(part * group, (part + 1) * group)
    scores = jnp.dot(keys[:, span], query_ref[part], preferred_element_type=F32)
    before = top_ref[part, 0, :1]
    top = jnp.maximum(before, jnp.max(scores, axis=0, keepdims=True))
    expo = jnp.exp2(scores - top).astype(BF16)
    ones = jnp.ones((ROWS, keys.shape[0]), BF16)
    weights = jnp.concatenate([values[span], ones], axis=0)
    summed = jnp.dot(weights, expo, preferred_element_type=F32)
    shrink = jnp.exp2(before - top)
    total = summed[group : group + 1] + top_ref[part, 1, :1] * shrink
    pieces = own_heads(summed[:group], rows)
    head = group // len(pieces)
    sums = [
        piece + sum_ref[part, at * head : (at + 1) * head] * shrink[:, at * rows : (at + 1) * rows]
        for at, piece in enumerate(pieces)
    ]
    return top, total, sums


def middle_kernel(
    choice_ref, pair_ref, inner_ref, beside_ref, outer_ref,
    gain_ref, wk_ref, wvt_ref, query_ref, top_ref, sum_ref,
    new_top_ref, new_sum_ref,
):
    rows = sum_ref.shape[2]
    candidates = [None, pair_ref[...], inner_ref[rows : 2 * rows], inner_ref[:rows], beside_ref[...]]
    candidates += [outer_ref[rows : 2 * rows], outer_ref[:rows]]
    nodes = chosen(range(EARLY, EARLY + MIDDLE), rows, choice_ref, candidates)
    keys, values = project(nodes, gain_ref[...], wk_ref, wvt_ref)
    for part in range(query_ref.shape[0]):
        top, total, sums = updated(keys, values, query_ref, top_ref, sum_ref, part)
        new_top_ref[part, 0] = jnp.broadcast_to(top, new_top_ref.shape[2:])
        new_top_ref[part, 1] = jnp.broadcast_to(total, new_top_ref.shape[2:])
        new_sum_ref[part] = jnp.concatenate(sums, axis=0)


def late_kernel(
    choice_ref, cells_ref, inner_ref, beside_ref, outer_ref, corner_ref,
    own_ref, gain_ref, wk_ref, wvt_ref, query_ref, top_ref, sum_ref, wout_ref, wlat_ref,
    state_ref, latent_ref, to_pair_ref, to_other_ref,
    attended_ref,
):
    rows = state_ref.shape[0]
    parts, group, _ = query_ref.shape
    candidates = [None] * 3 + [inner_ref[:rows], beside_ref[...]]
    candidates += [outer_ref[rows : 2 * rows], outer_ref[:rows], corner_ref[...]]
    entries = range(EARLY + MIDDLE, choice_ref.shape[0])
    nodes = chosen(entries, rows, choice_ref, candidates)
    keys, values = project(nodes, gain_ref[...], wk_ref, wvt_ref)
    for part in range(parts):
        _, total, sums = updated(keys, values, query_ref, top_ref, sum_ref, part)
        share = 1.0 / total
        sums = [one * share[:, at * rows : (at + 1) * rows] for at, one in enumerate(sums)]
        merged = jnp.concatenate(sums, axis=0)
        attended_ref[:, part * group : (part + 1) * group] = merged.T.astype(BF16)
    state = (
        own_ref[:rows].astype(F32)
        + jnp.dot(attended_ref[...], wout_ref[...], preferred_element_type=F32)
    ).astype(BF16)
    state_ref[...] = state
    value = jnp.dot(state, wlat_ref[...], preferred_element_type=F32)
    latent = (value / (1.0 + jnp.exp(-value))).astype(BF16)
    latent_ref[...] = latent
    cells = jnp.dot(cells_ref[...], latent, preferred_element_type=F32).astype(BF16)
    to_pair_ref[...] = cells[:ROWS]
    to_other_ref[...] = cells[ROWS:]


def hot_rows(values, rows, cols, line):
    odd = lax.axis_index("lon") % 2
    column = iota((8, cols), 1)
    node = iota((rows + 2 * SIDE, cols), 0).astype(F32)
    for off in range(TAPS):
        step = off - REACH
        where = jnp.broadcast_to(values, (8, cols))
        if step:
            where = pltpu.roll(where, (-step) % cols, 1)
        reach = column + step
        before = (rows + (1 - odd) * SIDE + REACH * line + reach + REACH).astype(F32)
        after = (rows + odd * SIDE + REACH * line + reach - cols).astype(F32)
        where = jnp.where(reach < 0, before, jnp.where(reach >= cols, after, where))
        yield jnp.where(node == where[:1], 1.0, 0.0).astype(BF16)


def shares_of(latent, weights):
    blocks, outputs, channels = weights.shape
    shares = lax.dot_general(
        weights.reshape(blocks * outputs, channels), latent, NT, preferred_element_type=F32
    ).astype(BF16)
    return [shares[at * outputs : (at + 1) * outputs] for at in range(blocks)]


def lines_of(line_ref, start, cols):
    values = line_ref[start : start + ROWS, :].astype(F32)
    return values[:1, :cols], values[:1, cols:]


def own_kernel(
    begin, state_ref, own_ref, inner_ref, outer_ref, latent_ref, weights_ref,
    out_ref, hot_ref, kept_ref,
):
    kept_ref[...] = state_ref[...]
    cols = out_ref.shape[2]
    rows = latent_ref.shape[0] - 2 * SIDE
    own = lines_of(own_ref, begin[0], cols)
    table = [list(hot_rows(own[line], rows, cols, line)) for line in range(2)]
    acc = [None, None]
    for (out_row, tap, off), share in zip(
        blocks_of(OWN), shares_of(latent_ref[...], weights_ref[...])
    ):
        line = out_row + tap - REACH
        piece = jnp.dot(share, table[line][off], preferred_element_type=F32)
        acc[out_row] = piece if acc[out_row] is None else acc[out_row] + piece
    for row in range(2):
        out_ref[row] = acc[row]
    odd = lax.axis_index("reg") % 2 == 1
    inner, outer = lines_of(inner_ref, begin[1], cols), lines_of(outer_ref, begin[2], cols)
    nodes = rows + 2 * SIDE
    for band, (yes, no) in enumerate(((inner, outer), (outer, inner))):
        for at, line in enumerate((0, 1) if band == 0 else (1, 0)):
            values = jnp.where(odd, yes[line], no[line])
            for off, hot in enumerate(hot_rows(values, rows, cols, line)):
                hot_ref[band, at, off, :nodes] = hot
                hot_ref[band, at, off, nodes:] = jnp.zeros((hot_ref.shape[3] - nodes, cols), BF16)


def band_kernel(from_inner, latent_ref, weights_ref, hot_ref, partial_ref, out_ref, one_ref, two_ref):
    odd = lax.axis_index("reg") % 2
    band = 1 - odd if from_inner else odd
    latent = latent_ref[...]
    lanes, cols = hot_ref.shape[3:]
    outputs = weights_ref.shape[1]
    blank = jnp.zeros((lanes - latent.shape[0], latent.shape[1]), BF16)
    blocks = len(blocks_of(ABOVE))
    weights = weights_ref[pl.ds(band * blocks, blocks)]
    shares = shares_of(jnp.concatenate([latent, blank], axis=0), weights)
    for off in range(TAPS):
        span = slice(off * lanes, (off + 1) * lanes)
        one_ref[:, span] = shares[off]
        for row in range(2):
            two_ref[row * outputs : (row + 1) * outputs, span] = shares[TAPS + 2 * off + row]
    depth = TAPS * lanes
    one = jnp.dot(one_ref[...], hot_ref[band, 0].reshape(depth, cols), preferred_element_type=F32)
    two = jnp.dot(two_ref[...], hot_ref[band, 1].reshape(depth, cols), preferred_element_type=F32)
    for row in range(2):
        total = partial_ref[row] + two[row * outputs : (row + 1) * outputs]
        total = total + jnp.where(band == row, one, 0.0)
        if from_inner:
            out_ref[row] = total
        else:
            out_ref[:, row, :] = total[: out_ref.shape[0]].astype(BF16)


def whole(memory=pltpu.VMEM):
    return pl.BlockSpec(memory_space=memory)


def struct(*shape, dtype=BF16):
    return jax.ShapeDtypeStruct(shape, dtype)


def params(limit):
    return pltpu.CompilerParams(vmem_limit_bytes=limit << 20)


def cost(flops, moved):
    return pl.CostEstimate(flops=int(flops), bytes_accessed=int(moved), transcendentals=0)


def shards(nodes, norm_gain, w_qkv, w_out, w_latent, neighbours, assignment, psi, w_dec):
    _, rows, width = nodes.shape
    channels = w_latent.shape[1]
    lat_rows, lon_cols = assignment.shape
    basis, _, out_ch = w_dec.shape
    sectors = lax.axis_size("lon")
    count = neighbours.shape[1]
    x = nodes.reshape(rows, width)
    gain = norm_gain.reshape(1, width)

    def paired(array, first):
        pairs = [(i, (i + 1) % sectors) for i in range(first, sectors, 2)]
        return lax.ppermute(array, "lon", pairs + [(j, i) for i, j in pairs])

    def exchanged(array, first):
        size = lax.axis_size("reg")
        pairs = [(i, i + 1) for i in range(first, size - 1, 2)]
        return lax.ppermute(array, "reg", pairs + [(j, i) for i, j in pairs])

    def in_hbm(*arrays):
        return [pltpu.with_memory_space_constraint(array, pltpu.HBM) for array in arrays]

    other = paired(x, 1)
    pair = paired(x, 0)

    outputs = -(-out_ch // ROWS) * ROWS
    head = width // HEADS
    members = LANES // head
    parts = HEADS // members
    def mixed(blocks, name, after):
        taps = psi.transpose(2, 3, 1, 0)
        mixing = w_dec.transpose(0, 2, 1)
        taps, mixing, after = lax.optimization_barrier((taps, mixing, after))
        weights = pl.pallas_call(
            functools.partial(mix_kernel, blocks),
            in_specs=[whole()] * 2,
            out_specs=whole(),
            out_shape=struct(len(blocks), outputs, channels),
            scratch_shapes=[
                pltpu.VMEM((2 * TAPS * TAPS, basis), F32),
                pltpu.VMEM((len(blocks) * ROWS, basis * ROWS), BF16),
            ],
            compiler_params=params(32),
            cost_estimate=cost(2e9, 6e6),
            name=name,
        )(taps, mixing)
        return weights, after

    own = pl.pallas_call(
        gather_kernel,
        in_specs=[whole(pltpu.HBM)] * 2,
        out_specs=whole(),
        out_shape=struct(rows + ROWS, width),
        scratch_shapes=[
            pltpu.VMEM(assignment.shape, jnp.int32),
            pltpu.SemaphoreType.DMA((2,)),
        ],
        compiler_params=params(32),
        cost_estimate=cost(1e3, 1e3),
        name="gather",
    )(*in_hbm(x, assignment))
    query, key, value, wk, wvt, choice, cells = pl.pallas_call(
        functools.partial(prepare_kernel, sectors),
        in_specs=[whole()] + [whole(pltpu.HBM)] * 4,
        out_specs=[whole()] * 7,
        out_shape=[
            struct(parts, LANES, members * rows),
            struct(rows, width),
            struct(width, rows),
            struct(width, width),
            struct(width, width),
            struct(count - 1, CANDIDATES, ROWS, LANES),
            struct(2 * ROWS, rows),
        ],
        scratch_shapes=[
            pltpu.VMEM((1, width), F32),
            pltpu.VMEM(w_qkv.shape, BF16),
            pltpu.SMEM(assignment.shape, jnp.int32),
            pltpu.SMEM(neighbours.shape, jnp.int32),
            pltpu.SemaphoreType.DMA((4,)),
        ],
        compiler_params=params(32),
        cost_estimate=cost(5e8, 1e6),
        name="prepare",
    )(own, *in_hbm(gain, w_qkv, assignment, neighbours))
    own, query = lax.optimization_barrier((own, query))
    message = jnp.concatenate([pair, own], axis=0)
    message_a = message
    other_a = other
    inner = exchanged(message_a, 0)
    outer = exchanged(message, 1)
    corner = exchanged(other, 1)
    beside = exchanged(other_a, 0)

    edges, other_m = mixed(blocks_of(ABOVE) + blocks_of(BELOW), "mix_edges", other)
    inner, edges = lax.optimization_barrier((inner, edges))
    top, summed = pl.pallas_call(
        early_kernel,
        in_specs=[whole()] * 11,
        out_specs=[whole()] * 2,
        out_shape=[
            struct(parts, 2, 8, members * rows, dtype=F32),
            struct(parts, LANES, rows, dtype=F32),
        ],
        scratch_shapes=[
            pltpu.VMEM(((1 + EARLY) * rows, width), BF16),
            pltpu.VMEM((parts, LANES + ROWS, (1 + EARLY) * rows), BF16),
        ],
        compiler_params=params(32),
        cost_estimate=cost(3e9, 6e6),
        name="early",
    )(choice, other, pair, inner, beside, gain, wk, wvt, query, key, value)
    top, summed = pl.pallas_call(
        middle_kernel,
        in_specs=[whole()] * 11,
        out_specs=[whole()] * 2,
        out_shape=[
            struct(parts, 2, 8, members * rows, dtype=F32),
            struct(parts, LANES, rows, dtype=F32),
        ],
        compiler_params=params(32),
        cost_estimate=cost(3e9, 6e6),
        name="middle",
    )(choice, pair, inner, beside, outer, gain, wk, wvt, query, top, summed)
    state, latent, to_pair, to_other = pl.pallas_call(
        late_kernel,
        in_specs=[whole()] * 15,
        out_specs=[whole()] * 4,
        out_shape=[pltpu.VMEM((rows, width), BF16), struct(rows, channels)]
        + [struct(ROWS, channels)] * 2,
        scratch_shapes=[pltpu.VMEM((rows, width), BF16)],
        compiler_params=params(32),
        cost_estimate=cost(3e9, 6e6),
        name="late",
    )(
        choice, cells, inner, beside, outer, corner,
        own, gain, wk, wvt, query, top, summed, w_out, w_latent,
    )

    from_pair = paired(to_pair, 0)
    from_other = paired(to_other, 1)
    middle, latent = mixed(blocks_of(OWN), "mix_own", latent)
    from_pair, middle = lax.optimization_barrier((from_pair, middle))
    extended = jnp.concatenate([latent, from_pair[:SIDE], from_other[:SIDE]], axis=0)
    far = exchanged(extended, 1)
    near = exchanged(extended, 0)

    lanes = -(-(rows + 2 * SIDE) // 256) * 256
    partial, hots, state = pl.pallas_call(
        functools.partial(own_kernel, (rows, 2 * rows, 2 * rows)),
        in_specs=[whole()] * 6,
        out_specs=[whole()] * 3,
        out_shape=[
            struct(lat_rows, outputs, lon_cols, dtype=F32),
            struct(2, 2, TAPS, lanes, lon_cols),
            struct(rows, width),
        ],
        compiler_params=params(32),
        cost_estimate=cost(1e9, 2.5e6),
        name="own_band",
    )(state, own, inner, outer, extended, middle)
    band_scratch = [
        pltpu.VMEM((outputs, TAPS * lanes), BF16),
        pltpu.VMEM((2 * outputs, TAPS * lanes), BF16),
    ]
    partial = pl.pallas_call(
        functools.partial(band_kernel, True),
        in_specs=[whole()] * 4,
        out_specs=whole(),
        out_shape=struct(lat_rows, outputs, lon_cols, dtype=F32),
        scratch_shapes=band_scratch,
        compiler_params=params(32),
        cost_estimate=cost(1e9, 2.5e6),
        name="inner_band",
    )(near, edges, hots, partial)
    fields = pl.pallas_call(
        functools.partial(band_kernel, False),
        in_specs=[whole()] * 4,
        out_specs=whole(),
        out_shape=struct(out_ch, lat_rows, lon_cols),
        scratch_shapes=band_scratch,
        compiler_params=params(32),
        cost_estimate=cost(1e9, 2.5e6),
        name="outer_band",
    )(far, edges, hots, partial)
    return (state.reshape(1, rows, width), fields.reshape(1, out_ch, lat_rows, lon_cols))


def solution(mesh):
    in_specs = (
        P(None, ("reg", "lon"), None),
        P(),
        P(),
        P(),
        P(),
        P(("reg", "lon"), None),
        P("reg", "lon"),
        P(None, "reg", None, None),
        P(),
    )
    out_specs = (P(None, ("reg", "lon"), None), P(None, None, "reg", "lon"))
    return jax.shard_map(shards, mesh=mesh, in_specs=in_specs, out_specs=out_specs, check_vma=False)
```

```python
import functools
import math

import jax
import jax.numpy as jnp
from jax import lax
from jax.experimental import pallas as pl
from jax.experimental.pallas import tpu as pltpu
from jax.sharding import PartitionSpec as P

HEADS = 16
REACH = 2
TAPS = 2 * REACH + 1
SIDE = 8
ROWS = 16
LANES = 128
EARLY = 2
CANDIDATES = 5
F32 = jnp.float32
BF16 = jnp.bfloat16
NT = (((1,), (1,)), ((), ()))

ABOVE = ((-2, (0,)), (-1, (0, 1)))
OWN = ((0, (0, 1)), (1, (0, 1)))
BELOW = ((3, (1,)), (2, (0, 1)))


def blocks_of(band):
    return [
        (out_row, src - out_row + REACH, off)
        for src, out_rows in band
        for off in range(TAPS)
        for out_row in out_rows
    ]


def iota(shape, dim):
    return lax.broadcasted_iota(jnp.int32, shape, dim)


def normalise(rows, gain):
    values = rows.astype(F32)
    center = values - jnp.mean(values, axis=-1, keepdims=True)
    spread = jnp.mean(center * center, axis=-1, keepdims=True)
    return (center * lax.rsqrt(spread + 1e-05) * gain).astype(BF16)


def mix_kernel(blocks, psi_ref, dec_ref, mixed_ref, psi_rows_ref, taps_ref):
    basis, out_ch, channels = dec_ref.shape
    depth = basis * ROWS
    for tap in range(TAPS):
        for off in range(TAPS):
            at = (tap * TAPS + off) * 2
            psi_rows_ref[at : at + 2, :] = psi_ref[tap, off]
    spread = (iota((basis, depth), 1) // ROWS == iota((basis, depth), 0)).astype(F32)
    expanded = jnp.dot(psi_rows_ref[...], spread, preferred_element_type=F32)
    pick = iota((ROWS, depth), 1) % ROWS == iota((ROWS, depth), 0)
    for at, (out_row, tap, off) in enumerate(blocks):
        source = (tap * TAPS + off) * 2 + out_row
        taps = jnp.broadcast_to(expanded[source : source + 1], (ROWS, depth))
        taps_ref[at * ROWS : (at + 1) * ROWS, :] = jnp.where(pick, taps, 0.0).astype(BF16)
    for first in range(0, out_ch, ROWS):
        size = min(ROWS, out_ch - first)
        pieces = []
        for base in range(basis):
            pieces.append(dec_ref[base, first : first + size, :])
            if size < ROWS:
                pieces.append(jnp.zeros((ROWS - size, channels), BF16))
        mixing = jnp.concatenate(pieces, axis=0)
        mixed = jnp.dot(taps_ref[...], mixing, preferred_element_type=F32).astype(BF16)
        mixed_ref[:, first : first + ROWS, :] = mixed.reshape(len(blocks), ROWS, channels)


def listed_blocks(sectors, listed_ref):
    reg_here, lon_here = lax.axis_index("reg"), lax.axis_index("lon")
    toward = 1 - 2 * (reg_here % 2)
    found = []
    for at in range(1, listed_ref.shape[1]):
        block = listed_ref[0, at]
        step_reg = (block // sectors - reg_here) * toward
        step_lon = (block % sectors - lon_here + 1 + sectors) % sectors - 1
        lean = step_lon * (1 - 2 * (lon_here % 2))
        side = jnp.where(lean == 0, 0, jnp.where(lean > 0, 1, 4))
        ahead = jnp.where(lean < 0, 0, 1)
        behind = jnp.where(lean < 0, 7, 4 + side)
        found.append(jnp.where(step_reg == 0, ahead, jnp.where(step_reg > 0, 2 + side, behind)))
    for low in range(len(found)):
        for high in range(low + 1, len(found)):
            less, more = jnp.minimum(found[low], found[high]), jnp.maximum(found[low], found[high])
            found[low], found[high] = less, more
    return found


def gather_kernel(x_hbm, assign_hbm, own_ref, assign_ref, sems):
    rows = own_ref.shape[0] - ROWS
    copies = [
        pltpu.make_async_copy(assign_hbm, assign_ref, sems.at[0]),
        pltpu.make_async_copy(x_hbm, own_ref.at[pl.ds(0, rows)], sems.at[1]),
    ]
    for copy in copies:
        copy.start()
    copies[0].wait()
    local = lax.rem(assign_ref[...], rows).astype(F32)
    line = jnp.concatenate([local[:1], local[1:2]], axis=1)
    line = jnp.broadcast_to(line, (ROWS, line.shape[1]))
    own_ref[rows:] = jnp.where(iota(line.shape, 0) == 0, line, 0.0).astype(BF16)
    copies[1].wait()


def prepare_kernel(
    sectors,
    own_ref, gain_hbm, wqkv_hbm, assign_hbm, listed_hbm,
    query_ref, key_ref, value_ref, wk_ref, wvt_ref, choice_ref, cells_ref,
    gain_ref, wqkv_ref, cell_ref, listed_ref, sems,
):
    copies = [
        pltpu.make_async_copy(source, target, sems.at[at])
        for at, (source, target) in enumerate(
            (
                (gain_hbm, gain_ref),
                (wqkv_hbm, wqkv_ref),
                (assign_hbm, cell_ref),
                (listed_hbm, listed_ref),
            )
        )
    ]
    for copy in copies:
        copy.start()
    rows, width = key_ref.shape
    group, members = query_ref.shape[1], query_ref.shape[2] // rows
    head = group // members
    for copy in copies[2:]:
        copy.wait()
    for at, number in enumerate(listed_blocks(sectors, listed_ref)):
        for candidate in range(CANDIDATES):
            same = jnp.full((ROWS, LANES), jnp.where(number == at + candidate, 1.0, 0.0), F32)
            choice_ref[at, candidate] = same.astype(BF16)
    lat_rows, lon_cols = cell_ref.shape
    place, node = iota((ROWS, rows), 0), iota((ROWS, rows), 1)
    odd = lax.axis_index("lon") % 2
    for side, first in enumerate(((1 - odd) * (lon_cols - REACH), odd * (lon_cols - REACH))):
        hit = jnp.zeros((ROWS, rows), F32)
        for row in range(lat_rows):
            for col in range(REACH):
                cell = cell_ref[row, first + col] % rows
                hit = jnp.where((place == row * REACH + col) & (node == cell), 1.0, hit)
        cells_ref[side * ROWS : (side + 1) * ROWS] = hit.astype(BF16)
    copies[0].wait()
    normed = normalise(own_ref[:rows], gain_ref[...])
    copies[1].wait()
    query = jnp.dot(normed, wqkv_ref[:, :width], preferred_element_type=F32)
    query_t = (query * (math.log2(math.e) / head**0.5)).T.astype(BF16)
    mask = (iota((group, members * rows), 0) // head) == (iota((group, members * rows), 1) // rows)
    for part in range(width // group):
        piece = query_t[part * group : (part + 1) * group]
        wide = jnp.concatenate([piece] * members, axis=1)
        query_ref[part] = jnp.where(mask, wide, jnp.zeros_like(wide))
    wk = wqkv_ref[:, width : 2 * width]
    wk_ref[...] = wk
    key_ref[...] = jnp.dot(normed, wk, preferred_element_type=F32).astype(BF16)
    wvt = wqkv_ref[:, 2 * width :].astype(F32).T.astype(BF16)
    wvt_ref[...] = wvt
    value_ref[...] = lax.dot_general(wvt, normed, NT, preferred_element_type=F32).astype(BF16)


def chosen(entries, rows, choice_ref, candidates):
    tall, wide = rows // ROWS, candidates[-1].shape[1] // LANES
    near = []
    for entry in entries:
        total = None
        for at in range(CANDIDATES):
            weight = jnp.concatenate([choice_ref[entry, at]] * wide, axis=1)
            part = candidates[entry + at] * jnp.concatenate([weight] * tall, axis=0)
            total = part if total is None else total + part
        near.append(total)
    return jnp.concatenate(near, axis=0)


def project(nodes, gain, wk_ref, wvt_ref):
    normed = normalise(nodes, gain)
    keys = jnp.dot(normed, wk_ref[...], preferred_element_type=F32).astype(BF16)
    values = lax.dot_general(wvt_ref[...], normed, NT, preferred_element_type=F32).astype(BF16)
    return keys, values


def own_heads(summed, rows):
    members = summed.shape[1] // rows
    head = summed.shape[0] // members
    return [
        summed[at * head : (at + 1) * head, at * rows : (at + 1) * rows] for at in range(members)
    ]


def early_kernel(
    choice_ref, other_ref, pair_ref, inner_ref, outer_ref,
    gain_ref, wk_ref, wvt_ref, query_ref, key_ref, value_ref,
    top_ref, sum_ref, keys_ref, values_ref,
):
    rows = key_ref.shape[0]
    parts, group, _ = query_ref.shape
    candidates = [other_ref[...], pair_ref[...]]
    candidates += [ref[rows : 2 * rows] if center else ref[:rows] for ref in (inner_ref, outer_ref) for center in (1, 0)]
    nodes = chosen(range(EARLY), rows, choice_ref, candidates)
    keys, values = project(nodes, gain_ref[...], wk_ref, wvt_ref)
    keys_ref[:rows] = key_ref[...]
    keys_ref[rows:] = keys
    for part in range(parts):
        span = slice(part * group, (part + 1) * group)
        values_ref[part, :group, :rows] = value_ref[span]
        values_ref[part, :group, rows:] = values[span]
        values_ref[part, group:, :] = jnp.ones((ROWS, keys_ref.shape[0]), BF16)

    spans = [slice(part * group, (part + 1) * group) for part in range(parts)]
    scores = [
        jnp.dot(keys_ref[:, span], query_ref[part], preferred_element_type=F32)
        for part, span in enumerate(spans)
    ]
    tops = [jnp.max(one, axis=0, keepdims=True) for one in scores]
    expos = [jnp.exp2(one - top).astype(BF16) for one, top in zip(scores, tops)]
    sums = [
        jnp.dot(values_ref[part], expo, preferred_element_type=F32) for part, expo in enumerate(expos)
    ]
    for part, (top, summed) in enumerate(zip(tops, sums)):
        top_ref[part, 0] = jnp.broadcast_to(top, top_ref.shape[2:])
        top_ref[part, 1] = jnp.broadcast_to(summed[group : group + 1], top_ref.shape[2:])
        sum_ref[part] = jnp.concatenate(own_heads(summed[:group], rows), axis=0)


def late_kernel(
    choice_ref, cells_ref, inner_ref, outer_ref, beside_ref, corner_ref,
    own_ref, gain_ref, wk_ref, wvt_ref, query_ref, top_ref, sum_ref, wout_ref, wlat_ref,
    state_ref, latent_ref, to_pair_ref, to_other_ref,
):
    rows, width = state_ref.shape
    parts, group, lanes = query_ref.shape
    members = lanes // rows
    head = group // members
    candidates = [None, None]
    candidates += [ref[rows : 2 * rows] if center else ref[:rows] for ref in (inner_ref, outer_ref) for center in (1, 0)]
    candidates += [beside_ref[...], corner_ref[...]]
    nodes = chosen(range(EARLY, choice_ref.shape[0]), rows, choice_ref, candidates)
    keys, values = project(nodes, gain_ref[...], wk_ref, wvt_ref)
    ones = jnp.ones((ROWS, nodes.shape[0]), BF16)
    spans = [slice(part * group, (part + 1) * group) for part in range(parts)]
    scores = [
        jnp.dot(keys[:, span], query_ref[part], preferred_element_type=F32)
        for part, span in enumerate(spans)
    ]
    befores = [top_ref[part, 0, :1] for part in range(parts)]
    tops = [
        jnp.maximum(before, jnp.max(one, axis=0, keepdims=True))
        for before, one in zip(befores, scores)
    ]
    expos = [jnp.exp2(one - top).astype(BF16) for one, top in zip(scores, tops)]
    sums = [
        jnp.dot(jnp.concatenate([values[span], ones], axis=0), expo, preferred_element_type=F32)
        for span, expo in zip(spans, expos)
    ]
    attended = []
    for part, summed in enumerate(sums):
        shrink = jnp.exp2(befores[part] - tops[part])
        share = 1.0 / (summed[group : group + 1] + top_ref[part, 1, :1] * shrink)
        merged = []
        for member, piece in enumerate(own_heads(summed[:group], rows)):
            span = slice(member * rows, (member + 1) * rows)
            earlier = sum_ref[part, member * head : (member + 1) * head]
            merged.append((piece + earlier * shrink[:, span]) * share[:, span])
        attended.append(jnp.concatenate(merged, axis=0).T.astype(BF16))
    attended = jnp.concatenate(attended, axis=1)
    state = (
        own_ref[:rows].astype(F32)
        + jnp.dot(attended, wout_ref[...], preferred_element_type=F32)
    ).astype(BF16)
    state_ref[...] = state
    value = jnp.dot(state, wlat_ref[...], preferred_element_type=F32)
    latent = (value / (1.0 + jnp.exp(-value))).astype(BF16)
    latent_ref[...] = latent
    cells = jnp.dot(cells_ref[...], latent, preferred_element_type=F32).astype(BF16)
    to_pair_ref[...] = cells[:ROWS]
    to_other_ref[...] = cells[ROWS:]


def hot_rows(values, rows, cols, line):
    odd = lax.axis_index("lon") % 2
    column = iota((8, cols), 1)
    node = iota((rows + 2 * SIDE, cols), 0).astype(F32)
    for off in range(TAPS):
        step = off - REACH
        where = jnp.broadcast_to(values, (8, cols))
        if step:
            where = pltpu.roll(where, (-step) % cols, 1)
        reach = column + step
        before = (rows + (1 - odd) * SIDE + REACH * line + reach + REACH).astype(F32)
        after = (rows + odd * SIDE + REACH * line + reach - cols).astype(F32)
        where = jnp.where(reach < 0, before, jnp.where(reach >= cols, after, where))
        yield jnp.where(node == where[:1], 1.0, 0.0).astype(BF16)


def shares_of(latent, weights):
    blocks, outputs, channels = weights.shape
    shares = lax.dot_general(
        weights.reshape(blocks * outputs, channels), latent, NT, preferred_element_type=F32
    ).astype(BF16)
    return [shares[at * outputs : (at + 1) * outputs] for at in range(blocks)]


def lines_of(line_ref, start, cols):
    values = line_ref[start : start + ROWS, :].astype(F32)
    return values[:1, :cols], values[:1, cols:]


def own_kernel(
    begin, state_ref, own_ref, inner_ref, outer_ref, latent_ref, weights_ref,
    out_ref, hot_ref, kept_ref,
):
    kept_ref[...] = state_ref[...]
    cols = out_ref.shape[2]
    rows = latent_ref.shape[0] - 2 * SIDE
    own = lines_of(own_ref, begin[0], cols)
    table = [list(hot_rows(own[line], rows, cols, line)) for line in range(2)]
    acc = [None, None]
    for (out_row, tap, off), share in zip(
        blocks_of(OWN), shares_of(latent_ref[...], weights_ref[...])
    ):
        line = out_row + tap - REACH
        piece = jnp.dot(share, table[line][off], preferred_element_type=F32)
        acc[out_row] = piece if acc[out_row] is None else acc[out_row] + piece
    for row in range(2):
        out_ref[row] = acc[row]
    odd = lax.axis_index("reg") % 2 == 1
    inner, outer = lines_of(inner_ref, begin[1], cols), lines_of(outer_ref, begin[2], cols)
    nodes = rows + 2 * SIDE
    for band, (yes, no) in enumerate(((inner, outer), (outer, inner))):
        for at, line in enumerate((0, 1) if band == 0 else (1, 0)):
            values = jnp.where(odd, yes[line], no[line])
            for off, hot in enumerate(hot_rows(values, rows, cols, line)):
                hot_ref[band, at, off, :nodes] = hot
                hot_ref[band, at, off, nodes:] = jnp.zeros((hot_ref.shape[3] - nodes, cols), BF16)


def band_kernel(from_inner, latent_ref, weights_ref, hot_ref, partial_ref, out_ref, one_ref, two_ref):
    odd = lax.axis_index("reg") % 2
    band = 1 - odd if from_inner else odd
    latent = latent_ref[...]
    lanes, cols = hot_ref.shape[3:]
    outputs = weights_ref.shape[1]
    blank = jnp.zeros((lanes - latent.shape[0], latent.shape[1]), BF16)
    blocks = len(blocks_of(ABOVE))
    weights = weights_ref[pl.ds(band * blocks, blocks)]
    shares = shares_of(jnp.concatenate([latent, blank], axis=0), weights)
    for off in range(TAPS):
        span = slice(off * lanes, (off + 1) * lanes)
        one_ref[:, span] = shares[off]
        for row in range(2):
            two_ref[row * outputs : (row + 1) * outputs, span] = shares[TAPS + 2 * off + row]
    depth = TAPS * lanes
    one = jnp.dot(one_ref[...], hot_ref[band, 0].reshape(depth, cols), preferred_element_type=F32)
    two = jnp.dot(two_ref[...], hot_ref[band, 1].reshape(depth, cols), preferred_element_type=F32)
    for row in range(2):
        total = partial_ref[row] + two[row * outputs : (row + 1) * outputs]
        total = total + jnp.where(band == row, one, 0.0)
        if from_inner:
            out_ref[row] = total
        else:
            out_ref[:, row, :] = total[: out_ref.shape[0]].astype(BF16)


def whole(memory=pltpu.VMEM):
    return pl.BlockSpec(memory_space=memory)


def struct(*shape, dtype=BF16):
    return jax.ShapeDtypeStruct(shape, dtype)


def params(limit):
    return pltpu.CompilerParams(vmem_limit_bytes=limit << 20)


def cost(flops, moved):
    return pl.CostEstimate(flops=int(flops), bytes_accessed=int(moved), transcendentals=0)


def shards(nodes, norm_gain, w_qkv, w_out, w_latent, neighbours, assignment, psi, w_dec):
    _, rows, width = nodes.shape
    channels = w_latent.shape[1]
    lat_rows, lon_cols = assignment.shape
    basis, _, out_ch = w_dec.shape
    sectors = lax.axis_size("lon")
    count = neighbours.shape[1]
    x = nodes.reshape(rows, width)
    gain = norm_gain.reshape(1, width)

    def paired(array, first):
        pairs = [(i, (i + 1) % sectors) for i in range(first, sectors, 2)]
        return lax.ppermute(array, "lon", pairs + [(j, i) for i, j in pairs])

    def exchanged(array, first):
        size = lax.axis_size("reg")
        pairs = [(i, i + 1) for i in range(first, size - 1, 2)]
        return lax.ppermute(array, "reg", pairs + [(j, i) for i, j in pairs])

    def in_hbm(*arrays):
        return [pltpu.with_memory_space_constraint(array, pltpu.HBM) for array in arrays]

    other = paired(x, 1)
    pair = paired(x, 0)

    outputs = -(-out_ch // ROWS) * ROWS
    head = width // HEADS
    members = LANES // head
    parts = HEADS // members
    def mixed(blocks, name, after):
        taps = psi.transpose(2, 3, 1, 0)
        mixing = w_dec.transpose(0, 2, 1)
        taps, mixing, after = lax.optimization_barrier((taps, mixing, after))
        weights = pl.pallas_call(
            functools.partial(mix_kernel, blocks),
            in_specs=[whole()] * 2,
            out_specs=whole(),
            out_shape=struct(len(blocks), outputs, channels),
            scratch_shapes=[
                pltpu.VMEM((2 * TAPS * TAPS, basis), F32),
                pltpu.VMEM((len(blocks) * ROWS, basis * ROWS), BF16),
            ],
            compiler_params=params(32),
            cost_estimate=cost(2e9, 6e6),
            name=name,
        )(taps, mixing)
        return weights, after

    own = pl.pallas_call(
        gather_kernel,
        in_specs=[whole(pltpu.HBM)] * 2,
        out_specs=whole(),
        out_shape=struct(rows + ROWS, width),
        scratch_shapes=[
            pltpu.VMEM(assignment.shape, jnp.int32),
            pltpu.SemaphoreType.DMA((2,)),
        ],
        compiler_params=params(32),
        cost_estimate=cost(1e3, 1e3),
        name="gather",
    )(*in_hbm(x, assignment))
    query, key, value, wk, wvt, choice, cells = pl.pallas_call(
        functools.partial(prepare_kernel, sectors),
        in_specs=[whole()] + [whole(pltpu.HBM)] * 4,
        out_specs=[whole()] * 7,
        out_shape=[
            struct(parts, LANES, members * rows),
            struct(rows, width),
            struct(width, rows),
            struct(width, width),
            struct(width, width),
            struct(count - 1, CANDIDATES, ROWS, LANES),
            struct(2 * ROWS, rows),
        ],
        scratch_shapes=[
            pltpu.VMEM((1, width), F32),
            pltpu.VMEM(w_qkv.shape, BF16),
            pltpu.SMEM(assignment.shape, jnp.int32),
            pltpu.SMEM(neighbours.shape, jnp.int32),
            pltpu.SemaphoreType.DMA((4,)),
        ],
        compiler_params=params(32),
        cost_estimate=cost(5e8, 1e6),
        name="prepare",
    )(own, *in_hbm(gain, w_qkv, assignment, neighbours))
    own, query = lax.optimization_barrier((own, query))
    message = jnp.concatenate([pair, own], axis=0)
    message_a = message
    other_a = other
    inner = exchanged(message_a, 0)
    outer = exchanged(message, 1)
    corner = exchanged(other, 1)
    beside = exchanged(other_a, 0)

    edges, other_m = mixed(blocks_of(ABOVE) + blocks_of(BELOW), "mix_edges", other)
    inner, edges = lax.optimization_barrier((inner, edges))
    top, summed = pl.pallas_call(
        early_kernel,
        in_specs=[whole()] * 11,
        out_specs=[whole()] * 2,
        out_shape=[
            struct(parts, 2, 8, members * rows, dtype=F32),
            struct(parts, LANES, rows, dtype=F32),
        ],
        scratch_shapes=[
            pltpu.VMEM(((1 + EARLY) * rows, width), BF16),
            pltpu.VMEM((parts, LANES + ROWS, (1 + EARLY) * rows), BF16),
        ],
        compiler_params=params(32),
        cost_estimate=cost(3e9, 6e6),
        name="early",
    )(choice, other, pair, inner, outer, gain, wk, wvt, query, key, value)
    state, latent, to_pair, to_other = pl.pallas_call(
        late_kernel,
        in_specs=[whole()] * 15,
        out_specs=[whole()] * 4,
        out_shape=[pltpu.VMEM((rows, width), BF16), struct(rows, channels)]
        + [struct(ROWS, channels)] * 2,
        compiler_params=params(32),
        cost_estimate=cost(3e9, 6e6),
        name="late",
    )(
        choice, cells, inner, outer, beside, corner,
        own, gain, wk, wvt, query, top, summed, w_out, w_latent,
    )

    from_pair = paired(to_pair, 0)
    from_other = paired(to_other, 1)
    middle, latent = mixed(blocks_of(OWN), "mix_own", latent)
    from_pair, middle = lax.optimization_barrier((from_pair, middle))
    extended = jnp.concatenate([latent, from_pair[:SIDE], from_other[:SIDE]], axis=0)
    far = exchanged(extended, 1)
    near = exchanged(extended, 0)

    lanes = -(-(rows + 2 * SIDE) // 256) * 256
    partial, hots, state = pl.pallas_call(
        functools.partial(own_kernel, (rows, 2 * rows, 2 * rows)),
        in_specs=[whole()] * 6,
        out_specs=[whole()] * 3,
        out_shape=[
            struct(lat_rows, outputs, lon_cols, dtype=F32),
            struct(2, 2, TAPS, lanes, lon_cols),
            struct(rows, width),
        ],
        compiler_params=params(32),
        cost_estimate=cost(1e9, 2.5e6),
        name="own_band",
    )(state, own, inner, outer, extended, middle)
    band_scratch = [
        pltpu.VMEM((outputs, TAPS * lanes), BF16),
        pltpu.VMEM((2 * outputs, TAPS * lanes), BF16),
    ]
    partial = pl.pallas_call(
        functools.partial(band_kernel, True),
        in_specs=[whole()] * 4,
        out_specs=whole(),
        out_shape=struct(lat_rows, outputs, lon_cols, dtype=F32),
        scratch_shapes=band_scratch,
        compiler_params=params(32),
        cost_estimate=cost(1e9, 2.5e6),
        name="inner_band",
    )(near, edges, hots, partial)
    fields = pl.pallas_call(
        functools.partial(band_kernel, False),
        in_specs=[whole()] * 4,
        out_specs=whole(),
        out_shape=struct(out_ch, lat_rows, lon_cols),
        scratch_shapes=band_scratch,
        compiler_params=params(32),
        cost_estimate=cost(1e9, 2.5e6),
        name="outer_band",
    )(far, edges, hots, partial)
    return (state.reshape(1, rows, width), fields.reshape(1, out_ch, lat_rows, lon_cols))


def solution(mesh):
    in_specs = (
        P(None, ("reg", "lon"), None),
        P(),
        P(),
        P(),
        P(),
        P(("reg", "lon"), None),
        P("reg", "lon"),
        P(None, "reg", None, None),
        P(),
    )
    out_specs = (P(None, ("reg", "lon"), None), P(None, None, "reg", "lon"))
    return jax.shard_map(shards, mesh=mesh, in_specs=in_specs, out_specs=out_specs, check_vma=False)
```

```python
import functools
import math

import jax
import jax.numpy as jnp
from jax import lax
from jax.experimental import pallas as pl
from jax.experimental.pallas import tpu as pltpu
from jax.sharding import PartitionSpec as P

HEADS = 16
REACH = 2
TAPS = 2 * REACH + 1
SIDE = 8
ROWS = 16
LANES = 128
EARLY = 2
CANDIDATES = 5
F32 = jnp.float32
BF16 = jnp.bfloat16
NT = (((1,), (1,)), ((), ()))

ABOVE = ((-2, (0,)), (-1, (0, 1)))
OWN = ((0, (0, 1)), (1, (0, 1)))
BELOW = ((3, (1,)), (2, (0, 1)))


def blocks_of(band):
    return [
        (out_row, src - out_row + REACH, off)
        for src, out_rows in band
        for off in range(TAPS)
        for out_row in out_rows
    ]


def iota(shape, dim):
    return lax.broadcasted_iota(jnp.int32, shape, dim)


def normalise(rows, gain):
    values = rows.astype(F32)
    center = values - jnp.mean(values, axis=-1, keepdims=True)
    spread = jnp.mean(center * center, axis=-1, keepdims=True)
    return (center * lax.rsqrt(spread + 1e-05) * gain).astype(BF16)


def mix_kernel(blocks, psi_ref, dec_ref, mixed_ref, psi_rows_ref, taps_ref):
    basis, out_ch, channels = dec_ref.shape
    depth = basis * ROWS
    for tap in range(TAPS):
        for off in range(TAPS):
            at = (tap * TAPS + off) * 2
            psi_rows_ref[at : at + 2, :] = psi_ref[tap, off]
    spread = (iota((basis, depth), 1) // ROWS == iota((basis, depth), 0)).astype(F32)
    expanded = jnp.dot(psi_rows_ref[...], spread, preferred_element_type=F32)
    pick = iota((ROWS, depth), 1) % ROWS == iota((ROWS, depth), 0)
    for at, (out_row, tap, off) in enumerate(blocks):
        source = (tap * TAPS + off) * 2 + out_row
        taps = jnp.broadcast_to(expanded[source : source + 1], (ROWS, depth))
        taps_ref[at * ROWS : (at + 1) * ROWS, :] = jnp.where(pick, taps, 0.0).astype(BF16)
    for first in range(0, out_ch, ROWS):
        size = min(ROWS, out_ch - first)
        pieces = []
        for base in range(basis):
            pieces.append(dec_ref[base, first : first + size, :])
            if size < ROWS:
                pieces.append(jnp.zeros((ROWS - size, channels), BF16))
        mixing = jnp.concatenate(pieces, axis=0)
        mixed = jnp.dot(taps_ref[...], mixing, preferred_element_type=F32).astype(BF16)
        mixed_ref[:, first : first + ROWS, :] = mixed.reshape(len(blocks), ROWS, channels)


def listed_blocks(sectors, listed_ref):
    reg_here, lon_here = lax.axis_index("reg"), lax.axis_index("lon")
    toward = 1 - 2 * (reg_here % 2)
    found = []
    for at in range(1, listed_ref.shape[1]):
        block = listed_ref[0, at]
        step_reg = (block // sectors - reg_here) * toward
        step_lon = (block % sectors - lon_here + 1 + sectors) % sectors - 1
        lean = step_lon * (1 - 2 * (lon_here % 2))
        side = jnp.where(lean == 0, 0, jnp.where(lean > 0, 1, 4))
        ahead = jnp.where(lean < 0, 0, 1)
        behind = jnp.where(lean < 0, 7, 4 + side)
        found.append(jnp.where(step_reg == 0, ahead, jnp.where(step_reg > 0, 2 + side, behind)))
    for low in range(len(found)):
        for high in range(low + 1, len(found)):
            less, more = jnp.minimum(found[low], found[high]), jnp.maximum(found[low], found[high])
            found[low], found[high] = less, more
    return found


def gather_kernel(x_hbm, assign_hbm, own_ref, assign_ref, sems):
    rows = own_ref.shape[0] - ROWS
    copies = [
        pltpu.make_async_copy(assign_hbm, assign_ref, sems.at[0]),
        pltpu.make_async_copy(x_hbm, own_ref.at[pl.ds(0, rows)], sems.at[1]),
    ]
    for copy in copies:
        copy.start()
    copies[0].wait()
    local = lax.rem(assign_ref[...], rows).astype(F32)
    line = jnp.concatenate([local[:1], local[1:2]], axis=1)
    line = jnp.broadcast_to(line, (ROWS, line.shape[1]))
    own_ref[rows:] = jnp.where(iota(line.shape, 0) == 0, line, 0.0).astype(BF16)
    copies[1].wait()


def prepare_kernel(
    sectors,
    own_ref, gain_hbm, wqkv_hbm, assign_hbm, listed_hbm,
    query_ref, key_ref, value_ref, wk_ref, wvt_ref, choice_ref, cells_ref,
    gain_ref, wqkv_ref, cell_ref, listed_ref, sems,
):
    copies = [
        pltpu.make_async_copy(source, target, sems.at[at])
        for at, (source, target) in enumerate(
            (
                (gain_hbm, gain_ref),
                (wqkv_hbm, wqkv_ref),
                (assign_hbm, cell_ref),
                (listed_hbm, listed_ref),
            )
        )
    ]
    for copy in copies:
        copy.start()
    rows, width = key_ref.shape
    group, members = query_ref.shape[1], query_ref.shape[2] // rows
    head = group // members
    for copy in copies[2:]:
        copy.wait()
    for at, number in enumerate(listed_blocks(sectors, listed_ref)):
        for candidate in range(CANDIDATES):
            same = jnp.full((ROWS, LANES), jnp.where(number == at + candidate, 1.0, 0.0), F32)
            choice_ref[at, candidate] = same.astype(BF16)
    lat_rows, lon_cols = cell_ref.shape
    place, node = iota((ROWS, rows), 0), iota((ROWS, rows), 1)
    odd = lax.axis_index("lon") % 2
    for side, first in enumerate(((1 - odd) * (lon_cols - REACH), odd * (lon_cols - REACH))):
        hit = jnp.zeros((ROWS, rows), F32)
        for row in range(lat_rows):
            for col in range(REACH):
                cell = cell_ref[row, first + col] % rows
                hit = jnp.where((place == row * REACH + col) & (node == cell), 1.0, hit)
        cells_ref[side * ROWS : (side + 1) * ROWS] = hit.astype(BF16)
    copies[0].wait()
    normed = normalise(own_ref[:rows], gain_ref[...])
    copies[1].wait()
    query = jnp.dot(normed, wqkv_ref[:, :width], preferred_element_type=F32)
    query_t = (query * (math.log2(math.e) / head**0.5)).T.astype(BF16)
    mask = (iota((group, members * rows), 0) // head) == (iota((group, members * rows), 1) // rows)
    for part in range(width // group):
        piece = query_t[part * group : (part + 1) * group]
        wide = jnp.concatenate([piece] * members, axis=1)
        query_ref[part] = jnp.where(mask, wide, jnp.zeros_like(wide))
    wk = wqkv_ref[:, width : 2 * width]
    wk_ref[...] = wk
    key_ref[...] = jnp.dot(normed, wk, preferred_element_type=F32).astype(BF16)
    wvt = wqkv_ref[:, 2 * width :].astype(F32).T.astype(BF16)
    wvt_ref[...] = wvt
    value_ref[...] = lax.dot_general(wvt, normed, NT, preferred_element_type=F32).astype(BF16)


def chosen(entries, rows, choice_ref, candidates):
    tall, wide = rows // ROWS, candidates[-1].shape[1] // LANES
    near = []
    for entry in entries:
        total = None
        for at in range(CANDIDATES):
            weight = jnp.concatenate([choice_ref[entry, at]] * wide, axis=1)
            part = candidates[entry + at] * jnp.concatenate([weight] * tall, axis=0)
            total = part if total is None else total + part
        near.append(total)
    return jnp.concatenate(near, axis=0)


def project(nodes, gain, wk_ref, wvt_ref):
    normed = normalise(nodes, gain)
    keys = jnp.dot(normed, wk_ref[...], preferred_element_type=F32).astype(BF16)
    values = lax.dot_general(wvt_ref[...], normed, NT, preferred_element_type=F32).astype(BF16)
    return keys, values


def own_heads(summed, rows):
    members = summed.shape[1] // rows
    head = summed.shape[0] // members
    return [
        summed[at * head : (at + 1) * head, at * rows : (at + 1) * rows] for at in range(members)
    ]


def early_kernel(
    choice_ref, other_ref, pair_ref, inner_ref, outer_ref,
    gain_ref, wk_ref, wvt_ref, query_ref, key_ref, value_ref,
    top_ref, sum_ref, keys_ref, values_ref,
):
    rows = key_ref.shape[0]
    parts, group, _ = query_ref.shape
    candidates = [other_ref[...], pair_ref[...]]
    candidates += [ref[rows : 2 * rows] if center else ref[:rows] for ref in (inner_ref, outer_ref) for center in (1, 0)]
    nodes = chosen(range(EARLY), rows, choice_ref, candidates)
    keys, values = project(nodes, gain_ref[...], wk_ref, wvt_ref)
    keys_ref[:rows] = key_ref[...]
    keys_ref[rows:] = keys
    for part in range(parts):
        span = slice(part * group, (part + 1) * group)
        values_ref[part, :group, :rows] = value_ref[span]
        values_ref[part, :group, rows:] = values[span]
        values_ref[part, group:, :] = jnp.ones((ROWS, keys_ref.shape[0]), BF16)

    spans = [slice(part * group, (part + 1) * group) for part in range(parts)]
    scores = [
        jnp.dot(keys_ref[:, span], query_ref[part], preferred_element_type=F32)
        for part, span in enumerate(spans)
    ]
    tops = [jnp.max(one, axis=0, keepdims=True) for one in scores]
    expos = [jnp.exp2(one - top).astype(BF16) for one, top in zip(scores, tops)]
    sums = [
        jnp.dot(values_ref[part], expo, preferred_element_type=F32) for part, expo in enumerate(expos)
    ]
    for part, (top, summed) in enumerate(zip(tops, sums)):
        top_ref[part, 0] = jnp.broadcast_to(top, top_ref.shape[2:])
        top_ref[part, 1] = jnp.broadcast_to(summed[group : group + 1], top_ref.shape[2:])
        sum_ref[part] = jnp.concatenate(own_heads(summed[:group], rows), axis=0)


def late_kernel(
    choice_ref, cells_ref, inner_ref, outer_ref, beside_ref, corner_ref,
    own_ref, gain_ref, wk_ref, wvt_ref, query_ref, top_ref, sum_ref, wout_ref, wlat_ref,
    state_ref, latent_ref, to_pair_ref, to_other_ref,
):
    rows, width = state_ref.shape
    parts, group, lanes = query_ref.shape
    members = lanes // rows
    head = group // members
    candidates = [None, None]
    candidates += [ref[rows : 2 * rows] if center else ref[:rows] for ref in (inner_ref, outer_ref) for center in (1, 0)]
    candidates += [beside_ref[...], corner_ref[...]]
    nodes = chosen(range(EARLY, choice_ref.shape[0]), rows, choice_ref, candidates)
    keys, values = project(nodes, gain_ref[...], wk_ref, wvt_ref)
    ones = jnp.ones((ROWS, nodes.shape[0]), BF16)
    spans = [slice(part * group, (part + 1) * group) for part in range(parts)]
    scores = [
        jnp.dot(keys[:, span], query_ref[part], preferred_element_type=F32)
        for part, span in enumerate(spans)
    ]
    befores = [top_ref[part, 0, :1] for part in range(parts)]
    tops = [
        jnp.maximum(before, jnp.max(one, axis=0, keepdims=True))
        for before, one in zip(befores, scores)
    ]
    expos = [jnp.exp2(one - top).astype(BF16) for one, top in zip(scores, tops)]
    sums = [
        jnp.dot(jnp.concatenate([values[span], ones], axis=0), expo, preferred_element_type=F32)
        for span, expo in zip(spans, expos)
    ]
    attended = []
    for part, summed in enumerate(sums):
        shrink = jnp.exp2(befores[part] - tops[part])
        share = 1.0 / (summed[group : group + 1] + top_ref[part, 1, :1] * shrink)
        merged = []
        for member, piece in enumerate(own_heads(summed[:group], rows)):
            span = slice(member * rows, (member + 1) * rows)
            earlier = sum_ref[part, member * head : (member + 1) * head]
            merged.append((piece + earlier * shrink[:, span]) * share[:, span])
        attended.append(jnp.concatenate(merged, axis=0).T.astype(BF16))
    attended = jnp.concatenate(attended, axis=1)
    state = (
        own_ref[:rows].astype(F32)
        + jnp.dot(attended, wout_ref[...], preferred_element_type=F32)
    ).astype(BF16)
    state_ref[...] = state
    value = jnp.dot(state, wlat_ref[...], preferred_element_type=F32)
    latent = (value / (1.0 + jnp.exp(-value))).astype(BF16)
    latent_ref[...] = latent
    cells = jnp.dot(cells_ref[...], latent, preferred_element_type=F32).astype(BF16)
    to_pair_ref[...] = cells[:ROWS]
    to_other_ref[...] = cells[ROWS:]


def hot_rows(values, rows, cols, line):
    odd = lax.axis_index("lon") % 2
    column = iota((8, cols), 1)
    node = iota((rows + 2 * SIDE, cols), 0).astype(F32)
    for off in range(TAPS):
        step = off - REACH
        where = jnp.broadcast_to(values, (8, cols))
        if step:
            where = pltpu.roll(where, (-step) % cols, 1)
        reach = column + step
        before = (rows + (1 - odd) * SIDE + REACH * line + reach + REACH).astype(F32)
        after = (rows + odd * SIDE + REACH * line + reach - cols).astype(F32)
        where = jnp.where(reach < 0, before, jnp.where(reach >= cols, after, where))
        yield jnp.where(node == where[:1], 1.0, 0.0).astype(BF16)


def shares_of(latent, weights):
    blocks, outputs, channels = weights.shape
    shares = lax.dot_general(
        weights.reshape(blocks * outputs, channels), latent, NT, preferred_element_type=F32
    ).astype(BF16)
    return [shares[at * outputs : (at + 1) * outputs] for at in range(blocks)]


def lines_of(line_ref, start, cols):
    values = line_ref[start : start + ROWS, :].astype(F32)
    return values[:1, :cols], values[:1, cols:]


def own_kernel(
    begin, state_ref, own_ref, inner_ref, outer_ref, latent_ref, weights_ref,
    out_ref, hot_ref, kept_ref,
):
    kept_ref[...] = state_ref[...]
    cols = out_ref.shape[2]
    rows = latent_ref.shape[0] - 2 * SIDE
    own = lines_of(own_ref, begin[0], cols)
    table = [list(hot_rows(own[line], rows, cols, line)) for line in range(2)]
    acc = [None, None]
    for (out_row, tap, off), share in zip(
        blocks_of(OWN), shares_of(latent_ref[...], weights_ref[...])
    ):
        line = out_row + tap - REACH
        piece = jnp.dot(share, table[line][off], preferred_element_type=F32)
        acc[out_row] = piece if acc[out_row] is None else acc[out_row] + piece
    for row in range(2):
        out_ref[row] = acc[row]
    odd = lax.axis_index("reg") % 2 == 1
    inner, outer = lines_of(inner_ref, begin[1], cols), lines_of(outer_ref, begin[2], cols)
    nodes = rows + 2 * SIDE
    for band, (yes, no) in enumerate(((inner, outer), (outer, inner))):
        for at, line in enumerate((0, 1) if band == 0 else (1, 0)):
            values = jnp.where(odd, yes[line], no[line])
            for off, hot in enumerate(hot_rows(values, rows, cols, line)):
                hot_ref[band, at, off, :nodes] = hot
                hot_ref[band, at, off, nodes:] = jnp.zeros((hot_ref.shape[3] - nodes, cols), BF16)


def band_kernel(
    from_inner, latent_ref, weights_ref, hot_ref, partial_ref, out_ref, one_ref, two_ref, paired_ref
):
    odd = lax.axis_index("reg") % 2
    band = 1 - odd if from_inner else odd
    latent = latent_ref[...]
    lanes, cols = hot_ref.shape[3:]
    outputs = weights_ref.shape[1]
    blank = jnp.zeros((lanes - latent.shape[0], latent.shape[1]), BF16)
    blocks = len(blocks_of(ABOVE))
    weights = weights_ref[pl.ds(band * blocks, blocks)]
    shares = shares_of(jnp.concatenate([latent, blank], axis=0), weights)
    for off in range(TAPS):
        span = slice(off * lanes, (off + 1) * lanes)
        one_ref[:, span] = shares[off]
        for row in range(2):
            two_ref[row * outputs : (row + 1) * outputs, span] = shares[TAPS + 2 * off + row]
    depth = TAPS * lanes
    one = jnp.dot(one_ref[...], hot_ref[band, 0].reshape(depth, cols), preferred_element_type=F32)
    two = jnp.dot(two_ref[...], hot_ref[band, 1].reshape(depth, cols), preferred_element_type=F32)
    for row in range(2):
        total = partial_ref[row] + two[row * outputs : (row + 1) * outputs]
        total = total + jnp.where(band == row, one, 0.0)
        if from_inner:
            out_ref[row] = total
        else:
            for tile in range(cols // LANES):
                part = total[:, tile * LANES : (tile + 1) * LANES]
                paired_ref[tile, pl.ds(row, outputs, stride=2), :] = part
    if not from_inner:
        out_ch = out_ref.shape[0]
        tiles = [paired_ref[tile, : 2 * out_ch, :] for tile in range(cols // LANES)]
        out_ref[...] = jnp.concatenate(tiles, axis=1).astype(BF16).reshape(out_ref.shape)


def whole(memory=pltpu.VMEM):
    return pl.BlockSpec(memory_space=memory)


def struct(*shape, dtype=BF16):
    return jax.ShapeDtypeStruct(shape, dtype)


def params(limit):
    return pltpu.CompilerParams(vmem_limit_bytes=limit << 20)


def cost(flops, moved):
    return pl.CostEstimate(flops=int(flops), bytes_accessed=int(moved), transcendentals=0)


def shards(nodes, norm_gain, w_qkv, w_out, w_latent, neighbours, assignment, psi, w_dec):
    _, rows, width = nodes.shape
    channels = w_latent.shape[1]
    lat_rows, lon_cols = assignment.shape
    basis, _, out_ch = w_dec.shape
    sectors = lax.axis_size("lon")
    count = neighbours.shape[1]
    x = nodes.reshape(rows, width)
    gain = norm_gain.reshape(1, width)

    def paired(array, first):
        pairs = [(i, (i + 1) % sectors) for i in range(first, sectors, 2)]
        return lax.ppermute(array, "lon", pairs + [(j, i) for i, j in pairs])

    def exchanged(array, first):
        size = lax.axis_size("reg")
        pairs = [(i, i + 1) for i in range(first, size - 1, 2)]
        return lax.ppermute(array, "reg", pairs + [(j, i) for i, j in pairs])

    def in_hbm(*arrays):
        return [pltpu.with_memory_space_constraint(array, pltpu.HBM) for array in arrays]

    other = paired(x, 1)
    pair = paired(x, 0)

    outputs = -(-out_ch // ROWS) * ROWS
    head = width // HEADS
    members = LANES // head
    parts = HEADS // members
    def mixed(blocks, name, after):
        taps = psi.transpose(2, 3, 1, 0)
        mixing = w_dec.transpose(0, 2, 1)
        taps, mixing, after = lax.optimization_barrier((taps, mixing, after))
        weights = pl.pallas_call(
            functools.partial(mix_kernel, blocks),
            in_specs=[whole()] * 2,
            out_specs=whole(),
            out_shape=struct(len(blocks), outputs, channels),
            scratch_shapes=[
                pltpu.VMEM((2 * TAPS * TAPS, basis), F32),
                pltpu.VMEM((len(blocks) * ROWS, basis * ROWS), BF16),
            ],
            compiler_params=params(32),
            cost_estimate=cost(2e9, 6e6),
            name=name,
        )(taps, mixing)
        return weights, after

    own = pl.pallas_call(
        gather_kernel,
        in_specs=[whole(pltpu.HBM)] * 2,
        out_specs=whole(),
        out_shape=struct(rows + ROWS, width),
        scratch_shapes=[
            pltpu.VMEM(assignment.shape, jnp.int32),
            pltpu.SemaphoreType.DMA((2,)),
        ],
        compiler_params=params(32),
        cost_estimate=cost(1e3, 1e3),
        name="gather",
    )(*in_hbm(x, assignment))
    query, key, value, wk, wvt, choice, cells = pl.pallas_call(
        functools.partial(prepare_kernel, sectors),
        in_specs=[whole()] + [whole(pltpu.HBM)] * 4,
        out_specs=[whole()] * 7,
        out_shape=[
            struct(parts, LANES, members * rows),
            struct(rows, width),
            struct(width, rows),
            struct(width, width),
            struct(width, width),
            struct(count - 1, CANDIDATES, ROWS, LANES),
            struct(2 * ROWS, rows),
        ],
        scratch_shapes=[
            pltpu.VMEM((1, width), F32),
            pltpu.VMEM(w_qkv.shape, BF16),
            pltpu.SMEM(assignment.shape, jnp.int32),
            pltpu.SMEM(neighbours.shape, jnp.int32),
            pltpu.SemaphoreType.DMA((4,)),
        ],
        compiler_params=params(32),
        cost_estimate=cost(5e8, 1e6),
        name="prepare",
    )(own, *in_hbm(gain, w_qkv, assignment, neighbours))
    own, query = lax.optimization_barrier((own, query))
    message = jnp.concatenate([pair, own], axis=0)
    message_a = message
    other_a = other
    inner = exchanged(message_a, 0)
    outer = exchanged(message, 1)
    corner = exchanged(other, 1)
    beside = exchanged(other_a, 0)

    edges, other_m = mixed(blocks_of(ABOVE) + blocks_of(BELOW), "mix_edges", other)
    inner, edges = lax.optimization_barrier((inner, edges))
    top, summed = pl.pallas_call(
        early_kernel,
        in_specs=[whole()] * 11,
        out_specs=[whole()] * 2,
        out_shape=[
            struct(parts, 2, 8, members * rows, dtype=F32),
            struct(parts, LANES, rows, dtype=F32),
        ],
        scratch_shapes=[
            pltpu.VMEM(((1 + EARLY) * rows, width), BF16),
            pltpu.VMEM((parts, LANES + ROWS, (1 + EARLY) * rows), BF16),
        ],
        compiler_params=params(32),
        cost_estimate=cost(3e9, 6e6),
        name="early",
    )(choice, other, pair, inner, outer, gain, wk, wvt, query, key, value)
    state, latent, to_pair, to_other = pl.pallas_call(
        late_kernel,
        in_specs=[whole()] * 15,
        out_specs=[whole()] * 4,
        out_shape=[pltpu.VMEM((rows, width), BF16), struct(rows, channels)]
        + [struct(ROWS, channels)] * 2,
        compiler_params=params(32),
        cost_estimate=cost(3e9, 6e6),
        name="late",
    )(
        choice, cells, inner, outer, beside, corner,
        own, gain, wk, wvt, query, top, summed, w_out, w_latent,
    )

    from_pair = paired(to_pair, 0)
    from_other = paired(to_other, 1)
    middle, latent = mixed(blocks_of(OWN), "mix_own", latent)
    from_pair, middle = lax.optimization_barrier((from_pair, middle))
    extended = jnp.concatenate([latent, from_pair[:SIDE], from_other[:SIDE]], axis=0)
    far = exchanged(extended, 1)
    near = exchanged(extended, 0)

    lanes = -(-(rows + 2 * SIDE) // 256) * 256
    partial, hots, state = pl.pallas_call(
        functools.partial(own_kernel, (rows, 2 * rows, 2 * rows)),
        in_specs=[whole()] * 6,
        out_specs=[whole()] * 3,
        out_shape=[
            struct(lat_rows, outputs, lon_cols, dtype=F32),
            struct(2, 2, TAPS, lanes, lon_cols),
            struct(rows, width),
        ],
        compiler_params=params(32),
        cost_estimate=cost(1e9, 2.5e6),
        name="own_band",
    )(state, own, inner, outer, extended, middle)
    band_scratch = [
        pltpu.VMEM((outputs, TAPS * lanes), BF16),
        pltpu.VMEM((2 * outputs, TAPS * lanes), BF16),
        pltpu.VMEM((lon_cols // LANES, 2 * outputs, LANES), F32),
    ]
    partial = pl.pallas_call(
        functools.partial(band_kernel, True),
        in_specs=[whole()] * 4,
        out_specs=whole(),
        out_shape=struct(lat_rows, outputs, lon_cols, dtype=F32),
        scratch_shapes=band_scratch,
        compiler_params=params(32),
        cost_estimate=cost(1e9, 2.5e6),
        name="inner_band",
    )(near, edges, hots, partial)
    fields = pl.pallas_call(
        functools.partial(band_kernel, False),
        in_specs=[whole()] * 4,
        out_specs=whole(),
        out_shape=struct(out_ch, lat_rows, lon_cols),
        scratch_shapes=band_scratch,
        compiler_params=params(32),
        cost_estimate=cost(1e9, 2.5e6),
        name="outer_band",
    )(far, edges, hots, partial)
    return (state.reshape(1, rows, width), fields.reshape(1, out_ch, lat_rows, lon_cols))


def solution(mesh):
    in_specs = (
        P(None, ("reg", "lon"), None),
        P(),
        P(),
        P(),
        P(),
        P(("reg", "lon"), None),
        P("reg", "lon"),
        P(None, "reg", None, None),
        P(),
    )
    out_specs = (P(None, ("reg", "lon"), None), P(None, None, "reg", "lon"))
    return jax.shard_map(shards, mesh=mesh, in_specs=in_specs, out_specs=out_specs, check_vma=False)
```

```python
import functools
import math

import jax
import jax.numpy as jnp
from jax import lax
from jax.experimental import pallas as pl
from jax.experimental.pallas import tpu as pltpu
from jax.sharding import PartitionSpec as P

HEADS = 16
REACH = 2
TAPS = 2 * REACH + 1
SIDE = 8
ROWS = 16
LANES = 128
EARLY = 2
CANDIDATES = 5
F32 = jnp.float32
BF16 = jnp.bfloat16
NT = (((1,), (1,)), ((), ()))

ABOVE = ((-2, (0,)), (-1, (0, 1)))
OWN = ((0, (0, 1)), (1, (0, 1)))
BELOW = ((3, (1,)), (2, (0, 1)))


def blocks_of(band):
    return [
        (out_row, src - out_row + REACH, off)
        for src, out_rows in band
        for off in range(TAPS)
        for out_row in out_rows
    ]


def iota(shape, dim):
    return lax.broadcasted_iota(jnp.int32, shape, dim)


def normalise(rows, gain):
    values = rows.astype(F32)
    center = values - jnp.mean(values, axis=-1, keepdims=True)
    spread = jnp.mean(center * center, axis=-1, keepdims=True)
    return (center * lax.rsqrt(spread + 1e-05) * gain).astype(BF16)


def mix_kernel(blocks, psi_ref, dec_ref, mixed_ref, psi_rows_ref, taps_ref):
    basis, out_ch, channels = dec_ref.shape
    depth = basis * ROWS
    for tap in range(TAPS):
        for off in range(TAPS):
            at = (tap * TAPS + off) * 2
            psi_rows_ref[at : at + 2, :] = psi_ref[tap, off]
    spread = (iota((basis, depth), 1) // ROWS == iota((basis, depth), 0)).astype(F32)
    expanded = jnp.dot(psi_rows_ref[...], spread, preferred_element_type=F32)
    pick = iota((ROWS, depth), 1) % ROWS == iota((ROWS, depth), 0)
    for at, (out_row, tap, off) in enumerate(blocks):
        source = (tap * TAPS + off) * 2 + out_row
        taps = jnp.broadcast_to(expanded[source : source + 1], (ROWS, depth))
        taps_ref[at * ROWS : (at + 1) * ROWS, :] = jnp.where(pick, taps, 0.0).astype(BF16)
    for first in range(0, out_ch, ROWS):
        size = min(ROWS, out_ch - first)
        pieces = []
        for base in range(basis):
            pieces.append(dec_ref[base, first : first + size, :])
            if size < ROWS:
                pieces.append(jnp.zeros((ROWS - size, channels), BF16))
        mixing = jnp.concatenate(pieces, axis=0)
        mixed = jnp.dot(taps_ref[...], mixing, preferred_element_type=F32).astype(BF16)
        mixed_ref[:, first : first + ROWS, :] = mixed.reshape(len(blocks), ROWS, channels)


def listed_blocks(sectors, listed_ref):
    reg_here, lon_here = lax.axis_index("reg"), lax.axis_index("lon")
    toward = 1 - 2 * (reg_here % 2)
    found = []
    for at in range(1, listed_ref.shape[1]):
        block = listed_ref[0, at]
        step_reg = (block // sectors - reg_here) * toward
        step_lon = (block % sectors - lon_here + 1 + sectors) % sectors - 1
        lean = step_lon * (1 - 2 * (lon_here % 2))
        side = jnp.where(lean == 0, 0, jnp.where(lean > 0, 1, 4))
        ahead = jnp.where(lean < 0, 0, 1)
        behind = jnp.where(lean < 0, 7, 4 + side)
        found.append(jnp.where(step_reg == 0, ahead, jnp.where(step_reg > 0, 2 + side, behind)))
    for low in range(len(found)):
        for high in range(low + 1, len(found)):
            less, more = jnp.minimum(found[low], found[high]), jnp.maximum(found[low], found[high])
            found[low], found[high] = less, more
    return found


def gather_kernel(x_hbm, assign_hbm, own_ref, assign_ref, sems):
    rows = own_ref.shape[0] - ROWS
    copies = [
        pltpu.make_async_copy(assign_hbm, assign_ref, sems.at[0]),
        pltpu.make_async_copy(x_hbm, own_ref.at[pl.ds(0, rows)], sems.at[1]),
    ]
    for copy in copies:
        copy.start()
    copies[0].wait()
    local = lax.rem(assign_ref[...], rows).astype(F32)
    line = jnp.concatenate([local[:1], local[1:2]], axis=1)
    line = jnp.broadcast_to(line, (ROWS, line.shape[1]))
    own_ref[rows:] = jnp.where(iota(line.shape, 0) == 0, line, 0.0).astype(BF16)
    copies[1].wait()


def prepare_kernel(
    sectors,
    own_ref, gain_hbm, wqkv_hbm, assign_hbm, listed_hbm,
    query_ref, key_ref, value_ref, wk_ref, wvt_ref, choice_ref, cells_ref,
    gain_ref, wqkv_ref, cell_ref, listed_ref, sems,
):
    copies = [
        pltpu.make_async_copy(source, target, sems.at[at])
        for at, (source, target) in enumerate(
            (
                (gain_hbm, gain_ref),
                (wqkv_hbm, wqkv_ref),
                (assign_hbm, cell_ref),
                (listed_hbm, listed_ref),
            )
        )
    ]
    for copy in copies:
        copy.start()
    rows, width = key_ref.shape
    group, members = query_ref.shape[1], query_ref.shape[2] // rows
    head = group // members
    for copy in copies[2:]:
        copy.wait()
    for at, number in enumerate(listed_blocks(sectors, listed_ref)):
        for candidate in range(CANDIDATES):
            same = jnp.full((ROWS, LANES), jnp.where(number == at + candidate, 1.0, 0.0), F32)
            choice_ref[at, candidate] = same.astype(BF16)
    lat_rows, lon_cols = cell_ref.shape
    place, node = iota((ROWS, rows), 0), iota((ROWS, rows), 1)
    odd = lax.axis_index("lon") % 2
    for side, first in enumerate(((1 - odd) * (lon_cols - REACH), odd * (lon_cols - REACH))):
        hit = jnp.zeros((ROWS, rows), F32)
        for row in range(lat_rows):
            for col in range(REACH):
                cell = cell_ref[row, first + col] % rows
                hit = jnp.where((place == row * REACH + col) & (node == cell), 1.0, hit)
        cells_ref[side * ROWS : (side + 1) * ROWS] = hit.astype(BF16)
    copies[0].wait()
    normed = normalise(own_ref[:rows], gain_ref[...])
    copies[1].wait()
    query = jnp.dot(normed, wqkv_ref[:, :width], preferred_element_type=F32)
    query_t = (query * (math.log2(math.e) / head**0.5)).T.astype(BF16)
    mask = (iota((group, members * rows), 0) // head) == (iota((group, members * rows), 1) // rows)
    for part in range(width // group):
        piece = query_t[part * group : (part + 1) * group]
        wide = jnp.concatenate([piece] * members, axis=1)
        query_ref[part] = jnp.where(mask, wide, jnp.zeros_like(wide))
    wk = wqkv_ref[:, width : 2 * width]
    wk_ref[...] = wk
    key_ref[...] = jnp.dot(normed, wk, preferred_element_type=F32).astype(BF16)
    wvt = wqkv_ref[:, 2 * width :].astype(F32).T.astype(BF16)
    wvt_ref[...] = wvt
    value_ref[...] = lax.dot_general(wvt, normed, NT, preferred_element_type=F32).astype(BF16)


def chosen(entries, rows, choice_ref, candidates):
    tall, wide = rows // ROWS, candidates[-1].shape[1] // LANES
    near = []
    for entry in entries:
        total = None
        for at in range(CANDIDATES):
            weight = jnp.concatenate([choice_ref[entry, at]] * wide, axis=1)
            part = candidates[entry + at] * jnp.concatenate([weight] * tall, axis=0)
            total = part if total is None else total + part
        near.append(total)
    return jnp.concatenate(near, axis=0)


def project(nodes, gain, wk_ref, wvt_ref):
    normed = normalise(nodes, gain)
    keys = jnp.dot(normed, wk_ref[...], preferred_element_type=F32).astype(BF16)
    values = lax.dot_general(wvt_ref[...], normed, NT, preferred_element_type=F32).astype(BF16)
    return keys, values


def own_heads(summed, rows):
    members = summed.shape[1] // rows
    head = summed.shape[0] // members
    return [
        summed[at * head : (at + 1) * head, at * rows : (at + 1) * rows] for at in range(members)
    ]


def early_kernel(
    choice_ref, other_ref, pair_ref, inner_ref, outer_ref,
    gain_ref, wk_ref, wvt_ref, query_ref, key_ref, value_ref,
    top_ref, sum_ref, keys_ref, values_ref,
):
    rows = key_ref.shape[0]
    parts, group, _ = query_ref.shape
    candidates = [other_ref[...], pair_ref[...]]
    candidates += [ref[rows : 2 * rows] if center else ref[:rows] for ref in (inner_ref, outer_ref) for center in (1, 0)]
    nodes = chosen(range(EARLY), rows, choice_ref, candidates)
    keys, values = project(nodes, gain_ref[...], wk_ref, wvt_ref)
    keys_ref[:rows] = key_ref[...]
    keys_ref[rows:] = keys
    for part in range(parts):
        span = slice(part * group, (part + 1) * group)
        values_ref[part, :group, :rows] = value_ref[span]
        values_ref[part, :group, rows:] = values[span]
        values_ref[part, group:, :] = jnp.ones((ROWS, keys_ref.shape[0]), BF16)

    spans = [slice(part * group, (part + 1) * group) for part in range(parts)]
    scores = [
        jnp.dot(keys_ref[:, span], query_ref[part], preferred_element_type=F32)
        for part, span in enumerate(spans)
    ]
    tops = [jnp.max(one, axis=0, keepdims=True) for one in scores]
    expos = [jnp.exp2(one - top).astype(BF16) for one, top in zip(scores, tops)]
    sums = [
        jnp.dot(values_ref[part], expo, preferred_element_type=F32) for part, expo in enumerate(expos)
    ]
    for part, (top, summed) in enumerate(zip(tops, sums)):
        top_ref[part, 0] = jnp.broadcast_to(top, top_ref.shape[2:])
        top_ref[part, 1] = jnp.broadcast_to(summed[group : group + 1], top_ref.shape[2:])
        sum_ref[part] = jnp.concatenate(own_heads(summed[:group], rows), axis=0)


def late_kernel(
    choice_ref, cells_ref, inner_ref, outer_ref, beside_ref, corner_ref,
    own_ref, gain_ref, wk_ref, wvt_ref, query_ref, top_ref, sum_ref, wout_ref, wlat_ref,
    state_ref, latent_ref, to_pair_ref, to_other_ref,
):
    rows, width = state_ref.shape
    parts, group, lanes = query_ref.shape
    members = lanes // rows
    head = group // members
    candidates = [None, None]
    candidates += [ref[rows : 2 * rows] if center else ref[:rows] for ref in (inner_ref, outer_ref) for center in (1, 0)]
    candidates += [beside_ref[...], corner_ref[...]]
    nodes = chosen(range(EARLY, choice_ref.shape[0]), rows, choice_ref, candidates)
    keys, values = project(nodes, gain_ref[...], wk_ref, wvt_ref)
    ones = jnp.ones((ROWS, nodes.shape[0]), BF16)
    spans = [slice(part * group, (part + 1) * group) for part in range(parts)]
    scores = [
        jnp.dot(keys[:, span], query_ref[part], preferred_element_type=F32)
        for part, span in enumerate(spans)
    ]
    befores = [top_ref[part, 0, :1] for part in range(parts)]
    tops = [
        jnp.maximum(before, jnp.max(one, axis=0, keepdims=True))
        for before, one in zip(befores, scores)
    ]
    expos = [jnp.exp2(one - top).astype(BF16) for one, top in zip(scores, tops)]
    sums = [
        jnp.dot(jnp.concatenate([values[span], ones], axis=0), expo, preferred_element_type=F32)
        for span, expo in zip(spans, expos)
    ]
    attended = []
    for part, summed in enumerate(sums):
        shrink = jnp.exp2(befores[part] - tops[part])
        share = 1.0 / (summed[group : group + 1] + top_ref[part, 1, :1] * shrink)
        merged = []
        for member, piece in enumerate(own_heads(summed[:group], rows)):
            span = slice(member * rows, (member + 1) * rows)
            earlier = sum_ref[part, member * head : (member + 1) * head]
            merged.append((piece + earlier * shrink[:, span]) * share[:, span])
        attended.append(jnp.concatenate(merged, axis=0).T.astype(BF16))
    attended = jnp.concatenate(attended, axis=1)
    state = (
        own_ref[:rows].astype(F32)
        + jnp.dot(attended, wout_ref[...], preferred_element_type=F32)
    ).astype(BF16)
    state_ref[...] = state
    value = jnp.dot(state, wlat_ref[...], preferred_element_type=F32)
    latent = (value / (1.0 + jnp.exp(-value))).astype(BF16)
    latent_ref[...] = latent
    cells = jnp.dot(cells_ref[...], latent, preferred_element_type=F32).astype(BF16)
    to_pair_ref[...] = cells[:ROWS]
    to_other_ref[...] = cells[ROWS:]


def hot_rows(values, rows, cols, line):
    odd = lax.axis_index("lon") % 2
    column = iota((8, cols), 1)
    node = iota((rows + 2 * SIDE, cols), 0).astype(F32)
    for off in range(TAPS):
        step = off - REACH
        where = jnp.broadcast_to(values, (8, cols))
        if step:
            where = pltpu.roll(where, (-step) % cols, 1)
        reach = column + step
        before = (rows + (1 - odd) * SIDE + REACH * line + reach + REACH).astype(F32)
        after = (rows + odd * SIDE + REACH * line + reach - cols).astype(F32)
        where = jnp.where(reach < 0, before, jnp.where(reach >= cols, after, where))
        yield jnp.where(node == where[:1], 1.0, 0.0).astype(BF16)


def shares_of(latent, weights):
    blocks, outputs, channels = weights.shape
    shares = lax.dot_general(
        weights.reshape(blocks * outputs, channels), latent, NT, preferred_element_type=F32
    ).astype(BF16)
    return [shares[at * outputs : (at + 1) * outputs] for at in range(blocks)]


def lines_of(line_ref, start, cols):
    values = line_ref[start : start + ROWS, :].astype(F32)
    return values[:1, :cols], values[:1, cols:]


def own_kernel(
    begin, state_ref, own_ref, inner_ref, outer_ref, latent_ref, weights_ref,
    out_ref, hot_ref, kept_ref,
):
    kept_ref[...] = state_ref[...]
    cols = out_ref.shape[2]
    rows = latent_ref.shape[0] - 2 * SIDE
    own = lines_of(own_ref, begin[0], cols)
    table = [list(hot_rows(own[line], rows, cols, line)) for line in range(2)]
    acc = [None, None]
    for (out_row, tap, off), share in zip(
        blocks_of(OWN), shares_of(latent_ref[...], weights_ref[...])
    ):
        line = out_row + tap - REACH
        piece = jnp.dot(share, table[line][off], preferred_element_type=F32)
        acc[out_row] = piece if acc[out_row] is None else acc[out_row] + piece
    for row in range(2):
        out_ref[row] = acc[row]
    odd = lax.axis_index("reg") % 2 == 1
    inner, outer = lines_of(inner_ref, begin[1], cols), lines_of(outer_ref, begin[2], cols)
    nodes = rows + 2 * SIDE
    for band, (yes, no) in enumerate(((inner, outer), (outer, inner))):
        for at, line in enumerate((0, 1) if band == 0 else (1, 0)):
            values = jnp.where(odd, yes[line], no[line])
            for off, hot in enumerate(hot_rows(values, rows, cols, line)):
                hot_ref[band, at, off, :nodes] = hot
                hot_ref[band, at, off, nodes:] = jnp.zeros((hot_ref.shape[3] - nodes, cols), BF16)


def band_kernel(
    from_inner, latent_ref, weights_ref, hot_ref, partial_ref, out_ref, one_ref, two_ref, paired_ref
):
    odd = lax.axis_index("reg") % 2
    band = 1 - odd if from_inner else odd
    latent = latent_ref[...]
    lanes, cols = hot_ref.shape[3:]
    outputs = weights_ref.shape[1]
    blank = jnp.zeros((lanes - latent.shape[0], latent.shape[1]), BF16)
    blocks = len(blocks_of(ABOVE))
    weights = weights_ref[pl.ds(band * blocks, blocks)]
    shares = shares_of(jnp.concatenate([latent, blank], axis=0), weights)
    for off in range(TAPS):
        span = slice(off * lanes, (off + 1) * lanes)
        one_ref[:, span] = shares[off]
        for row in range(2):
            two_ref[row * outputs : (row + 1) * outputs, span] = shares[TAPS + 2 * off + row]
    depth = TAPS * lanes
    one = jnp.dot(one_ref[...], hot_ref[band, 0].reshape(depth, cols), preferred_element_type=F32)
    two = jnp.dot(two_ref[...], hot_ref[band, 1].reshape(depth, cols), preferred_element_type=F32)
    for row in range(2):
        total = partial_ref[row] + two[row * outputs : (row + 1) * outputs]
        total = total + jnp.where(band == row, one, 0.0)
        if from_inner:
            out_ref[row] = total
        else:
            for tile in range(cols // LANES):
                part = total[:, tile * LANES : (tile + 1) * LANES]
                paired_ref[tile, pl.ds(row, outputs, stride=2), :] = part
    if not from_inner:
        out_ch = out_ref.shape[0]
        tiles = [paired_ref[tile, : 2 * out_ch, :] for tile in range(cols // LANES)]
        out_ref[...] = jnp.concatenate(tiles, axis=1).astype(BF16).reshape(out_ref.shape)


def whole(memory=pltpu.VMEM):
    return pl.BlockSpec(memory_space=memory)


def struct(*shape, dtype=BF16):
    return jax.ShapeDtypeStruct(shape, dtype)


def params(limit):
    return pltpu.CompilerParams(vmem_limit_bytes=limit << 20)


def cost(flops, moved):
    return pl.CostEstimate(flops=int(flops), bytes_accessed=int(moved), transcendentals=0)


def shards(nodes, norm_gain, w_qkv, w_out, w_latent, neighbours, assignment, psi, w_dec):
    _, rows, width = nodes.shape
    channels = w_latent.shape[1]
    lat_rows, lon_cols = assignment.shape
    basis, _, out_ch = w_dec.shape
    sectors = lax.axis_size("lon")
    count = neighbours.shape[1]
    x = nodes.reshape(rows, width)
    gain = norm_gain.reshape(1, width)

    def paired(array, first):
        pairs = [(i, (i + 1) % sectors) for i in range(first, sectors, 2)]
        return lax.ppermute(array, "lon", pairs + [(j, i) for i, j in pairs])

    def exchanged(array, first):
        size = lax.axis_size("reg")
        pairs = [(i, i + 1) for i in range(first, size - 1, 2)]
        return lax.ppermute(array, "reg", pairs + [(j, i) for i, j in pairs])

    def in_hbm(*arrays):
        return [pltpu.with_memory_space_constraint(array, pltpu.HBM) for array in arrays]

    other = paired(x, 1)
    pair = paired(x, 0)

    outputs = -(-out_ch // ROWS) * ROWS
    head = width // HEADS
    members = LANES // head
    parts = HEADS // members
    def mixed(blocks, name, after):
        taps = psi.transpose(2, 3, 1, 0)
        mixing = w_dec.transpose(0, 2, 1)
        taps, mixing, after = lax.optimization_barrier((taps, mixing, after))
        weights = pl.pallas_call(
            functools.partial(mix_kernel, blocks),
            in_specs=[whole()] * 2,
            out_specs=whole(),
            out_shape=struct(len(blocks), outputs, channels),
            scratch_shapes=[
                pltpu.VMEM((2 * TAPS * TAPS, basis), F32),
                pltpu.VMEM((len(blocks) * ROWS, basis * ROWS), BF16),
            ],
            compiler_params=params(32),
            cost_estimate=cost(2e9, 6e6),
            name=name,
        )(taps, mixing)
        return weights, after

    own = pl.pallas_call(
        gather_kernel,
        in_specs=[whole(pltpu.HBM)] * 2,
        out_specs=whole(),
        out_shape=struct(rows + ROWS, width),
        scratch_shapes=[
            pltpu.VMEM(assignment.shape, jnp.int32),
            pltpu.SemaphoreType.DMA((2,)),
        ],
        compiler_params=params(32),
        cost_estimate=cost(1e3, 1e3),
        name="gather",
    )(*in_hbm(x, assignment))
    query, key, value, wk, wvt, choice, cells = pl.pallas_call(
        functools.partial(prepare_kernel, sectors),
        in_specs=[whole()] + [whole(pltpu.HBM)] * 4,
        out_specs=[whole()] * 7,
        out_shape=[
            struct(parts, LANES, members * rows),
            struct(rows, width),
            struct(width, rows),
            struct(width, width),
            struct(width, width),
            struct(count - 1, CANDIDATES, ROWS, LANES),
            struct(2 * ROWS, rows),
        ],
        scratch_shapes=[
            pltpu.VMEM((1, width), F32),
            pltpu.VMEM(w_qkv.shape, BF16),
            pltpu.SMEM(assignment.shape, jnp.int32),
            pltpu.SMEM(neighbours.shape, jnp.int32),
            pltpu.SemaphoreType.DMA((4,)),
        ],
        compiler_params=params(32),
        cost_estimate=cost(5e8, 1e6),
        name="prepare",
    )(own, *in_hbm(gain, w_qkv, assignment, neighbours))
    own, query = lax.optimization_barrier((own, query))
    message = jnp.concatenate([pair, own], axis=0)
    message_a = message
    other_a = other
    inner = exchanged(message_a, 0)
    outer = exchanged(message, 1)
    corner = exchanged(other, 1)
    beside = exchanged(other_a, 0)

    edges, other_m = mixed(blocks_of(ABOVE) + blocks_of(BELOW), "mix_edges", other)
    inner, edges = lax.optimization_barrier((inner, edges))
    top, summed = pl.pallas_call(
        early_kernel,
        in_specs=[whole()] * 11,
        out_specs=[whole()] * 2,
        out_shape=[
            struct(parts, 2, 8, members * rows, dtype=F32),
            struct(parts, LANES, rows, dtype=F32),
        ],
        scratch_shapes=[
            pltpu.VMEM(((1 + EARLY) * rows, width), BF16),
            pltpu.VMEM((parts, LANES + ROWS, (1 + EARLY) * rows), BF16),
        ],
        compiler_params=params(32),
        cost_estimate=cost(3e9, 6e6),
        name="early",
    )(choice, other, pair, inner, outer, gain, wk, wvt, query, key, value)
    state, latent, to_pair, to_other = pl.pallas_call(
        late_kernel,
        in_specs=[whole()] * 15,
        out_specs=[whole()] * 4,
        out_shape=[pltpu.VMEM((rows, width), BF16), struct(rows, channels)]
        + [struct(ROWS, channels)] * 2,
        compiler_params=params(32),
        cost_estimate=cost(3e9, 6e6),
        name="late",
    )(
        choice, cells, inner, outer, beside, corner,
        own, gain, wk, wvt, query, top, summed, w_out, w_latent,
    )

    from_pair = paired(to_pair, 0)
    from_other = paired(to_other, 1)
    middle, latent = mixed(blocks_of(OWN), "mix_own", latent)
    from_other, from_pair, middle = lax.optimization_barrier((from_other, from_pair, middle))
    extended = jnp.concatenate([latent, from_pair[:SIDE], from_other[:SIDE]], axis=0)
    far = exchanged(extended, 1)
    near = exchanged(extended, 0)

    lanes = -(-(rows + 2 * SIDE) // 256) * 256
    partial, hots, state = pl.pallas_call(
        functools.partial(own_kernel, (rows, 2 * rows, 2 * rows)),
        in_specs=[whole()] * 6,
        out_specs=[whole()] * 3,
        out_shape=[
            struct(lat_rows, outputs, lon_cols, dtype=F32),
            struct(2, 2, TAPS, lanes, lon_cols),
            struct(rows, width),
        ],
        compiler_params=params(32),
        cost_estimate=cost(1e9, 2.5e6),
        name="own_band",
    )(state, own, inner, outer, extended, middle)
    band_scratch = [
        pltpu.VMEM((outputs, TAPS * lanes), BF16),
        pltpu.VMEM((2 * outputs, TAPS * lanes), BF16),
        pltpu.VMEM((lon_cols // LANES, 2 * outputs, LANES), F32),
    ]
    partial = pl.pallas_call(
        functools.partial(band_kernel, True),
        in_specs=[whole()] * 4,
        out_specs=whole(),
        out_shape=struct(lat_rows, outputs, lon_cols, dtype=F32),
        scratch_shapes=band_scratch,
        compiler_params=params(32),
        cost_estimate=cost(1e9, 2.5e6),
        name="inner_band",
    )(near, edges, hots, partial)
    fields = pl.pallas_call(
        functools.partial(band_kernel, False),
        in_specs=[whole()] * 4,
        out_specs=whole(),
        out_shape=struct(out_ch, lat_rows, lon_cols),
        scratch_shapes=band_scratch,
        compiler_params=params(32),
        cost_estimate=cost(1e9, 2.5e6),
        name="outer_band",
    )(far, edges, hots, partial)
    return (state.reshape(1, rows, width), fields.reshape(1, out_ch, lat_rows, lon_cols))


def solution(mesh):
    in_specs = (
        P(None, ("reg", "lon"), None),
        P(),
        P(),
        P(),
        P(),
        P(("reg", "lon"), None),
        P("reg", "lon"),
        P(None, "reg", None, None),
        P(),
    )
    out_specs = (P(None, ("reg", "lon"), None), P(None, None, "reg", "lon"))
    return jax.shard_map(shards, mesh=mesh, in_specs=in_specs, out_specs=out_specs, check_vma=False)
```

```python
import functools
import math

import jax
import jax.numpy as jnp
from jax import lax
from jax.experimental import pallas as pl
from jax.experimental.pallas import tpu as pltpu
from jax.sharding import PartitionSpec as P

HEADS = 16
REACH = 2
TAPS = 2 * REACH + 1
SIDE = 8
ROWS = 16
LANES = 128
EARLY = 2
CANDIDATES = 5
F32 = jnp.float32
BF16 = jnp.bfloat16
NT = (((1,), (1,)), ((), ()))

ABOVE = ((-2, (0,)), (-1, (0, 1)))
OWN = ((0, (0, 1)), (1, (0, 1)))
BELOW = ((3, (1,)), (2, (0, 1)))


def blocks_of(band):
    return [
        (out_row, src - out_row + REACH, off)
        for src, out_rows in band
        for off in range(TAPS)
        for out_row in out_rows
    ]


def iota(shape, dim):
    return lax.broadcasted_iota(jnp.int32, shape, dim)


def normalise(rows, gain):
    values = rows.astype(F32)
    center = values - jnp.mean(values, axis=-1, keepdims=True)
    spread = jnp.mean(center * center, axis=-1, keepdims=True)
    return (center * lax.rsqrt(spread + 1e-05) * gain).astype(BF16)


def mix_kernel(blocks, psi_ref, dec_ref, *refs):
    if len(refs) > 3:
        refs[2][...] = refs[0][...]
        refs = (refs[1], *refs[3:])
    mixed_ref, psi_rows_ref, taps_ref = refs
    basis, out_ch, channels = dec_ref.shape
    depth = basis * ROWS
    for tap in range(TAPS):
        for off in range(TAPS):
            at = (tap * TAPS + off) * 2
            psi_rows_ref[at : at + 2, :] = psi_ref[tap, off]
    spread = (iota((basis, depth), 1) // ROWS == iota((basis, depth), 0)).astype(F32)
    expanded = jnp.dot(psi_rows_ref[...], spread, preferred_element_type=F32)
    pick = iota((ROWS, depth), 1) % ROWS == iota((ROWS, depth), 0)
    for at, (out_row, tap, off) in enumerate(blocks):
        source = (tap * TAPS + off) * 2 + out_row
        taps = jnp.broadcast_to(expanded[source : source + 1], (ROWS, depth))
        taps_ref[at * ROWS : (at + 1) * ROWS, :] = jnp.where(pick, taps, 0.0).astype(BF16)
    for first in range(0, out_ch, ROWS):
        size = min(ROWS, out_ch - first)
        pieces = []
        for base in range(basis):
            pieces.append(dec_ref[base, first : first + size, :])
            if size < ROWS:
                pieces.append(jnp.zeros((ROWS - size, channels), BF16))
        mixing = jnp.concatenate(pieces, axis=0)
        mixed = jnp.dot(taps_ref[...], mixing, preferred_element_type=F32).astype(BF16)
        mixed_ref[:, first : first + ROWS, :] = mixed.reshape(len(blocks), ROWS, channels)


def listed_blocks(sectors, listed_ref):
    reg_here, lon_here = lax.axis_index("reg"), lax.axis_index("lon")
    toward = 1 - 2 * (reg_here % 2)
    found = []
    for at in range(1, listed_ref.shape[1]):
        block = listed_ref[0, at]
        step_reg = (block // sectors - reg_here) * toward
        step_lon = (block % sectors - lon_here + 1 + sectors) % sectors - 1
        lean = step_lon * (1 - 2 * (lon_here % 2))
        side = jnp.where(lean == 0, 0, jnp.where(lean > 0, 1, 4))
        ahead = jnp.where(lean < 0, 0, 1)
        behind = jnp.where(lean < 0, 7, 4 + side)
        found.append(jnp.where(step_reg == 0, ahead, jnp.where(step_reg > 0, 2 + side, behind)))
    for low in range(len(found)):
        for high in range(low + 1, len(found)):
            less, more = jnp.minimum(found[low], found[high]), jnp.maximum(found[low], found[high])
            found[low], found[high] = less, more
    return found


def gather_kernel(x_hbm, assign_hbm, own_ref, assign_ref, sems):
    rows = own_ref.shape[0] - ROWS
    copies = [
        pltpu.make_async_copy(assign_hbm, assign_ref, sems.at[0]),
        pltpu.make_async_copy(x_hbm, own_ref.at[pl.ds(0, rows)], sems.at[1]),
    ]
    for copy in copies:
        copy.start()
    copies[0].wait()
    local = lax.rem(assign_ref[...], rows).astype(F32)
    line = jnp.concatenate([local[:1], local[1:2]], axis=1)
    line = jnp.broadcast_to(line, (ROWS, line.shape[1]))
    own_ref[rows:] = jnp.where(iota(line.shape, 0) == 0, line, 0.0).astype(BF16)
    copies[1].wait()


def prepare_kernel(
    sectors,
    own_ref, gain_hbm, wqkv_hbm, assign_hbm, listed_hbm,
    query_ref, key_ref, value_ref, wk_ref, wvt_ref, choice_ref, cells_ref,
    gain_ref, wqkv_ref, cell_ref, listed_ref, sems,
):
    copies = [
        pltpu.make_async_copy(source, target, sems.at[at])
        for at, (source, target) in enumerate(
            (
                (gain_hbm, gain_ref),
                (wqkv_hbm, wqkv_ref),
                (assign_hbm, cell_ref),
                (listed_hbm, listed_ref),
            )
        )
    ]
    for copy in copies:
        copy.start()
    rows, width = key_ref.shape
    group, members = query_ref.shape[1], query_ref.shape[2] // rows
    head = group // members
    for copy in copies[2:]:
        copy.wait()
    for at, number in enumerate(listed_blocks(sectors, listed_ref)):
        for candidate in range(CANDIDATES):
            same = jnp.full((ROWS, LANES), jnp.where(number == at + candidate, 1.0, 0.0), F32)
            choice_ref[at, candidate] = same.astype(BF16)
    lat_rows, lon_cols = cell_ref.shape
    place, node = iota((ROWS, rows), 0), iota((ROWS, rows), 1)
    odd = lax.axis_index("lon") % 2
    for side, first in enumerate(((1 - odd) * (lon_cols - REACH), odd * (lon_cols - REACH))):
        hit = jnp.zeros((ROWS, rows), F32)
        for row in range(lat_rows):
            for col in range(REACH):
                cell = cell_ref[row, first + col] % rows
                hit = jnp.where((place == row * REACH + col) & (node == cell), 1.0, hit)
        cells_ref[side * ROWS : (side + 1) * ROWS] = hit.astype(BF16)
    copies[0].wait()
    normed = normalise(own_ref[:rows], gain_ref[...])
    copies[1].wait()
    query = jnp.dot(normed, wqkv_ref[:, :width], preferred_element_type=F32)
    query_t = (query * (math.log2(math.e) / head**0.5)).T.astype(BF16)
    mask = (iota((group, members * rows), 0) // head) == (iota((group, members * rows), 1) // rows)
    for part in range(width // group):
        piece = query_t[part * group : (part + 1) * group]
        wide = jnp.concatenate([piece] * members, axis=1)
        query_ref[part] = jnp.where(mask, wide, jnp.zeros_like(wide))
    wk = wqkv_ref[:, width : 2 * width]
    wk_ref[...] = wk
    key_ref[...] = jnp.dot(normed, wk, preferred_element_type=F32).astype(BF16)
    wvt = wqkv_ref[:, 2 * width :].astype(F32).T.astype(BF16)
    wvt_ref[...] = wvt
    value_ref[...] = lax.dot_general(wvt, normed, NT, preferred_element_type=F32).astype(BF16)


def chosen(entries, rows, choice_ref, candidates):
    tall, wide = rows // ROWS, candidates[-1].shape[1] // LANES
    near = []
    for entry in entries:
        total = None
        for at in range(CANDIDATES):
            weight = jnp.concatenate([choice_ref[entry, at]] * wide, axis=1)
            part = candidates[entry + at] * jnp.concatenate([weight] * tall, axis=0)
            total = part if total is None else total + part
        near.append(total)
    return jnp.concatenate(near, axis=0)


def project(nodes, gain, wk_ref, wvt_ref):
    normed = normalise(nodes, gain)
    keys = jnp.dot(normed, wk_ref[...], preferred_element_type=F32).astype(BF16)
    values = lax.dot_general(wvt_ref[...], normed, NT, preferred_element_type=F32).astype(BF16)
    return keys, values


def own_heads(summed, rows):
    members = summed.shape[1] // rows
    head = summed.shape[0] // members
    return [
        summed[at * head : (at + 1) * head, at * rows : (at + 1) * rows] for at in range(members)
    ]


def early_kernel(
    choice_ref, other_ref, pair_ref, inner_ref, outer_ref,
    gain_ref, wk_ref, wvt_ref, query_ref, key_ref, value_ref,
    top_ref, sum_ref, keys_ref, values_ref,
):
    rows = key_ref.shape[0]
    parts, group, _ = query_ref.shape
    candidates = [other_ref[...], pair_ref[...]]
    candidates += [ref[rows : 2 * rows] if center else ref[:rows] for ref in (inner_ref, outer_ref) for center in (1, 0)]
    nodes = chosen(range(EARLY), rows, choice_ref, candidates)
    keys, values = project(nodes, gain_ref[...], wk_ref, wvt_ref)
    keys_ref[:rows] = key_ref[...]
    keys_ref[rows:] = keys
    for part in range(parts):
        span = slice(part * group, (part + 1) * group)
        values_ref[part, :group, :rows] = value_ref[span]
        values_ref[part, :group, rows:] = values[span]
        values_ref[part, group:, :] = jnp.ones((ROWS, keys_ref.shape[0]), BF16)

    spans = [slice(part * group, (part + 1) * group) for part in range(parts)]
    scores = [
        jnp.dot(keys_ref[:, span], query_ref[part], preferred_element_type=F32)
        for part, span in enumerate(spans)
    ]
    tops = [jnp.max(one, axis=0, keepdims=True) for one in scores]
    expos = [jnp.exp2(one - top).astype(BF16) for one, top in zip(scores, tops)]
    sums = [
        jnp.dot(values_ref[part], expo, preferred_element_type=F32) for part, expo in enumerate(expos)
    ]
    for part, (top, summed) in enumerate(zip(tops, sums)):
        top_ref[part, 0] = jnp.broadcast_to(top, top_ref.shape[2:])
        top_ref[part, 1] = jnp.broadcast_to(summed[group : group + 1], top_ref.shape[2:])
        sum_ref[part] = jnp.concatenate(own_heads(summed[:group], rows), axis=0)


def late_kernel(
    choice_ref, cells_ref, inner_ref, outer_ref, beside_ref, corner_ref,
    own_ref, gain_ref, wk_ref, wvt_ref, query_ref, top_ref, sum_ref, wout_ref, wlat_ref,
    state_ref, latent_ref, to_pair_ref, to_other_ref,
):
    rows, width = state_ref.shape
    parts, group, lanes = query_ref.shape
    members = lanes // rows
    head = group // members
    candidates = [None, None]
    candidates += [ref[rows : 2 * rows] if center else ref[:rows] for ref in (inner_ref, outer_ref) for center in (1, 0)]
    candidates += [beside_ref[...], corner_ref[...]]
    nodes = chosen(range(EARLY, choice_ref.shape[0]), rows, choice_ref, candidates)
    keys, values = project(nodes, gain_ref[...], wk_ref, wvt_ref)
    ones = jnp.ones((ROWS, nodes.shape[0]), BF16)
    spans = [slice(part * group, (part + 1) * group) for part in range(parts)]
    scores = [
        jnp.dot(keys[:, span], query_ref[part], preferred_element_type=F32)
        for part, span in enumerate(spans)
    ]
    befores = [top_ref[part, 0, :1] for part in range(parts)]
    tops = [
        jnp.maximum(before, jnp.max(one, axis=0, keepdims=True))
        for before, one in zip(befores, scores)
    ]
    expos = [jnp.exp2(one - top).astype(BF16) for one, top in zip(scores, tops)]
    sums = [
        jnp.dot(jnp.concatenate([values[span], ones], axis=0), expo, preferred_element_type=F32)
        for span, expo in zip(spans, expos)
    ]
    attended = []
    for part, summed in enumerate(sums):
        shrink = jnp.exp2(befores[part] - tops[part])
        share = 1.0 / (summed[group : group + 1] + top_ref[part, 1, :1] * shrink)
        merged = []
        for member, piece in enumerate(own_heads(summed[:group], rows)):
            span = slice(member * rows, (member + 1) * rows)
            earlier = sum_ref[part, member * head : (member + 1) * head]
            merged.append((piece + earlier * shrink[:, span]) * share[:, span])
        attended.append(jnp.concatenate(merged, axis=0).T.astype(BF16))
    attended = jnp.concatenate(attended, axis=1)
    state = (
        own_ref[:rows].astype(F32)
        + jnp.dot(attended, wout_ref[...], preferred_element_type=F32)
    ).astype(BF16)
    state_ref[...] = state
    value = jnp.dot(state, wlat_ref[...], preferred_element_type=F32)
    latent = (value / (1.0 + jnp.exp(-value))).astype(BF16)
    latent_ref[...] = latent
    cells = jnp.dot(cells_ref[...], latent, preferred_element_type=F32).astype(BF16)
    to_pair_ref[...] = cells[:ROWS]
    to_other_ref[...] = cells[ROWS:]


def hot_rows(values, rows, cols, line):
    odd = lax.axis_index("lon") % 2
    column = iota((8, cols), 1)
    node = iota((rows + 2 * SIDE, cols), 0).astype(F32)
    for off in range(TAPS):
        step = off - REACH
        where = jnp.broadcast_to(values, (8, cols))
        if step:
            where = pltpu.roll(where, (-step) % cols, 1)
        reach = column + step
        before = (rows + (1 - odd) * SIDE + REACH * line + reach + REACH).astype(F32)
        after = (rows + odd * SIDE + REACH * line + reach - cols).astype(F32)
        where = jnp.where(reach < 0, before, jnp.where(reach >= cols, after, where))
        yield jnp.where(node == where[:1], 1.0, 0.0).astype(BF16)


def shares_of(latent, weights):
    blocks, outputs, channels = weights.shape
    shares = lax.dot_general(
        weights.reshape(blocks * outputs, channels), latent, NT, preferred_element_type=F32
    ).astype(BF16)
    return [shares[at * outputs : (at + 1) * outputs] for at in range(blocks)]


def lines_of(line_ref, start, cols):
    values = line_ref[start : start + ROWS, :].astype(F32)
    return values[:1, :cols], values[:1, cols:]


def own_kernel(
    begin, own_ref, inner_ref, outer_ref, latent_ref, weights_ref, out_ref, hot_ref
):
    cols = out_ref.shape[2]
    rows = latent_ref.shape[0] - 2 * SIDE
    own = lines_of(own_ref, begin[0], cols)
    table = [list(hot_rows(own[line], rows, cols, line)) for line in range(2)]
    acc = [None, None]
    for (out_row, tap, off), share in zip(
        blocks_of(OWN), shares_of(latent_ref[...], weights_ref[...])
    ):
        line = out_row + tap - REACH
        piece = jnp.dot(share, table[line][off], preferred_element_type=F32)
        acc[out_row] = piece if acc[out_row] is None else acc[out_row] + piece
    for row in range(2):
        out_ref[row] = acc[row]
    odd = lax.axis_index("reg") % 2 == 1
    inner, outer = lines_of(inner_ref, begin[1], cols), lines_of(outer_ref, begin[2], cols)
    nodes = rows + 2 * SIDE
    for band, (yes, no) in enumerate(((inner, outer), (outer, inner))):
        for at, line in enumerate((0, 1) if band == 0 else (1, 0)):
            values = jnp.where(odd, yes[line], no[line])
            for off, hot in enumerate(hot_rows(values, rows, cols, line)):
                hot_ref[band, at, off, :nodes] = hot
                hot_ref[band, at, off, nodes:] = jnp.zeros((hot_ref.shape[3] - nodes, cols), BF16)


def band_kernel(
    from_inner, latent_ref, weights_ref, hot_ref, partial_ref, out_ref, one_ref, two_ref, paired_ref
):
    odd = lax.axis_index("reg") % 2
    band = 1 - odd if from_inner else odd
    latent = latent_ref[...]
    lanes, cols = hot_ref.shape[3:]
    outputs = weights_ref.shape[1]
    blank = jnp.zeros((lanes - latent.shape[0], latent.shape[1]), BF16)
    blocks = len(blocks_of(ABOVE))
    weights = weights_ref[pl.ds(band * blocks, blocks)]
    shares = shares_of(jnp.concatenate([latent, blank], axis=0), weights)
    for off in range(TAPS):
        span = slice(off * lanes, (off + 1) * lanes)
        one_ref[:, span] = shares[off]
        for row in range(2):
            two_ref[row * outputs : (row + 1) * outputs, span] = shares[TAPS + 2 * off + row]
    depth = TAPS * lanes
    one = jnp.dot(one_ref[...], hot_ref[band, 0].reshape(depth, cols), preferred_element_type=F32)
    two = jnp.dot(two_ref[...], hot_ref[band, 1].reshape(depth, cols), preferred_element_type=F32)
    for row in range(2):
        total = partial_ref[row] + two[row * outputs : (row + 1) * outputs]
        total = total + jnp.where(band == row, one, 0.0)
        if from_inner:
            out_ref[row] = total
        else:
            for tile in range(cols // LANES):
                part = total[:, tile * LANES : (tile + 1) * LANES]
                paired_ref[tile, pl.ds(row, outputs, stride=2), :] = part
    if not from_inner:
        out_ch = out_ref.shape[0]
        tiles = [paired_ref[tile, : 2 * out_ch, :] for tile in range(cols // LANES)]
        out_ref[...] = jnp.concatenate(tiles, axis=1).astype(BF16).reshape(out_ref.shape)


def whole(memory=pltpu.VMEM):
    return pl.BlockSpec(memory_space=memory)


def struct(*shape, dtype=BF16):
    return jax.ShapeDtypeStruct(shape, dtype)


def params(limit):
    return pltpu.CompilerParams(vmem_limit_bytes=limit << 20)


def cost(flops, moved):
    return pl.CostEstimate(flops=int(flops), bytes_accessed=int(moved), transcendentals=0)


def shards(nodes, norm_gain, w_qkv, w_out, w_latent, neighbours, assignment, psi, w_dec):
    _, rows, width = nodes.shape
    channels = w_latent.shape[1]
    lat_rows, lon_cols = assignment.shape
    basis, _, out_ch = w_dec.shape
    sectors = lax.axis_size("lon")
    count = neighbours.shape[1]
    x = nodes.reshape(rows, width)
    gain = norm_gain.reshape(1, width)

    def paired(array, first):
        pairs = [(i, (i + 1) % sectors) for i in range(first, sectors, 2)]
        return lax.ppermute(array, "lon", pairs + [(j, i) for i, j in pairs])

    def exchanged(array, first):
        size = lax.axis_size("reg")
        pairs = [(i, i + 1) for i in range(first, size - 1, 2)]
        return lax.ppermute(array, "reg", pairs + [(j, i) for i, j in pairs])

    def in_hbm(*arrays):
        return [pltpu.with_memory_space_constraint(array, pltpu.HBM) for array in arrays]

    other = paired(x, 1)
    pair = paired(x, 0)

    outputs = -(-out_ch // ROWS) * ROWS
    head = width // HEADS
    members = LANES // head
    parts = HEADS // members
    def mixed(blocks, name, after, kept=()):
        taps = psi.transpose(2, 3, 1, 0)
        mixing = w_dec.transpose(0, 2, 1)
        taps, mixing, after = lax.optimization_barrier((taps, mixing, after))
        weights = pl.pallas_call(
            functools.partial(mix_kernel, blocks),
            in_specs=[whole()] * (2 + len(kept)),
            out_specs=[whole()] * (1 + len(kept)),
            out_shape=[struct(len(blocks), outputs, channels)]
            + [struct(*array.shape) for array in kept],
            scratch_shapes=[
                pltpu.VMEM((2 * TAPS * TAPS, basis), F32),
                pltpu.VMEM((len(blocks) * ROWS, basis * ROWS), BF16),
            ],
            compiler_params=params(32),
            cost_estimate=cost(2e9, 6e6),
            name=name,
        )(taps, mixing, *kept)
        return *weights, after

    own = pl.pallas_call(
        gather_kernel,
        in_specs=[whole(pltpu.HBM)] * 2,
        out_specs=whole(),
        out_shape=struct(rows + ROWS, width),
        scratch_shapes=[
            pltpu.VMEM(assignment.shape, jnp.int32),
            pltpu.SemaphoreType.DMA((2,)),
        ],
        compiler_params=params(32),
        cost_estimate=cost(1e3, 1e3),
        name="gather",
    )(*in_hbm(x, assignment))
    query, key, value, wk, wvt, choice, cells = pl.pallas_call(
        functools.partial(prepare_kernel, sectors),
        in_specs=[whole()] + [whole(pltpu.HBM)] * 4,
        out_specs=[whole()] * 7,
        out_shape=[
            struct(parts, LANES, members * rows),
            struct(rows, width),
            struct(width, rows),
            struct(width, width),
            struct(width, width),
            struct(count - 1, CANDIDATES, ROWS, LANES),
            struct(2 * ROWS, rows),
        ],
        scratch_shapes=[
            pltpu.VMEM((1, width), F32),
            pltpu.VMEM(w_qkv.shape, BF16),
            pltpu.SMEM(assignment.shape, jnp.int32),
            pltpu.SMEM(neighbours.shape, jnp.int32),
            pltpu.SemaphoreType.DMA((4,)),
        ],
        compiler_params=params(32),
        cost_estimate=cost(5e8, 1e6),
        name="prepare",
    )(own, *in_hbm(gain, w_qkv, assignment, neighbours))
    own, query = lax.optimization_barrier((own, query))
    message = jnp.concatenate([pair, own], axis=0)
    message_a = message
    other_a = other
    inner = exchanged(message_a, 0)
    outer = exchanged(message, 1)
    corner = exchanged(other, 1)
    beside = exchanged(other_a, 0)

    edges, other_m = mixed(blocks_of(ABOVE) + blocks_of(BELOW), "mix_edges", other)
    inner, edges = lax.optimization_barrier((inner, edges))
    top, summed = pl.pallas_call(
        early_kernel,
        in_specs=[whole()] * 11,
        out_specs=[whole()] * 2,
        out_shape=[
            struct(parts, 2, 8, members * rows, dtype=F32),
            struct(parts, LANES, rows, dtype=F32),
        ],
        scratch_shapes=[
            pltpu.VMEM(((1 + EARLY) * rows, width), BF16),
            pltpu.VMEM((parts, LANES + ROWS, (1 + EARLY) * rows), BF16),
        ],
        compiler_params=params(32),
        cost_estimate=cost(3e9, 6e6),
        name="early",
    )(choice, other, pair, inner, outer, gain, wk, wvt, query, key, value)
    state, latent, to_pair, to_other = pl.pallas_call(
        late_kernel,
        in_specs=[whole()] * 15,
        out_specs=[whole()] * 4,
        out_shape=[pltpu.VMEM((rows, width), BF16), struct(rows, channels)]
        + [struct(ROWS, channels)] * 2,
        compiler_params=params(32),
        cost_estimate=cost(3e9, 6e6),
        name="late",
    )(
        choice, cells, inner, outer, beside, corner,
        own, gain, wk, wvt, query, top, summed, w_out, w_latent,
    )

    from_pair = paired(to_pair, 0)
    from_other = paired(to_other, 1)
    middle, state, latent = mixed(blocks_of(OWN), "mix_own", latent, (state,))
    from_pair, middle = lax.optimization_barrier((from_pair, middle))
    extended = jnp.concatenate([latent, from_pair[:SIDE], from_other[:SIDE]], axis=0)
    far = exchanged(extended, 1)
    cut = rows // 2
    near = [exchanged(latent[:cut], 0), exchanged(extended[cut:], 0)]
    near = jnp.concatenate(near, axis=0)

    lanes = -(-(rows + 2 * SIDE) // 256) * 256
    partial, hots = pl.pallas_call(
        functools.partial(own_kernel, (rows, 2 * rows, 2 * rows)),
        in_specs=[whole()] * 5,
        out_specs=[whole()] * 2,
        out_shape=[
            struct(lat_rows, outputs, lon_cols, dtype=F32),
            struct(2, 2, TAPS, lanes, lon_cols),
        ],
        compiler_params=params(32),
        cost_estimate=cost(1e9, 2.5e6),
        name="own_band",
    )(own, inner, outer, extended, middle)
    band_scratch = [
        pltpu.VMEM((outputs, TAPS * lanes), BF16),
        pltpu.VMEM((2 * outputs, TAPS * lanes), BF16),
        pltpu.VMEM((lon_cols // LANES, 2 * outputs, LANES), F32),
    ]
    partial = pl.pallas_call(
        functools.partial(band_kernel, True),
        in_specs=[whole()] * 4,
        out_specs=whole(),
        out_shape=struct(lat_rows, outputs, lon_cols, dtype=F32),
        scratch_shapes=band_scratch,
        compiler_params=params(32),
        cost_estimate=cost(1e9, 2.5e6),
        name="inner_band",
    )(near, edges, hots, partial)
    fields = pl.pallas_call(
        functools.partial(band_kernel, False),
        in_specs=[whole()] * 4,
        out_specs=whole(),
        out_shape=struct(out_ch, lat_rows, lon_cols),
        scratch_shapes=band_scratch,
        compiler_params=params(32),
        cost_estimate=cost(1e9, 2.5e6),
        name="outer_band",
    )(far, edges, hots, partial)
    return (state.reshape(1, rows, width), fields.reshape(1, out_ch, lat_rows, lon_cols))


def solution(mesh):
    in_specs = (
        P(None, ("reg", "lon"), None),
        P(),
        P(),
        P(),
        P(),
        P(("reg", "lon"), None),
        P("reg", "lon"),
        P(None, "reg", None, None),
        P(),
    )
    out_specs = (P(None, ("reg", "lon"), None), P(None, None, "reg", "lon"))
    return jax.shard_map(shards, mesh=mesh, in_specs=in_specs, out_specs=out_specs, check_vma=False)
```

```python
import functools
import math

import jax
import jax.numpy as jnp
from jax import lax
from jax.experimental import pallas as pl
from jax.experimental.pallas import tpu as pltpu
from jax.sharding import PartitionSpec as P

HEADS = 16
REACH = 2
TAPS = 2 * REACH + 1
SIDE = 8
ROWS = 16
LANES = 128
EARLY = 2
CANDIDATES = 5
F32 = jnp.float32
BF16 = jnp.bfloat16
NT = (((1,), (1,)), ((), ()))

ABOVE = ((-2, (0,)), (-1, (0, 1)))
OWN = ((0, (0, 1)), (1, (0, 1)))
BELOW = ((3, (1,)), (2, (0, 1)))


def blocks_of(band):
    return [
        (out_row, src - out_row + REACH, off)
        for src, out_rows in band
        for off in range(TAPS)
        for out_row in out_rows
    ]


def iota(shape, dim):
    return lax.broadcasted_iota(jnp.int32, shape, dim)


def normalise(rows, gain):
    values = rows.astype(F32)
    center = values - jnp.mean(values, axis=-1, keepdims=True)
    spread = jnp.mean(center * center, axis=-1, keepdims=True)
    return (center * lax.rsqrt(spread + 1e-05) * gain).astype(BF16)


def mix_kernel(blocks, psi_ref, dec_ref, mixed_ref, psi_rows_ref, taps_ref):
    basis, out_ch, channels = dec_ref.shape
    depth = basis * ROWS
    for tap in range(TAPS):
        for off in range(TAPS):
            at = (tap * TAPS + off) * 2
            psi_rows_ref[at : at + 2, :] = psi_ref[tap, off]
    spread = (iota((basis, depth), 1) // ROWS == iota((basis, depth), 0)).astype(F32)
    expanded = jnp.dot(psi_rows_ref[...], spread, preferred_element_type=F32)
    pick = iota((ROWS, depth), 1) % ROWS == iota((ROWS, depth), 0)
    for at, (out_row, tap, off) in enumerate(blocks):
        source = (tap * TAPS + off) * 2 + out_row
        taps = jnp.broadcast_to(expanded[source : source + 1], (ROWS, depth))
        taps_ref[at * ROWS : (at + 1) * ROWS, :] = jnp.where(pick, taps, 0.0).astype(BF16)
    for first in range(0, out_ch, ROWS):
        size = min(ROWS, out_ch - first)
        pieces = []
        for base in range(basis):
            pieces.append(dec_ref[base, first : first + size, :])
            if size < ROWS:
                pieces.append(jnp.zeros((ROWS - size, channels), BF16))
        mixing = jnp.concatenate(pieces, axis=0)
        mixed = jnp.dot(taps_ref[...], mixing, preferred_element_type=F32).astype(BF16)
        mixed_ref[:, first : first + ROWS, :] = mixed.reshape(len(blocks), ROWS, channels)


def listed_blocks(sectors, listed_ref):
    reg_here, lon_here = lax.axis_index("reg"), lax.axis_index("lon")
    toward = 1 - 2 * (reg_here % 2)
    found = []
    for at in range(1, listed_ref.shape[1]):
        block = listed_ref[0, at]
        step_reg = (block // sectors - reg_here) * toward
        step_lon = (block % sectors - lon_here + 1 + sectors) % sectors - 1
        lean = step_lon * (1 - 2 * (lon_here % 2))
        side = jnp.where(lean == 0, 0, jnp.where(lean > 0, 1, 4))
        ahead = jnp.where(lean < 0, 0, 1)
        behind = jnp.where(lean < 0, 7, 4 + side)
        found.append(jnp.where(step_reg == 0, ahead, jnp.where(step_reg > 0, 2 + side, behind)))
    for low in range(len(found)):
        for high in range(low + 1, len(found)):
            less, more = jnp.minimum(found[low], found[high]), jnp.maximum(found[low], found[high])
            found[low], found[high] = less, more
    return found


def gather_kernel(x_hbm, assign_hbm, own_ref, assign_ref, sems):
    rows = own_ref.shape[0] - ROWS
    copies = [
        pltpu.make_async_copy(assign_hbm, assign_ref, sems.at[0]),
        pltpu.make_async_copy(x_hbm, own_ref.at[pl.ds(0, rows)], sems.at[1]),
    ]
    for copy in copies:
        copy.start()
    copies[0].wait()
    local = lax.rem(assign_ref[...], rows).astype(F32)
    line = jnp.concatenate([local[:1], local[1:2]], axis=1)
    line = jnp.broadcast_to(line, (ROWS, line.shape[1]))
    own_ref[rows:] = jnp.where(iota(line.shape, 0) == 0, line, 0.0).astype(BF16)
    copies[1].wait()


def prepare_kernel(
    sectors,
    own_ref, gain_hbm, wqkv_hbm, assign_hbm, listed_hbm,
    query_ref, key_ref, value_ref, wk_ref, wvt_ref, choice_ref, cells_ref,
    gain_ref, wqkv_ref, cell_ref, listed_ref, sems,
):
    copies = [
        pltpu.make_async_copy(source, target, sems.at[at])
        for at, (source, target) in enumerate(
            (
                (gain_hbm, gain_ref),
                (wqkv_hbm, wqkv_ref),
                (assign_hbm, cell_ref),
                (listed_hbm, listed_ref),
            )
        )
    ]
    for copy in copies:
        copy.start()
    rows, width = key_ref.shape
    group, members = query_ref.shape[1], query_ref.shape[2] // rows
    head = group // members
    for copy in copies[2:]:
        copy.wait()
    for at, number in enumerate(listed_blocks(sectors, listed_ref)):
        for candidate in range(CANDIDATES):
            same = jnp.full((ROWS, LANES), jnp.where(number == at + candidate, 1.0, 0.0), F32)
            choice_ref[at, candidate] = same.astype(BF16)
    lat_rows, lon_cols = cell_ref.shape
    place, node = iota((ROWS, rows), 0), iota((ROWS, rows), 1)
    odd = lax.axis_index("lon") % 2
    for side, first in enumerate(((1 - odd) * (lon_cols - REACH), odd * (lon_cols - REACH))):
        hit = jnp.zeros((ROWS, rows), F32)
        for row in range(lat_rows):
            for col in range(REACH):
                cell = cell_ref[row, first + col] % rows
                hit = jnp.where((place == row * REACH + col) & (node == cell), 1.0, hit)
        cells_ref[side * ROWS : (side + 1) * ROWS] = hit.astype(BF16)
    copies[0].wait()
    normed = normalise(own_ref[:rows], gain_ref[...])
    copies[1].wait()
    query = jnp.dot(normed, wqkv_ref[:, :width], preferred_element_type=F32)
    query_t = (query * (math.log2(math.e) / head**0.5)).T.astype(BF16)
    mask = (iota((group, members * rows), 0) // head) == (iota((group, members * rows), 1) // rows)
    for part in range(width // group):
        piece = query_t[part * group : (part + 1) * group]
        wide = jnp.concatenate([piece] * members, axis=1)
        query_ref[part] = jnp.where(mask, wide, jnp.zeros_like(wide))
    wk = wqkv_ref[:, width : 2 * width]
    wk_ref[...] = wk
    key_ref[...] = jnp.dot(normed, wk, preferred_element_type=F32).astype(BF16)
    wvt = wqkv_ref[:, 2 * width :].astype(F32).T.astype(BF16)
    wvt_ref[...] = wvt
    value_ref[...] = lax.dot_general(wvt, normed, NT, preferred_element_type=F32).astype(BF16)


def chosen(entries, rows, choice_ref, candidates):
    tall, wide = rows // ROWS, candidates[-1].shape[1] // LANES
    near = []
    for entry in entries:
        total = None
        for at in range(CANDIDATES):
            weight = jnp.concatenate([choice_ref[entry, at]] * wide, axis=1)
            part = candidates[entry + at] * jnp.concatenate([weight] * tall, axis=0)
            total = part if total is None else total + part
        near.append(total)
    return jnp.concatenate(near, axis=0)


def project(nodes, gain, wk_ref, wvt_ref):
    normed = normalise(nodes, gain)
    keys = jnp.dot(normed, wk_ref[...], preferred_element_type=F32).astype(BF16)
    values = lax.dot_general(wvt_ref[...], normed, NT, preferred_element_type=F32).astype(BF16)
    return keys, values


def own_heads(summed, rows):
    members = summed.shape[1] // rows
    head = summed.shape[0] // members
    return [
        summed[at * head : (at + 1) * head, at * rows : (at + 1) * rows] for at in range(members)
    ]


def early_kernel(
    choice_ref, other_ref, pair_ref, inner_ref, outer_ref,
    gain_ref, wk_ref, wvt_ref, query_ref, key_ref, value_ref,
    top_ref, sum_ref, keys_ref, values_ref,
):
    rows = key_ref.shape[0]
    parts, group, _ = query_ref.shape
    candidates = [other_ref[...], pair_ref[...]]
    candidates += [ref[rows : 2 * rows] if center else ref[:rows] for ref in (inner_ref, outer_ref) for center in (1, 0)]
    nodes = chosen(range(EARLY), rows, choice_ref, candidates)
    keys, values = project(nodes, gain_ref[...], wk_ref, wvt_ref)
    keys_ref[:rows] = key_ref[...]
    keys_ref[rows:] = keys
    for part in range(parts):
        span = slice(part * group, (part + 1) * group)
        values_ref[part, :group, :rows] = value_ref[span]
        values_ref[part, :group, rows:] = values[span]
        values_ref[part, group:, :] = jnp.ones((ROWS, keys_ref.shape[0]), BF16)

    spans = [slice(part * group, (part + 1) * group) for part in range(parts)]
    scores = [
        jnp.dot(keys_ref[:, span], query_ref[part], preferred_element_type=F32)
        for part, span in enumerate(spans)
    ]
    tops = [jnp.max(one, axis=0, keepdims=True) for one in scores]
    expos = [jnp.exp2(one - top).astype(BF16) for one, top in zip(scores, tops)]
    sums = [
        jnp.dot(values_ref[part], expo, preferred_element_type=F32) for part, expo in enumerate(expos)
    ]
    for part, (top, summed) in enumerate(zip(tops, sums)):
        top_ref[part, 0] = jnp.broadcast_to(top, top_ref.shape[2:])
        top_ref[part, 1] = jnp.broadcast_to(summed[group : group + 1], top_ref.shape[2:])
        sum_ref[part] = jnp.concatenate(own_heads(summed[:group], rows), axis=0)


def late_kernel(
    choice_ref, cells_ref, inner_ref, outer_ref, beside_ref, corner_ref,
    own_ref, gain_ref, wk_ref, wvt_ref, query_ref, top_ref, sum_ref, wout_ref, wlat_ref,
    state_ref, latent_ref, to_pair_ref, to_other_ref,
):
    rows, width = state_ref.shape
    parts, group, lanes = query_ref.shape
    members = lanes // rows
    head = group // members
    candidates = [None, None]
    candidates += [ref[rows : 2 * rows] if center else ref[:rows] for ref in (inner_ref, outer_ref) for center in (1, 0)]
    candidates += [beside_ref[...], corner_ref[...]]
    nodes = chosen(range(EARLY, choice_ref.shape[0]), rows, choice_ref, candidates)
    keys, values = project(nodes, gain_ref[...], wk_ref, wvt_ref)
    ones = jnp.ones((ROWS, nodes.shape[0]), BF16)
    spans = [slice(part * group, (part + 1) * group) for part in range(parts)]
    scores = [
        jnp.dot(keys[:, span], query_ref[part], preferred_element_type=F32)
        for part, span in enumerate(spans)
    ]
    befores = [top_ref[part, 0, :1] for part in range(parts)]
    tops = [
        jnp.maximum(before, jnp.max(one, axis=0, keepdims=True))
        for before, one in zip(befores, scores)
    ]
    expos = [jnp.exp2(one - top).astype(BF16) for one, top in zip(scores, tops)]
    sums = [
        jnp.dot(jnp.concatenate([values[span], ones], axis=0), expo, preferred_element_type=F32)
        for span, expo in zip(spans, expos)
    ]
    attended = []
    for part, summed in enumerate(sums):
        shrink = jnp.exp2(befores[part] - tops[part])
        share = 1.0 / (summed[group : group + 1] + top_ref[part, 1, :1] * shrink)
        merged = []
        for member, piece in enumerate(own_heads(summed[:group], rows)):
            span = slice(member * rows, (member + 1) * rows)
            earlier = sum_ref[part, member * head : (member + 1) * head]
            merged.append((piece + earlier * shrink[:, span]) * share[:, span])
        attended.append(jnp.concatenate(merged, axis=0).T.astype(BF16))
    attended = jnp.concatenate(attended, axis=1)
    state = (
        own_ref[:rows].astype(F32)
        + jnp.dot(attended, wout_ref[...], preferred_element_type=F32)
    ).astype(BF16)
    state_ref[...] = state
    value = jnp.dot(state, wlat_ref[...], preferred_element_type=F32)
    latent = (value / (1.0 + jnp.exp(-value))).astype(BF16)
    latent_ref[...] = latent
    cells = jnp.dot(cells_ref[...], latent, preferred_element_type=F32).astype(BF16)
    to_pair_ref[...] = cells[:ROWS]
    to_other_ref[...] = cells[ROWS:]


def hot_rows(values, rows, cols, line):
    odd = lax.axis_index("lon") % 2
    column = iota((8, cols), 1)
    node = iota((rows + 2 * SIDE, cols), 0).astype(F32)
    for off in range(TAPS):
        step = off - REACH
        where = jnp.broadcast_to(values, (8, cols))
        if step:
            where = pltpu.roll(where, (-step) % cols, 1)
        reach = column + step
        before = (rows + (1 - odd) * SIDE + REACH * line + reach + REACH).astype(F32)
        after = (rows + odd * SIDE + REACH * line + reach - cols).astype(F32)
        where = jnp.where(reach < 0, before, jnp.where(reach >= cols, after, where))
        yield jnp.where(node == where[:1], 1.0, 0.0).astype(BF16)


def shares_of(latent, weights):
    blocks, outputs, channels = weights.shape
    shares = lax.dot_general(
        weights.reshape(blocks * outputs, channels), latent, NT, preferred_element_type=F32
    ).astype(BF16)
    return [shares[at * outputs : (at + 1) * outputs] for at in range(blocks)]


def lines_of(line_ref, start, cols):
    values = line_ref[start : start + ROWS, :].astype(F32)
    return values[:1, :cols], values[:1, cols:]


def own_kernel(
    begin, state_ref, own_ref, inner_ref, outer_ref, latent_ref, weights_ref,
    out_ref, hot_ref, kept_ref,
):
    kept_ref[...] = state_ref[...]
    cols = out_ref.shape[2]
    rows = latent_ref.shape[0] - 2 * SIDE
    own = lines_of(own_ref, begin[0], cols)
    table = [list(hot_rows(own[line], rows, cols, line)) for line in range(2)]
    acc = [None, None]
    for (out_row, tap, off), share in zip(
        blocks_of(OWN), shares_of(latent_ref[...], weights_ref[...])
    ):
        line = out_row + tap - REACH
        piece = jnp.dot(share, table[line][off], preferred_element_type=F32)
        acc[out_row] = piece if acc[out_row] is None else acc[out_row] + piece
    for row in range(2):
        out_ref[row] = acc[row]
    odd = lax.axis_index("reg") % 2 == 1
    inner, outer = lines_of(inner_ref, begin[1], cols), lines_of(outer_ref, begin[2], cols)
    nodes = rows + 2 * SIDE
    for band, (yes, no) in enumerate(((inner, outer), (outer, inner))):
        for at, line in enumerate((0, 1) if band == 0 else (1, 0)):
            values = jnp.where(odd, yes[line], no[line])
            for off, hot in enumerate(hot_rows(values, rows, cols, line)):
                hot_ref[band, at, off, :nodes] = hot
                hot_ref[band, at, off, nodes:] = jnp.zeros((hot_ref.shape[3] - nodes, cols), BF16)


def band_kernel(
    from_inner, latent_ref, weights_ref, hot_ref, partial_ref, out_ref, one_ref, two_ref, paired_ref
):
    odd = lax.axis_index("reg") % 2
    band = 1 - odd if from_inner else odd
    latent = latent_ref[...]
    lanes, cols = hot_ref.shape[3:]
    outputs = weights_ref.shape[1]
    blank = jnp.zeros((lanes - latent.shape[0], latent.shape[1]), BF16)
    blocks = len(blocks_of(ABOVE))
    weights = weights_ref[pl.ds(band * blocks, blocks)]
    shares = shares_of(jnp.concatenate([latent, blank], axis=0), weights)
    for off in range(TAPS):
        span = slice(off * lanes, (off + 1) * lanes)
        one_ref[:, span] = shares[off]
        for row in range(2):
            two_ref[row * outputs : (row + 1) * outputs, span] = shares[TAPS + 2 * off + row]
    depth = TAPS * lanes
    one = jnp.dot(one_ref[...], hot_ref[band, 0].reshape(depth, cols), preferred_element_type=F32)
    two = jnp.dot(two_ref[...], hot_ref[band, 1].reshape(depth, cols), preferred_element_type=F32)
    for row in range(2):
        total = partial_ref[row] + two[row * outputs : (row + 1) * outputs]
        total = total + jnp.where(band == row, one, 0.0)
        if from_inner:
            out_ref[row] = total
        else:
            for tile in range(cols // LANES):
                part = total[:, tile * LANES : (tile + 1) * LANES]
                paired_ref[tile, pl.ds(row, outputs, stride=2), :] = part
    if not from_inner:
        out_ch = out_ref.shape[0]
        tiles = [paired_ref[tile, : 2 * out_ch, :] for tile in range(cols // LANES)]
        out_ref[...] = jnp.concatenate(tiles, axis=1).astype(BF16).reshape(out_ref.shape)


def whole(memory=pltpu.VMEM):
    return pl.BlockSpec(memory_space=memory)


def struct(*shape, dtype=BF16):
    return jax.ShapeDtypeStruct(shape, dtype)


def params(limit):
    return pltpu.CompilerParams(vmem_limit_bytes=limit << 20)


def cost(flops, moved):
    return pl.CostEstimate(flops=int(flops), bytes_accessed=int(moved), transcendentals=0)


def shards(nodes, norm_gain, w_qkv, w_out, w_latent, neighbours, assignment, psi, w_dec):
    _, rows, width = nodes.shape
    channels = w_latent.shape[1]
    lat_rows, lon_cols = assignment.shape
    basis, _, out_ch = w_dec.shape
    sectors = lax.axis_size("lon")
    count = neighbours.shape[1]
    x = nodes.reshape(rows, width)
    gain = norm_gain.reshape(1, width)

    def paired(array, first):
        pairs = [(i, (i + 1) % sectors) for i in range(first, sectors, 2)]
        return lax.ppermute(array, "lon", pairs + [(j, i) for i, j in pairs])

    def exchanged(array, first):
        size = lax.axis_size("reg")
        pairs = [(i, i + 1) for i in range(first, size - 1, 2)]
        return lax.ppermute(array, "reg", pairs + [(j, i) for i, j in pairs])

    def in_hbm(*arrays):
        return [pltpu.with_memory_space_constraint(array, pltpu.HBM) for array in arrays]

    other = paired(x, 1)
    pair = paired(x, 0)

    outputs = -(-out_ch // ROWS) * ROWS
    head = width // HEADS
    members = LANES // head
    parts = HEADS // members
    def mixed(blocks, name, after):
        taps = psi.transpose(2, 3, 1, 0)
        mixing = w_dec.transpose(0, 2, 1)
        taps, mixing, after = lax.optimization_barrier((taps, mixing, after))
        weights = pl.pallas_call(
            functools.partial(mix_kernel, blocks),
            in_specs=[whole()] * 2,
            out_specs=whole(),
            out_shape=struct(len(blocks), outputs, channels),
            scratch_shapes=[
                pltpu.VMEM((2 * TAPS * TAPS, basis), F32),
                pltpu.VMEM((len(blocks) * ROWS, basis * ROWS), BF16),
            ],
            compiler_params=params(32),
            cost_estimate=cost(2e9, 6e6),
            name=name,
        )(taps, mixing)
        return weights, after

    own = pl.pallas_call(
        gather_kernel,
        in_specs=[whole(pltpu.HBM)] * 2,
        out_specs=whole(),
        out_shape=struct(rows + ROWS, width),
        scratch_shapes=[
            pltpu.VMEM(assignment.shape, jnp.int32),
            pltpu.SemaphoreType.DMA((2,)),
        ],
        compiler_params=params(32),
        cost_estimate=cost(1e3, 1e3),
        name="gather",
    )(*in_hbm(x, assignment))
    query, key, value, wk, wvt, choice, cells = pl.pallas_call(
        functools.partial(prepare_kernel, sectors),
        in_specs=[whole()] + [whole(pltpu.HBM)] * 4,
        out_specs=[whole()] * 7,
        out_shape=[
            struct(parts, LANES, members * rows),
            struct(rows, width),
            struct(width, rows),
            struct(width, width),
            struct(width, width),
            struct(count - 1, CANDIDATES, ROWS, LANES),
            struct(2 * ROWS, rows),
        ],
        scratch_shapes=[
            pltpu.VMEM((1, width), F32),
            pltpu.VMEM(w_qkv.shape, BF16),
            pltpu.SMEM(assignment.shape, jnp.int32),
            pltpu.SMEM(neighbours.shape, jnp.int32),
            pltpu.SemaphoreType.DMA((4,)),
        ],
        compiler_params=params(32),
        cost_estimate=cost(5e8, 1e6),
        name="prepare",
    )(own, *in_hbm(gain, w_qkv, assignment, neighbours))
    own, query = lax.optimization_barrier((own, query))
    message = jnp.concatenate([pair, own], axis=0)
    message_a = message
    other_a = other
    inner = exchanged(message_a, 0)
    outer = exchanged(message, 1)
    corner = exchanged(other, 1)
    beside = exchanged(other_a, 0)

    edges, other_m = mixed(blocks_of(ABOVE) + blocks_of(BELOW), "mix_edges", other)
    inner, edges = lax.optimization_barrier((inner, edges))
    top, summed = pl.pallas_call(
        early_kernel,
        in_specs=[whole()] * 11,
        out_specs=[whole()] * 2,
        out_shape=[
            struct(parts, 2, 8, members * rows, dtype=F32),
            struct(parts, LANES, rows, dtype=F32),
        ],
        scratch_shapes=[
            pltpu.VMEM(((1 + EARLY) * rows, width), BF16),
            pltpu.VMEM((parts, LANES + ROWS, (1 + EARLY) * rows), BF16),
        ],
        compiler_params=params(32),
        cost_estimate=cost(3e9, 6e6),
        name="early",
    )(choice, other, pair, inner, outer, gain, wk, wvt, query, key, value)
    state, latent, to_pair, to_other = pl.pallas_call(
        late_kernel,
        in_specs=[whole()] * 15,
        out_specs=[whole()] * 4,
        out_shape=[pltpu.VMEM((rows, width), BF16), struct(rows, channels)]
        + [struct(ROWS, channels)] * 2,
        compiler_params=params(32),
        cost_estimate=cost(3e9, 6e6),
        name="late",
    )(
        choice, cells, inner, outer, beside, corner,
        own, gain, wk, wvt, query, top, summed, w_out, w_latent,
    )

    from_pair = paired(to_pair, 0)
    from_other = paired(to_other, 1)
    middle, latent = mixed(blocks_of(OWN), "mix_own", latent)
    from_pair, middle = lax.optimization_barrier((from_pair, middle))
    extended = jnp.concatenate([latent, from_pair[:SIDE], from_other[:SIDE]], axis=0)
    far = exchanged(extended, 1)
    cut = rows // 2
    near = [exchanged(latent[:cut], 0), exchanged(extended[cut:], 0)]
    near = jnp.concatenate(near, axis=0)

    lanes = -(-(rows + 2 * SIDE) // 256) * 256
    partial, hots, state = pl.pallas_call(
        functools.partial(own_kernel, (rows, 2 * rows, 2 * rows)),
        in_specs=[whole()] * 6,
        out_specs=[whole()] * 3,
        out_shape=[
            struct(lat_rows, outputs, lon_cols, dtype=F32),
            struct(2, 2, TAPS, lanes, lon_cols),
            struct(rows, width),
        ],
        compiler_params=params(32),
        cost_estimate=cost(1e9, 2.5e6),
        name="own_band",
    )(state, own, inner, outer, extended, middle)
    band_scratch = [
        pltpu.VMEM((outputs, TAPS * lanes), BF16),
        pltpu.VMEM((2 * outputs, TAPS * lanes), BF16),
        pltpu.VMEM((lon_cols // LANES, 2 * outputs, LANES), F32),
    ]
    partial = pl.pallas_call(
        functools.partial(band_kernel, True),
        in_specs=[whole()] * 4,
        out_specs=whole(),
        out_shape=struct(lat_rows, outputs, lon_cols, dtype=F32),
        scratch_shapes=band_scratch,
        compiler_params=params(32),
        cost_estimate=cost(1e9, 2.5e6),
        name="inner_band",
    )(near, edges, hots, partial)
    fields = pl.pallas_call(
        functools.partial(band_kernel, False),
        in_specs=[whole()] * 4,
        out_specs=whole(),
        out_shape=struct(out_ch, lat_rows, lon_cols),
        scratch_shapes=band_scratch,
        compiler_params=params(32),
        cost_estimate=cost(1e9, 2.5e6),
        name="outer_band",
    )(far, edges, hots, partial)
    return (state.reshape(1, rows, width), fields.reshape(1, out_ch, lat_rows, lon_cols))


def solution(mesh):
    in_specs = (
        P(None, ("reg", "lon"), None),
        P(),
        P(),
        P(),
        P(),
        P(("reg", "lon"), None),
        P("reg", "lon"),
        P(None, "reg", None, None),
        P(),
    )
    out_specs = (P(None, ("reg", "lon"), None), P(None, None, "reg", "lon"))
    return jax.shard_map(shards, mesh=mesh, in_specs=in_specs, out_specs=out_specs, check_vma=False)
```

```python
import functools
import math

import jax
import jax.numpy as jnp
from jax import lax
from jax.experimental import pallas as pl
from jax.experimental.pallas import tpu as pltpu
from jax.sharding import PartitionSpec as P

HEADS = 16
REACH = 2
TAPS = 2 * REACH + 1
SIDE = 8
ROWS = 16
LANES = 128
EARLY = 2
CANDIDATES = 5
F32 = jnp.float32
BF16 = jnp.bfloat16
NT = (((1,), (1,)), ((), ()))

ABOVE = ((-2, (0,)), (-1, (0, 1)))
OWN = ((0, (0, 1)), (1, (0, 1)))
BELOW = ((3, (1,)), (2, (0, 1)))


def blocks_of(band):
    return [
        (out_row, src - out_row + REACH, off)
        for src, out_rows in band
        for off in range(TAPS)
        for out_row in out_rows
    ]


def iota(shape, dim):
    return lax.broadcasted_iota(jnp.int32, shape, dim)


def normalise(rows, gain):
    values = rows.astype(F32)
    center = values - jnp.mean(values, axis=-1, keepdims=True)
    spread = jnp.mean(center * center, axis=-1, keepdims=True)
    return (center * lax.rsqrt(spread + 1e-05) * gain).astype(BF16)


def mix_kernel(blocks, psi_ref, dec_ref, mixed_ref, psi_rows_ref, taps_ref):
    basis, out_ch, channels = dec_ref.shape
    depth = basis * ROWS
    for tap in range(TAPS):
        for off in range(TAPS):
            at = (tap * TAPS + off) * 2
            psi_rows_ref[at : at + 2, :] = psi_ref[tap, off]
    spread = (iota((basis, depth), 1) // ROWS == iota((basis, depth), 0)).astype(F32)
    expanded = jnp.dot(psi_rows_ref[...], spread, preferred_element_type=F32)
    pick = iota((ROWS, depth), 1) % ROWS == iota((ROWS, depth), 0)
    for at, (out_row, tap, off) in enumerate(blocks):
        source = (tap * TAPS + off) * 2 + out_row
        taps = jnp.broadcast_to(expanded[source : source + 1], (ROWS, depth))
        taps_ref[at * ROWS : (at + 1) * ROWS, :] = jnp.where(pick, taps, 0.0).astype(BF16)
    for first in range(0, out_ch, ROWS):
        size = min(ROWS, out_ch - first)
        pieces = []
        for base in range(basis):
            pieces.append(dec_ref[base, first : first + size, :])
            if size < ROWS:
                pieces.append(jnp.zeros((ROWS - size, channels), BF16))
        mixing = jnp.concatenate(pieces, axis=0)
        mixed = jnp.dot(taps_ref[...], mixing, preferred_element_type=F32).astype(BF16)
        mixed_ref[:, first : first + ROWS, :] = mixed.reshape(len(blocks), ROWS, channels)


def listed_blocks(sectors, listed_ref):
    reg_here, lon_here = lax.axis_index("reg"), lax.axis_index("lon")
    toward = 1 - 2 * (reg_here % 2)
    found = []
    for at in range(1, listed_ref.shape[1]):
        block = listed_ref[0, at]
        step_reg = (block // sectors - reg_here) * toward
        step_lon = (block % sectors - lon_here + 1 + sectors) % sectors - 1
        lean = step_lon * (1 - 2 * (lon_here % 2))
        side = jnp.where(lean == 0, 0, jnp.where(lean > 0, 1, 4))
        ahead = jnp.where(lean < 0, 0, 1)
        behind = jnp.where(lean < 0, 7, 4 + side)
        found.append(jnp.where(step_reg == 0, ahead, jnp.where(step_reg > 0, 2 + side, behind)))
    for low in range(len(found)):
        for high in range(low + 1, len(found)):
            less, more = jnp.minimum(found[low], found[high]), jnp.maximum(found[low], found[high])
            found[low], found[high] = less, more
    return found


def gather_kernel(x_hbm, assign_hbm, own_ref, assign_ref, sems):
    rows = own_ref.shape[0] - ROWS
    copies = [
        pltpu.make_async_copy(assign_hbm, assign_ref, sems.at[0]),
        pltpu.make_async_copy(x_hbm, own_ref.at[pl.ds(0, rows)], sems.at[1]),
    ]
    for copy in copies:
        copy.start()
    copies[0].wait()
    local = lax.rem(assign_ref[...], rows).astype(F32)
    line = jnp.concatenate([local[:1], local[1:2]], axis=1)
    line = jnp.broadcast_to(line, (ROWS, line.shape[1]))
    own_ref[rows:] = jnp.where(iota(line.shape, 0) == 0, line, 0.0).astype(BF16)
    copies[1].wait()


def prepare_kernel(
    sectors,
    own_ref, gain_hbm, wqkv_hbm, assign_hbm, listed_hbm,
    query_ref, key_ref, value_ref, wk_ref, wvt_ref, choice_ref, cells_ref,
    gain_ref, wqkv_ref, cell_ref, listed_ref, sems,
):
    copies = [
        pltpu.make_async_copy(source, target, sems.at[at])
        for at, (source, target) in enumerate(
            (
                (gain_hbm, gain_ref),
                (wqkv_hbm, wqkv_ref),
                (assign_hbm, cell_ref),
                (listed_hbm, listed_ref),
            )
        )
    ]
    for copy in copies:
        copy.start()
    rows, width = key_ref.shape
    group, members = query_ref.shape[1], query_ref.shape[2] // rows
    head = group // members
    for copy in copies[2:]:
        copy.wait()
    for at, number in enumerate(listed_blocks(sectors, listed_ref)):
        for candidate in range(CANDIDATES):
            same = jnp.full((ROWS, LANES), jnp.where(number == at + candidate, 1.0, 0.0), F32)
            choice_ref[at, candidate] = same.astype(BF16)
    lat_rows, lon_cols = cell_ref.shape
    place, node = iota((ROWS, rows), 0), iota((ROWS, rows), 1)
    odd = lax.axis_index("lon") % 2
    for side, first in enumerate(((1 - odd) * (lon_cols - REACH), odd * (lon_cols - REACH))):
        hit = jnp.zeros((ROWS, rows), F32)
        for row in range(lat_rows):
            for col in range(REACH):
                cell = cell_ref[row, first + col] % rows
                hit = jnp.where((place == row * REACH + col) & (node == cell), 1.0, hit)
        cells_ref[side * ROWS : (side + 1) * ROWS] = hit.astype(BF16)
    copies[0].wait()
    normed = normalise(own_ref[:rows], gain_ref[...])
    copies[1].wait()
    query = jnp.dot(normed, wqkv_ref[:, :width], preferred_element_type=F32)
    query_t = (query * (math.log2(math.e) / head**0.5)).T.astype(BF16)
    mask = (iota((group, members * rows), 0) // head) == (iota((group, members * rows), 1) // rows)
    for part in range(width // group):
        piece = query_t[part * group : (part + 1) * group]
        wide = jnp.concatenate([piece] * members, axis=1)
        query_ref[part] = jnp.where(mask, wide, jnp.zeros_like(wide))
    wk = wqkv_ref[:, width : 2 * width]
    wk_ref[...] = wk
    key_ref[...] = jnp.dot(normed, wk, preferred_element_type=F32).astype(BF16)
    wvt = wqkv_ref[:, 2 * width :].astype(F32).T.astype(BF16)
    wvt_ref[...] = wvt
    value_ref[...] = lax.dot_general(wvt, normed, NT, preferred_element_type=F32).astype(BF16)


def chosen(entries, rows, choice_ref, candidates):
    tall, wide = rows // ROWS, candidates[-1].shape[1] // LANES
    near = []
    for entry in entries:
        total = None
        for at in range(CANDIDATES):
            weight = jnp.concatenate([choice_ref[entry, at]] * wide, axis=1)
            part = candidates[entry + at] * jnp.concatenate([weight] * tall, axis=0)
            total = part if total is None else total + part
        near.append(total)
    return jnp.concatenate(near, axis=0)


def project(nodes, gain, wk_ref, wvt_ref):
    normed = normalise(nodes, gain)
    keys = jnp.dot(normed, wk_ref[...], preferred_element_type=F32).astype(BF16)
    values = jnp.dot(wvt_ref[...], normed.T, preferred_element_type=F32).astype(BF16)
    return keys, values


def own_heads(summed, rows):
    members = summed.shape[1] // rows
    head = summed.shape[0] // members
    return [
        summed[at * head : (at + 1) * head, at * rows : (at + 1) * rows] for at in range(members)
    ]


def early_kernel(
    choice_ref, other_ref, pair_ref, inner_ref, outer_ref,
    gain_ref, wk_ref, wvt_ref, query_ref, key_ref, value_ref,
    top_ref, sum_ref, keys_ref, values_ref,
):
    rows = key_ref.shape[0]
    parts, group, _ = query_ref.shape
    candidates = [other_ref[...], pair_ref[...]]
    candidates += [ref[rows : 2 * rows] if center else ref[:rows] for ref in (inner_ref, outer_ref) for center in (1, 0)]
    nodes = chosen(range(EARLY), rows, choice_ref, candidates)
    keys, values = project(nodes, gain_ref[...], wk_ref, wvt_ref)
    keys_ref[:rows] = key_ref[...]
    keys_ref[rows:] = keys
    for part in range(parts):
        span = slice(part * group, (part + 1) * group)
        values_ref[part, :group, :rows] = value_ref[span]
        values_ref[part, :group, rows:] = values[span]
        values_ref[part, group:, :] = jnp.ones((ROWS, keys_ref.shape[0]), BF16)

    spans = [slice(part * group, (part + 1) * group) for part in range(parts)]
    scores = [
        jnp.dot(keys_ref[:, span], query_ref[part], preferred_element_type=F32)
        for part, span in enumerate(spans)
    ]
    tops = [jnp.max(one, axis=0, keepdims=True) for one in scores]
    expos = [jnp.exp2(one - top).astype(BF16) for one, top in zip(scores, tops)]
    sums = [
        jnp.dot(values_ref[part], expo, preferred_element_type=F32) for part, expo in enumerate(expos)
    ]
    for part, (top, summed) in enumerate(zip(tops, sums)):
        top_ref[part, 0] = jnp.broadcast_to(top, top_ref.shape[2:])
        top_ref[part, 1] = jnp.broadcast_to(summed[group : group + 1], top_ref.shape[2:])
        sum_ref[part] = jnp.concatenate(own_heads(summed[:group], rows), axis=0)


def late_kernel(
    choice_ref, cells_ref, inner_ref, outer_ref, beside_ref, corner_ref,
    own_ref, gain_ref, wk_ref, wvt_ref, query_ref, top_ref, sum_ref, wout_ref, wlat_ref,
    state_ref, latent_ref, to_pair_ref, to_other_ref,
):
    rows, width = state_ref.shape
    parts, group, lanes = query_ref.shape
    members = lanes // rows
    head = group // members
    candidates = [None, None]
    candidates += [ref[rows : 2 * rows] if center else ref[:rows] for ref in (inner_ref, outer_ref) for center in (1, 0)]
    candidates += [beside_ref[...], corner_ref[...]]
    nodes = chosen(range(EARLY, choice_ref.shape[0]), rows, choice_ref, candidates)
    keys, values = project(nodes, gain_ref[...], wk_ref, wvt_ref)
    ones = jnp.ones((ROWS, nodes.shape[0]), BF16)
    spans = [slice(part * group, (part + 1) * group) for part in range(parts)]
    scores = [
        jnp.dot(keys[:, span], query_ref[part], preferred_element_type=F32)
        for part, span in enumerate(spans)
    ]
    befores = [top_ref[part, 0, :1] for part in range(parts)]
    tops = [
        jnp.maximum(before, jnp.max(one, axis=0, keepdims=True))
        for before, one in zip(befores, scores)
    ]
    expos = [jnp.exp2(one - top).astype(BF16) for one, top in zip(scores, tops)]
    sums = [
        jnp.dot(jnp.concatenate([values[span], ones], axis=0), expo, preferred_element_type=F32)
        for span, expo in zip(spans, expos)
    ]
    attended = []
    for part, summed in enumerate(sums):
        shrink = jnp.exp2(befores[part] - tops[part])
        share = 1.0 / (summed[group : group + 1] + top_ref[part, 1, :1] * shrink)
        merged = []
        for member, piece in enumerate(own_heads(summed[:group], rows)):
            span = slice(member * rows, (member + 1) * rows)
            earlier = sum_ref[part, member * head : (member + 1) * head]
            merged.append((piece + earlier * shrink[:, span]) * share[:, span])
        attended.append(jnp.concatenate(merged, axis=0).T.astype(BF16))
    attended = jnp.concatenate(attended, axis=1)
    state = (
        own_ref[:rows].astype(F32)
        + jnp.dot(attended, wout_ref[...], preferred_element_type=F32)
    ).astype(BF16)
    state_ref[...] = state
    value = jnp.dot(state, wlat_ref[...], preferred_element_type=F32)
    latent = (value / (1.0 + jnp.exp(-value))).astype(BF16)
    latent_ref[...] = latent
    cells = jnp.dot(cells_ref[...], latent, preferred_element_type=F32).astype(BF16)
    to_pair_ref[...] = cells[:ROWS]
    to_other_ref[...] = cells[ROWS:]


def hot_rows(values, rows, cols, line):
    odd = lax.axis_index("lon") % 2
    column = iota((8, cols), 1)
    node = iota((rows + 2 * SIDE, cols), 0).astype(F32)
    for off in range(TAPS):
        step = off - REACH
        where = jnp.broadcast_to(values, (8, cols))
        if step:
            where = pltpu.roll(where, (-step) % cols, 1)
        reach = column + step
        before = (rows + (1 - odd) * SIDE + REACH * line + reach + REACH).astype(F32)
        after = (rows + odd * SIDE + REACH * line + reach - cols).astype(F32)
        where = jnp.where(reach < 0, before, jnp.where(reach >= cols, after, where))
        yield jnp.where(node == where[:1], 1.0, 0.0).astype(BF16)


def shares_of(latent, weights):
    blocks, outputs, channels = weights.shape
    shares = jnp.dot(
        weights.reshape(blocks * outputs, channels), latent.T, preferred_element_type=F32
    ).astype(BF16)
    return [shares[at * outputs : (at + 1) * outputs] for at in range(blocks)]


def lines_of(line_ref, start, cols):
    values = line_ref[start : start + ROWS, :].astype(F32)
    return values[:1, :cols], values[:1, cols:]


def own_kernel(
    begin, state_ref, own_ref, inner_ref, outer_ref, latent_ref, weights_ref,
    out_ref, hot_ref, kept_ref,
):
    kept_ref[...] = state_ref[...]
    cols = out_ref.shape[2]
    rows = latent_ref.shape[0] - 2 * SIDE
    own = lines_of(own_ref, begin[0], cols)
    table = [list(hot_rows(own[line], rows, cols, line)) for line in range(2)]
    acc = [None, None]
    for (out_row, tap, off), share in zip(
        blocks_of(OWN), shares_of(latent_ref[...], weights_ref[...])
    ):
        line = out_row + tap - REACH
        piece = jnp.dot(share, table[line][off], preferred_element_type=F32)
        acc[out_row] = piece if acc[out_row] is None else acc[out_row] + piece
    for row in range(2):
        out_ref[row] = acc[row]
    odd = lax.axis_index("reg") % 2 == 1
    inner, outer = lines_of(inner_ref, begin[1], cols), lines_of(outer_ref, begin[2], cols)
    nodes = rows + 2 * SIDE
    for band, (yes, no) in enumerate(((inner, outer), (outer, inner))):
        for at, line in enumerate((0, 1) if band == 0 else (1, 0)):
            values = jnp.where(odd, yes[line], no[line])
            for off, hot in enumerate(hot_rows(values, rows, cols, line)):
                hot_ref[band, at, off, :nodes] = hot
                hot_ref[band, at, off, nodes:] = jnp.zeros((hot_ref.shape[3] - nodes, cols), BF16)


def band_kernel(
    from_inner, latent_ref, weights_ref, hot_ref, partial_ref, out_ref, one_ref, two_ref, paired_ref
):
    odd = lax.axis_index("reg") % 2
    band = 1 - odd if from_inner else odd
    latent = latent_ref[...]
    lanes, cols = hot_ref.shape[3:]
    outputs = weights_ref.shape[1]
    blank = jnp.zeros((lanes - latent.shape[0], latent.shape[1]), BF16)
    blocks = len(blocks_of(ABOVE))
    weights = weights_ref[pl.ds(band * blocks, blocks)]
    shares = shares_of(jnp.concatenate([latent, blank], axis=0), weights)
    for off in range(TAPS):
        span = slice(off * lanes, (off + 1) * lanes)
        one_ref[:, span] = shares[off]
        for row in range(2):
            two_ref[row * outputs : (row + 1) * outputs, span] = shares[TAPS + 2 * off + row]
    depth = TAPS * lanes
    one = jnp.dot(one_ref[...], hot_ref[band, 0].reshape(depth, cols), preferred_element_type=F32)
    two = jnp.dot(two_ref[...], hot_ref[band, 1].reshape(depth, cols), preferred_element_type=F32)
    for row in range(2):
        total = partial_ref[row] + two[row * outputs : (row + 1) * outputs]
        total = total + jnp.where(band == row, one, 0.0)
        if from_inner:
            out_ref[row] = total
        else:
            for tile in range(cols // LANES):
                part = total[:, tile * LANES : (tile + 1) * LANES]
                paired_ref[tile, pl.ds(row, outputs, stride=2), :] = part
    if not from_inner:
        out_ch = out_ref.shape[0]
        tiles = [paired_ref[tile, : 2 * out_ch, :] for tile in range(cols // LANES)]
        out_ref[...] = jnp.concatenate(tiles, axis=1).astype(BF16).reshape(out_ref.shape)


def whole(memory=pltpu.VMEM):
    return pl.BlockSpec(memory_space=memory)


def struct(*shape, dtype=BF16):
    return jax.ShapeDtypeStruct(shape, dtype)


def params(limit):
    return pltpu.CompilerParams(vmem_limit_bytes=limit << 20)


def cost(flops, moved):
    return pl.CostEstimate(flops=int(flops), bytes_accessed=int(moved), transcendentals=0)


def shards(nodes, norm_gain, w_qkv, w_out, w_latent, neighbours, assignment, psi, w_dec):
    _, rows, width = nodes.shape
    channels = w_latent.shape[1]
    lat_rows, lon_cols = assignment.shape
    basis, _, out_ch = w_dec.shape
    sectors = lax.axis_size("lon")
    count = neighbours.shape[1]
    x = nodes.reshape(rows, width)
    gain = norm_gain.reshape(1, width)

    def paired(array, first):
        pairs = [(i, (i + 1) % sectors) for i in range(first, sectors, 2)]
        return lax.ppermute(array, "lon", pairs + [(j, i) for i, j in pairs])

    def exchanged(array, first):
        size = lax.axis_size("reg")
        pairs = [(i, i + 1) for i in range(first, size - 1, 2)]
        return lax.ppermute(array, "reg", pairs + [(j, i) for i, j in pairs])

    def in_hbm(*arrays):
        return [pltpu.with_memory_space_constraint(array, pltpu.HBM) for array in arrays]

    other = paired(x, 1)
    pair = paired(x, 0)

    outputs = -(-out_ch // ROWS) * ROWS
    head = width // HEADS
    members = LANES // head
    parts = HEADS // members
    def mixed(blocks, name, after):
        taps = psi.transpose(2, 3, 1, 0)
        mixing = w_dec.transpose(0, 2, 1)
        taps, mixing, after = lax.optimization_barrier((taps, mixing, after))
        weights = pl.pallas_call(
            functools.partial(mix_kernel, blocks),
            in_specs=[whole()] * 2,
            out_specs=whole(),
            out_shape=struct(len(blocks), outputs, channels),
            scratch_shapes=[
                pltpu.VMEM((2 * TAPS * TAPS, basis), F32),
                pltpu.VMEM((len(blocks) * ROWS, basis * ROWS), BF16),
            ],
            compiler_params=params(32),
            cost_estimate=cost(2e9, 6e6),
            name=name,
        )(taps, mixing)
        return weights, after

    own = pl.pallas_call(
        gather_kernel,
        in_specs=[whole(pltpu.HBM)] * 2,
        out_specs=whole(),
        out_shape=struct(rows + ROWS, width),
        scratch_shapes=[
            pltpu.VMEM(assignment.shape, jnp.int32),
            pltpu.SemaphoreType.DMA((2,)),
        ],
        compiler_params=params(32),
        cost_estimate=cost(1e3, 1e3),
        name="gather",
    )(*in_hbm(x, assignment))
    query, key, value, wk, wvt, choice, cells = pl.pallas_call(
        functools.partial(prepare_kernel, sectors),
        in_specs=[whole()] + [whole(pltpu.HBM)] * 4,
        out_specs=[whole()] * 7,
        out_shape=[
            struct(parts, LANES, members * rows),
            struct(rows, width),
            struct(width, rows),
            struct(width, width),
            struct(width, width),
            struct(count - 1, CANDIDATES, ROWS, LANES),
            struct(2 * ROWS, rows),
        ],
        scratch_shapes=[
            pltpu.VMEM((1, width), F32),
            pltpu.VMEM(w_qkv.shape, BF16),
            pltpu.SMEM(assignment.shape, jnp.int32),
            pltpu.SMEM(neighbours.shape, jnp.int32),
            pltpu.SemaphoreType.DMA((4,)),
        ],
        compiler_params=params(32),
        cost_estimate=cost(5e8, 1e6),
        name="prepare",
    )(own, *in_hbm(gain, w_qkv, assignment, neighbours))
    own, query = lax.optimization_barrier((own, query))
    message = jnp.concatenate([pair, own], axis=0)
    message_a = message
    other_a = other
    inner = exchanged(message_a, 0)
    outer = exchanged(message, 1)
    corner = exchanged(other, 1)
    beside = exchanged(other_a, 0)

    edges, other_m = mixed(blocks_of(ABOVE) + blocks_of(BELOW), "mix_edges", other)
    inner, edges = lax.optimization_barrier((inner, edges))
    top, summed = pl.pallas_call(
        early_kernel,
        in_specs=[whole()] * 11,
        out_specs=[whole()] * 2,
        out_shape=[
            struct(parts, 2, 8, members * rows, dtype=F32),
            struct(parts, LANES, rows, dtype=F32),
        ],
        scratch_shapes=[
            pltpu.VMEM(((1 + EARLY) * rows, width), BF16),
            pltpu.VMEM((parts, LANES + ROWS, (1 + EARLY) * rows), BF16),
        ],
        compiler_params=params(32),
        cost_estimate=cost(3e9, 6e6),
        name="early",
    )(choice, other, pair, inner, outer, gain, wk, wvt, query, key, value)
    state, latent, to_pair, to_other = pl.pallas_call(
        late_kernel,
        in_specs=[whole()] * 15,
        out_specs=[whole()] * 4,
        out_shape=[pltpu.VMEM((rows, width), BF16), struct(rows, channels)]
        + [struct(ROWS, channels)] * 2,
        compiler_params=params(32),
        cost_estimate=cost(3e9, 6e6),
        name="late",
    )(
        choice, cells, inner, outer, beside, corner,
        own, gain, wk, wvt, query, top, summed, w_out, w_latent,
    )

    from_pair = paired(to_pair, 0)
    from_other = paired(to_other, 1)
    middle, latent = mixed(blocks_of(OWN), "mix_own", latent)
    from_pair, middle = lax.optimization_barrier((from_pair, middle))
    extended = jnp.concatenate([latent, from_pair[:SIDE], from_other[:SIDE]], axis=0)
    far = exchanged(extended, 1)
    near = exchanged(extended, 0)

    lanes = -(-(rows + 2 * SIDE) // 256) * 256
    partial, hots, state = pl.pallas_call(
        functools.partial(own_kernel, (rows, 2 * rows, 2 * rows)),
        in_specs=[whole()] * 6,
        out_specs=[whole()] * 3,
        out_shape=[
            struct(lat_rows, outputs, lon_cols, dtype=F32),
            struct(2, 2, TAPS, lanes, lon_cols),
            struct(rows, width),
        ],
        compiler_params=params(32),
        cost_estimate=cost(1e9, 2.5e6),
        name="own_band",
    )(state, own, inner, outer, extended, middle)
    band_scratch = [
        pltpu.VMEM((outputs, TAPS * lanes), BF16),
        pltpu.VMEM((2 * outputs, TAPS * lanes), BF16),
        pltpu.VMEM((lon_cols // LANES, 2 * outputs, LANES), F32),
    ]
    partial = pl.pallas_call(
        functools.partial(band_kernel, True),
        in_specs=[whole()] * 4,
        out_specs=whole(),
        out_shape=struct(lat_rows, outputs, lon_cols, dtype=F32),
        scratch_shapes=band_scratch,
        compiler_params=params(32),
        cost_estimate=cost(1e9, 2.5e6),
        name="inner_band",
    )(near, edges, hots, partial)
    fields = pl.pallas_call(
        functools.partial(band_kernel, False),
        in_specs=[whole()] * 4,
        out_specs=whole(),
        out_shape=struct(out_ch, lat_rows, lon_cols),
        scratch_shapes=band_scratch,
        compiler_params=params(32),
        cost_estimate=cost(1e9, 2.5e6),
        name="outer_band",
    )(far, edges, hots, partial)
    return (state.reshape(1, rows, width), fields.reshape(1, out_ch, lat_rows, lon_cols))


def solution(mesh):
    in_specs = (
        P(None, ("reg", "lon"), None),
        P(),
        P(),
        P(),
        P(),
        P(("reg", "lon"), None),
        P("reg", "lon"),
        P(None, "reg", None, None),
        P(),
    )
    out_specs = (P(None, ("reg", "lon"), None), P(None, None, "reg", "lon"))
    return jax.shard_map(shards, mesh=mesh, in_specs=in_specs, out_specs=out_specs, check_vma=False)
```

```python
import functools
import math

import jax
import jax.numpy as jnp
from jax import lax
from jax.experimental import pallas as pl
from jax.experimental.pallas import tpu as pltpu
from jax.sharding import PartitionSpec as P

HEADS = 16
REACH = 2
TAPS = 2 * REACH + 1
SIDE = 8
ROWS = 16
LANES = 128
EARLY = 2
CANDIDATES = 5
F32 = jnp.float32
BF16 = jnp.bfloat16
NT = (((1,), (1,)), ((), ()))

ABOVE = ((-2, (0,)), (-1, (0, 1)))
OWN = ((0, (0, 1)), (1, (0, 1)))
BELOW = ((3, (1,)), (2, (0, 1)))


def blocks_of(band):
    return [
        (out_row, src - out_row + REACH, off)
        for src, out_rows in band
        for off in range(TAPS)
        for out_row in out_rows
    ]


def iota(shape, dim):
    return lax.broadcasted_iota(jnp.int32, shape, dim)


def normalise(rows, gain):
    values = rows.astype(F32)
    center = values - jnp.mean(values, axis=-1, keepdims=True)
    spread = jnp.mean(center * center, axis=-1, keepdims=True)
    return (center * lax.rsqrt(spread + 1e-05) * gain).astype(BF16)


def mix_kernel(blocks, psi_ref, dec_ref, mixed_ref, psi_rows_ref, taps_ref):
    basis, out_ch, channels = dec_ref.shape
    depth = basis * ROWS
    for tap in range(TAPS):
        for off in range(TAPS):
            at = (tap * TAPS + off) * 2
            psi_rows_ref[at : at + 2, :] = psi_ref[tap, off]
    spread = (iota((basis, depth), 1) // ROWS == iota((basis, depth), 0)).astype(F32)
    expanded = jnp.dot(psi_rows_ref[...], spread, preferred_element_type=F32)
    pick = iota((ROWS, depth), 1) % ROWS == iota((ROWS, depth), 0)
    for at, (out_row, tap, off) in enumerate(blocks):
        source = (tap * TAPS + off) * 2 + out_row
        taps = jnp.broadcast_to(expanded[source : source + 1], (ROWS, depth))
        taps_ref[at * ROWS : (at + 1) * ROWS, :] = jnp.where(pick, taps, 0.0).astype(BF16)
    for first in range(0, out_ch, ROWS):
        size = min(ROWS, out_ch - first)
        pieces = []
        for base in range(basis):
            pieces.append(dec_ref[base, first : first + size, :])
            if size < ROWS:
                pieces.append(jnp.zeros((ROWS - size, channels), BF16))
        mixing = jnp.concatenate(pieces, axis=0)
        mixed = jnp.dot(taps_ref[...], mixing, preferred_element_type=F32).astype(BF16)
        mixed_ref[:, first : first + ROWS, :] = mixed.reshape(len(blocks), ROWS, channels)


def listed_blocks(sectors, listed_ref):
    reg_here, lon_here = lax.axis_index("reg"), lax.axis_index("lon")
    toward = 1 - 2 * (reg_here % 2)
    found = []
    for at in range(1, listed_ref.shape[1]):
        block = listed_ref[0, at]
        step_reg = (block // sectors - reg_here) * toward
        step_lon = (block % sectors - lon_here + 1 + sectors) % sectors - 1
        lean = step_lon * (1 - 2 * (lon_here % 2))
        side = jnp.where(lean == 0, 0, jnp.where(lean > 0, 1, 4))
        ahead = jnp.where(lean < 0, 0, 1)
        behind = jnp.where(lean < 0, 7, 4 + side)
        found.append(jnp.where(step_reg == 0, ahead, jnp.where(step_reg > 0, 2 + side, behind)))
    for low in range(len(found)):
        for high in range(low + 1, len(found)):
            less, more = jnp.minimum(found[low], found[high]), jnp.maximum(found[low], found[high])
            found[low], found[high] = less, more
    return found


def gather_kernel(x_hbm, assign_hbm, own_ref, assign_ref, sems):
    rows = own_ref.shape[0] - ROWS
    copies = [
        pltpu.make_async_copy(assign_hbm, assign_ref, sems.at[0]),
        pltpu.make_async_copy(x_hbm, own_ref.at[pl.ds(0, rows)], sems.at[1]),
    ]
    for copy in copies:
        copy.start()
    copies[0].wait()
    local = lax.rem(assign_ref[...], rows).astype(F32)
    line = jnp.concatenate([local[:1], local[1:2]], axis=1)
    line = jnp.broadcast_to(line, (ROWS, line.shape[1]))
    own_ref[rows:] = jnp.where(iota(line.shape, 0) == 0, line, 0.0).astype(BF16)
    copies[1].wait()


def prepare_kernel(
    sectors,
    own_ref, gain_hbm, wqkv_hbm, assign_hbm, listed_hbm,
    query_ref, key_ref, value_ref, wk_ref, wvt_ref, choice_ref, cells_ref, wide_ref,
    gain_ref, wqkv_ref, cell_ref, listed_ref, sems,
):
    copies = [
        pltpu.make_async_copy(source, target, sems.at[at])
        for at, (source, target) in enumerate(
            (
                (gain_hbm, gain_ref),
                (wqkv_hbm, wqkv_ref),
                (assign_hbm, cell_ref),
                (listed_hbm, listed_ref),
            )
        )
    ]
    for copy in copies:
        copy.start()
    rows, width = key_ref.shape
    group, members = query_ref.shape[1], query_ref.shape[2] // rows
    head = group // members
    for copy in copies[2:]:
        copy.wait()
    for at, number in enumerate(listed_blocks(sectors, listed_ref)):
        for candidate in range(CANDIDATES):
            same = jnp.full((ROWS, LANES), jnp.where(number == at + candidate, 1.0, 0.0), F32)
            choice_ref[at, candidate] = same.astype(BF16)
    lat_rows, lon_cols = cell_ref.shape
    place, node = iota((ROWS, rows), 0), iota((ROWS, rows), 1)
    odd = lax.axis_index("lon") % 2
    for side, first in enumerate(((1 - odd) * (lon_cols - REACH), odd * (lon_cols - REACH))):
        hit = jnp.zeros((ROWS, rows), F32)
        for row in range(lat_rows):
            for col in range(REACH):
                cell = cell_ref[row, first + col] % rows
                hit = jnp.where((place == row * REACH + col) & (node == cell), 1.0, hit)
        cells_ref[rows + side * ROWS : rows + (side + 1) * ROWS] = hit.astype(BF16)
    cells_ref[:rows] = (iota((rows, rows), 0) == iota((rows, rows), 1)).astype(F32).astype(BF16)
    wide_ref[...] = jnp.dot(cells_ref[...], own_ref[:rows], preferred_element_type=F32).astype(BF16)
    copies[0].wait()
    normed = normalise(own_ref[:rows], gain_ref[...])
    copies[1].wait()
    query = jnp.dot(normed, wqkv_ref[:, :width], preferred_element_type=F32)
    query_t = (query * (math.log2(math.e) / head**0.5)).T.astype(BF16)
    mask = (iota((group, members * rows), 0) // head) == (iota((group, members * rows), 1) // rows)
    for part in range(width // group):
        piece = query_t[part * group : (part + 1) * group]
        wide = jnp.concatenate([piece] * members, axis=1)
        query_ref[part] = jnp.where(mask, wide, jnp.zeros_like(wide))
    wk = wqkv_ref[:, width : 2 * width]
    wk_ref[...] = wk
    key_ref[...] = jnp.dot(normed, wk, preferred_element_type=F32).astype(BF16)
    wvt = wqkv_ref[:, 2 * width :].astype(F32).T.astype(BF16)
    wvt_ref[...] = wvt
    value_ref[...] = lax.dot_general(wvt, normed, NT, preferred_element_type=F32).astype(BF16)


def chosen(entries, rows, choice_ref, candidates):
    tall, wide = rows // ROWS, candidates[-1].shape[1] // LANES
    near = []
    for entry in entries:
        total = None
        for at in range(CANDIDATES):
            weight = jnp.concatenate([choice_ref[entry, at]] * wide, axis=1)
            part = candidates[entry + at] * jnp.concatenate([weight] * tall, axis=0)
            total = part if total is None else total + part
        near.append(total)
    return jnp.concatenate(near, axis=0)


def project(nodes, gain, wk_ref, wvt_ref):
    normed = normalise(nodes, gain)
    keys = jnp.dot(normed, wk_ref[...], preferred_element_type=F32).astype(BF16)
    values = lax.dot_general(wvt_ref[...], normed, NT, preferred_element_type=F32).astype(BF16)
    return keys, values


def own_heads(summed, rows):
    members = summed.shape[1] // rows
    head = summed.shape[0] // members
    return [
        summed[at * head : (at + 1) * head, at * rows : (at + 1) * rows] for at in range(members)
    ]


def early_kernel(
    choice_ref, other_ref, pair_ref, inner_ref, outer_ref,
    gain_ref, wk_ref, wvt_ref, query_ref, key_ref, value_ref,
    top_ref, sum_ref, keys_ref, values_ref,
):
    rows = key_ref.shape[0]
    parts, group, _ = query_ref.shape
    candidates = [other_ref[...], pair_ref[...]]
    candidates += [ref[rows : 2 * rows] if center else ref[:rows] for ref in (inner_ref, outer_ref) for center in (1, 0)]
    nodes = chosen(range(EARLY), rows, choice_ref, candidates)
    keys, values = project(nodes, gain_ref[...], wk_ref, wvt_ref)
    keys_ref[:rows] = key_ref[...]
    keys_ref[rows:] = keys
    for part in range(parts):
        span = slice(part * group, (part + 1) * group)
        values_ref[part, :group, :rows] = value_ref[span]
        values_ref[part, :group, rows:] = values[span]
        values_ref[part, group:, :] = jnp.ones((ROWS, keys_ref.shape[0]), BF16)

    spans = [slice(part * group, (part + 1) * group) for part in range(parts)]
    scores = [
        jnp.dot(keys_ref[:, span], query_ref[part], preferred_element_type=F32)
        for part, span in enumerate(spans)
    ]
    tops = [jnp.max(one, axis=0, keepdims=True) for one in scores]
    expos = [jnp.exp2(one - top).astype(BF16) for one, top in zip(scores, tops)]
    sums = [
        jnp.dot(values_ref[part], expo, preferred_element_type=F32) for part, expo in enumerate(expos)
    ]
    for part, (top, summed) in enumerate(zip(tops, sums)):
        top_ref[part, 0] = jnp.broadcast_to(top, top_ref.shape[2:])
        top_ref[part, 1] = jnp.broadcast_to(summed[group : group + 1], top_ref.shape[2:])
        sum_ref[part] = jnp.concatenate(own_heads(summed[:group], rows), axis=0)


def late_kernel(
    choice_ref, cells_ref, inner_ref, outer_ref, beside_ref, corner_ref,
    wide_ref, gain_ref, wk_ref, wvt_ref, query_ref, top_ref, sum_ref, wout_ref, wlat_ref,
    state_ref, latent_ref, to_pair_ref, to_other_ref,
):
    rows, width = state_ref.shape
    parts, group, lanes = query_ref.shape
    members = lanes // rows
    head = group // members
    candidates = [None, None]
    candidates += [ref[rows : 2 * rows] if center else ref[:rows] for ref in (inner_ref, outer_ref) for center in (1, 0)]
    candidates += [beside_ref[...], corner_ref[...]]
    nodes = chosen(range(EARLY, choice_ref.shape[0]), rows, choice_ref, candidates)
    keys, values = project(nodes, gain_ref[...], wk_ref, wvt_ref)
    ones = jnp.ones((ROWS, nodes.shape[0]), BF16)
    spans = [slice(part * group, (part + 1) * group) for part in range(parts)]
    scores = [
        jnp.dot(keys[:, span], query_ref[part], preferred_element_type=F32)
        for part, span in enumerate(spans)
    ]
    befores = [top_ref[part, 0, :1] for part in range(parts)]
    tops = [
        jnp.maximum(before, jnp.max(one, axis=0, keepdims=True))
        for before, one in zip(befores, scores)
    ]
    expos = [jnp.exp2(one - top).astype(BF16) for one, top in zip(scores, tops)]
    sums = [
        jnp.dot(jnp.concatenate([values[span], ones], axis=0), expo, preferred_element_type=F32)
        for span, expo in zip(spans, expos)
    ]
    attended = []
    for part, summed in enumerate(sums):
        shrink = jnp.exp2(befores[part] - tops[part])
        share = 1.0 / (summed[group : group + 1] + top_ref[part, 1, :1] * shrink)
        merged = []
        for member, piece in enumerate(own_heads(summed[:group], rows)):
            span = slice(member * rows, (member + 1) * rows)
            earlier = sum_ref[part, member * head : (member + 1) * head]
            merged.append((piece + earlier * shrink[:, span]) * share[:, span])
        merged = jnp.concatenate(merged, axis=0).astype(BF16)
        turned = lax.dot_general(cells_ref[...], merged, NT, preferred_element_type=F32)
        attended.append(turned.astype(BF16))
    attended = jnp.concatenate(attended, axis=1)
    state = (
        wide_ref[...].astype(F32) + jnp.dot(attended, wout_ref[...], preferred_element_type=F32)
    ).astype(BF16)
    state_ref[...] = state[:rows]
    value = jnp.dot(state, wlat_ref[...], preferred_element_type=F32)
    latent = (value / (1.0 + jnp.exp(-value))).astype(BF16)
    latent_ref[...] = latent[:rows]
    to_pair_ref[...] = latent[rows : rows + ROWS]
    to_other_ref[...] = latent[rows + ROWS :]


def hot_rows(values, rows, cols, line):
    odd = lax.axis_index("lon") % 2
    column = iota((8, cols), 1)
    node = iota((rows + 2 * SIDE, cols), 0).astype(F32)
    for off in range(TAPS):
        step = off - REACH
        where = jnp.broadcast_to(values, (8, cols))
        if step:
            where = pltpu.roll(where, (-step) % cols, 1)
        reach = column + step
        before = (rows + (1 - odd) * SIDE + REACH * line + reach + REACH).astype(F32)
        after = (rows + odd * SIDE + REACH * line + reach - cols).astype(F32)
        where = jnp.where(reach < 0, before, jnp.where(reach >= cols, after, where))
        yield jnp.where(node == where[:1], 1.0, 0.0).astype(BF16)


def shares_of(latent, weights):
    blocks, outputs, channels = weights.shape
    shares = lax.dot_general(
        weights.reshape(blocks * outputs, channels), latent, NT, preferred_element_type=F32
    ).astype(BF16)
    return [shares[at * outputs : (at + 1) * outputs] for at in range(blocks)]


def lines_of(line_ref, start, cols):
    values = line_ref[start : start + ROWS, :].astype(F32)
    return values[:1, :cols], values[:1, cols:]


def own_kernel(
    begin, state_ref, own_ref, inner_ref, outer_ref, latent_ref, weights_ref,
    out_ref, hot_ref, kept_ref,
):
    kept_ref[...] = state_ref[...]
    cols = out_ref.shape[2]
    rows = latent_ref.shape[0] - 2 * SIDE
    own = lines_of(own_ref, begin[0], cols)
    table = [list(hot_rows(own[line], rows, cols, line)) for line in range(2)]
    acc = [None, None]
    for (out_row, tap, off), share in zip(
        blocks_of(OWN), shares_of(latent_ref[...], weights_ref[...])
    ):
        line = out_row + tap - REACH
        piece = jnp.dot(share, table[line][off], preferred_element_type=F32)
        acc[out_row] = piece if acc[out_row] is None else acc[out_row] + piece
    for row in range(2):
        out_ref[row] = acc[row]
    odd = lax.axis_index("reg") % 2 == 1
    inner, outer = lines_of(inner_ref, begin[1], cols), lines_of(outer_ref, begin[2], cols)
    nodes = rows + 2 * SIDE
    for band, (yes, no) in enumerate(((inner, outer), (outer, inner))):
        for at, line in enumerate((0, 1) if band == 0 else (1, 0)):
            values = jnp.where(odd, yes[line], no[line])
            for off, hot in enumerate(hot_rows(values, rows, cols, line)):
                hot_ref[band, at, off, :nodes] = hot
                hot_ref[band, at, off, nodes:] = jnp.zeros((hot_ref.shape[3] - nodes, cols), BF16)


def band_kernel(
    from_inner, latent_ref, weights_ref, hot_ref, partial_ref, out_ref, one_ref, two_ref, paired_ref
):
    odd = lax.axis_index("reg") % 2
    band = 1 - odd if from_inner else odd
    latent = latent_ref[...]
    lanes, cols = hot_ref.shape[3:]
    outputs = weights_ref.shape[1]
    blank = jnp.zeros((lanes - latent.shape[0], latent.shape[1]), BF16)
    blocks = len(blocks_of(ABOVE))
    weights = weights_ref[pl.ds(band * blocks, blocks)]
    shares = shares_of(jnp.concatenate([latent, blank], axis=0), weights)
    for off in range(TAPS):
        span = slice(off * lanes, (off + 1) * lanes)
        one_ref[:, span] = shares[off]
        for row in range(2):
            two_ref[row * outputs : (row + 1) * outputs, span] = shares[TAPS + 2 * off + row]
    depth = TAPS * lanes
    one = jnp.dot(one_ref[...], hot_ref[band, 0].reshape(depth, cols), preferred_element_type=F32)
    two = jnp.dot(two_ref[...], hot_ref[band, 1].reshape(depth, cols), preferred_element_type=F32)
    for row in range(2):
        total = partial_ref[row] + two[row * outputs : (row + 1) * outputs]
        total = total + jnp.where(band == row, one, 0.0)
        if from_inner:
            out_ref[row] = total
        else:
            for tile in range(cols // LANES):
                part = total[:, tile * LANES : (tile + 1) * LANES]
                paired_ref[tile, pl.ds(row, outputs, stride=2), :] = part
    if not from_inner:
        out_ch = out_ref.shape[0]
        tiles = [paired_ref[tile, : 2 * out_ch, :] for tile in range(cols // LANES)]
        out_ref[...] = jnp.concatenate(tiles, axis=1).astype(BF16).reshape(out_ref.shape)


def whole(memory=pltpu.VMEM):
    return pl.BlockSpec(memory_space=memory)


def struct(*shape, dtype=BF16):
    return jax.ShapeDtypeStruct(shape, dtype)


def params(limit):
    return pltpu.CompilerParams(vmem_limit_bytes=limit << 20)


def cost(flops, moved):
    return pl.CostEstimate(flops=int(flops), bytes_accessed=int(moved), transcendentals=0)


def shards(nodes, norm_gain, w_qkv, w_out, w_latent, neighbours, assignment, psi, w_dec):
    _, rows, width = nodes.shape
    channels = w_latent.shape[1]
    lat_rows, lon_cols = assignment.shape
    basis, _, out_ch = w_dec.shape
    sectors = lax.axis_size("lon")
    count = neighbours.shape[1]
    x = nodes.reshape(rows, width)
    gain = norm_gain.reshape(1, width)

    def paired(array, first):
        pairs = [(i, (i + 1) % sectors) for i in range(first, sectors, 2)]
        return lax.ppermute(array, "lon", pairs + [(j, i) for i, j in pairs])

    def exchanged(array, first):
        size = lax.axis_size("reg")
        pairs = [(i, i + 1) for i in range(first, size - 1, 2)]
        return lax.ppermute(array, "reg", pairs + [(j, i) for i, j in pairs])

    def in_hbm(*arrays):
        return [pltpu.with_memory_space_constraint(array, pltpu.HBM) for array in arrays]

    other = paired(x, 1)
    pair = paired(x, 0)

    outputs = -(-out_ch // ROWS) * ROWS
    head = width // HEADS
    members = LANES // head
    parts = HEADS // members
    def mixed(blocks, name, after):
        taps = psi.transpose(2, 3, 1, 0)
        mixing = w_dec.transpose(0, 2, 1)
        taps, mixing, after = lax.optimization_barrier((taps, mixing, after))
        weights = pl.pallas_call(
            functools.partial(mix_kernel, blocks),
            in_specs=[whole()] * 2,
            out_specs=whole(),
            out_shape=struct(len(blocks), outputs, channels),
            scratch_shapes=[
                pltpu.VMEM((2 * TAPS * TAPS, basis), F32),
                pltpu.VMEM((len(blocks) * ROWS, basis * ROWS), BF16),
            ],
            compiler_params=params(32),
            cost_estimate=cost(2e9, 6e6),
            name=name,
        )(taps, mixing)
        return weights, after

    own = pl.pallas_call(
        gather_kernel,
        in_specs=[whole(pltpu.HBM)] * 2,
        out_specs=whole(),
        out_shape=struct(rows + ROWS, width),
        scratch_shapes=[
            pltpu.VMEM(assignment.shape, jnp.int32),
            pltpu.SemaphoreType.DMA((2,)),
        ],
        compiler_params=params(32),
        cost_estimate=cost(1e3, 1e3),
        name="gather",
    )(*in_hbm(x, assignment))
    query, key, value, wk, wvt, choice, cells, wide = pl.pallas_call(
        functools.partial(prepare_kernel, sectors),
        in_specs=[whole()] + [whole(pltpu.HBM)] * 4,
        out_specs=[whole()] * 8,
        out_shape=[
            struct(parts, LANES, members * rows),
            struct(rows, width),
            struct(width, rows),
            struct(width, width),
            struct(width, width),
            struct(count - 1, CANDIDATES, ROWS, LANES),
            struct(rows + 2 * ROWS, rows),
            struct(rows + 2 * ROWS, width),
        ],
        scratch_shapes=[
            pltpu.VMEM((1, width), F32),
            pltpu.VMEM(w_qkv.shape, BF16),
            pltpu.SMEM(assignment.shape, jnp.int32),
            pltpu.SMEM(neighbours.shape, jnp.int32),
            pltpu.SemaphoreType.DMA((4,)),
        ],
        compiler_params=params(32),
        cost_estimate=cost(5e8, 1e6),
        name="prepare",
    )(own, *in_hbm(gain, w_qkv, assignment, neighbours))
    own, query = lax.optimization_barrier((own, query))
    message = jnp.concatenate([pair, own], axis=0)
    message_a = message
    other_a = other
    inner = exchanged(message_a, 0)
    outer = exchanged(message, 1)
    corner = exchanged(other, 1)
    beside = exchanged(other_a, 0)

    edges, other_m = mixed(blocks_of(ABOVE) + blocks_of(BELOW), "mix_edges", other)
    inner, edges = lax.optimization_barrier((inner, edges))
    top, summed = pl.pallas_call(
        early_kernel,
        in_specs=[whole()] * 11,
        out_specs=[whole()] * 2,
        out_shape=[
            struct(parts, 2, 8, members * rows, dtype=F32),
            struct(parts, LANES, rows, dtype=F32),
        ],
        scratch_shapes=[
            pltpu.VMEM(((1 + EARLY) * rows, width), BF16),
            pltpu.VMEM((parts, LANES + ROWS, (1 + EARLY) * rows), BF16),
        ],
        compiler_params=params(32),
        cost_estimate=cost(3e9, 6e6),
        name="early",
    )(choice, other, pair, inner, outer, gain, wk, wvt, query, key, value)
    state, latent, to_pair, to_other = pl.pallas_call(
        late_kernel,
        in_specs=[whole()] * 15,
        out_specs=[whole()] * 4,
        out_shape=[pltpu.VMEM((rows, width), BF16), struct(rows, channels)]
        + [struct(ROWS, channels)] * 2,
        compiler_params=params(32),
        cost_estimate=cost(3e9, 6e6),
        name="late",
    )(
        choice, cells, inner, outer, beside, corner,
        wide, gain, wk, wvt, query, top, summed, w_out, w_latent,
    )

    from_pair = paired(to_pair, 0)
    from_other = paired(to_other, 1)
    middle, latent = mixed(blocks_of(OWN), "mix_own", latent)
    from_pair, middle = lax.optimization_barrier((from_pair, middle))
    extended = jnp.concatenate([latent, from_pair[:SIDE], from_other[:SIDE]], axis=0)
    far = exchanged(extended, 1)
    near = exchanged(extended, 0)

    lanes = -(-(rows + 2 * SIDE) // 256) * 256
    partial, hots, state = pl.pallas_call(
        functools.partial(own_kernel, (rows, 2 * rows, 2 * rows)),
        in_specs=[whole()] * 6,
        out_specs=[whole()] * 3,
        out_shape=[
            struct(lat_rows, outputs, lon_cols, dtype=F32),
            struct(2, 2, TAPS, lanes, lon_cols),
            struct(rows, width),
        ],
        compiler_params=params(32),
        cost_estimate=cost(1e9, 2.5e6),
        name="own_band",
    )(state, own, inner, outer, extended, middle)
    band_scratch = [
        pltpu.VMEM((outputs, TAPS * lanes), BF16),
        pltpu.VMEM((2 * outputs, TAPS * lanes), BF16),
        pltpu.VMEM((lon_cols // LANES, 2 * outputs, LANES), F32),
    ]
    partial = pl.pallas_call(
        functools.partial(band_kernel, True),
        in_specs=[whole()] * 4,
        out_specs=whole(),
        out_shape=struct(lat_rows, outputs, lon_cols, dtype=F32),
        scratch_shapes=band_scratch,
        compiler_params=params(32),
        cost_estimate=cost(1e9, 2.5e6),
        name="inner_band",
    )(near, edges, hots, partial)
    fields = pl.pallas_call(
        functools.partial(band_kernel, False),
        in_specs=[whole()] * 4,
        out_specs=whole(),
        out_shape=struct(out_ch, lat_rows, lon_cols),
        scratch_shapes=band_scratch,
        compiler_params=params(32),
        cost_estimate=cost(1e9, 2.5e6),
        name="outer_band",
    )(far, edges, hots, partial)
    return (state.reshape(1, rows, width), fields.reshape(1, out_ch, lat_rows, lon_cols))


def solution(mesh):
    in_specs = (
        P(None, ("reg", "lon"), None),
        P(),
        P(),
        P(),
        P(),
        P(("reg", "lon"), None),
        P("reg", "lon"),
        P(None, "reg", None, None),
        P(),
    )
    out_specs = (P(None, ("reg", "lon"), None), P(None, None, "reg", "lon"))
    return jax.shard_map(shards, mesh=mesh, in_specs=in_specs, out_specs=out_specs, check_vma=False)
```

```python
import functools
import math

import jax
import jax.numpy as jnp
from jax import lax
from jax.experimental import pallas as pl
from jax.experimental.pallas import tpu as pltpu
from jax.sharding import PartitionSpec as P

HEADS = 16
REACH = 2
TAPS = 2 * REACH + 1
SIDE = 8
ROWS = 16
LANES = 128
EARLY = 2
CANDIDATES = 5
F32 = jnp.float32
BF16 = jnp.bfloat16
NT = (((1,), (1,)), ((), ()))

ABOVE = ((-2, (0,)), (-1, (0, 1)))
OWN = ((0, (0, 1)), (1, (0, 1)))
BELOW = ((3, (1,)), (2, (0, 1)))


def blocks_of(band):
    return [
        (out_row, src - out_row + REACH, off)
        for src, out_rows in band
        for off in range(TAPS)
        for out_row in out_rows
    ]


def iota(shape, dim):
    return lax.broadcasted_iota(jnp.int32, shape, dim)


def normalise(rows, gain):
    values = rows.astype(F32)
    center = values - jnp.mean(values, axis=-1, keepdims=True)
    spread = jnp.mean(center * center, axis=-1, keepdims=True)
    return (center * lax.rsqrt(spread + 1e-05) * gain).astype(BF16)


def mix_kernel(blocks, psi_ref, dec_ref, mixed_ref, psi_rows_ref, taps_ref):
    basis, out_ch, channels = dec_ref.shape
    depth = basis * ROWS
    for tap in range(TAPS):
        for off in range(TAPS):
            at = (tap * TAPS + off) * 2
            psi_rows_ref[at : at + 2, :] = psi_ref[tap, off]
    spread = (iota((basis, depth), 1) // ROWS == iota((basis, depth), 0)).astype(F32)
    expanded = jnp.dot(psi_rows_ref[...], spread, preferred_element_type=F32)
    pick = iota((ROWS, depth), 1) % ROWS == iota((ROWS, depth), 0)
    for at, (out_row, tap, off) in enumerate(blocks):
        source = (tap * TAPS + off) * 2 + out_row
        taps = jnp.broadcast_to(expanded[source : source + 1], (ROWS, depth))
        taps_ref[at * ROWS : (at + 1) * ROWS, :] = jnp.where(pick, taps, 0.0).astype(BF16)
    for first in range(0, out_ch, ROWS):
        size = min(ROWS, out_ch - first)
        pieces = []
        for base in range(basis):
            pieces.append(dec_ref[base, first : first + size, :])
            if size < ROWS:
                pieces.append(jnp.zeros((ROWS - size, channels), BF16))
        mixing = jnp.concatenate(pieces, axis=0)
        mixed = jnp.dot(taps_ref[...], mixing, preferred_element_type=F32).astype(BF16)
        mixed_ref[:, first : first + ROWS, :] = mixed.reshape(len(blocks), ROWS, channels)


def listed_blocks(sectors, listed_ref):
    reg_here, lon_here = lax.axis_index("reg"), lax.axis_index("lon")
    toward = 1 - 2 * (reg_here % 2)
    found = []
    for at in range(1, listed_ref.shape[1]):
        block = listed_ref[0, at]
        step_reg = (block // sectors - reg_here) * toward
        step_lon = (block % sectors - lon_here + 1 + sectors) % sectors - 1
        lean = step_lon * (1 - 2 * (lon_here % 2))
        side = jnp.where(lean == 0, 0, jnp.where(lean > 0, 1, 4))
        ahead = jnp.where(lean < 0, 0, 1)
        behind = jnp.where(lean < 0, 7, 4 + side)
        found.append(jnp.where(step_reg == 0, ahead, jnp.where(step_reg > 0, 2 + side, behind)))
    for low in range(len(found)):
        for high in range(low + 1, len(found)):
            less, more = jnp.minimum(found[low], found[high]), jnp.maximum(found[low], found[high])
            found[low], found[high] = less, more
    return found


def gather_kernel(x_hbm, assign_hbm, own_ref, assign_ref, sems):
    rows = own_ref.shape[0] - ROWS
    copies = [
        pltpu.make_async_copy(assign_hbm, assign_ref, sems.at[0]),
        pltpu.make_async_copy(x_hbm, own_ref.at[pl.ds(0, rows)], sems.at[1]),
    ]
    for copy in copies:
        copy.start()
    copies[0].wait()
    local = lax.rem(assign_ref[...], rows).astype(F32)
    line = jnp.concatenate([local[:1], local[1:2]], axis=1)
    line = jnp.broadcast_to(line, (ROWS, line.shape[1]))
    own_ref[rows:] = jnp.where(iota(line.shape, 0) == 0, line, 0.0).astype(BF16)
    copies[1].wait()


def prepare_kernel(
    sectors,
    own_ref, gain_hbm, wqkv_hbm, assign_hbm, listed_hbm,
    query_ref, key_ref, value_ref, wk_ref, wvt_ref, choice_ref, cells_ref,
    gain_ref, wqkv_ref, cell_ref, listed_ref, sems,
):
    copies = [
        pltpu.make_async_copy(source, target, sems.at[at])
        for at, (source, target) in enumerate(
            (
                (gain_hbm, gain_ref),
                (wqkv_hbm, wqkv_ref),
                (assign_hbm, cell_ref),
                (listed_hbm, listed_ref),
            )
        )
    ]
    for copy in copies:
        copy.start()
    rows, width = key_ref.shape
    group, members = query_ref.shape[1], query_ref.shape[2] // rows
    head = group // members
    for copy in copies[2:]:
        copy.wait()
    for at, number in enumerate(listed_blocks(sectors, listed_ref)):
        for candidate in range(CANDIDATES):
            same = jnp.full((ROWS, LANES), jnp.where(number == at + candidate, 1.0, 0.0), F32)
            choice_ref[at, candidate] = same.astype(BF16)
    lat_rows, lon_cols = cell_ref.shape
    place, node = iota((ROWS, rows), 0), iota((ROWS, rows), 1)
    odd = lax.axis_index("lon") % 2
    for side, first in enumerate(((1 - odd) * (lon_cols - REACH), odd * (lon_cols - REACH))):
        hit = jnp.zeros((ROWS, rows), F32)
        for row in range(lat_rows):
            for col in range(REACH):
                cell = cell_ref[row, first + col] % rows
                hit = jnp.where((place == row * REACH + col) & (node == cell), 1.0, hit)
        cells_ref[side * ROWS : (side + 1) * ROWS] = hit.astype(BF16)
    copies[0].wait()
    normed = normalise(own_ref[:rows], gain_ref[...])
    copies[1].wait()
    query = jnp.dot(normed, wqkv_ref[:, :width], preferred_element_type=F32)
    query_t = (query * (math.log2(math.e) / head**0.5)).T.astype(BF16)
    mask = (iota((group, members * rows), 0) // head) == (iota((group, members * rows), 1) // rows)
    for part in range(width // group):
        piece = query_t[part * group : (part + 1) * group]
        wide = jnp.concatenate([piece] * members, axis=1)
        query_ref[part] = jnp.where(mask, wide, jnp.zeros_like(wide))
    wk = wqkv_ref[:, width : 2 * width]
    wk_ref[...] = wk
    key_ref[...] = jnp.dot(normed, wk, preferred_element_type=F32).astype(BF16)
    wvt = wqkv_ref[:, 2 * width :].astype(F32).T.astype(BF16)
    wvt_ref[...] = wvt
    value_ref[...] = lax.dot_general(wvt, normed, NT, preferred_element_type=F32).astype(BF16)


def chosen(entries, rows, choice_ref, candidates):
    tall, wide = rows // ROWS, candidates[-1].shape[1] // LANES
    near = []
    for entry in entries:
        total = candidates[entry]
        for at in range(1, CANDIDATES):
            weight = jnp.concatenate([choice_ref[entry, at]] * wide, axis=1)
            weight = jnp.concatenate([weight] * tall, axis=0)
            total = jnp.where(weight > 0, candidates[entry + at], total)
        near.append(total)
    return jnp.concatenate(near, axis=0)


def project(nodes, gain, wk_ref, wvt_ref):
    normed = normalise(nodes, gain)
    keys = jnp.dot(normed, wk_ref[...], preferred_element_type=F32).astype(BF16)
    values = lax.dot_general(wvt_ref[...], normed, NT, preferred_element_type=F32).astype(BF16)
    return keys, values


def own_heads(summed, rows):
    members = summed.shape[1] // rows
    head = summed.shape[0] // members
    return [
        summed[at * head : (at + 1) * head, at * rows : (at + 1) * rows] for at in range(members)
    ]


def early_kernel(
    choice_ref, other_ref, pair_ref, inner_ref, outer_ref,
    gain_ref, wk_ref, wvt_ref, query_ref, key_ref, value_ref,
    top_ref, sum_ref, keys_ref, values_ref,
):
    rows = key_ref.shape[0]
    parts, group, _ = query_ref.shape
    candidates = [other_ref[...], pair_ref[...]]
    candidates += [ref[rows : 2 * rows] if center else ref[:rows] for ref in (inner_ref, outer_ref) for center in (1, 0)]
    nodes = chosen(range(EARLY), rows, choice_ref, candidates)
    keys, values = project(nodes, gain_ref[...], wk_ref, wvt_ref)
    keys_ref[:rows] = key_ref[...]
    keys_ref[rows:] = keys
    for part in range(parts):
        span = slice(part * group, (part + 1) * group)
        values_ref[part, :group, :rows] = value_ref[span]
        values_ref[part, :group, rows:] = values[span]
        values_ref[part, group:, :] = jnp.ones((ROWS, keys_ref.shape[0]), BF16)

    spans = [slice(part * group, (part + 1) * group) for part in range(parts)]
    scores = [
        jnp.dot(keys_ref[:, span], query_ref[part], preferred_element_type=F32)
        for part, span in enumerate(spans)
    ]
    tops = [jnp.max(one, axis=0, keepdims=True) for one in scores]
    expos = [jnp.exp2(one - top).astype(BF16) for one, top in zip(scores, tops)]
    sums = [
        jnp.dot(values_ref[part], expo, preferred_element_type=F32) for part, expo in enumerate(expos)
    ]
    for part, (top, summed) in enumerate(zip(tops, sums)):
        top_ref[part, 0] = jnp.broadcast_to(top, top_ref.shape[2:])
        top_ref[part, 1] = jnp.broadcast_to(summed[group : group + 1], top_ref.shape[2:])
        sum_ref[part] = jnp.concatenate(own_heads(summed[:group], rows), axis=0)


def late_kernel(
    choice_ref, cells_ref, inner_ref, outer_ref, beside_ref, corner_ref,
    own_ref, gain_ref, wk_ref, wvt_ref, query_ref, top_ref, sum_ref, wout_ref, wlat_ref,
    state_ref, latent_ref, to_pair_ref, to_other_ref,
):
    rows, width = state_ref.shape
    parts, group, lanes = query_ref.shape
    members = lanes // rows
    head = group // members
    candidates = [None, None]
    candidates += [ref[rows : 2 * rows] if center else ref[:rows] for ref in (inner_ref, outer_ref) for center in (1, 0)]
    candidates += [beside_ref[...], corner_ref[...]]
    nodes = chosen(range(EARLY, choice_ref.shape[0]), rows, choice_ref, candidates)
    keys, values = project(nodes, gain_ref[...], wk_ref, wvt_ref)
    ones = jnp.ones((ROWS, nodes.shape[0]), BF16)
    spans = [slice(part * group, (part + 1) * group) for part in range(parts)]
    scores = [
        jnp.dot(keys[:, span], query_ref[part], preferred_element_type=F32)
        for part, span in enumerate(spans)
    ]
    befores = [top_ref[part, 0, :1] for part in range(parts)]
    tops = [
        jnp.maximum(before, jnp.max(one, axis=0, keepdims=True))
        for before, one in zip(befores, scores)
    ]
    expos = [jnp.exp2(one - top).astype(BF16) for one, top in zip(scores, tops)]
    sums = [
        jnp.dot(jnp.concatenate([values[span], ones], axis=0), expo, preferred_element_type=F32)
        for span, expo in zip(spans, expos)
    ]
    attended = []
    for part, summed in enumerate(sums):
        shrink = jnp.exp2(befores[part] - tops[part])
        share = 1.0 / (summed[group : group + 1] + top_ref[part, 1, :1] * shrink)
        merged = []
        for member, piece in enumerate(own_heads(summed[:group], rows)):
            span = slice(member * rows, (member + 1) * rows)
            earlier = sum_ref[part, member * head : (member + 1) * head]
            merged.append((piece + earlier * shrink[:, span]) * share[:, span])
        attended.append(jnp.concatenate(merged, axis=0).T.astype(BF16))
    attended = jnp.concatenate(attended, axis=1)
    state = (
        own_ref[:rows].astype(F32)
        + jnp.dot(attended, wout_ref[...], preferred_element_type=F32)
    ).astype(BF16)
    state_ref[...] = state
    value = jnp.dot(state, wlat_ref[...], preferred_element_type=F32)
    latent = (value / (1.0 + jnp.exp(-value))).astype(BF16)
    latent_ref[...] = latent
    cells = jnp.dot(cells_ref[...], latent, preferred_element_type=F32).astype(BF16)
    to_pair_ref[...] = cells[:ROWS]
    to_other_ref[...] = cells[ROWS:]


def hot_rows(values, rows, cols, line):
    odd = lax.axis_index("lon") % 2
    column = iota((8, cols), 1)
    node = iota((rows + 2 * SIDE, cols), 0).astype(F32)
    for off in range(TAPS):
        step = off - REACH
        where = jnp.broadcast_to(values, (8, cols))
        if step:
            where = pltpu.roll(where, (-step) % cols, 1)
        reach = column + step
        before = (rows + (1 - odd) * SIDE + REACH * line + reach + REACH).astype(F32)
        after = (rows + odd * SIDE + REACH * line + reach - cols).astype(F32)
        where = jnp.where(reach < 0, before, jnp.where(reach >= cols, after, where))
        yield jnp.where(node == where[:1], 1.0, 0.0).astype(BF16)


def shares_of(latent, weights):
    blocks, outputs, channels = weights.shape
    shares = lax.dot_general(
        weights.reshape(blocks * outputs, channels), latent, NT, preferred_element_type=F32
    ).astype(BF16)
    return [shares[at * outputs : (at + 1) * outputs] for at in range(blocks)]


def lines_of(line_ref, start, cols):
    values = line_ref[start : start + ROWS, :].astype(F32)
    return values[:1, :cols], values[:1, cols:]


def own_kernel(
    begin, state_ref, own_ref, inner_ref, outer_ref, latent_ref, weights_ref,
    out_ref, hot_ref, kept_ref,
):
    kept_ref[...] = state_ref[...]
    cols = out_ref.shape[2]
    rows = latent_ref.shape[0] - 2 * SIDE
    own = lines_of(own_ref, begin[0], cols)
    table = [list(hot_rows(own[line], rows, cols, line)) for line in range(2)]
    acc = [None, None]
    for (out_row, tap, off), share in zip(
        blocks_of(OWN), shares_of(latent_ref[...], weights_ref[...])
    ):
        line = out_row + tap - REACH
        piece = jnp.dot(share, table[line][off], preferred_element_type=F32)
        acc[out_row] = piece if acc[out_row] is None else acc[out_row] + piece
    for row in range(2):
        out_ref[row] = acc[row]
    odd = lax.axis_index("reg") % 2 == 1
    inner, outer = lines_of(inner_ref, begin[1], cols), lines_of(outer_ref, begin[2], cols)
    nodes = rows + 2 * SIDE
    for band, (yes, no) in enumerate(((inner, outer), (outer, inner))):
        for at, line in enumerate((0, 1) if band == 0 else (1, 0)):
            values = jnp.where(odd, yes[line], no[line])
            for off, hot in enumerate(hot_rows(values, rows, cols, line)):
                hot_ref[band, at, off, :nodes] = hot
                hot_ref[band, at, off, nodes:] = jnp.zeros((hot_ref.shape[3] - nodes, cols), BF16)


def band_kernel(
    from_inner, latent_ref, weights_ref, hot_ref, partial_ref, out_ref, one_ref, two_ref, paired_ref
):
    odd = lax.axis_index("reg") % 2
    band = 1 - odd if from_inner else odd
    latent = latent_ref[...]
    lanes, cols = hot_ref.shape[3:]
    outputs = weights_ref.shape[1]
    blank = jnp.zeros((lanes - latent.shape[0], latent.shape[1]), BF16)
    blocks = len(blocks_of(ABOVE))
    weights = weights_ref[pl.ds(band * blocks, blocks)]
    shares = shares_of(jnp.concatenate([latent, blank], axis=0), weights)
    for off in range(TAPS):
        span = slice(off * lanes, (off + 1) * lanes)
        one_ref[:, span] = shares[off]
        for row in range(2):
            two_ref[row * outputs : (row + 1) * outputs, span] = shares[TAPS + 2 * off + row]
    depth = TAPS * lanes
    one = jnp.dot(one_ref[...], hot_ref[band, 0].reshape(depth, cols), preferred_element_type=F32)
    two = jnp.dot(two_ref[...], hot_ref[band, 1].reshape(depth, cols), preferred_element_type=F32)
    for row in range(2):
        total = partial_ref[row] + two[row * outputs : (row + 1) * outputs]
        total = total + jnp.where(band == row, one, 0.0)
        if from_inner:
            out_ref[row] = total
        else:
            for tile in range(cols // LANES):
                part = total[:, tile * LANES : (tile + 1) * LANES]
                paired_ref[tile, pl.ds(row, outputs, stride=2), :] = part
    if not from_inner:
        out_ch = out_ref.shape[0]
        tiles = [paired_ref[tile, : 2 * out_ch, :] for tile in range(cols // LANES)]
        out_ref[...] = jnp.concatenate(tiles, axis=1).astype(BF16).reshape(out_ref.shape)


def whole(memory=pltpu.VMEM):
    return pl.BlockSpec(memory_space=memory)


def struct(*shape, dtype=BF16):
    return jax.ShapeDtypeStruct(shape, dtype)


def params(limit):
    return pltpu.CompilerParams(vmem_limit_bytes=limit << 20)


def cost(flops, moved):
    return pl.CostEstimate(flops=int(flops), bytes_accessed=int(moved), transcendentals=0)


def shards(nodes, norm_gain, w_qkv, w_out, w_latent, neighbours, assignment, psi, w_dec):
    _, rows, width = nodes.shape
    channels = w_latent.shape[1]
    lat_rows, lon_cols = assignment.shape
    basis, _, out_ch = w_dec.shape
    sectors = lax.axis_size("lon")
    count = neighbours.shape[1]
    x = nodes.reshape(rows, width)
    gain = norm_gain.reshape(1, width)

    def paired(array, first):
        pairs = [(i, (i + 1) % sectors) for i in range(first, sectors, 2)]
        return lax.ppermute(array, "lon", pairs + [(j, i) for i, j in pairs])

    def exchanged(array, first):
        size = lax.axis_size("reg")
        pairs = [(i, i + 1) for i in range(first, size - 1, 2)]
        return lax.ppermute(array, "reg", pairs + [(j, i) for i, j in pairs])

    def in_hbm(*arrays):
        return [pltpu.with_memory_space_constraint(array, pltpu.HBM) for array in arrays]

    other = paired(x, 1)
    pair = paired(x, 0)

    outputs = -(-out_ch // ROWS) * ROWS
    head = width // HEADS
    members = LANES // head
    parts = HEADS // members
    def mixed(blocks, name, after):
        taps = psi.transpose(2, 3, 1, 0)
        mixing = w_dec.transpose(0, 2, 1)
        taps, mixing, after = lax.optimization_barrier((taps, mixing, after))
        weights = pl.pallas_call(
            functools.partial(mix_kernel, blocks),
            in_specs=[whole()] * 2,
            out_specs=whole(),
            out_shape=struct(len(blocks), outputs, channels),
            scratch_shapes=[
                pltpu.VMEM((2 * TAPS * TAPS, basis), F32),
                pltpu.VMEM((len(blocks) * ROWS, basis * ROWS), BF16),
            ],
            compiler_params=params(32),
            cost_estimate=cost(2e9, 6e6),
            name=name,
        )(taps, mixing)
        return weights, after

    own = pl.pallas_call(
        gather_kernel,
        in_specs=[whole(pltpu.HBM)] * 2,
        out_specs=whole(),
        out_shape=struct(rows + ROWS, width),
        scratch_shapes=[
            pltpu.VMEM(assignment.shape, jnp.int32),
            pltpu.SemaphoreType.DMA((2,)),
        ],
        compiler_params=params(32),
        cost_estimate=cost(1e3, 1e3),
        name="gather",
    )(*in_hbm(x, assignment))
    query, key, value, wk, wvt, choice, cells = pl.pallas_call(
        functools.partial(prepare_kernel, sectors),
        in_specs=[whole()] + [whole(pltpu.HBM)] * 4,
        out_specs=[whole()] * 7,
        out_shape=[
            struct(parts, LANES, members * rows),
            struct(rows, width),
            struct(width, rows),
            struct(width, width),
            struct(width, width),
            struct(count - 1, CANDIDATES, ROWS, LANES),
            struct(2 * ROWS, rows),
        ],
        scratch_shapes=[
            pltpu.VMEM((1, width), F32),
            pltpu.VMEM(w_qkv.shape, BF16),
            pltpu.SMEM(assignment.shape, jnp.int32),
            pltpu.SMEM(neighbours.shape, jnp.int32),
            pltpu.SemaphoreType.DMA((4,)),
        ],
        compiler_params=params(32),
        cost_estimate=cost(5e8, 1e6),
        name="prepare",
    )(own, *in_hbm(gain, w_qkv, assignment, neighbours))
    own, query = lax.optimization_barrier((own, query))
    message = jnp.concatenate([pair, own], axis=0)
    message_a = message
    other_a = other
    inner = exchanged(message_a, 0)
    outer = exchanged(message, 1)
    corner = exchanged(other, 1)
    beside = exchanged(other_a, 0)

    edges, other_m = mixed(blocks_of(ABOVE) + blocks_of(BELOW), "mix_edges", other)
    inner, edges = lax.optimization_barrier((inner, edges))
    top, summed = pl.pallas_call(
        early_kernel,
        in_specs=[whole()] * 11,
        out_specs=[whole()] * 2,
        out_shape=[
            struct(parts, 2, 8, members * rows, dtype=F32),
            struct(parts, LANES, rows, dtype=F32),
        ],
        scratch_shapes=[
            pltpu.VMEM(((1 + EARLY) * rows, width), BF16),
            pltpu.VMEM((parts, LANES + ROWS, (1 + EARLY) * rows), BF16),
        ],
        compiler_params=params(32),
        cost_estimate=cost(3e9, 6e6),
        name="early",
    )(choice, other, pair, inner, outer, gain, wk, wvt, query, key, value)
    state, latent, to_pair, to_other = pl.pallas_call(
        late_kernel,
        in_specs=[whole()] * 15,
        out_specs=[whole()] * 4,
        out_shape=[pltpu.VMEM((rows, width), BF16), struct(rows, channels)]
        + [struct(ROWS, channels)] * 2,
        compiler_params=params(32),
        cost_estimate=cost(3e9, 6e6),
        name="late",
    )(
        choice, cells, inner, outer, beside, corner,
        own, gain, wk, wvt, query, top, summed, w_out, w_latent,
    )

    from_pair = paired(to_pair, 0)
    from_other = paired(to_other, 1)
    middle, latent = mixed(blocks_of(OWN), "mix_own", latent)
    from_pair, middle = lax.optimization_barrier((from_pair, middle))
    extended = jnp.concatenate([latent, from_pair[:SIDE], from_other[:SIDE]], axis=0)
    far = exchanged(extended, 1)
    near = exchanged(extended, 0)

    lanes = -(-(rows + 2 * SIDE) // 256) * 256
    partial, hots, state = pl.pallas_call(
        functools.partial(own_kernel, (rows, 2 * rows, 2 * rows)),
        in_specs=[whole()] * 6,
        out_specs=[whole()] * 3,
        out_shape=[
            struct(lat_rows, outputs, lon_cols, dtype=F32),
            struct(2, 2, TAPS, lanes, lon_cols),
            struct(rows, width),
        ],
        compiler_params=params(32),
        cost_estimate=cost(1e9, 2.5e6),
        name="own_band",
    )(state, own, inner, outer, extended, middle)
    band_scratch = [
        pltpu.VMEM((outputs, TAPS * lanes), BF16),
        pltpu.VMEM((2 * outputs, TAPS * lanes), BF16),
        pltpu.VMEM((lon_cols // LANES, 2 * outputs, LANES), F32),
    ]
    partial = pl.pallas_call(
        functools.partial(band_kernel, True),
        in_specs=[whole()] * 4,
        out_specs=whole(),
        out_shape=struct(lat_rows, outputs, lon_cols, dtype=F32),
        scratch_shapes=band_scratch,
        compiler_params=params(32),
        cost_estimate=cost(1e9, 2.5e6),
        name="inner_band",
    )(near, edges, hots, partial)
    fields = pl.pallas_call(
        functools.partial(band_kernel, False),
        in_specs=[whole()] * 4,
        out_specs=whole(),
        out_shape=struct(out_ch, lat_rows, lon_cols),
        scratch_shapes=band_scratch,
        compiler_params=params(32),
        cost_estimate=cost(1e9, 2.5e6),
        name="outer_band",
    )(far, edges, hots, partial)
    return (state.reshape(1, rows, width), fields.reshape(1, out_ch, lat_rows, lon_cols))


def solution(mesh):
    in_specs = (
        P(None, ("reg", "lon"), None),
        P(),
        P(),
        P(),
        P(),
        P(("reg", "lon"), None),
        P("reg", "lon"),
        P(None, "reg", None, None),
        P(),
    )
    out_specs = (P(None, ("reg", "lon"), None), P(None, None, "reg", "lon"))
    return jax.shard_map(shards, mesh=mesh, in_specs=in_specs, out_specs=out_specs, check_vma=False)
```

```python
import functools
import math

import jax
import jax.numpy as jnp
from jax import lax
from jax.experimental import pallas as pl
from jax.experimental.pallas import tpu as pltpu
from jax.sharding import PartitionSpec as P

HEADS = 16
REACH = 2
TAPS = 2 * REACH + 1
SIDE = 8
ROWS = 16
LANES = 128
EARLY = 2
CANDIDATES = 5
F32 = jnp.float32
BF16 = jnp.bfloat16
NT = (((1,), (1,)), ((), ()))

ABOVE = ((-2, (0,)), (-1, (0, 1)))
OWN = ((0, (0, 1)), (1, (0, 1)))
BELOW = ((3, (1,)), (2, (0, 1)))


def blocks_of(band):
    return [
        (out_row, src - out_row + REACH, off)
        for src, out_rows in band
        for off in range(TAPS)
        for out_row in out_rows
    ]


def iota(shape, dim):
    return lax.broadcasted_iota(jnp.int32, shape, dim)


def normalise(rows, gain):
    values = rows.astype(F32)
    center = values - jnp.mean(values, axis=-1, keepdims=True)
    spread = jnp.mean(center * center, axis=-1, keepdims=True)
    return (center * lax.rsqrt(spread + 1e-05) * gain).astype(BF16)


def mix_kernel(blocks, psi_ref, dec_ref, mixed_ref, psi_rows_ref, taps_ref):
    basis, out_ch, channels = dec_ref.shape
    depth = basis * ROWS
    for tap in range(TAPS):
        for off in range(TAPS):
            at = (tap * TAPS + off) * 2
            psi_rows_ref[at : at + 2, :] = psi_ref[tap, off]
    spread = (iota((basis, depth), 1) // ROWS == iota((basis, depth), 0)).astype(F32)
    expanded = jnp.dot(psi_rows_ref[...], spread, preferred_element_type=F32)
    pick = iota((ROWS, depth), 1) % ROWS == iota((ROWS, depth), 0)
    for at, (out_row, tap, off) in enumerate(blocks):
        source = (tap * TAPS + off) * 2 + out_row
        taps = jnp.broadcast_to(expanded[source : source + 1], (ROWS, depth))
        taps_ref[at * ROWS : (at + 1) * ROWS, :] = jnp.where(pick, taps, 0.0).astype(BF16)
    for first in range(0, out_ch, ROWS):
        size = min(ROWS, out_ch - first)
        pieces = []
        for base in range(basis):
            pieces.append(dec_ref[base, first : first + size, :])
            if size < ROWS:
                pieces.append(jnp.zeros((ROWS - size, channels), BF16))
        mixing = jnp.concatenate(pieces, axis=0)
        mixed = jnp.dot(taps_ref[...], mixing, preferred_element_type=F32).astype(BF16)
        mixed_ref[:, first : first + ROWS, :] = mixed.reshape(len(blocks), ROWS, channels)


def listed_blocks(sectors, listed_ref):
    reg_here, lon_here = lax.axis_index("reg"), lax.axis_index("lon")
    toward = 1 - 2 * (reg_here % 2)
    found = []
    for at in range(1, listed_ref.shape[1]):
        block = listed_ref[0, at]
        step_reg = (block // sectors - reg_here) * toward
        step_lon = (block % sectors - lon_here + 1 + sectors) % sectors - 1
        lean = step_lon * (1 - 2 * (lon_here % 2))
        side = jnp.where(lean == 0, 0, jnp.where(lean > 0, 1, 4))
        ahead = jnp.where(lean < 0, 0, 1)
        behind = jnp.where(lean < 0, 7, 4 + side)
        found.append(jnp.where(step_reg == 0, ahead, jnp.where(step_reg > 0, 2 + side, behind)))
    for low in range(len(found)):
        for high in range(low + 1, len(found)):
            less, more = jnp.minimum(found[low], found[high]), jnp.maximum(found[low], found[high])
            found[low], found[high] = less, more
    return found


def gather_kernel(x_hbm, assign_hbm, own_ref, assign_ref, sems):
    rows = own_ref.shape[0] - ROWS
    copies = [
        pltpu.make_async_copy(assign_hbm, assign_ref, sems.at[0]),
        pltpu.make_async_copy(x_hbm, own_ref.at[pl.ds(0, rows)], sems.at[1]),
    ]
    for copy in copies:
        copy.start()
    copies[0].wait()
    local = lax.rem(assign_ref[...], rows).astype(F32)
    line = jnp.concatenate([local[:1], local[1:2]], axis=1)
    line = jnp.broadcast_to(line, (ROWS, line.shape[1]))
    own_ref[rows:] = jnp.where(iota(line.shape, 0) == 0, line, 0.0).astype(BF16)
    copies[1].wait()


def prepare_kernel(
    sectors,
    own_ref, gain_hbm, wqkv_hbm, assign_hbm, listed_hbm,
    query_ref, key_ref, value_ref, wk_ref, wvt_ref, choice_ref, cells_ref,
    gain_ref, wqkv_ref, cell_ref, listed_ref, sems,
):
    copies = [
        pltpu.make_async_copy(source, target, sems.at[at])
        for at, (source, target) in enumerate(
            (
                (gain_hbm, gain_ref),
                (wqkv_hbm, wqkv_ref),
                (assign_hbm, cell_ref),
                (listed_hbm, listed_ref),
            )
        )
    ]
    for copy in copies:
        copy.start()
    rows, width = key_ref.shape
    group, members = query_ref.shape[1], query_ref.shape[2] // rows
    head = group // members
    for copy in copies[2:]:
        copy.wait()
    for at, number in enumerate(listed_blocks(sectors, listed_ref)):
        for candidate in range(CANDIDATES):
            same = jnp.full((ROWS, LANES), jnp.where(number == at + candidate, 1.0, 0.0), F32)
            choice_ref[at, candidate] = same.astype(BF16)
    lat_rows, lon_cols = cell_ref.shape
    place, node = iota((ROWS, rows), 0), iota((ROWS, rows), 1)
    odd = lax.axis_index("lon") % 2
    for side, first in enumerate(((1 - odd) * (lon_cols - REACH), odd * (lon_cols - REACH))):
        hit = jnp.zeros((ROWS, rows), F32)
        for row in range(lat_rows):
            for col in range(REACH):
                cell = cell_ref[row, first + col] % rows
                hit = jnp.where((place == row * REACH + col) & (node == cell), 1.0, hit)
        cells_ref[side * ROWS : (side + 1) * ROWS] = hit.astype(BF16)
    copies[0].wait()
    normed = normalise(own_ref[:rows], gain_ref[...])
    copies[1].wait()
    query = jnp.dot(normed, wqkv_ref[:, :width], preferred_element_type=F32)
    query_t = (query * (math.log2(math.e) / head**0.5)).T.astype(BF16)
    mask = (iota((group, members * rows), 0) // head) == (iota((group, members * rows), 1) // rows)
    for part in range(width // group):
        piece = query_t[part * group : (part + 1) * group]
        wide = jnp.concatenate([piece] * members, axis=1)
        query_ref[part] = jnp.where(mask, wide, jnp.zeros_like(wide))
    wk = wqkv_ref[:, width : 2 * width]
    wk_ref[...] = wk
    key_ref[...] = jnp.dot(normed, wk, preferred_element_type=F32).astype(BF16)
    wvt = wqkv_ref[:, 2 * width :].astype(F32).T.astype(BF16)
    wvt_ref[...] = wvt
    value_ref[...] = lax.dot_general(wvt, normed, NT, preferred_element_type=F32).astype(BF16)


def chosen(entries, rows, choice_ref, candidates):
    tall, wide = rows // ROWS, candidates[-1].shape[1] // LANES
    near = []
    for entry in entries:
        total = None
        for at in range(CANDIDATES):
            weight = jnp.concatenate([choice_ref[entry, at]] * wide, axis=1)
            part = candidates[entry + at] * jnp.concatenate([weight] * tall, axis=0)
            total = part if total is None else total + part
        near.append(total)
    return jnp.concatenate(near, axis=0)


def project(nodes, gain, wk_ref, wvt_ref):
    normed = normalise(nodes, gain)
    keys = jnp.dot(normed, wk_ref[...], preferred_element_type=F32).astype(BF16)
    values = lax.dot_general(wvt_ref[...], normed, NT, preferred_element_type=F32).astype(BF16)
    return keys, values


def own_heads(summed, rows):
    members = summed.shape[1] // rows
    head = summed.shape[0] // members
    return [
        summed[at * head : (at + 1) * head, at * rows : (at + 1) * rows] for at in range(members)
    ]


def early_kernel(
    choice_ref, other_ref, pair_ref, inner_ref, outer_ref,
    gain_ref, wk_ref, wvt_ref, query_ref, key_ref, value_ref,
    top_ref, sum_ref, keys_ref, values_ref,
):
    rows = key_ref.shape[0]
    parts, group, _ = query_ref.shape
    candidates = [other_ref[...], pair_ref[...]]
    candidates += [ref[rows : 2 * rows] if center else ref[:rows] for ref in (inner_ref, outer_ref) for center in (1, 0)]
    nodes = chosen(range(EARLY), rows, choice_ref, candidates)
    keys, values = project(nodes, gain_ref[...], wk_ref, wvt_ref)
    keys_ref[:rows] = key_ref[...]
    keys_ref[rows:] = keys
    for part in range(parts):
        span = slice(part * group, (part + 1) * group)
        values_ref[part, :group, :rows] = value_ref[span]
        values_ref[part, :group, rows:] = values[span]
        values_ref[part, group:, :] = jnp.ones((ROWS, keys_ref.shape[0]), BF16)

    spans = [slice(part * group, (part + 1) * group) for part in range(parts)]
    scores = [
        jnp.dot(keys_ref[:, span], query_ref[part], preferred_element_type=F32)
        for part, span in enumerate(spans)
    ]
    tops = [jnp.max(one, axis=0, keepdims=True) for one in scores]
    expos = [jnp.exp2(one - top).astype(BF16) for one, top in zip(scores, tops)]
    sums = [
        jnp.dot(values_ref[part], expo, preferred_element_type=F32) for part, expo in enumerate(expos)
    ]
    for part, (top, summed) in enumerate(zip(tops, sums)):
        top_ref[part, 0] = jnp.broadcast_to(top, top_ref.shape[2:])
        top_ref[part, 1] = jnp.broadcast_to(summed[group : group + 1], top_ref.shape[2:])
        sum_ref[part] = jnp.concatenate(own_heads(summed[:group], rows), axis=0)


def late_kernel(
    choice_ref, cells_ref, inner_ref, outer_ref, beside_ref, corner_ref,
    own_ref, gain_ref, wk_ref, wvt_ref, query_ref, top_ref, sum_ref, wout_ref, wlat_ref,
    state_ref, latent_ref, to_pair_ref, to_other_ref,
):
    rows, width = state_ref.shape
    parts, group, lanes = query_ref.shape
    members = lanes // rows
    head = group // members
    candidates = [None, None]
    candidates += [ref[rows : 2 * rows] if center else ref[:rows] for ref in (inner_ref, outer_ref) for center in (1, 0)]
    candidates += [beside_ref[...], corner_ref[...]]
    nodes = chosen(range(EARLY, choice_ref.shape[0]), rows, choice_ref, candidates)
    keys, values = project(nodes, gain_ref[...], wk_ref, wvt_ref)
    ones = jnp.ones((ROWS, nodes.shape[0]), BF16)
    spans = [slice(part * group, (part + 1) * group) for part in range(parts)]
    scores = [
        jnp.dot(keys[:, span], query_ref[part], preferred_element_type=F32)
        for part, span in enumerate(spans)
    ]
    befores = [top_ref[part, 0, :1] for part in range(parts)]
    tops = [
        jnp.maximum(before, jnp.max(one, axis=0, keepdims=True))
        for before, one in zip(befores, scores)
    ]
    expos = [jnp.exp2(one - top).astype(BF16) for one, top in zip(scores, tops)]
    sums = [
        jnp.dot(jnp.concatenate([values[span], ones], axis=0), expo, preferred_element_type=F32)
        for span, expo in zip(spans, expos)
    ]
    attended = []
    for part, summed in enumerate(sums):
        shrink = jnp.exp2(befores[part] - tops[part])
        share = 1.0 / (summed[group : group + 1] + top_ref[part, 1, :1] * shrink)
        merged = []
        for member, piece in enumerate(own_heads(summed[:group], rows)):
            span = slice(member * rows, (member + 1) * rows)
            earlier = sum_ref[part, member * head : (member + 1) * head]
            merged.append((piece + earlier * shrink[:, span]) * share[:, span])
        attended.append(jnp.concatenate(merged, axis=0).T.astype(BF16))
    attended = jnp.concatenate(attended, axis=1)
    state = (
        own_ref[:rows].astype(F32)
        + jnp.dot(attended, wout_ref[...], preferred_element_type=F32)
    ).astype(BF16)
    state_ref[...] = state
    value = jnp.dot(state, wlat_ref[...], preferred_element_type=F32)
    latent = (value / (1.0 + jnp.exp(-value))).astype(BF16)
    latent_ref[...] = latent
    cells = jnp.dot(cells_ref[...], latent, preferred_element_type=F32).astype(BF16)
    to_pair_ref[...] = cells[:ROWS]
    to_other_ref[...] = cells[ROWS:]


def hot_rows(values, rows, cols, line):
    odd = lax.axis_index("lon") % 2
    column = iota((8, cols), 1)
    node = iota((rows + 2 * SIDE, cols), 0).astype(F32)
    for off in range(TAPS):
        step = off - REACH
        where = jnp.broadcast_to(values, (8, cols))
        if step:
            where = pltpu.roll(where, (-step) % cols, 1)
        reach = column + step
        before = (rows + (1 - odd) * SIDE + REACH * line + reach + REACH).astype(F32)
        after = (rows + odd * SIDE + REACH * line + reach - cols).astype(F32)
        where = jnp.where(reach < 0, before, jnp.where(reach >= cols, after, where))
        yield jnp.where(node == where[:1], 1.0, 0.0).astype(BF16)


def shares_of(latent, weights):
    blocks, outputs, channels = weights.shape
    shares = lax.dot_general(
        weights.reshape(blocks * outputs, channels), latent, NT, preferred_element_type=F32
    ).astype(BF16)
    return [shares[at * outputs : (at + 1) * outputs] for at in range(blocks)]


def lines_of(line_ref, start, cols):
    values = line_ref[start : start + ROWS, :].astype(F32)
    return values[:1, :cols], values[:1, cols:]


def own_kernel(
    begin, state_ref, own_ref, inner_ref, outer_ref, latent_ref, weights_ref,
    out_ref, hot_ref, kept_ref,
):
    kept_ref[...] = state_ref[...]
    cols = out_ref.shape[2]
    rows = latent_ref.shape[0] - 2 * SIDE
    own = lines_of(own_ref, begin[0], cols)
    table = [list(hot_rows(own[line], rows, cols, line)) for line in range(2)]
    acc = [None, None]
    for (out_row, tap, off), share in zip(
        blocks_of(OWN), shares_of(latent_ref[...], weights_ref[...])
    ):
        line = out_row + tap - REACH
        piece = jnp.dot(share, table[line][off], preferred_element_type=F32)
        acc[out_row] = piece if acc[out_row] is None else acc[out_row] + piece
    for row in range(2):
        out_ref[row] = acc[row]
    odd = lax.axis_index("reg") % 2 == 1
    inner, outer = lines_of(inner_ref, begin[1], cols), lines_of(outer_ref, begin[2], cols)
    nodes = rows + 2 * SIDE
    for band, (yes, no) in enumerate(((inner, outer), (outer, inner))):
        for at, line in enumerate((0, 1) if band == 0 else (1, 0)):
            values = jnp.where(odd, yes[line], no[line])
            for off, hot in enumerate(hot_rows(values, rows, cols, line)):
                hot_ref[band, at, off, :nodes] = hot
                hot_ref[band, at, off, nodes:] = jnp.zeros((hot_ref.shape[3] - nodes, cols), BF16)


def band_kernel(
    from_inner, latent_ref, weights_ref, hot_ref, partial_ref, out_ref, one_ref, two_ref, paired_ref
):
    odd = lax.axis_index("reg") % 2
    band = 1 - odd if from_inner else odd
    latent = latent_ref[...]
    lanes, cols = hot_ref.shape[3:]
    outputs = weights_ref.shape[1]
    blank = jnp.zeros((lanes - latent.shape[0], latent.shape[1]), BF16)
    blocks = len(blocks_of(ABOVE))
    weights = weights_ref[pl.ds(band * blocks, blocks)]
    padded = jnp.concatenate([latent, blank], axis=0)
    single, double = shares_of(padded, weights[:TAPS]), shares_of(padded, weights[TAPS:])
    for off in range(TAPS):
        span = slice(off * lanes, (off + 1) * lanes)
        one_ref[:, span] = single[off]
        for row in range(2):
            two_ref[row * outputs : (row + 1) * outputs, span] = double[2 * off + row]
    depth = TAPS * lanes
    one = jnp.dot(one_ref[...], hot_ref[band, 0].reshape(depth, cols), preferred_element_type=F32)
    two = jnp.dot(two_ref[...], hot_ref[band, 1].reshape(depth, cols), preferred_element_type=F32)
    for row in range(2):
        total = partial_ref[row] + two[row * outputs : (row + 1) * outputs]
        total = total + jnp.where(band == row, one, 0.0)
        if from_inner:
            out_ref[row] = total
        else:
            for tile in range(cols // LANES):
                part = total[:, tile * LANES : (tile + 1) * LANES]
                paired_ref[tile, pl.ds(row, outputs, stride=2), :] = part
    if not from_inner:
        out_ch = out_ref.shape[0]
        tiles = [paired_ref[tile, : 2 * out_ch, :] for tile in range(cols // LANES)]
        out_ref[...] = jnp.concatenate(tiles, axis=1).astype(BF16).reshape(out_ref.shape)


def whole(memory=pltpu.VMEM):
    return pl.BlockSpec(memory_space=memory)


def struct(*shape, dtype=BF16):
    return jax.ShapeDtypeStruct(shape, dtype)


def params(limit):
    return pltpu.CompilerParams(vmem_limit_bytes=limit << 20)


def cost(flops, moved):
    return pl.CostEstimate(flops=int(flops), bytes_accessed=int(moved), transcendentals=0)


def shards(nodes, norm_gain, w_qkv, w_out, w_latent, neighbours, assignment, psi, w_dec):
    _, rows, width = nodes.shape
    channels = w_latent.shape[1]
    lat_rows, lon_cols = assignment.shape
    basis, _, out_ch = w_dec.shape
    sectors = lax.axis_size("lon")
    count = neighbours.shape[1]
    x = nodes.reshape(rows, width)
    gain = norm_gain.reshape(1, width)

    def paired(array, first):
        pairs = [(i, (i + 1) % sectors) for i in range(first, sectors, 2)]
        return lax.ppermute(array, "lon", pairs + [(j, i) for i, j in pairs])

    def exchanged(array, first):
        size = lax.axis_size("reg")
        pairs = [(i, i + 1) for i in range(first, size - 1, 2)]
        return lax.ppermute(array, "reg", pairs + [(j, i) for i, j in pairs])

    def in_hbm(*arrays):
        return [pltpu.with_memory_space_constraint(array, pltpu.HBM) for array in arrays]

    other = paired(x, 1)
    pair = paired(x, 0)

    outputs = -(-out_ch // ROWS) * ROWS
    head = width // HEADS
    members = LANES // head
    parts = HEADS // members
    def mixed(blocks, name, after):
        taps = psi.transpose(2, 3, 1, 0)
        mixing = w_dec.transpose(0, 2, 1)
        taps, mixing, after = lax.optimization_barrier((taps, mixing, after))
        weights = pl.pallas_call(
            functools.partial(mix_kernel, blocks),
            in_specs=[whole()] * 2,
            out_specs=whole(),
            out_shape=struct(len(blocks), outputs, channels),
            scratch_shapes=[
                pltpu.VMEM((2 * TAPS * TAPS, basis), F32),
                pltpu.VMEM((len(blocks) * ROWS, basis * ROWS), BF16),
            ],
            compiler_params=params(32),
            cost_estimate=cost(2e9, 6e6),
            name=name,
        )(taps, mixing)
        return weights, after

    own = pl.pallas_call(
        gather_kernel,
        in_specs=[whole(pltpu.HBM)] * 2,
        out_specs=whole(),
        out_shape=struct(rows + ROWS, width),
        scratch_shapes=[
            pltpu.VMEM(assignment.shape, jnp.int32),
            pltpu.SemaphoreType.DMA((2,)),
        ],
        compiler_params=params(32),
        cost_estimate=cost(1e3, 1e3),
        name="gather",
    )(*in_hbm(x, assignment))
    query, key, value, wk, wvt, choice, cells = pl.pallas_call(
        functools.partial(prepare_kernel, sectors),
        in_specs=[whole()] + [whole(pltpu.HBM)] * 4,
        out_specs=[whole()] * 7,
        out_shape=[
            struct(parts, LANES, members * rows),
            struct(rows, width),
            struct(width, rows),
            struct(width, width),
            struct(width, width),
            struct(count - 1, CANDIDATES, ROWS, LANES),
            struct(2 * ROWS, rows),
        ],
        scratch_shapes=[
            pltpu.VMEM((1, width), F32),
            pltpu.VMEM(w_qkv.shape, BF16),
            pltpu.SMEM(assignment.shape, jnp.int32),
            pltpu.SMEM(neighbours.shape, jnp.int32),
            pltpu.SemaphoreType.DMA((4,)),
        ],
        compiler_params=params(32),
        cost_estimate=cost(5e8, 1e6),
        name="prepare",
    )(own, *in_hbm(gain, w_qkv, assignment, neighbours))
    own, query = lax.optimization_barrier((own, query))
    message = jnp.concatenate([pair, own], axis=0)
    message_a = message
    other_a = other
    inner = exchanged(message_a, 0)
    outer = exchanged(message, 1)
    corner = exchanged(other, 1)
    beside = exchanged(other_a, 0)

    edges, other_m = mixed(blocks_of(ABOVE) + blocks_of(BELOW), "mix_edges", other)
    inner, edges = lax.optimization_barrier((inner, edges))
    top, summed = pl.pallas_call(
        early_kernel,
        in_specs=[whole()] * 11,
        out_specs=[whole()] * 2,
        out_shape=[
            struct(parts, 2, 8, members * rows, dtype=F32),
            struct(parts, LANES, rows, dtype=F32),
        ],
        scratch_shapes=[
            pltpu.VMEM(((1 + EARLY) * rows, width), BF16),
            pltpu.VMEM((parts, LANES + ROWS, (1 + EARLY) * rows), BF16),
        ],
        compiler_params=params(32),
        cost_estimate=cost(3e9, 6e6),
        name="early",
    )(choice, other, pair, inner, outer, gain, wk, wvt, query, key, value)
    state, latent, to_pair, to_other = pl.pallas_call(
        late_kernel,
        in_specs=[whole()] * 15,
        out_specs=[whole()] * 4,
        out_shape=[pltpu.VMEM((rows, width), BF16), struct(rows, channels)]
        + [struct(ROWS, channels)] * 2,
        compiler_params=params(32),
        cost_estimate=cost(3e9, 6e6),
        name="late",
    )(
        choice, cells, inner, outer, beside, corner,
        own, gain, wk, wvt, query, top, summed, w_out, w_latent,
    )

    from_pair = paired(to_pair, 0)
    from_other = paired(to_other, 1)
    middle, latent = mixed(blocks_of(OWN), "mix_own", latent)
    from_pair, middle = lax.optimization_barrier((from_pair, middle))
    extended = jnp.concatenate([latent, from_pair[:SIDE], from_other[:SIDE]], axis=0)
    far = exchanged(extended, 1)
    near = exchanged(extended, 0)

    lanes = -(-(rows + 2 * SIDE) // 256) * 256
    partial, hots, state = pl.pallas_call(
        functools.partial(own_kernel, (rows, 2 * rows, 2 * rows)),
        in_specs=[whole()] * 6,
        out_specs=[whole()] * 3,
        out_shape=[
            struct(lat_rows, outputs, lon_cols, dtype=F32),
            struct(2, 2, TAPS, lanes, lon_cols),
            struct(rows, width),
        ],
        compiler_params=params(32),
        cost_estimate=cost(1e9, 2.5e6),
        name="own_band",
    )(state, own, inner, outer, extended, middle)
    band_scratch = [
        pltpu.VMEM((outputs, TAPS * lanes), BF16),
        pltpu.VMEM((2 * outputs, TAPS * lanes), BF16),
        pltpu.VMEM((lon_cols // LANES, 2 * outputs, LANES), F32),
    ]
    partial = pl.pallas_call(
        functools.partial(band_kernel, True),
        in_specs=[whole()] * 4,
        out_specs=whole(),
        out_shape=struct(lat_rows, outputs, lon_cols, dtype=F32),
        scratch_shapes=band_scratch,
        compiler_params=params(32),
        cost_estimate=cost(1e9, 2.5e6),
        name="inner_band",
    )(near, edges, hots, partial)
    fields = pl.pallas_call(
        functools.partial(band_kernel, False),
        in_specs=[whole()] * 4,
        out_specs=whole(),
        out_shape=struct(out_ch, lat_rows, lon_cols),
        scratch_shapes=band_scratch,
        compiler_params=params(32),
        cost_estimate=cost(1e9, 2.5e6),
        name="outer_band",
    )(far, edges, hots, partial)
    return (state.reshape(1, rows, width), fields.reshape(1, out_ch, lat_rows, lon_cols))


def solution(mesh):
    in_specs = (
        P(None, ("reg", "lon"), None),
        P(),
        P(),
        P(),
        P(),
        P(("reg", "lon"), None),
        P("reg", "lon"),
        P(None, "reg", None, None),
        P(),
    )
    out_specs = (P(None, ("reg", "lon"), None), P(None, None, "reg", "lon"))
    return jax.shard_map(shards, mesh=mesh, in_specs=in_specs, out_specs=out_specs, check_vma=False)
```

```python
import functools
import math

import jax
import jax.numpy as jnp
from jax import lax
from jax.experimental import pallas as pl
from jax.experimental.pallas import tpu as pltpu
from jax.sharding import PartitionSpec as P

HEADS = 16
REACH = 2
TAPS = 2 * REACH + 1
SIDE = 8
ROWS = 16
LANES = 128
EARLY = 2
CANDIDATES = 5
F32 = jnp.float32
BF16 = jnp.bfloat16
NT = (((1,), (1,)), ((), ()))

ABOVE = ((-2, (0,)), (-1, (0, 1)))
OWN = ((0, (0, 1)), (1, (0, 1)))
BELOW = ((3, (1,)), (2, (0, 1)))


def blocks_of(band):
    return [
        (out_row, src - out_row + REACH, off)
        for src, out_rows in band
        for off in range(TAPS)
        for out_row in out_rows
    ]


def iota(shape, dim):
    return lax.broadcasted_iota(jnp.int32, shape, dim)


def normalise(rows, gain):
    values = rows.astype(F32)
    center = values - jnp.mean(values, axis=-1, keepdims=True)
    spread = jnp.mean(center * center, axis=-1, keepdims=True)
    return (center * lax.rsqrt(spread + 1e-05) * gain).astype(BF16)


def mix_kernel(blocks, psi_ref, dec_ref, mixed_ref, psi_rows_ref, taps_ref):
    basis, out_ch, channels = dec_ref.shape
    depth = basis * ROWS
    for tap in range(TAPS):
        for off in range(TAPS):
            at = (tap * TAPS + off) * 2
            psi_rows_ref[at : at + 2, :] = psi_ref[tap, off]
    spread = (iota((basis, depth), 1) // ROWS == iota((basis, depth), 0)).astype(F32)
    expanded = jnp.dot(psi_rows_ref[...], spread, preferred_element_type=F32)
    pick = iota((ROWS, depth), 1) % ROWS == iota((ROWS, depth), 0)
    for at, (out_row, tap, off) in enumerate(blocks):
        source = (tap * TAPS + off) * 2 + out_row
        taps = jnp.broadcast_to(expanded[source : source + 1], (ROWS, depth))
        taps_ref[at * ROWS : (at + 1) * ROWS, :] = jnp.where(pick, taps, 0.0).astype(BF16)
    for first in range(0, out_ch, ROWS):
        size = min(ROWS, out_ch - first)
        pieces = []
        for base in range(basis):
            pieces.append(dec_ref[base, first : first + size, :])
            if size < ROWS:
                pieces.append(jnp.zeros((ROWS - size, channels), BF16))
        mixing = jnp.concatenate(pieces, axis=0)
        mixed = jnp.dot(taps_ref[...], mixing, preferred_element_type=F32).astype(BF16)
        mixed_ref[:, first : first + ROWS, :] = mixed.reshape(len(blocks), ROWS, channels)


def listed_blocks(sectors, listed_ref):
    reg_here, lon_here = lax.axis_index("reg"), lax.axis_index("lon")
    toward = 1 - 2 * (reg_here % 2)
    found = []
    for at in range(1, listed_ref.shape[1]):
        block = listed_ref[0, at]
        step_reg = (block // sectors - reg_here) * toward
        step_lon = (block % sectors - lon_here + 1 + sectors) % sectors - 1
        lean = step_lon * (1 - 2 * (lon_here % 2))
        side = jnp.where(lean == 0, 0, jnp.where(lean > 0, 1, 4))
        ahead = jnp.where(lean < 0, 0, 1)
        behind = jnp.where(lean < 0, 7, 4 + side)
        found.append(jnp.where(step_reg == 0, ahead, jnp.where(step_reg > 0, 2 + side, behind)))
    for low in range(len(found)):
        for high in range(low + 1, len(found)):
            less, more = jnp.minimum(found[low], found[high]), jnp.maximum(found[low], found[high])
            found[low], found[high] = less, more
    return found


def gather_kernel(x_hbm, assign_hbm, own_ref, assign_ref, sems):
    rows = own_ref.shape[0] - ROWS
    copies = [
        pltpu.make_async_copy(assign_hbm, assign_ref, sems.at[0]),
        pltpu.make_async_copy(x_hbm, own_ref.at[pl.ds(0, rows)], sems.at[1]),
    ]
    for copy in copies:
        copy.start()
    copies[0].wait()
    local = lax.rem(assign_ref[...], rows).astype(F32)
    line = jnp.concatenate([local[:1], local[1:2]], axis=1)
    line = jnp.broadcast_to(line, (ROWS, line.shape[1]))
    own_ref[rows:] = jnp.where(iota(line.shape, 0) == 0, line, 0.0).astype(BF16)
    copies[1].wait()


def prepare_kernel(
    sectors,
    own_ref, gain_hbm, wqkv_hbm, assign_hbm, listed_hbm,
    query_ref, key_ref, value_ref, wk_ref, wvt_ref, choice_ref, cells_ref,
    gain_ref, wqkv_ref, cell_ref, listed_ref, sems,
):
    copies = [
        pltpu.make_async_copy(source, target, sems.at[at])
        for at, (source, target) in enumerate(
            (
                (gain_hbm, gain_ref),
                (wqkv_hbm, wqkv_ref),
                (assign_hbm, cell_ref),
                (listed_hbm, listed_ref),
            )
        )
    ]
    for copy in copies:
        copy.start()
    rows, width = key_ref.shape
    group, members = query_ref.shape[1], query_ref.shape[2] // rows
    head = group // members
    for copy in copies[2:]:
        copy.wait()
    for at, number in enumerate(listed_blocks(sectors, listed_ref)):
        for candidate in range(CANDIDATES):
            same = jnp.full((ROWS, LANES), jnp.where(number == at + candidate, 1.0, 0.0), F32)
            choice_ref[at, candidate] = same.astype(BF16)
    lat_rows, lon_cols = cell_ref.shape
    place, node = iota((ROWS, rows), 0), iota((ROWS, rows), 1)
    odd = lax.axis_index("lon") % 2
    for side, first in enumerate(((1 - odd) * (lon_cols - REACH), odd * (lon_cols - REACH))):
        hit = jnp.zeros((ROWS, rows), F32)
        for row in range(lat_rows):
            for col in range(REACH):
                cell = cell_ref[row, first + col] % rows
                hit = jnp.where((place == row * REACH + col) & (node == cell), 1.0, hit)
        cells_ref[side * ROWS : (side + 1) * ROWS] = hit.astype(BF16)
    copies[0].wait()
    normed = normalise(own_ref[:rows], gain_ref[...])
    copies[1].wait()
    query = jnp.dot(normed, wqkv_ref[:, :width], preferred_element_type=F32)
    query_t = (query * (math.log2(math.e) / head**0.5)).T.astype(BF16)
    mask = (iota((group, members * rows), 0) // head) == (iota((group, members * rows), 1) // rows)
    for part in range(width // group):
        piece = query_t[part * group : (part + 1) * group]
        wide = jnp.concatenate([piece] * members, axis=1)
        query_ref[part] = jnp.where(mask, wide, jnp.zeros_like(wide))
    wk = wqkv_ref[:, width : 2 * width]
    wk_ref[...] = wk
    key_ref[...] = jnp.dot(normed, wk, preferred_element_type=F32).astype(BF16)
    wvt = wqkv_ref[:, 2 * width :].astype(F32).T.astype(BF16)
    wvt_ref[...] = wvt
    value_ref[...] = lax.dot_general(wvt, normed, NT, preferred_element_type=F32).astype(BF16)


def chosen(entries, rows, choice_ref, candidates):
    tall, wide = rows // ROWS, candidates[-1].shape[1] // LANES
    near = []
    for entry in entries:
        total = None
        for at in range(CANDIDATES):
            weight = jnp.concatenate([choice_ref[entry, at]] * wide, axis=1)
            part = candidates[entry + at] * jnp.concatenate([weight] * tall, axis=0)
            total = part if total is None else total + part
        near.append(total)
    return jnp.concatenate(near, axis=0)


def project(nodes, gain, wk_ref, wvt_ref):
    normed = normalise(nodes, gain)
    keys = jnp.dot(normed, wk_ref[...], preferred_element_type=F32).astype(BF16)
    values = lax.dot_general(wvt_ref[...], normed, NT, preferred_element_type=F32).astype(BF16)
    return keys, values


def own_heads(summed, rows):
    members = summed.shape[1] // rows
    head = summed.shape[0] // members
    return [
        summed[at * head : (at + 1) * head, at * rows : (at + 1) * rows] for at in range(members)
    ]


def early_kernel(
    choice_ref, other_ref, pair_ref, inner_ref, outer_ref,
    gain_ref, wk_ref, wvt_ref, query_ref, key_ref, value_ref,
    top_ref, sum_ref, keys_ref, values_ref,
):
    rows = key_ref.shape[0]
    parts, group, _ = query_ref.shape
    candidates = [other_ref[...], pair_ref[...]]
    candidates += [ref[rows : 2 * rows] if center else ref[:rows] for ref in (inner_ref, outer_ref) for center in (1, 0)]
    nodes = chosen(range(EARLY), rows, choice_ref, candidates)
    keys, values = project(nodes, gain_ref[...], wk_ref, wvt_ref)
    keys_ref[:rows] = key_ref[...]
    keys_ref[rows:] = keys
    for part in range(parts):
        span = slice(part * group, (part + 1) * group)
        values_ref[part, :group, :rows] = value_ref[span]
        values_ref[part, :group, rows:] = values[span]
        values_ref[part, group:, :] = jnp.ones((ROWS, keys_ref.shape[0]), BF16)

    spans = [slice(part * group, (part + 1) * group) for part in range(parts)]
    scores = [
        jnp.dot(keys_ref[:, span], query_ref[part], preferred_element_type=F32)
        for part, span in enumerate(spans)
    ]
    tops = [jnp.max(one, axis=0, keepdims=True) for one in scores]
    expos = [jnp.exp2(one - top).astype(BF16) for one, top in zip(scores, tops)]
    sums = [
        jnp.dot(values_ref[part], expo, preferred_element_type=F32) for part, expo in enumerate(expos)
    ]
    for part, (top, summed) in enumerate(zip(tops, sums)):
        top_ref[part, 0] = jnp.broadcast_to(top, top_ref.shape[2:])
        top_ref[part, 1] = jnp.broadcast_to(summed[group : group + 1], top_ref.shape[2:])
        sum_ref[part] = jnp.concatenate(own_heads(summed[:group], rows), axis=0)


def late_kernel(
    choice_ref, cells_ref, inner_ref, outer_ref, beside_ref, corner_ref,
    own_ref, gain_ref, wk_ref, wvt_ref, query_ref, top_ref, sum_ref, wout_ref, wlat_ref,
    state_ref, latent_ref, to_pair_ref, to_other_ref,
):
    rows, width = state_ref.shape
    parts, group, lanes = query_ref.shape
    members = lanes // rows
    head = group // members
    candidates = [None, None]
    candidates += [ref[rows : 2 * rows] if center else ref[:rows] for ref in (inner_ref, outer_ref) for center in (1, 0)]
    candidates += [beside_ref[...], corner_ref[...]]
    nodes = chosen(range(EARLY, choice_ref.shape[0]), rows, choice_ref, candidates)
    keys, values = project(nodes, gain_ref[...], wk_ref, wvt_ref)
    ones = jnp.ones((ROWS, nodes.shape[0]), BF16)
    spans = [slice(part * group, (part + 1) * group) for part in range(parts)]
    scores = [
        jnp.dot(keys[:, span], query_ref[part], preferred_element_type=F32)
        for part, span in enumerate(spans)
    ]
    befores = [top_ref[part, 0, :1] for part in range(parts)]
    tops = [
        jnp.maximum(before, jnp.max(one, axis=0, keepdims=True))
        for before, one in zip(befores, scores)
    ]
    expos = [jnp.exp2(one - top).astype(BF16) for one, top in zip(scores, tops)]
    sums = [
        jnp.dot(jnp.concatenate([values[span], ones], axis=0), expo, preferred_element_type=F32)
        for span, expo in zip(spans, expos)
    ]
    attended = []
    for part, summed in enumerate(sums):
        shrink = jnp.exp2(befores[part] - tops[part])
        share = 1.0 / (summed[group : group + 1] + top_ref[part, 1, :1] * shrink)
        merged = []
        for member, piece in enumerate(own_heads(summed[:group], rows)):
            span = slice(member * rows, (member + 1) * rows)
            earlier = sum_ref[part, member * head : (member + 1) * head]
            merged.append((piece + earlier * shrink[:, span]) * share[:, span])
        attended.append(jnp.concatenate(merged, axis=0).T.astype(BF16))
    attended = jnp.concatenate(attended, axis=1)
    state = (
        own_ref[:rows].astype(F32)
        + jnp.dot(attended, wout_ref[...], preferred_element_type=F32)
    ).astype(BF16)
    state_ref[...] = state
    value = jnp.dot(state, wlat_ref[...], preferred_element_type=F32)
    latent = (value / (1.0 + jnp.exp(-value))).astype(BF16)
    latent_ref[...] = latent
    cells = jnp.dot(cells_ref[...], latent, preferred_element_type=F32).astype(BF16)
    to_pair_ref[...] = cells[:ROWS]
    to_other_ref[...] = cells[ROWS:]


def hot_rows(values, rows, cols, line):
    odd = lax.axis_index("lon") % 2
    column = iota((8, cols), 1)
    node = iota((rows + 2 * SIDE, cols), 0).astype(F32)
    for off in range(TAPS):
        step = off - REACH
        where = jnp.broadcast_to(values, (8, cols))
        if step:
            where = pltpu.roll(where, (-step) % cols, 1)
        reach = column + step
        before = (rows + (1 - odd) * SIDE + REACH * line + reach + REACH).astype(F32)
        after = (rows + odd * SIDE + REACH * line + reach - cols).astype(F32)
        where = jnp.where(reach < 0, before, jnp.where(reach >= cols, after, where))
        yield jnp.where(node == where[:1], 1.0, 0.0).astype(BF16)


def shares_of(latent, weights):
    blocks, outputs, channels = weights.shape
    shares = lax.dot_general(
        weights.reshape(blocks * outputs, channels), latent, NT, preferred_element_type=F32
    ).astype(BF16)
    return [shares[at * outputs : (at + 1) * outputs] for at in range(blocks)]


def lines_of(line_ref, start, cols):
    values = line_ref[start : start + ROWS, :].astype(F32)
    return values[:1, :cols], values[:1, cols:]


def own_kernel(
    begin, state_ref, own_ref, inner_ref, outer_ref, latent_ref, weights_ref,
    out_ref, hot_ref, kept_ref,
):
    kept_ref[...] = state_ref[...]
    cols = out_ref.shape[2]
    rows = latent_ref.shape[0] - 2 * SIDE
    own = lines_of(own_ref, begin[0], cols)
    table = [list(hot_rows(own[line], rows, cols, line)) for line in range(2)]
    acc = [None, None]
    for (out_row, tap, off), share in zip(
        blocks_of(OWN), shares_of(latent_ref[...], weights_ref[...])
    ):
        line = out_row + tap - REACH
        piece = jnp.dot(share, table[line][off], preferred_element_type=F32)
        acc[out_row] = piece if acc[out_row] is None else acc[out_row] + piece
    for row in range(2):
        out_ref[row] = acc[row]
    odd = lax.axis_index("reg") % 2 == 1
    inner, outer = lines_of(inner_ref, begin[1], cols), lines_of(outer_ref, begin[2], cols)
    nodes = rows + 2 * SIDE
    for band, (yes, no) in enumerate(((inner, outer), (outer, inner))):
        for at, line in enumerate((0, 1) if band == 0 else (1, 0)):
            values = jnp.where(odd, yes[line], no[line])
            for off, hot in enumerate(hot_rows(values, rows, cols, line)):
                hot_ref[band, at, off, :nodes] = hot
                hot_ref[band, at, off, nodes:] = jnp.zeros((hot_ref.shape[3] - nodes, cols), BF16)


def band_kernel(
    from_inner, latent_ref, weights_ref, hot_ref, partial_ref, out_ref, one_ref, two_ref, paired_ref
):
    odd = lax.axis_index("reg") % 2
    band = 1 - odd if from_inner else odd
    latent = latent_ref[...]
    lanes, cols = hot_ref.shape[3:]
    outputs = weights_ref.shape[1]
    blank = jnp.zeros((lanes - latent.shape[0], latent.shape[1]), BF16)
    blocks = len(blocks_of(ABOVE))
    weights = weights_ref[pl.ds(band * blocks, blocks)]
    shares = shares_of(jnp.concatenate([latent, blank], axis=0), weights)
    for off in range(TAPS):
        span = slice(off * lanes, (off + 1) * lanes)
        one_ref[:, span] = shares[off]
        for row in range(2):
            two_ref[row * outputs : (row + 1) * outputs, span] = shares[TAPS + 2 * off + row]
    depth = TAPS * lanes
    one = jnp.dot(one_ref[...], hot_ref[band, 0].reshape(depth, cols), preferred_element_type=F32)
    two = jnp.dot(two_ref[...], hot_ref[band, 1].reshape(depth, cols), preferred_element_type=F32)
    for row in range(2):
        total = partial_ref[row] + two[row * outputs : (row + 1) * outputs]
        total = total + jnp.where(band == row, one, 0.0)
        if from_inner:
            out_ref[row] = total
        else:
            for tile in range(cols // LANES):
                part = total[:, tile * LANES : (tile + 1) * LANES]
                paired_ref[tile, pl.ds(row, outputs, stride=2), :] = part
    if not from_inner:
        out_ch = out_ref.shape[0]
        tiles = [paired_ref[tile, : 2 * out_ch, :] for tile in range(cols // LANES)]
        out_ref[...] = jnp.concatenate(tiles, axis=1).astype(BF16).reshape(out_ref.shape)


def whole(memory=pltpu.VMEM):
    return pl.BlockSpec(memory_space=memory)


def struct(*shape, dtype=BF16):
    return jax.ShapeDtypeStruct(shape, dtype)


def params(limit):
    return pltpu.CompilerParams(vmem_limit_bytes=limit << 20)


def cost(flops, moved):
    return pl.CostEstimate(flops=int(flops), bytes_accessed=int(moved), transcendentals=0)


def shards(nodes, norm_gain, w_qkv, w_out, w_latent, neighbours, assignment, psi, w_dec):
    _, rows, width = nodes.shape
    channels = w_latent.shape[1]
    lat_rows, lon_cols = assignment.shape
    basis, _, out_ch = w_dec.shape
    sectors = lax.axis_size("lon")
    count = neighbours.shape[1]
    x = nodes.reshape(rows, width)
    gain = norm_gain.reshape(1, width)

    def paired(array, first):
        pairs = [(i, (i + 1) % sectors) for i in range(first, sectors, 2)]
        return lax.ppermute(array, "lon", pairs + [(j, i) for i, j in pairs])

    def exchanged(array, first):
        size = lax.axis_size("reg")
        pairs = [(i, i + 1) for i in range(first, size - 1, 2)]
        return lax.ppermute(array, "reg", pairs + [(j, i) for i, j in pairs])

    def in_hbm(*arrays):
        return [pltpu.with_memory_space_constraint(array, pltpu.HBM) for array in arrays]

    other = paired(x, 1)
    pair = paired(x, 0)

    outputs = -(-out_ch // ROWS) * ROWS
    head = width // HEADS
    members = LANES // head
    parts = HEADS // members
    def mixed(blocks, name, after):
        taps = psi.transpose(2, 3, 1, 0)
        mixing = w_dec.transpose(0, 2, 1)
        taps, mixing, after = lax.optimization_barrier((taps, mixing, after))
        weights = pl.pallas_call(
            functools.partial(mix_kernel, blocks),
            in_specs=[whole()] * 2,
            out_specs=whole(),
            out_shape=struct(len(blocks), outputs, channels),
            scratch_shapes=[
                pltpu.VMEM((2 * TAPS * TAPS, basis), F32),
                pltpu.VMEM((len(blocks) * ROWS, basis * ROWS), BF16),
            ],
            compiler_params=params(32),
            cost_estimate=cost(2e9, 6e6),
            name=name,
        )(taps, mixing)
        return weights, after

    own = pl.pallas_call(
        gather_kernel,
        in_specs=[whole(pltpu.HBM)] * 2,
        out_specs=whole(),
        out_shape=struct(rows + ROWS, width),
        scratch_shapes=[
            pltpu.VMEM(assignment.shape, jnp.int32),
            pltpu.SemaphoreType.DMA((2,)),
        ],
        compiler_params=params(32),
        cost_estimate=cost(1e3, 1e3),
        name="gather",
    )(*in_hbm(x, assignment))
    query, key, value, wk, wvt, choice, cells = pl.pallas_call(
        functools.partial(prepare_kernel, sectors),
        in_specs=[whole()] + [whole(pltpu.HBM)] * 4,
        out_specs=[whole()] * 7,
        out_shape=[
            struct(parts, LANES, members * rows),
            struct(rows, width),
            struct(width, rows),
            struct(width, width),
            struct(width, width),
            struct(count - 1, CANDIDATES, ROWS, LANES),
            struct(2 * ROWS, rows),
        ],
        scratch_shapes=[
            pltpu.VMEM((1, width), F32),
            pltpu.VMEM(w_qkv.shape, BF16),
            pltpu.SMEM(assignment.shape, jnp.int32),
            pltpu.SMEM(neighbours.shape, jnp.int32),
            pltpu.SemaphoreType.DMA((4,)),
        ],
        compiler_params=params(32),
        cost_estimate=cost(5e8, 1e6),
        name="prepare",
    )(own, *in_hbm(gain, w_qkv, assignment, neighbours))
    own, query = lax.optimization_barrier((own, query))
    message = jnp.concatenate([pair, own], axis=0)
    message_a = message
    other_a = other
    inner = exchanged(message_a, 0)
    outer = exchanged(message, 1)
    corner = exchanged(other, 1)
    beside = exchanged(other_a, 0)

    edges, other_m = mixed(blocks_of(ABOVE) + blocks_of(BELOW), "mix_edges", other)
    inner, edges = lax.optimization_barrier((inner, edges))
    top, summed = pl.pallas_call(
        early_kernel,
        in_specs=[whole()] * 11,
        out_specs=[whole()] * 2,
        out_shape=[
            struct(parts, 2, 8, members * rows, dtype=F32),
            struct(parts, LANES, rows, dtype=F32),
        ],
        scratch_shapes=[
            pltpu.VMEM(((1 + EARLY) * rows, width), BF16),
            pltpu.VMEM((parts, LANES + ROWS, (1 + EARLY) * rows), BF16),
        ],
        compiler_params=params(32),
        cost_estimate=cost(3e9, 6e6),
        name="early",
    )(choice, other, pair, inner, outer, gain, wk, wvt, query, key, value)
    state, latent, to_pair, to_other = pl.pallas_call(
        late_kernel,
        in_specs=[whole()] * 15,
        out_specs=[whole()] * 4,
        out_shape=[pltpu.VMEM((rows, width), BF16), struct(rows, channels)]
        + [struct(ROWS, channels)] * 2,
        compiler_params=params(32),
        cost_estimate=cost(3e9, 6e6),
        name="late",
    )(
        choice, cells, inner, outer, beside, corner,
        own, gain, wk, wvt, query, top, summed, w_out, w_latent,
    )

    from_pair = paired(to_pair[:SIDE], 0)
    from_other = paired(to_other[:SIDE], 1)
    middle, latent = mixed(blocks_of(OWN), "mix_own", latent)
    from_pair, middle = lax.optimization_barrier((from_pair, middle))
    extended = jnp.concatenate([latent, from_pair, from_other], axis=0)
    far = exchanged(extended, 1)
    near = exchanged(extended, 0)

    lanes = -(-(rows + 2 * SIDE) // 256) * 256
    partial, hots, state = pl.pallas_call(
        functools.partial(own_kernel, (rows, 2 * rows, 2 * rows)),
        in_specs=[whole()] * 6,
        out_specs=[whole()] * 3,
        out_shape=[
            struct(lat_rows, outputs, lon_cols, dtype=F32),
            struct(2, 2, TAPS, lanes, lon_cols),
            struct(rows, width),
        ],
        compiler_params=params(32),
        cost_estimate=cost(1e9, 2.5e6),
        name="own_band",
    )(state, own, inner, outer, extended, middle)
    band_scratch = [
        pltpu.VMEM((outputs, TAPS * lanes), BF16),
        pltpu.VMEM((2 * outputs, TAPS * lanes), BF16),
        pltpu.VMEM((lon_cols // LANES, 2 * outputs, LANES), F32),
    ]
    partial = pl.pallas_call(
        functools.partial(band_kernel, True),
        in_specs=[whole()] * 4,
        out_specs=whole(),
        out_shape=struct(lat_rows, outputs, lon_cols, dtype=F32),
        scratch_shapes=band_scratch,
        compiler_params=params(32),
        cost_estimate=cost(1e9, 2.5e6),
        name="inner_band",
    )(near, edges, hots, partial)
    fields = pl.pallas_call(
        functools.partial(band_kernel, False),
        in_specs=[whole()] * 4,
        out_specs=whole(),
        out_shape=struct(out_ch, lat_rows, lon_cols),
        scratch_shapes=band_scratch,
        compiler_params=params(32),
        cost_estimate=cost(1e9, 2.5e6),
        name="outer_band",
    )(far, edges, hots, partial)
    return (state.reshape(1, rows, width), fields.reshape(1, out_ch, lat_rows, lon_cols))


def solution(mesh):
    in_specs = (
        P(None, ("reg", "lon"), None),
        P(),
        P(),
        P(),
        P(),
        P(("reg", "lon"), None),
        P("reg", "lon"),
        P(None, "reg", None, None),
        P(),
    )
    out_specs = (P(None, ("reg", "lon"), None), P(None, None, "reg", "lon"))
    return jax.shard_map(shards, mesh=mesh, in_specs=in_specs, out_specs=out_specs, check_vma=False)
```
